32 devices in a mesh: gx: 8 (over z, x), gy: 4 (over y, core).
Axes of the slice: x: 2, y: 2, z: 4, core: 2. Of those that a mesh axis runs over, the one named last changes fastest.
Arguments:
- source: float32 [5, 4, 4, 4, 16, 8, 128], P(None, None, None, None, 'gx', 'gy'), may hold values from -18 to 18
- jacobian: float32 [3, 5, 5, 16, 8, 128], P(None, None, None, 'gx', 'gy'), may hold values from -1.8 to 1.8
- damping: float32 [16, 8, 128], P('gx', 'gy'), may hold values from 0.3 to 1.2
- orient: int32 [3, 16, 8, 128], P(None, 'gx', 'gy'), may hold values 0 or 1
- smoother: bfloat16 [5, 5, 4, 4, 4, 16, 8, 128], P(None, None, None, None, None, 'gx', 'gy'), may hold values from -0.4 to 0.4, as said below
- coarse_smoother: bfloat16 [5, 5, 2, 2, 2, 16, 8, 128], P(None, None, None, None, None, 'gx', 'gy'), may hold values from -0.61 to 1.11, as said below
Outputs:
- corrected: float32 [5, 4, 4, 4, 16, 8, 128], P(None, None, None, None, 'gx', 'gy')
The draws below stay inside these ranges and needn't reach their ends.
Inputs may be any that keep to these rules, and one draw needn't show every extreme that they name: `smoother`: each 5 x 5 block is a positive node scale times the identity plus independent entries. `coarse_smoother`: each 5 x 5 block is a positive node scale times the identity plus independent entries.
All inputs are finite; a program needn't handle non-finite values. No bound on the sum of `orient` on one device may be relied on, other than what follows from the above.
Results may differ from the reference program's by a relative error of at most 0.0003.
Values sent between devices are 32-bit elements; how exact they have to be, the bound alone decides.
No kernel may reach another device: no remote copies, remote signals or barrier semaphores. Data moves between devices by JAX's collectives and lax.ppermute only.
A program may use at most 64 MiB of HBM per device.

```python
import math
import jax
import jax.numpy as jnp
import numpy as np

VARS = 5
NODES = 4
CNODES = 2
CSWEEPS = 3
NZE = 128
NXE = 16
NYE = 8


def block_inverse(key, node_count, scale_low, scale_high, normal_weight):
    noise_key = jax.random.fold_in(key, 0)
    scale_key = jax.random.fold_in(key, 2)
    shape_full = (5, 5, node_count, node_count, node_count, NXE, NYE, NZE)
    noise = normal_weight * jnp.clip(jax.random.normal(noise_key, shape_full, jnp.float32), -4.0, 4.0)
    scales = jax.random.uniform(scale_key, (1, 1, node_count, node_count, node_count, NXE, NYE, NZE), jnp.float32, scale_low, scale_high)
    identity = jnp.eye(5, dtype=jnp.float32).reshape(5, 5, 1, 1, 1, 1, 1, 1)
    return ((identity + noise) * scales).astype(jnp.bfloat16)


def draw_smoother(key, part):
    key = jax.random.fold_in(key, 5)
    return block_inverse(key, NODES, 0.06, 0.18, 0.3)


def draw_coarse_smoother(key, part):
    key = jax.random.fold_in(key, 9)
    return block_inverse(key, CNODES, 0.25, 0.5, 0.3)


def touch_ends(values, key, low, largest):
    spot = [jax.random.randint(jax.random.fold_in(key, axis), (), 0, length) for axis, length in enumerate(values.shape)]
    widest = values.shape.index(max(values.shape))
    beside = spot[:widest] + [(spot[widest] + 1) % values.shape[widest]] + spot[widest + 1:]
    return values.at[tuple(spot)].set(low).at[tuple(beside)].set(largest)


def block_scale(stream_key, extent, cuts, low, largest):
    gain = 1.0
    for dim, parts in cuts:
        heights = jax.random.uniform(jax.random.fold_in(jax.random.fold_in(stream_key, 6), dim), (parts,), jnp.float32, low / len(cuts), largest / len(cuts))
        gain = gain * jnp.repeat(jnp.exp(heights), extent[dim] // parts).reshape((-1,) + (1,) * (len(extent) - 1 - dim))
    return gain


def normal_values(own_key, shape, deviation, bound, shards=(), held_as=jnp.bfloat16):
    loudness = block_scale(own_key, shape, shards, -0.22, 0.18) if shards else 1.0
    drawn = jax.random.normal(own_key, shape, jnp.float32) * deviation * loudness
    return jnp.minimum(jnp.maximum(drawn, -bound), bound).astype(held_as)


def setup_inputs(seed: int = 0) -> dict:
    keys = jax.random.split(jax.random.key(seed), 7)
    source = normal_values(keys[0], (VARS, NODES, NODES, NODES, NXE, NYE, NZE), 3.0, 18.0, ((4, 8), (5, 4)), jnp.float32)
    jacobian = normal_values(keys[1], (3, VARS, VARS, NXE, NYE, NZE), 0.3, 1.8, ((3, 8), (4, 4)), jnp.float32)
    damping = jnp.clip(0.3 + 0.90000004 * jax.random.uniform(keys[2], (NXE, NYE, NZE), jnp.float32) ** block_scale(keys[2], (NXE, NYE, NZE), ((0, 8), (1, 4)), -0.2, 0.2), 0.3, 1.2)
    orient = touch_ends((jax.random.randint(keys[3], (3, NXE, NYE, NZE), 0, 2) < 1).astype(jnp.int32), jax.random.fold_in(keys[3], 1), 0, 1)
    smoother = draw_smoother(jax.random.fold_in(keys[6], 71), 0)
    coarse_smoother = draw_coarse_smoother(jax.random.fold_in(keys[6], 71), 0)
    return dict(source=source, jacobian=jacobian, damping=damping, orient=orient, smoother=smoother, coarse_smoother=coarse_smoother)


SIGMA_SHIFT = 2.0
OMEGA_DAMP = 0.8

def lobatto(node_count):
    if node_count == 2:
        node_points = np.array([-1.0, 1.0])
    else:
        node_points = np.array([-1.0, -1.0 / math.sqrt(5.0), 1.0 / math.sqrt(5.0), 1.0])
    weights = np.ones(node_count)
    for row_index in range(node_count):
        for col_index in range(node_count):
            if row_index != col_index:
                weights[row_index] = weights[row_index] / (node_points[row_index] - node_points[col_index])
    slopes = np.zeros((node_count, node_count))
    for row_index in range(node_count):
        for col_index in range(node_count):
            if row_index != col_index:
                slopes[row_index, col_index] = weights[col_index] / weights[row_index] / (node_points[row_index] - node_points[col_index])
        slopes[row_index, row_index] = -np.sum(slopes[row_index])
    return (node_points, slopes)

def interp_table():
    node_points = lobatto(4)[0]
    return np.stack([(1.0 - node_points) / 2.0, (1.0 + node_points) / 2.0], 1)

def apply_along(grid_field, matrix, node_axis):
    pieces = [jnp.take(grid_field, column, axis=node_axis) for column in range(matrix.shape[1])]
    outputs = []
    for target in range(matrix.shape[0]):
        running = float(matrix[target, 0]) * pieces[0]
        for column in range(1, matrix.shape[1]):
            running = running + float(matrix[target, column]) * pieces[column]
        outputs.append(running)
    return jnp.stack(outputs, axis=node_axis)

def mix_vars(matrix, grid_field):
    parts_out = []
    for out_var in range(5):
        running = None
        for in_var in range(5):
            weight_now = matrix[out_var, in_var].astype(jnp.float32)
            weight_now = weight_now.reshape((1,) * (grid_field.ndim - 1 - weight_now.ndim) + weight_now.shape)
            product_term = weight_now * grid_field[in_var]
            running = product_term if in_var == 0 else running + product_term
        parts_out.append(running)
    return jnp.stack(parts_out)

def face_slot(direction, node_index):
    return (slice(None),) * (direction + 1) + (node_index,)

def operator_apply(grid_field, jacobian, damping, orient, fetch):
    node_count = grid_field.shape[1]
    slope_table = lobatto(node_count)[1]
    lift_scale = node_count * (node_count - 1) / 2.0
    result_sum = SIGMA_SHIFT * grid_field
    for direction in range(3):
        flux_term = mix_vars(jacobian[direction], grid_field)
        result_sum = result_sum + apply_along(flux_term, slope_table, direction + 1)
        low_trace = jnp.take(grid_field, 0, axis=direction + 1)
        high_trace = jnp.take(grid_field, node_count - 1, axis=direction + 1)
        turned_flag = orient[direction] == 1
        high_turned = jnp.where(turned_flag, jnp.flip(high_trace, 1), high_trace)
        left_in, right_in = fetch(direction, low_trace, high_turned)
        right_in = jnp.where(turned_flag, jnp.flip(right_in, 1), right_in)
        jump_right = right_in - high_trace
        jump_left = left_in - low_trace
        upper_term = 0.5 * lift_scale * (mix_vars(jacobian[direction], jump_right) - damping * jump_right)
        lower_term = -0.5 * lift_scale * (mix_vars(jacobian[direction], jump_left) + damping * jump_left)
        result_sum = result_sum.at[face_slot(direction, node_count - 1)].add(upper_term)
        result_sum = result_sum.at[face_slot(direction, 0)].add(lower_term)
    return result_sum

def roll_fetch(direction, low_trace, high_turned):
    elem_axis = 3 + direction
    return (jnp.roll(high_turned, 1, axis=elem_axis), jnp.roll(low_trace, -1, axis=elem_axis))

def restrict(grid_field):
    interp = interp_table().T
    for node_axis in (1, 2, 3):
        grid_field = apply_along(grid_field, interp, node_axis)
    return grid_field

def prolong(grid_field):
    interp = interp_table()
    for node_axis in (1, 2, 3):
        grid_field = apply_along(grid_field, interp, node_axis)
    return grid_field

def coarse_solve(coarse_rhs, jacobian, damping, orient, inverse, fetch):
    coarse = OMEGA_DAMP * mix_vars(inverse, coarse_rhs)
    for sweep_index in range(CSWEEPS - 1):
        update = coarse_rhs - operator_apply(coarse, jacobian, damping, orient, fetch)
        coarse = coarse + OMEGA_DAMP * mix_vars(inverse, update)
    return coarse

def reference(source, jacobian, damping, orient, smoother, coarse_smoother):
    first_pass = OMEGA_DAMP * mix_vars(smoother, source)
    update = source - operator_apply(first_pass, jacobian, damping, orient, roll_fetch)
    second = first_pass + OMEGA_DAMP * mix_vars(smoother, update)
    residual = source - operator_apply(second, jacobian, damping, orient, roll_fetch)
    coarse_rhs = restrict(residual)
    coarse = coarse_solve(coarse_rhs, jacobian, damping, orient, coarse_smoother, roll_fetch)
    return second + prolong(coarse)
```

```python
import functools
import math

import jax
import jax.numpy as jnp
import numpy as np
from jax import lax
from jax.experimental import pallas as pl
from jax.experimental.pallas import tpu as pltpu
from jax.sharding import PartitionSpec as P


F32 = jnp.float32
OMEGA = 0.8
H4 = 3.0
ROOT = 1.0 / math.sqrt(5.0)
NEAR = (1.0 + ROOT) / 2.0
FAR = (1.0 - ROOT) / 2.0


def lobatto_slopes():
    points = np.array([-1.0, -ROOT, ROOT, 1.0])
    weights = np.ones(4)
    for i in range(4):
        for j in range(4):
            if i != j:
                weights[i] = weights[i] / (points[i] - points[j])
    slopes = np.zeros((4, 4))
    for i in range(4):
        for j in range(4):
            if i != j:
                slopes[i, j] = weights[j] / weights[i] / (points[i] - points[j])
        slopes[i, i] = -np.sum(slopes[i])
    return slopes


D4 = lobatto_slopes()


def rows():
    return lax.broadcasted_iota(jnp.int32, (8, 128), 0)


def x_low():
    return (rows() & 2) == 0


def y_low():
    return (rows() & 1) == 0


def c_low():
    return (rows() & 4) == 0


def sroll(value, shift):
    return pltpu.roll(value, shift % 8, 0)


def lroll(value, shift):
    return pltpu.roll(value, shift % 128, 1)


def twice(value):
    return jnp.concatenate([value, value], axis=0)


def axis_low(direction):
    return (x_low(), 2) if direction == 0 else (y_low(), 1)


def pack_low(first, second, direction):
    low, step = axis_low(direction)
    return jnp.where(low, first, sroll(second, step))


def pack_high(first, second, direction):
    low, step = axis_low(direction)
    return jnp.where(low, sroll(first, -step), second)


def slopes_along(u0, u1, u2, u3):
    e0, o0, e1, o1 = u0 + u3, u0 - u3, u1 + u2, u1 - u2
    diff = e1 - e0
    even_a = float((D4[0, 1] + D4[0, 2]) / 2.0) * diff
    even_b = float((D4[1, 2] - 0.0) / 2.0) * diff
    odd_a = float((D4[0, 0] - D4[0, 3]) / 2.0) * o0 + float((D4[0, 1] - D4[0, 2]) / 2.0) * o1
    odd_b = float((D4[1, 0] - D4[1, 3]) / 2.0) * o0 - float(D4[1, 2] / 2.0) * o1
    return even_a + odd_a, even_b + odd_b, odd_b - even_b, odd_a - even_a


def mix(matrix, fields):
    out = []
    for o in range(5):
        total = matrix[o][0] * fields[0]
        for i in range(1, 5):
            total = total + matrix[o][i] * fields[i]
        out.append(total)
    return out


def parity(axis):
    return lax.rem(lax.axis_index(axis), 2) == 0


def put_pair(even_ref, odd_ref, index, low_face, high_face, is_even):
    even_ref[index] = jnp.where(is_even, high_face, low_face)
    odd_ref[index] = jnp.where(is_even, low_face, high_face)


def fine_faces(u_ref, flag_ref, xe, xo, ye, yo):
    even_x, even_y = parity("gx"), parity("gy")
    fx, fy = flag_ref[0] != 0, flag_ref[1] != 0
    for v in range(5):
        for n in range(4):
            low = pack_low(u_ref[v, 0, n, 0], u_ref[v, 0, n, 1], 0)
            h = [jnp.where(fx, u_ref[v, 3, 3 - n, q], u_ref[v, 3, n, q]) for q in range(2)]
            put_pair(xe, xo, (v, n), low, pack_high(h[0], h[1], 0), even_x)
            low = pack_low(u_ref[v, n, 0, 0], u_ref[v, n, 0, 1], 1)
            h = [jnp.where(fy, u_ref[v, 3 - n, 3, q], u_ref[v, n, 3, q]) for q in range(2)]
            put_pair(ye, yo, (v, n), low, pack_high(h[0], h[1], 1), even_y)


def first_kernel(src_hbm, smooth_hbm, orient_ref, src_ref, smooth_ref, u_ref, flag_ref, xe, xo, ye, yo, sems):
    copies = []
    for slot, a in enumerate((0, 3, 1, 2)):
        pair = (
            pltpu.make_async_copy(src_hbm.at[:, a], src_ref.at[:, a], sems.at[0, slot]),
            pltpu.make_async_copy(smooth_hbm.at[:, a], smooth_ref.at[:, a], sems.at[1, slot]),
        )
        for one in pair:
            one.start()
        copies.append((a, pair))
    for d in range(3):
        flag_ref[d] = twice(orient_ref[d])
    for a, pair in copies:
        for one in pair:
            one.wait()

        def one_line(b, carry, a=a):
            src = [[src_ref[v, a, b, q] for q in range(2)] for v in range(5)]
            for o in range(5):
                total = [None, None]
                for i in range(5):
                    block = smooth_ref[5 * o + i, a, b].astype(F32)
                    for q in range(2):
                        term = block[8 * q : 8 * q + 8] * src[i][q]
                        total[q] = term if i == 0 else total[q] + term
                for q in range(2):
                    u_ref[o, a, b, q] = OMEGA * total[q]
            return carry

        lax.fori_loop(0, 4, one_line, 0)
    fine_faces(u_ref, flag_ref, xe, xo, ye, yo)


def prepare_tables(jac_ref, damp_ref, jac8_ref, damp8_ref, face_ref):
    damp = twice(damp_ref[...])
    damp8_ref[...] = damp
    for d in range(3):
        for k in range(25):
            value = twice(jac_ref[25 * d + k])
            jac8_ref[25 * d + k] = value
            if d < 2:
                low, step = axis_low(d)
                diagonal = k % 6 == 0
                upper = H4 * (value - damp if diagonal else value)
                lower = H4 * (value + damp if diagonal else value)
                face_ref[2 * d, k] = jnp.where(low, sroll(upper, -step), upper)
                face_ref[2 * d + 1, k] = jnp.where(low, lower, sroll(lower, step))


def volume(src_ref, u_ref, flag_ref, jac_ref, damp_ref, acc_ref):
    damp = H4 * damp_ref[...]

    def jacobian(d):
        return [[jac_ref[25 * d + 5 * o + i] for i in range(5)] for o in range(5)]

    def along(direction):
        low, step = axis_low(direction)
        flag = flag_ref[direction] != 0
        flag_before = sroll(flag_ref[direction], step) != 0

        def at(v, n, other, q):
            return (v, n, other, q) if direction == 0 else (v, other, n, q)

        def step_fn(j, carry):
            other, q = j // 2, j % 2
            u = [[u_ref[at(v, n, other, q)] for n in range(4)] for v in range(5)]
            waves = []
            jumps = []
            for v in range(5):
                back_low, back_high = u_ref[at(v, 0, 3 - other, q)], u_ref[at(v, 3, 3 - other, q)]
                right = sroll(jnp.where(flag_before, back_low, u[v][0]), -step)
                left = sroll(jnp.where(flag, back_high, u[v][3]), step)
                jump_right = jnp.where(low, right, 0.0) - u[v][3]
                jump_left = jnp.where(low, 0.0, left) - u[v][0]
                w = list(slopes_along(*u[v]))
                w[3] = w[3] + H4 * jump_right
                w[0] = w[0] - H4 * jump_left
                waves.append(w)
                jumps.append((damp * jump_left, None, None, damp * jump_right))
            matrix = jacobian(direction)
            for n in range(4):
                flux = mix(matrix, [waves[v][n] for v in range(5)])
                for v in range(5):
                    if direction == 0:
                        total = src_ref[at(v, n, other, q)] - 2.0 * u[v][n]
                    else:
                        total = acc_ref[at(v, n, other, q)]
                    total = total - flux[v]
                    if jumps[v][n] is not None:
                        total = total + jumps[v][n]
                    acc_ref[at(v, n, other, q)] = total
            return carry

        lax.fori_loop(0, 8, step_fn, 0)

    along(0)
    along(1)

    low = c_low()
    flag = jnp.where(low, lroll(flag_ref[2], 1), flag_ref[2]) != 0
    damp_z = damp
    coef = [
        [jnp.where(low, float(D4[2 * p, c]), float(D4[2 * p + 1, c ^ 1])).astype(F32) for c in range(4)]
        for p in range(2)
    ]

    def step_z(j, carry):
        a0, b = j // 4, j % 4
        here = (a0, 3 - a0)
        u = [[[u_ref[v, a, b, q] for q in range(2)] for v in range(5)] for a in here]
        turned = [[[sroll(u[s][v][q], 4) for q in range(2)] for v in range(5)] for s in range(2)]
        beside = []
        for s in range(2):
            line = []
            for v in range(5):
                face = jnp.where(low, turned[s][v][1], turned[s][v][0])
                line.append(jnp.where(low, lroll(face, 1), lroll(face, -1)))
            beside.append(line)
        matrix = jacobian(2)
        for s in range(2):
            waves = [[], []]
            jumps = []
            for v in range(5):
                own = jnp.where(low, u[s][v][0], u[s][v][1])
                jump = jnp.where(flag, beside[1 - s][v], beside[s][v]) - own
                jumps.append(damp_z * jump)
                lifted = H4 * jump
                for p in range(2):
                    w = coef[p][0] * u[s][v][0] + coef[p][1] * turned[s][v][0]
                    w = w + (coef[p][2] * u[s][v][1] + coef[p][3] * turned[s][v][1])
                    w = w - jnp.where(low, lifted, 0.0) if p == 0 else w + jnp.where(low, 0.0, lifted)
                    waves[p].append(w)
            for p in range(2):
                flux = mix(matrix, waves[p])
                for v in range(5):
                    part = jnp.where(low, jumps[v], 0.0) if p == 0 else jnp.where(low, 0.0, jumps[v])
                    acc_ref[v, here[s], b, p] = acc_ref[v, here[s], b, p] - flux[v] + part
        return carry

    lax.fori_loop(0, 8, step_z, 0)


def first_volume_kernel(src_ref, u_ref, flag_ref, jac_ref, damp_ref, acc_ref, jac8_ref, damp8_ref, face_ref):
    prepare_tables(jac_ref, damp_ref, jac8_ref, damp8_ref, face_ref)
    volume(src_ref, u_ref, flag_ref, jac8_ref, damp8_ref, acc_ref)


def second_volume_kernel(src_ref, u_ref, flag_ref, jac8_ref, damp8_ref, acc_ref):
    volume(src_ref, u_ref, flag_ref, jac8_ref, damp8_ref, acc_ref)


def remote_parts(even_refs, odd_refs, flag_ref, face_ref, part_ref):
    for d, axis in ((0, "gx"), (1, "gy")):
        is_even = parity(axis)
        low, step = axis_low(d)
        flag = flag_ref[d]
        flag = jnp.where(low, sroll(flag, -step), flag) != 0
        even, odd = even_refs[d], odd_refs[d]
        matrix = [[face_ref[2 * d, 5 * o + i] for i in range(5)] for o in range(5)]
        for n in range(4):
            take = lambda v, m: jnp.where(is_even, even[v, m], odd[v, m])
            right = [jnp.where(flag, take(v, 3 - n), take(v, n)) for v in range(5)]
            for v, value in enumerate(mix(matrix, right)):
                part_ref[2 * d, v, n, 0] = jnp.where(low, 0.0, -sroll(value, step))
                part_ref[2 * d, v, n, 1] = jnp.where(low, 0.0, -value)
        matrix = [[face_ref[2 * d + 1, 5 * o + i] for i in range(5)] for o in range(5)]
        for n in range(4):
            left = [jnp.where(is_even, odd[v, n], even[v, n]) for v in range(5)]
            for v, value in enumerate(mix(matrix, left)):
                part_ref[2 * d + 1, v, n, 0] = jnp.where(low, value, 0.0)
                part_ref[2 * d + 1, v, n, 1] = jnp.where(low, sroll(value, -step), 0.0)


def whole(acc_ref, part_ref, v, a, b, q):
    total = acc_ref[v, a, b, q]
    if a == 3:
        total = total + part_ref[0, v, b, q]
    if a == 0:
        total = total + part_ref[1, v, b, q]
    if b == 3:
        total = total + part_ref[2, v, a, q]
    if b == 0:
        total = total + part_ref[3, v, a, q]
    return total


def second_kernel(
    acc_ref, u_ref, smooth_ref, flag_ref, face_ref, rxe, rxo, rye, ryo, out_ref, xe, xo, ye, yo, part_ref
):
    remote_parts((rxe, rye), (rxo, ryo), flag_ref, face_ref, part_ref)
    for a in range(4):
        for b in range(4):
            left = [[whole(acc_ref, part_ref, v, a, b, q) for q in range(2)] for v in range(5)]
            for o in range(5):
                total = [None, None]
                for i in range(5):
                    block = smooth_ref[5 * o + i, a, b].astype(F32)
                    for q in range(2):
                        term = block[8 * q : 8 * q + 8] * left[i][q]
                        total[q] = term if i == 0 else total[q] + term
                for q in range(2):
                    out_ref[o, a, b, q] = u_ref[o, a, b, q] + OMEGA * total[q]
    fine_faces(out_ref, flag_ref, xe, xo, ye, yo)


def coarse_smooth(smooth_ref, fields):
    out = [[[None, None], [None, None]] for _ in range(5)]
    for i in range(2):
        for o in range(5):
            total = [None, None]
            for k in range(5):
                block = smooth_ref[5 * o + k, i].astype(F32)
                for j in range(2):
                    term = block[8 * j : 8 * j + 8] * fields[k][i][j]
                    total[j] = term if k == 0 else total[j] + term
            for j in range(2):
                out[o][i][j] = OMEGA * total[j]
    return out


def coarse_faces(field, flag_ref, xe, xo, ye, yo):
    even_x, even_y = parity("gx"), parity("gy")
    fx, fy = flag_ref[0] != 0, flag_ref[1] != 0
    for v in range(5):
        c = field[v]
        low = pack_low(c[0][0], c[0][1], 0)
        h = [jnp.where(fx, c[1][1 - j], c[1][j]) for j in range(2)]
        put_pair(xe, xo, v, low, pack_high(h[0], h[1], 0), even_x)
        low = pack_low(c[0][0], c[1][0], 1)
        h = [jnp.where(fy, c[1 - i][1], c[i][1]) for i in range(2)]
        put_pair(ye, yo, v, low, pack_high(h[0], h[1], 1), even_y)


def restrict_kernel(
    acc_ref, flag_ref, face_ref, smooth_ref, rxe, rxo, rye, ryo, rhs_ref, c_ref, xe, xo, ye, yo, part_ref
):
    remote_parts((rxe, rye), (rxo, ryo), flag_ref, face_ref, part_ref)
    low = c_low()
    rhs = [[[None, None], [None, None]] for _ in range(5)]
    for v in range(5):
        halves = [[[None, None], [None, None]] for _ in range(2)]
        for q in range(2):
            for b in range(4):
                r = [whole(acc_ref, part_ref, v, a, b, q) for a in range(4)]
                ends = (r[0] + NEAR * r[1] + FAR * r[2], r[3] + NEAR * r[2] + FAR * r[1])
                near = (1.0, NEAR, FAR, 0.0)[b], (0.0, FAR, NEAR, 1.0)[b]
                for i in range(2):
                    for j in range(2):
                        if near[j] == 0.0:
                            continue
                        term = ends[i] if near[j] == 1.0 else near[j] * ends[i]
                        halves[q][i][j] = term if halves[q][i][j] is None else halves[q][i][j] + term
        for i in range(2):
            for j in range(2):
                first, second = halves[0][i][j], halves[1][i][j]
                middle = jnp.where(low, second, first)
                value = jnp.where(low, first, second) + FAR * middle + NEAR * sroll(middle, 4)
                rhs[v][i][j] = value
                rhs_ref[v, i, j] = value
    c = coarse_smooth(smooth_ref, rhs)
    for v in range(5):
        for i in range(2):
            for j in range(2):
                c_ref[v, i, j] = c[v][i][j]
    coarse_faces(c, flag_ref, xe, xo, ye, yo)


def coarse_step(c_ref, rhs_ref, smooth_ref, flag_ref, jac_ref, damp_ref, rxe, rxo, rye, ryo):
    damp = 0.5 * damp_ref[...]
    c = [[[c_ref[v, i, j] for j in range(2)] for i in range(2)] for v in range(5)]
    acc = [[[rhs_ref[v, i, j] - 2.0 * c[v][i][j] for j in range(2)] for i in range(2)] for v in range(5)]
    for d, axis in ((0, "gx"), (1, "gy")):
        is_even = parity(axis)
        low, step = axis_low(d)
        flag = flag_ref[d] != 0
        matrix = [[jac_ref[25 * d + 5 * o + i] for i in range(5)] for o in range(5)]
        even, odd = ((rxe, rxo), (rye, ryo))[d]
        at = (lambda n, m: (n, m)) if d == 0 else (lambda n, m: (m, n))
        waves = [[[None] * 5, [None] * 5] for _ in range(2)]
        for v in range(5):
            got_right = jnp.where(is_even, even[v], odd[v])
            got_left = jnp.where(is_even, odd[v], even[v])
            lo = [c[v][at(0, m)[0]][at(0, m)[1]] for m in range(2)]
            hi = [c[v][at(1, m)[0]][at(1, m)[1]] for m in range(2)]
            right = [
                jnp.where(low, sroll(lo[0], -step), sroll(got_right, step)),
                jnp.where(low, sroll(lo[1], -step), got_right),
            ]
            right = [jnp.where(flag, right[1 - m], right[m]) for m in range(2)]
            left = [sroll(jnp.where(flag, hi[1 - m], hi[m]), step) for m in range(2)]
            left = [jnp.where(low, got_left, left[0]), jnp.where(low, sroll(got_left, -step), left[1])]
            for m in range(2):
                waves[1][m][v] = 0.5 * (right[m] - lo[m])
                waves[0][m][v] = 0.5 * (hi[m] - left[m])
                i, j = at(1, m)
                acc[v][i][j] = acc[v][i][j] + damp * (right[m] - hi[m])
                i, j = at(0, m)
                acc[v][i][j] = acc[v][i][j] + damp * (left[m] - lo[m])
        for n in range(2):
            for m in range(2):
                i, j = at(n, m)
                for v, value in enumerate(mix(matrix, waves[n][m])):
                    acc[v][i][j] = acc[v][i][j] - value
    low = c_low()
    flag = jnp.where(low, lroll(flag_ref[2], 1), flag_ref[2]) != 0
    half = jnp.where(low, 0.5, -0.5).astype(F32)
    matrix = [[jac_ref[50 + 5 * o + i] for i in range(5)] for o in range(5)]
    turned = [[[sroll(c[v][i][j], 4) for j in range(2)] for i in range(2)] for v in range(5)]
    beside = [
        [[jnp.where(low, lroll(t, 1), lroll(t, -1)) for t in turned[v][i]] for i in range(2)] for v in range(5)
    ]
    for i in range(2):
        for j in range(2):
            wave = []
            for v in range(5):
                next_to = jnp.where(flag, beside[v][1 - i][j], beside[v][i][j])
                wave.append(half * (turned[v][i][j] - next_to))
                acc[v][i][j] = acc[v][i][j] + damp * (next_to - c[v][i][j])
            for v, value in enumerate(mix(matrix, wave)):
                acc[v][i][j] = acc[v][i][j] - value
    change = coarse_smooth(smooth_ref, acc)
    return [[[c[v][i][j] + change[v][i][j] for j in range(2)] for i in range(2)] for v in range(5)]


def coarse_kernel(
    c_ref, rhs_ref, smooth_ref, flag_ref, jac_ref, damp_ref, rxe, rxo, rye, ryo, out_ref, xe, xo, ye, yo
):
    c = coarse_step(c_ref, rhs_ref, smooth_ref, flag_ref, jac_ref, damp_ref, rxe, rxo, rye, ryo)
    for v in range(5):
        for i in range(2):
            for j in range(2):
                out_ref[v, i, j] = c[v][i][j]
    coarse_faces(c, flag_ref, xe, xo, ye, yo)


def spread(first, second):
    return first, NEAR * first + FAR * second, FAR * first + NEAR * second, second


def last_kernel(
    c_ref, rhs_ref, smooth_ref, flag_ref, jac_ref, damp_ref, rxe, rxo, rye, ryo, second_ref, out_hbm, out_ref, sems
):
    c = coarse_step(c_ref, rhs_ref, smooth_ref, flag_ref, jac_ref, damp_ref, rxe, rxo, rye, ryo)
    low = c_low()
    copies = []
    for v in range(5):
        by_c = [[None, None], [None, None]]
        for i in range(2):
            for j in range(2):
                value = c[v][i][j]
                inner = FAR * value + NEAR * sroll(value, 4)
                by_c[i][j] = (jnp.where(low, value, inner), jnp.where(low, inner, value))
        for q in range(2):
            lines = [spread(by_c[i][0][q], by_c[i][1][q]) for i in range(2)]
            for b in range(4):
                for a, value in enumerate(spread(lines[0][b], lines[1][b])):
                    out_ref[v, a, b, q] = second_ref[v, a, b, q] + value
        copy = pltpu.make_async_copy(out_ref.at[v], out_hbm.at[v], sems.at[v])
        copy.start()
        copies.append(copy)
    for copy in copies:
        copy.wait()


FINE = (5, 4, 4, 2, 8, 128)
FINE_MESSAGE = (5, 4, 8, 128)
COARSE = (5, 2, 2, 8, 128)
COARSE_MESSAGE = (5, 8, 128)


def vmem(shape, dtype=F32):
    return pltpu.VMEM(shape, dtype)


def here(array):
    return pltpu.with_memory_space_constraint(array, pltpu.VMEM)


def call(kernel, args, outs, in_hbm=(), out_hbm=(), scratch=(), flops=0):
    in_specs = [
        pl.BlockSpec(memory_space=pltpu.HBM if k in in_hbm else pltpu.VMEM) for k in range(len(args))
    ]
    out_specs = [
        pl.BlockSpec(memory_space=pltpu.HBM if k in out_hbm else pltpu.VMEM) for k in range(len(outs))
    ]
    args = [pltpu.with_memory_space_constraint(a, pltpu.HBM) if k in in_hbm else here(a) for k, a in enumerate(args)]
    return pl.pallas_call(
        kernel,
        out_shape=outs,
        in_specs=in_specs,
        out_specs=out_specs,
        scratch_shapes=scratch,
        compiler_params=pltpu.CompilerParams(vmem_limit_bytes=8 * 2**20),
        cost_estimate=pl.CostEstimate(flops=flops, bytes_accessed=4 * 2**20, transcendentals=0),
    )(*args)


def partners(axis):
    size = lax.axis_size(axis)
    even = [(i, i ^ 1) for i in range(size)]
    odd = [(i, (i - 1) % size if i % 2 == 0 else (i + 1) % size) for i in range(size)]
    return even, odd


def exchange(xe, xo, ye, yo):
    even_x, odd_x = partners("gx")
    even_y, odd_y = partners("gy")
    xo = lax.ppermute(xo, "gx", odd_x)
    xe = lax.ppermute(xe, "gx", even_x)
    yo = lax.ppermute(yo, "gy", odd_y)
    ye = lax.ppermute(ye, "gy", even_y)
    return xe, xo, ye, yo


def body(source, jacobian, damping, orient, smoother, coarse_smoother):
    source = source.reshape(FINE)
    smoother = smoother.reshape(25, 4, 4, 16, 128)
    coarse_smoother = coarse_smoother.reshape(25, 2, 16, 128)
    jacobian = jacobian.reshape(75, 4, 128)
    damping = damping.reshape(4, 128)
    orient = orient.reshape(3, 4, 128)
    fine_messages = [vmem(FINE_MESSAGE)] * 4
    coarse_messages = [vmem(COARSE_MESSAGE)] * 4

    source, smoother, first, flag, *sent = call(
        first_kernel,
        (source, smoother, orient),
        [vmem(FINE), vmem(smoother.shape, smoother.dtype), vmem(FINE), vmem((3, 8, 128), jnp.int32)] + fine_messages,
        in_hbm=(0, 1),
        scratch=[pltpu.SemaphoreType.DMA((2, 4))],
        flops=2 * 25 * 64 * 512,
    )
    got = exchange(*sent)
    acc, jac8, damp8, face = call(
        first_volume_kernel,
        (source, first, flag, jacobian, damping),
        [vmem(FINE), vmem((75, 8, 128)), vmem((8, 128)), vmem((4, 25, 8, 128))],
        flops=9 * 2**20,
    )
    part = pltpu.VMEM((4, 5, 4, 2, 8, 128), F32)
    second, *sent = call(
        second_kernel,
        (acc, first, smoother, flag, face, *got),
        [vmem(FINE)] + fine_messages,
        scratch=[part],
        flops=3 * 2**20,
    )
    got = exchange(*sent)
    (acc,) = call(second_volume_kernel, (source, second, flag, jac8, damp8), [vmem(FINE)], flops=9 * 2**20)
    rhs, coarse, *sent = call(
        restrict_kernel,
        (acc, flag, face, coarse_smoother, *got),
        [vmem(COARSE), vmem(COARSE)] + coarse_messages,
        scratch=[part],
        flops=3 * 2**20,
    )
    got = exchange(*sent)
    coarse, *sent = call(
        coarse_kernel,
        (coarse, rhs, coarse_smoother, flag, jac8, damp8, *got),
        [vmem(COARSE)] + coarse_messages,
        flops=2**20,
    )
    got = exchange(*sent)
    (out,) = call(
        last_kernel,
        (coarse, rhs, coarse_smoother, flag, jac8, damp8, *got, second),
        [jax.ShapeDtypeStruct(FINE, F32)],
        out_hbm=(0,),
        scratch=[pltpu.VMEM(FINE, F32), pltpu.SemaphoreType.DMA((5,))],
        flops=2**20,
    )
    return out.reshape(5, 4, 4, 4, 2, 2, 128)


def solution(mesh):
    in_specs = (
        P(None, None, None, None, "gx", "gy", None),
        P(None, None, None, "gx", "gy", None),
        P("gx", "gy", None),
        P(None, "gx", "gy", None),
        P(None, None, None, None, None, "gx", "gy", None),
        P(None, None, None, None, None, "gx", "gy", None),
    )
    out_specs = P(None, None, None, None, "gx", "gy", None)
    return jax.shard_map(body, mesh=mesh, in_specs=in_specs, out_specs=out_specs, check_vma=False)
```

```python
import functools
import math

import jax
import jax.numpy as jnp
import numpy as np
from jax import lax
from jax.experimental import pallas as pl
from jax.experimental.pallas import tpu as pltpu
from jax.sharding import PartitionSpec as P


F32 = jnp.float32
OMEGA = 0.8
H4 = 3.0
ROOT = 1.0 / math.sqrt(5.0)
NEAR = (1.0 + ROOT) / 2.0
FAR = (1.0 - ROOT) / 2.0


def lobatto_slopes():
    points = np.array([-1.0, -ROOT, ROOT, 1.0])
    weights = np.ones(4)
    for i in range(4):
        for j in range(4):
            if i != j:
                weights[i] = weights[i] / (points[i] - points[j])
    slopes = np.zeros((4, 4))
    for i in range(4):
        for j in range(4):
            if i != j:
                slopes[i, j] = weights[j] / weights[i] / (points[i] - points[j])
        slopes[i, i] = -np.sum(slopes[i])
    return slopes


D4 = lobatto_slopes()


def rows():
    return lax.broadcasted_iota(jnp.int32, (8, 128), 0)


def x_low():
    return (rows() & 2) == 0


def y_low():
    return (rows() & 1) == 0


def c_low():
    return (rows() & 4) == 0


def sroll(value, shift):
    return pltpu.roll(value, shift % 8, 0)


def lroll(value, shift):
    return pltpu.roll(value, shift % 128, 1)


def twice(value):
    return jnp.concatenate([value, value], axis=0)


def axis_low(direction):
    return (x_low(), 2) if direction == 0 else (y_low(), 1)


def pack_low(first, second, direction):
    low, step = axis_low(direction)
    return jnp.where(low, first, sroll(second, step))


def pack_high(first, second, direction):
    low, step = axis_low(direction)
    return jnp.where(low, sroll(first, -step), second)


def slopes_along(u0, u1, u2, u3):
    e0, o0, e1, o1 = u0 + u3, u0 - u3, u1 + u2, u1 - u2
    diff = e1 - e0
    even_a = float((D4[0, 1] + D4[0, 2]) / 2.0) * diff
    even_b = float((D4[1, 2] - 0.0) / 2.0) * diff
    odd_a = float((D4[0, 0] - D4[0, 3]) / 2.0) * o0 + float((D4[0, 1] - D4[0, 2]) / 2.0) * o1
    odd_b = float((D4[1, 0] - D4[1, 3]) / 2.0) * o0 - float(D4[1, 2] / 2.0) * o1
    return even_a + odd_a, even_b + odd_b, odd_b - even_b, odd_a - even_a


def mix(matrix, fields):
    out = []
    for o in range(5):
        total = matrix[o][0] * fields[0]
        for i in range(1, 5):
            total = total + matrix[o][i] * fields[i]
        out.append(total)
    return out


def parity(axis):
    return lax.rem(lax.axis_index(axis), 2) == 0


def put_pair(even_ref, odd_ref, index, low_face, high_face, is_even):
    even_ref[index] = jnp.where(is_even, high_face, low_face)
    odd_ref[index] = jnp.where(is_even, low_face, high_face)


def partner_half(both_ref):
    return both_ref.at[jnp.where(parity("gx"), 0, 1)]


def fine_faces(u_ref, flag_ref, xe, xo, ye, yo):
    even_x, even_y = parity("gx"), parity("gy")
    fx, fy = flag_ref[0] != 0, flag_ref[1] != 0
    for v in range(5):
        for n in range(4):
            low = pack_low(u_ref[v, 0, n, 0], u_ref[v, 0, n, 1], 0)
            h = [jnp.where(fx, u_ref[v, 3, 3 - n, q], u_ref[v, 3, n, q]) for q in range(2)]
            put_pair(xe, xo, (v, n), low, pack_high(h[0], h[1], 0), even_x)
            low = pack_low(u_ref[v, n, 0, 0], u_ref[v, n, 0, 1], 1)
            h = [jnp.where(fy, u_ref[v, 3 - n, 3, q], u_ref[v, n, 3, q]) for q in range(2)]
            put_pair(ye, yo, (v, n), low, pack_high(h[0], h[1], 1), even_y)


def first_kernel(
    src_hbm, smooth_hbm, orient_hbm, src_ref, smooth_ref, u_ref, flag_ref, xe, xo, ye, yo, sems, orient_ref, orient_sem
):
    orient_copy = pltpu.make_async_copy(orient_hbm, orient_ref, orient_sem)
    orient_copy.start()
    copies = []
    for slot, a in enumerate((0, 3, 1, 2)):
        pair = (
            pltpu.make_async_copy(src_hbm.at[:, a], src_ref.at[:, a], sems.at[0, slot]),
            pltpu.make_async_copy(smooth_hbm.at[:, a], smooth_ref.at[:, a], sems.at[1, slot]),
        )
        for one in pair:
            one.start()
        copies.append((a, pair))
    orient_copy.wait()
    for d in range(3):
        flag_ref[d] = twice(orient_ref[d])
    for a, pair in copies:
        for one in pair:
            one.wait()

        def one_line(b, carry, a=a):
            src = [[src_ref[v, a, b, q] for q in range(2)] for v in range(5)]
            for o in range(5):
                total = [None, None]
                for i in range(5):
                    block = smooth_ref[5 * o + i, a, b].astype(F32)
                    for q in range(2):
                        term = block[8 * q : 8 * q + 8] * src[i][q]
                        total[q] = term if i == 0 else total[q] + term
                for q in range(2):
                    u_ref[o, a, b, q] = OMEGA * total[q]
            return carry

        lax.fori_loop(0, 4, one_line, 0)
    fine_faces(u_ref, flag_ref, xe, xo, ye, yo)


def prepare_tables(jac_ref, damp_ref, jac8_ref, damp8_ref, face_ref):
    damp = twice(damp_ref[...])
    damp8_ref[...] = damp
    for d in range(3):
        for k in range(25):
            value = twice(jac_ref[25 * d + k])
            jac8_ref[25 * d + k] = value
            if d < 2:
                low, step = axis_low(d)
                diagonal = k % 6 == 0
                upper = H4 * (value - damp if diagonal else value)
                lower = H4 * (value + damp if diagonal else value)
                face_ref[2 * d, k] = jnp.where(low, sroll(upper, -step), upper)
                face_ref[2 * d + 1, k] = jnp.where(low, lower, sroll(lower, step))


def volume(src_ref, u_ref, flag_ref, jac_ref, damp_ref, acc_ref):
    damp = H4 * damp_ref[...]

    def jacobian(d):
        return [[jac_ref[25 * d + 5 * o + i] for i in range(5)] for o in range(5)]

    def along(direction):
        low, step = axis_low(direction)
        flag = flag_ref[direction] != 0
        flag_before = sroll(flag_ref[direction], step) != 0

        def at(v, n, other, q):
            return (v, n, other, q) if direction == 0 else (v, other, n, q)

        def step_fn(j, carry):
            other, q = j // 2, j % 2
            u = [[u_ref[at(v, n, other, q)] for n in range(4)] for v in range(5)]
            waves = []
            jumps = []
            for v in range(5):
                back_low, back_high = u_ref[at(v, 0, 3 - other, q)], u_ref[at(v, 3, 3 - other, q)]
                right = sroll(jnp.where(flag_before, back_low, u[v][0]), -step)
                left = sroll(jnp.where(flag, back_high, u[v][3]), step)
                jump_right = jnp.where(low, right, 0.0) - u[v][3]
                jump_left = jnp.where(low, 0.0, left) - u[v][0]
                w = list(slopes_along(*u[v]))
                w[3] = w[3] + H4 * jump_right
                w[0] = w[0] - H4 * jump_left
                waves.append(w)
                jumps.append((damp * jump_left, None, None, damp * jump_right))
            matrix = jacobian(direction)
            for n in range(4):
                flux = mix(matrix, [waves[v][n] for v in range(5)])
                for v in range(5):
                    if direction == 0:
                        total = src_ref[at(v, n, other, q)] - 2.0 * u[v][n]
                    else:
                        total = acc_ref[at(v, n, other, q)]
                    total = total - flux[v]
                    if jumps[v][n] is not None:
                        total = total + jumps[v][n]
                    acc_ref[at(v, n, other, q)] = total
            return carry

        lax.fori_loop(0, 8, step_fn, 0)

    along(0)
    along(1)

    low = c_low()
    flag = jnp.where(low, lroll(flag_ref[2], 1), flag_ref[2]) != 0
    damp_z = damp
    coef = [
        [jnp.where(low, float(D4[2 * p, c]), float(D4[2 * p + 1, c ^ 1])).astype(F32) for c in range(4)]
        for p in range(2)
    ]

    def step_z(j, carry):
        a0, b = j // 4, j % 4
        here = (a0, 3 - a0)
        u = [[[u_ref[v, a, b, q] for q in range(2)] for v in range(5)] for a in here]
        turned = [[[sroll(u[s][v][q], 4) for q in range(2)] for v in range(5)] for s in range(2)]
        beside = []
        for s in range(2):
            line = []
            for v in range(5):
                face = jnp.where(low, turned[s][v][1], turned[s][v][0])
                line.append(jnp.where(low, lroll(face, 1), lroll(face, -1)))
            beside.append(line)
        matrix = jacobian(2)
        for s in range(2):
            waves = [[], []]
            jumps = []
            for v in range(5):
                own = jnp.where(low, u[s][v][0], u[s][v][1])
                jump = jnp.where(flag, beside[1 - s][v], beside[s][v]) - own
                jumps.append(damp_z * jump)
                lifted = H4 * jump
                for p in range(2):
                    w = coef[p][0] * u[s][v][0] + coef[p][1] * turned[s][v][0]
                    w = w + (coef[p][2] * u[s][v][1] + coef[p][3] * turned[s][v][1])
                    w = w - jnp.where(low, lifted, 0.0) if p == 0 else w + jnp.where(low, 0.0, lifted)
                    waves[p].append(w)
            for p in range(2):
                flux = mix(matrix, waves[p])
                for v in range(5):
                    part = jnp.where(low, jumps[v], 0.0) if p == 0 else jnp.where(low, 0.0, jumps[v])
                    acc_ref[v, here[s], b, p] = acc_ref[v, here[s], b, p] - flux[v] + part
        return carry

    lax.fori_loop(0, 8, step_z, 0)


def first_volume_kernel(src_ref, u_ref, flag_ref, jac_ref, damp_ref, acc_ref, jac8_ref, damp8_ref, face_ref):
    prepare_tables(jac_ref, damp_ref, jac8_ref, damp8_ref, face_ref)
    volume(src_ref, u_ref, flag_ref, jac8_ref, damp8_ref, acc_ref)


def second_volume_kernel(src_ref, u_ref, flag_ref, jac8_ref, damp8_ref, acc_ref):
    volume(src_ref, u_ref, flag_ref, jac8_ref, damp8_ref, acc_ref)


def remote_parts(even_refs, odd_refs, flag_ref, face_ref, part_ref):
    for d, axis in ((0, "gx"), (1, "gy")):
        is_even = parity(axis)
        low, step = axis_low(d)
        flag = flag_ref[d]
        flag = jnp.where(low, sroll(flag, -step), flag) != 0
        even = even_refs[d]
        odd = partner_half(odd_refs[d]) if d == 0 else odd_refs[d]
        matrix = [[face_ref[2 * d, 5 * o + i] for i in range(5)] for o in range(5)]
        for n in range(4):
            take = lambda v, m: jnp.where(is_even, even[v, m], odd[v, m])
            right = [jnp.where(flag, take(v, 3 - n), take(v, n)) for v in range(5)]
            for v, value in enumerate(mix(matrix, right)):
                part_ref[2 * d, v, n, 0] = jnp.where(low, 0.0, -sroll(value, step))
                part_ref[2 * d, v, n, 1] = jnp.where(low, 0.0, -value)
        matrix = [[face_ref[2 * d + 1, 5 * o + i] for i in range(5)] for o in range(5)]
        for n in range(4):
            left = [jnp.where(is_even, odd[v, n], even[v, n]) for v in range(5)]
            for v, value in enumerate(mix(matrix, left)):
                part_ref[2 * d + 1, v, n, 0] = jnp.where(low, value, 0.0)
                part_ref[2 * d + 1, v, n, 1] = jnp.where(low, sroll(value, -step), 0.0)


def whole(acc_ref, part_ref, v, a, b, q):
    total = acc_ref[v, a, b, q]
    if a == 3:
        total = total + part_ref[0, v, b, q]
    if a == 0:
        total = total + part_ref[1, v, b, q]
    if b == 3:
        total = total + part_ref[2, v, a, q]
    if b == 0:
        total = total + part_ref[3, v, a, q]
    return total


def second_kernel(
    acc_ref, u_ref, smooth_ref, flag_ref, face_ref, rxe, rxo, rye, ryo, out_ref, xe, xo, ye, yo, part_ref
):
    remote_parts((rxe, rye), (rxo, ryo), flag_ref, face_ref, part_ref)
    for a in range(4):
        for b in range(4):
            left = [[whole(acc_ref, part_ref, v, a, b, q) for q in range(2)] for v in range(5)]
            for o in range(5):
                total = [None, None]
                for i in range(5):
                    block = smooth_ref[5 * o + i, a, b].astype(F32)
                    for q in range(2):
                        term = block[8 * q : 8 * q + 8] * left[i][q]
                        total[q] = term if i == 0 else total[q] + term
                for q in range(2):
                    out_ref[o, a, b, q] = u_ref[o, a, b, q] + OMEGA * total[q]
    fine_faces(out_ref, flag_ref, xe, xo, ye, yo)


def coarse_smooth(smooth_ref, fields):
    out = [[[None, None], [None, None]] for _ in range(5)]
    for i in range(2):
        for o in range(5):
            total = [None, None]
            for k in range(5):
                block = smooth_ref[5 * o + k, i].astype(F32)
                for j in range(2):
                    term = block[8 * j : 8 * j + 8] * fields[k][i][j]
                    total[j] = term if k == 0 else total[j] + term
            for j in range(2):
                out[o][i][j] = OMEGA * total[j]
    return out


def coarse_faces(field, flag_ref, xe, xo, ye, yo):
    even_x, even_y = parity("gx"), parity("gy")
    fx, fy = flag_ref[0] != 0, flag_ref[1] != 0
    for v in range(5):
        c = field[v]
        low = pack_low(c[0][0], c[0][1], 0)
        h = [jnp.where(fx, c[1][1 - j], c[1][j]) for j in range(2)]
        put_pair(xe, xo, v, low, pack_high(h[0], h[1], 0), even_x)
        low = pack_low(c[0][0], c[1][0], 1)
        h = [jnp.where(fy, c[1 - i][1], c[i][1]) for i in range(2)]
        put_pair(ye, yo, v, low, pack_high(h[0], h[1], 1), even_y)


def restrict_kernel(
    acc_ref, flag_ref, face_ref, smooth_ref, rxe, rxo, rye, ryo, rhs_ref, c_ref, xe, xo, ye, yo, part_ref
):
    remote_parts((rxe, rye), (rxo, ryo), flag_ref, face_ref, part_ref)
    low = c_low()
    rhs = [[[None, None], [None, None]] for _ in range(5)]
    for v in range(5):
        halves = [[[None, None], [None, None]] for _ in range(2)]
        for q in range(2):
            for b in range(4):
                r = [whole(acc_ref, part_ref, v, a, b, q) for a in range(4)]
                ends = (r[0] + NEAR * r[1] + FAR * r[2], r[3] + NEAR * r[2] + FAR * r[1])
                near = (1.0, NEAR, FAR, 0.0)[b], (0.0, FAR, NEAR, 1.0)[b]
                for i in range(2):
                    for j in range(2):
                        if near[j] == 0.0:
                            continue
                        term = ends[i] if near[j] == 1.0 else near[j] * ends[i]
                        halves[q][i][j] = term if halves[q][i][j] is None else halves[q][i][j] + term
        for i in range(2):
            for j in range(2):
                first, second = halves[0][i][j], halves[1][i][j]
                middle = jnp.where(low, second, first)
                value = jnp.where(low, first, second) + FAR * middle + NEAR * sroll(middle, 4)
                rhs[v][i][j] = value
                rhs_ref[v, i, j] = value
    c = coarse_smooth(smooth_ref, rhs)
    for v in range(5):
        for i in range(2):
            for j in range(2):
                c_ref[v, i, j] = c[v][i][j]
    coarse_faces(c, flag_ref, xe, xo, ye, yo)


def coarse_step(c_ref, rhs_ref, smooth_ref, flag_ref, jac_ref, damp_ref, rxe, rxo, rye, ryo):
    damp = 0.5 * damp_ref[...]
    c = [[[c_ref[v, i, j] for j in range(2)] for i in range(2)] for v in range(5)]
    acc = [[[rhs_ref[v, i, j] - 2.0 * c[v][i][j] for j in range(2)] for i in range(2)] for v in range(5)]
    for d, axis in ((0, "gx"), (1, "gy")):
        is_even = parity(axis)
        low, step = axis_low(d)
        flag = flag_ref[d] != 0
        matrix = [[jac_ref[25 * d + 5 * o + i] for i in range(5)] for o in range(5)]
        even, odd = ((rxe, partner_half(rxo)), (rye, ryo))[d]
        at = (lambda n, m: (n, m)) if d == 0 else (lambda n, m: (m, n))
        waves = [[[None] * 5, [None] * 5] for _ in range(2)]
        for v in range(5):
            got_right = jnp.where(is_even, even[v], odd[v])
            got_left = jnp.where(is_even, odd[v], even[v])
            lo = [c[v][at(0, m)[0]][at(0, m)[1]] for m in range(2)]
            hi = [c[v][at(1, m)[0]][at(1, m)[1]] for m in range(2)]
            right = [
                jnp.where(low, sroll(lo[0], -step), sroll(got_right, step)),
                jnp.where(low, sroll(lo[1], -step), got_right),
            ]
            right = [jnp.where(flag, right[1 - m], right[m]) for m in range(2)]
            left = [sroll(jnp.where(flag, hi[1 - m], hi[m]), step) for m in range(2)]
            left = [jnp.where(low, got_left, left[0]), jnp.where(low, sroll(got_left, -step), left[1])]
            for m in range(2):
                waves[1][m][v] = 0.5 * (right[m] - lo[m])
                waves[0][m][v] = 0.5 * (hi[m] - left[m])
                i, j = at(1, m)
                acc[v][i][j] = acc[v][i][j] + damp * (right[m] - hi[m])
                i, j = at(0, m)
                acc[v][i][j] = acc[v][i][j] + damp * (left[m] - lo[m])
        for n in range(2):
            for m in range(2):
                i, j = at(n, m)
                for v, value in enumerate(mix(matrix, waves[n][m])):
                    acc[v][i][j] = acc[v][i][j] - value
    low = c_low()
    flag = jnp.where(low, lroll(flag_ref[2], 1), flag_ref[2]) != 0
    half = jnp.where(low, 0.5, -0.5).astype(F32)
    matrix = [[jac_ref[50 + 5 * o + i] for i in range(5)] for o in range(5)]
    turned = [[[sroll(c[v][i][j], 4) for j in range(2)] for i in range(2)] for v in range(5)]
    beside = [
        [[jnp.where(low, lroll(t, 1), lroll(t, -1)) for t in turned[v][i]] for i in range(2)] for v in range(5)
    ]
    for i in range(2):
        for j in range(2):
            wave = []
            for v in range(5):
                next_to = jnp.where(flag, beside[v][1 - i][j], beside[v][i][j])
                wave.append(half * (turned[v][i][j] - next_to))
                acc[v][i][j] = acc[v][i][j] + damp * (next_to - c[v][i][j])
            for v, value in enumerate(mix(matrix, wave)):
                acc[v][i][j] = acc[v][i][j] - value
    change = coarse_smooth(smooth_ref, acc)
    return [[[c[v][i][j] + change[v][i][j] for j in range(2)] for i in range(2)] for v in range(5)]


def coarse_kernel(
    c_ref, rhs_ref, smooth_ref, flag_ref, jac_ref, damp_ref, rxe, rxo, rye, ryo, out_ref, xe, xo, ye, yo
):
    c = coarse_step(c_ref, rhs_ref, smooth_ref, flag_ref, jac_ref, damp_ref, rxe, rxo, rye, ryo)
    for v in range(5):
        for i in range(2):
            for j in range(2):
                out_ref[v, i, j] = c[v][i][j]
    coarse_faces(c, flag_ref, xe, xo, ye, yo)


def spread(first, second):
    return first, NEAR * first + FAR * second, FAR * first + NEAR * second, second


def last_kernel(
    c_ref, rhs_ref, smooth_ref, flag_ref, jac_ref, damp_ref, rxe, rxo, rye, ryo, second_ref, out_hbm, out_ref, sems
):
    c = coarse_step(c_ref, rhs_ref, smooth_ref, flag_ref, jac_ref, damp_ref, rxe, rxo, rye, ryo)
    low = c_low()
    copies = []
    for v in range(5):
        by_c = [[None, None], [None, None]]
        for i in range(2):
            for j in range(2):
                value = c[v][i][j]
                inner = FAR * value + NEAR * sroll(value, 4)
                by_c[i][j] = (jnp.where(low, value, inner), jnp.where(low, inner, value))
        for q in range(2):
            lines = [spread(by_c[i][0][q], by_c[i][1][q]) for i in range(2)]
            for b in range(4):
                for a, value in enumerate(spread(lines[0][b], lines[1][b])):
                    out_ref[v, a, b, q] = second_ref[v, a, b, q] + value
        copy = pltpu.make_async_copy(out_ref.at[v], out_hbm.at[v], sems.at[v])
        copy.start()
        copies.append(copy)
    for copy in copies:
        copy.wait()


FINE = (5, 4, 4, 2, 8, 128)
FINE_MESSAGE = (5, 4, 8, 128)
COARSE = (5, 2, 2, 8, 128)
COARSE_MESSAGE = (5, 8, 128)


def vmem(shape, dtype=F32):
    return pltpu.VMEM(shape, dtype)


def here(array):
    return pltpu.with_memory_space_constraint(array, pltpu.VMEM)


def call(kernel, args, outs, in_hbm=(), free=(), out_hbm=(), scratch=(), flops=0):
    in_specs = [
        pl.BlockSpec(memory_space=pltpu.HBM if k in in_hbm else pltpu.VMEM) for k in range(len(args))
    ]
    out_specs = [
        pl.BlockSpec(memory_space=pltpu.HBM if k in out_hbm else pltpu.VMEM) for k in range(len(outs))
    ]
    args = [pltpu.with_memory_space_constraint(a, pltpu.HBM) if k in in_hbm else a if k in free else here(a) for k, a in enumerate(args)]
    return pl.pallas_call(
        kernel,
        out_shape=outs,
        in_specs=in_specs,
        out_specs=out_specs,
        scratch_shapes=scratch,
        compiler_params=pltpu.CompilerParams(vmem_limit_bytes=8 * 2**20),
        cost_estimate=pl.CostEstimate(flops=flops, bytes_accessed=4 * 2**20, transcendentals=0),
    )(*args)


def partners(axis):
    size = lax.axis_size(axis)
    even = [(i, i ^ 1) for i in range(size)]
    odd = [(i, (i - 1) % size if i % 2 == 0 else (i + 1) % size) for i in range(size)]
    return even, odd


def odd_groups(axis):
    size = lax.axis_size(axis)
    return [[i, (i + 1) % size] for i in range(1, size, 2)]


def exchange(xe, xo, ye, yo):
    even_x, _ = partners("gx")
    even_y, odd_y = partners("gy")
    xo = lax.all_gather(xo, "gx", axis_index_groups=odd_groups("gx"))
    xe = lax.ppermute(xe, "gx", even_x)
    yo = lax.ppermute(yo, "gy", odd_y)
    ye = lax.ppermute(ye, "gy", even_y)
    return xe, xo, ye, yo


def body(source, jacobian, damping, orient, smoother, coarse_smoother):
    source = source.reshape(FINE)
    smoother = smoother.reshape(25, 4, 4, 16, 128)
    coarse_smoother = coarse_smoother.reshape(25, 2, 16, 128)
    jacobian = jacobian.reshape(75, 4, 128)
    damping = damping.reshape(4, 128)
    orient = orient.reshape(3, 4, 128)
    fine_messages = [vmem(FINE_MESSAGE)] * 4
    fine_messages[1] = jax.ShapeDtypeStruct(FINE_MESSAGE, F32)
    coarse_messages = [vmem(COARSE_MESSAGE)] * 4
    coarse_messages[1] = jax.ShapeDtypeStruct(COARSE_MESSAGE, F32)

    source, smoother, first, flag, *sent = call(
        first_kernel,
        (source, smoother, orient),
        [vmem(FINE), vmem(smoother.shape, smoother.dtype), vmem(FINE), vmem((3, 8, 128), jnp.int32)] + fine_messages,
        in_hbm=(0, 1, 2),
        scratch=[pltpu.SemaphoreType.DMA((2, 4)), pltpu.VMEM((3, 4, 128), jnp.int32), pltpu.SemaphoreType.DMA],
        flops=2 * 25 * 64 * 512,
    )
    got = exchange(*sent)
    acc, jac8, damp8, face = call(
        first_volume_kernel,
        (source, first, flag, jacobian, damping),
        [vmem(FINE), vmem((75, 8, 128)), vmem((8, 128)), vmem((4, 25, 8, 128))],
        flops=9 * 2**20,
    )
    part = pltpu.VMEM((4, 5, 4, 2, 8, 128), F32)
    second, *sent = call(
        second_kernel,
        (acc, first, smoother, flag, face, *got),
        [vmem(FINE)] + fine_messages,
        free=(6,),
        scratch=[part],
        flops=3 * 2**20,
    )
    got = exchange(*sent)
    (acc,) = call(second_volume_kernel, (source, second, flag, jac8, damp8), [vmem(FINE)], flops=9 * 2**20)
    rhs, coarse, *sent = call(
        restrict_kernel,
        (acc, flag, face, coarse_smoother, *got),
        [vmem(COARSE), vmem(COARSE)] + coarse_messages,
        free=(5,),
        scratch=[part],
        flops=3 * 2**20,
    )
    got = exchange(*sent)
    coarse, *sent = call(
        coarse_kernel,
        (coarse, rhs, coarse_smoother, flag, jac8, damp8, *got),
        [vmem(COARSE)] + coarse_messages,
        free=(7,),
        flops=2**20,
    )
    got = exchange(*sent)
    (out,) = call(
        last_kernel,
        (coarse, rhs, coarse_smoother, flag, jac8, damp8, *got, second),
        [jax.ShapeDtypeStruct(FINE, F32)],
        out_hbm=(0,),
        free=(7,),
        scratch=[pltpu.VMEM(FINE, F32), pltpu.SemaphoreType.DMA((5,))],
        flops=2**20,
    )
    return out.reshape(5, 4, 4, 4, 2, 2, 128)


def solution(mesh):
    in_specs = (
        P(None, None, None, None, "gx", "gy", None),
        P(None, None, None, "gx", "gy", None),
        P("gx", "gy", None),
        P(None, "gx", "gy", None),
        P(None, None, None, None, None, "gx", "gy", None),
        P(None, None, None, None, None, "gx", "gy", None),
    )
    out_specs = P(None, None, None, None, "gx", "gy", None)
    return jax.shard_map(body, mesh=mesh, in_specs=in_specs, out_specs=out_specs, check_vma=False)
```

```python
import functools
import math

import jax
import jax.numpy as jnp
import numpy as np
from jax import lax
from jax.experimental import pallas as pl
from jax.experimental.pallas import tpu as pltpu
from jax.sharding import PartitionSpec as P


F32 = jnp.float32
OMEGA = 0.8
H4 = 3.0
ROOT = 1.0 / math.sqrt(5.0)
NEAR = (1.0 + ROOT) / 2.0
FAR = (1.0 - ROOT) / 2.0


def lobatto_slopes():
    points = np.array([-1.0, -ROOT, ROOT, 1.0])
    weights = np.ones(4)
    for i in range(4):
        for j in range(4):
            if i != j:
                weights[i] = weights[i] / (points[i] - points[j])
    slopes = np.zeros((4, 4))
    for i in range(4):
        for j in range(4):
            if i != j:
                slopes[i, j] = weights[j] / weights[i] / (points[i] - points[j])
        slopes[i, i] = -np.sum(slopes[i])
    return slopes


D4 = lobatto_slopes()
PD = np.array([[1.0, NEAR, FAR, 0.0], [0.0, FAR, NEAR, 1.0]]) @ D4


def sum_of(terms):
    total = None
    for weight, value in terms:
        total = weight * value if total is None else total + weight * value
    return total


def rows():
    return lax.broadcasted_iota(jnp.int32, (8, 128), 0)


def x_low():
    return (rows() & 2) == 0


def y_low():
    return (rows() & 1) == 0


def c_low():
    return (rows() & 4) == 0


def sroll(value, shift):
    return pltpu.roll(value, shift % 8, 0)


def lroll(value, shift):
    return pltpu.roll(value, shift % 128, 1)


def twice(value):
    return jnp.concatenate([value, value], axis=0)


def axis_low(direction):
    return (x_low(), 2) if direction == 0 else (y_low(), 1)


def pack_low(first, second, direction):
    low, step = axis_low(direction)
    return jnp.where(low, first, sroll(second, step))


def pack_high(first, second, direction):
    low, step = axis_low(direction)
    return jnp.where(low, sroll(first, -step), second)


def slopes_along(u0, u1, u2, u3):
    e0, o0, e1, o1 = u0 + u3, u0 - u3, u1 + u2, u1 - u2
    diff = e1 - e0
    even_a = float((D4[0, 1] + D4[0, 2]) / 2.0) * diff
    even_b = float((D4[1, 2] - 0.0) / 2.0) * diff
    odd_a = float((D4[0, 0] - D4[0, 3]) / 2.0) * o0 + float((D4[0, 1] - D4[0, 2]) / 2.0) * o1
    odd_b = float((D4[1, 0] - D4[1, 3]) / 2.0) * o0 - float(D4[1, 2] / 2.0) * o1
    return even_a + odd_a, even_b + odd_b, odd_b - even_b, odd_a - even_a


def mix(matrix, fields):
    out = []
    for o in range(5):
        total = matrix[o][0] * fields[0]
        for i in range(1, 5):
            total = total + matrix[o][i] * fields[i]
        out.append(total)
    return out


def parity(axis):
    return lax.rem(lax.axis_index(axis), 2) == 0


def put_pair(even_ref, odd_ref, index, low_face, high_face, is_even):
    even_ref[index] = jnp.where(is_even, high_face, low_face)
    odd_ref[index] = jnp.where(is_even, low_face, high_face)


def fine_faces(u_ref, flag_ref, xo, xe, yo, ye):
    even_x, even_y = parity("gx"), parity("gy")
    fx, fy = flag_ref[0] != 0, flag_ref[1] != 0
    for v in range(5):
        for n in range(4):
            low = pack_low(u_ref[v, 0, n, 0], u_ref[v, 0, n, 1], 0)
            h = [jnp.where(fx, u_ref[v, 3, 3 - n, q], u_ref[v, 3, n, q]) for q in range(2)]
            put_pair(xe, xo, (v, n), low, pack_high(h[0], h[1], 0), even_x)
            low = pack_low(u_ref[v, n, 0, 0], u_ref[v, n, 0, 1], 1)
            h = [jnp.where(fy, u_ref[v, 3 - n, 3, q], u_ref[v, n, 3, q]) for q in range(2)]
            put_pair(ye, yo, (v, n), low, pack_high(h[0], h[1], 1), even_y)


def restrict_c(first, second):
    low = c_low()
    middle = jnp.where(low, second, first)
    return jnp.where(low, first, second) + FAR * middle + NEAR * sroll(middle, 4)


def restrict_four(values):
    return values[0] + NEAR * values[1] + FAR * values[2], values[3] + NEAR * values[2] + FAR * values[1]


def put_coarse_faces(v, lows, highs, flag_ref, pairs):
    for d, axis in ((0, "gx"), (1, "gy")):
        flag = flag_ref[d] != 0
        low, high = lows[d], highs[d]
        turned = [jnp.where(flag, high[1 - m], high[m]) for m in range(2)]
        even_ref, odd_ref = pairs[d]
        put_pair(even_ref, odd_ref, v, pack_low(*low, d), pack_high(*turned, d), parity(axis))


def restricted_faces(u_ref, flag_ref, xo, xe, yo, ye):
    for v in range(5):
        line = {}
        for a in range(4):
            for b in range(4):
                if a in (0, 3) or b in (0, 3):
                    line[a, b] = restrict_c(u_ref[v, a, b, 0], u_ref[v, a, b, 1])
        lows = [restrict_four([line[0, n] for n in range(4)]), restrict_four([line[n, 0] for n in range(4)])]
        highs = [restrict_four([line[3, n] for n in range(4)]), restrict_four([line[n, 3] for n in range(4)])]
        put_coarse_faces(v, lows, highs, flag_ref, ((xe, xo), (ye, yo)))


def first_kernel(
    src_hbm, smooth_hbm, orient_hbm, src_ref, smooth_ref, u_ref, flag_ref, xo, xe, yo, ye, sems, orient_ref, orient_sem
):
    orient_copy = pltpu.make_async_copy(orient_hbm, orient_ref, orient_sem)
    orient_copy.start()
    copies = []
    for slot, a in enumerate((0, 3, 1, 2)):
        pair = (
            pltpu.make_async_copy(src_hbm.at[:, a], src_ref.at[:, a], sems.at[0, slot]),
            pltpu.make_async_copy(smooth_hbm.at[:, a], smooth_ref.at[:, a], sems.at[1, slot]),
        )
        for one in pair:
            one.start()
        copies.append((a, pair))
    orient_copy.wait()
    for d in range(3):
        flag_ref[d] = twice(orient_ref[d])
    for a, pair in copies:
        for one in pair:
            one.wait()

        def one_line(b, carry, a=a):
            src = [[src_ref[v, a, b, q] for q in range(2)] for v in range(5)]
            for o in range(5):
                total = [None, None]
                for i in range(5):
                    block = smooth_ref[5 * o + i, a, b].astype(F32)
                    for q in range(2):
                        term = block[8 * q : 8 * q + 8] * src[i][q]
                        total[q] = term if i == 0 else total[q] + term
                for q in range(2):
                    u_ref[o, a, b, q] = OMEGA * total[q]
            return carry

        lax.fori_loop(0, 4, one_line, 0)
    fine_faces(u_ref, flag_ref, xo, xe, yo, ye)


def prepare_tables(jac_ref, damp_ref, jac8_ref, damp8_ref, face_ref):
    damp = twice(damp_ref[...])
    damp8_ref[...] = damp
    for d in range(3):
        for k in range(25):
            value = twice(jac_ref[25 * d + k])
            jac8_ref[25 * d + k] = value
            if d < 2:
                low, step = axis_low(d)
                diagonal = k % 6 == 0
                upper = H4 * (value - damp if diagonal else value)
                lower = H4 * (value + damp if diagonal else value)
                face_ref[2 * d, k] = jnp.where(low, sroll(upper, -step), upper)
                face_ref[2 * d + 1, k] = jnp.where(low, lower, sroll(lower, step))


def volume(src_ref, u_ref, flag_ref, jac_ref, damp_ref, acc_ref):
    damp = H4 * damp_ref[...]

    def jacobian(d):
        return [[jac_ref[25 * d + 5 * o + i] for i in range(5)] for o in range(5)]

    def along(direction):
        low, step = axis_low(direction)
        flag = flag_ref[direction] != 0
        flag_before = sroll(flag_ref[direction], step) != 0

        def at(v, n, other, q):
            return (v, n, other, q) if direction == 0 else (v, other, n, q)

        def step_fn(j, carry):
            other, q = j // 2, j % 2
            u = [[u_ref[at(v, n, other, q)] for n in range(4)] for v in range(5)]
            waves = []
            jumps = []
            for v in range(5):
                back_low, back_high = u_ref[at(v, 0, 3 - other, q)], u_ref[at(v, 3, 3 - other, q)]
                right = sroll(jnp.where(flag_before, back_low, u[v][0]), -step)
                left = sroll(jnp.where(flag, back_high, u[v][3]), step)
                jump_right = jnp.where(low, right, 0.0) - u[v][3]
                jump_left = jnp.where(low, 0.0, left) - u[v][0]
                w = list(slopes_along(*u[v]))
                w[3] = w[3] + H4 * jump_right
                w[0] = w[0] - H4 * jump_left
                waves.append(w)
                jumps.append((damp * jump_left, None, None, damp * jump_right))
            matrix = jacobian(direction)
            for n in range(4):
                flux = mix(matrix, [waves[v][n] for v in range(5)])
                for v in range(5):
                    if direction == 0:
                        total = src_ref[at(v, n, other, q)] - 2.0 * u[v][n]
                    else:
                        total = acc_ref[at(v, n, other, q)]
                    total = total - flux[v]
                    if jumps[v][n] is not None:
                        total = total + jumps[v][n]
                    acc_ref[at(v, n, other, q)] = total
            return carry

        lax.fori_loop(0, 8, step_fn, 0)

    along(0)
    along(1)

    low = c_low()
    flag = jnp.where(low, lroll(flag_ref[2], 1), flag_ref[2]) != 0
    damp_z = damp
    coef = [
        [jnp.where(low, float(D4[2 * p, c]), float(D4[2 * p + 1, c ^ 1])).astype(F32) for c in range(4)]
        for p in range(2)
    ]

    def step_z(j, carry):
        a0, b = j // 4, j % 4
        here = (a0, 3 - a0)
        u = [[[u_ref[v, a, b, q] for q in range(2)] for v in range(5)] for a in here]
        turned = [[[sroll(u[s][v][q], 4) for q in range(2)] for v in range(5)] for s in range(2)]
        beside = []
        for s in range(2):
            line = []
            for v in range(5):
                face = jnp.where(low, turned[s][v][1], turned[s][v][0])
                line.append(jnp.where(low, lroll(face, 1), lroll(face, -1)))
            beside.append(line)
        matrix = jacobian(2)
        for s in range(2):
            waves = [[], []]
            jumps = []
            for v in range(5):
                own = jnp.where(low, u[s][v][0], u[s][v][1])
                jump = jnp.where(flag, beside[1 - s][v], beside[s][v]) - own
                jumps.append(damp_z * jump)
                lifted = H4 * jump
                for p in range(2):
                    w = coef[p][0] * u[s][v][0] + coef[p][1] * turned[s][v][0]
                    w = w + (coef[p][2] * u[s][v][1] + coef[p][3] * turned[s][v][1])
                    w = w - jnp.where(low, lifted, 0.0) if p == 0 else w + jnp.where(low, 0.0, lifted)
                    waves[p].append(w)
            for p in range(2):
                flux = mix(matrix, waves[p])
                for v in range(5):
                    part = jnp.where(low, jumps[v], 0.0) if p == 0 else jnp.where(low, 0.0, jumps[v])
                    acc_ref[v, here[s], b, p] = acc_ref[v, here[s], b, p] - flux[v] + part
        return carry

    lax.fori_loop(0, 8, step_z, 0)


def first_volume_kernel(src_ref, u_ref, flag_ref, jac_ref, damp_ref, acc_ref, jac8_ref, damp8_ref, face_ref):
    prepare_tables(jac_ref, damp_ref, jac8_ref, damp8_ref, face_ref)
    volume(src_ref, u_ref, flag_ref, jac8_ref, damp8_ref, acc_ref)


def remote_parts(even_refs, odd_refs, flag_ref, face_ref, part_ref):
    for d, axis in ((0, "gx"), (1, "gy")):
        is_even = parity(axis)
        low, step = axis_low(d)
        flag = flag_ref[d]
        flag = jnp.where(low, sroll(flag, -step), flag) != 0
        even, odd = even_refs[d], odd_refs[d]
        matrix = [[face_ref[2 * d, 5 * o + i] for i in range(5)] for o in range(5)]
        for n in range(4):
            take = lambda v, m: jnp.where(is_even, even[v, m], odd[v, m])
            right = [jnp.where(flag, take(v, 3 - n), take(v, n)) for v in range(5)]
            for v, value in enumerate(mix(matrix, right)):
                part_ref[2 * d, v, n, 0] = jnp.where(low, 0.0, -sroll(value, step))
                part_ref[2 * d, v, n, 1] = jnp.where(low, 0.0, -value)
        matrix = [[face_ref[2 * d + 1, 5 * o + i] for i in range(5)] for o in range(5)]
        for n in range(4):
            left = [jnp.where(is_even, odd[v, n], even[v, n]) for v in range(5)]
            for v, value in enumerate(mix(matrix, left)):
                part_ref[2 * d + 1, v, n, 0] = jnp.where(low, value, 0.0)
                part_ref[2 * d + 1, v, n, 1] = jnp.where(low, sroll(value, -step), 0.0)


def whole(acc_ref, part_ref, v, a, b, q):
    total = acc_ref[v, a, b, q]
    if a == 3:
        total = total + part_ref[0, v, b, q]
    if a == 0:
        total = total + part_ref[1, v, b, q]
    if b == 3:
        total = total + part_ref[2, v, a, q]
    if b == 0:
        total = total + part_ref[3, v, a, q]
    return total


def second_kernel(
    acc_ref, u_ref, smooth_ref, flag_ref, face_ref, rxo, rxe, ryo, rye, out_ref, xo, xe, yo, ye, part_ref
):
    remote_parts((rxe, rye), (rxo, ryo), flag_ref, face_ref, part_ref)
    for a in range(4):
        for b in range(4):
            left = [[whole(acc_ref, part_ref, v, a, b, q) for q in range(2)] for v in range(5)]
            for o in range(5):
                total = [None, None]
                for i in range(5):
                    block = smooth_ref[5 * o + i, a, b].astype(F32)
                    for q in range(2):
                        term = block[8 * q : 8 * q + 8] * left[i][q]
                        total[q] = term if i == 0 else total[q] + term
                for q in range(2):
                    out_ref[o, a, b, q] = u_ref[o, a, b, q] + OMEGA * total[q]
    restricted_faces(out_ref, flag_ref, xo, xe, yo, ye)


def coarse_smooth(smooth_ref, fields):
    out = [[[None, None], [None, None]] for _ in range(5)]
    for i in range(2):
        for o in range(5):
            total = [None, None]
            for k in range(5):
                block = smooth_ref[5 * o + k, i].astype(F32)
                for j in range(2):
                    term = block[8 * j : 8 * j + 8] * fields[k][i][j]
                    total[j] = term if k == 0 else total[j] + term
            for j in range(2):
                out[o][i][j] = OMEGA * total[j]
    return out


def coarse_faces(field, flag_ref, xo, xe, yo, ye):
    for v in range(5):
        c = field[v]
        lows = [[c[0][0], c[0][1]], [c[0][0], c[1][0]]]
        highs = [[c[1][0], c[1][1]], [c[0][1], c[1][1]]]
        put_coarse_faces(v, lows, highs, flag_ref, ((xe, xo), (ye, yo)))


def restricted_volume_kernel(src_ref, u_ref, flag_ref, jac_ref, damp_ref, acc_ref):
    damp = H4 * damp_ref[...]
    low_c = c_low()
    slope = [
        jnp.where(low_c, float(PD[0, c]), float(PD[1, c ^ 1])).astype(F32) for c in range(4)
    ]
    flags = [flag_ref[0] != 0, flag_ref[1] != 0, jnp.where(low_c, lroll(flag_ref[2], 1), flag_ref[2]) != 0]
    sign = jnp.where(low_c, -H4, H4).astype(F32)
    waves = [[[[None] * 5 for _ in range(2)] for _ in range(2)] for _ in range(3)]

    def slopes_four(values):
        return [sum_of([(float(PD[i, n]), values[n]) for n in range(4)]) for i in range(2)]

    for v in range(5):
        line, slope_c, ends = {}, {}, {}
        for a in range(4):
            for b in range(4):
                first, second = u_ref[v, a, b, 0], u_ref[v, a, b, 1]
                line[a, b] = restrict_c(first, second)
                slope_c[a, b] = (slope[0] * first + slope[1] * sroll(first, 4)) + (
                    slope[2] * second + slope[3] * sroll(second, 4)
                )
                ends[a, b] = jnp.where(low_c, first, second)

        def along_b(table):
            return [restrict_four([table[a, b] for b in range(4)]) for a in range(4)]

        def both(table):
            by_b = along_b(table)
            return [restrict_four([by_b[a][j] for a in range(4)]) for j in range(2)]

        by_b = along_b(line)
        by_a = [restrict_four([line[a, b] for a in range(4)]) for b in range(4)]
        flux_z = both(slope_c)
        trace_z = both(ends)
        sources = both({(a, b): restrict_c(src_ref[v, a, b, 0], src_ref[v, a, b, 1]) for a in range(4) for b in range(4)})
        acc = [[None, None], [None, None]]
        for j in range(2):
            value = restrict_four([by_b[a][j] for a in range(4)])
            flux = slopes_four([by_b[a][j] for a in range(4)])
            for i in range(2):
                acc[i][j] = sources[j][i] - 2.0 * value[i]
                waves[0][i][j][v] = flux[i]
        for i in range(2):
            flux = slopes_four([by_a[b][i] for b in range(4)])
            for j in range(2):
                waves[1][i][j][v] = flux[j]
        for d, lo, hi in ((0, by_b[0], by_b[3]), (1, by_a[0], by_a[3])):
            low, step = axis_low(d)
            flag = flags[d]
            flag_before = sroll(flag_ref[d], step) != 0
            for m in range(2):
                right = sroll(jnp.where(flag_before, lo[1 - m], lo[m]), -step)
                left = sroll(jnp.where(flag, hi[1 - m], hi[m]), step)
                jump_right = jnp.where(low, right, 0.0) - hi[m]
                jump_left = jnp.where(low, 0.0, left) - lo[m]
                i, j = (1, m) if d == 0 else (m, 1)
                waves[d][i][j][v] = waves[d][i][j][v] + H4 * jump_right
                acc[i][j] = acc[i][j] + damp * jump_right
                i, j = (0, m) if d == 0 else (m, 0)
                waves[d][i][j][v] = waves[d][i][j][v] - H4 * jump_left
                acc[i][j] = acc[i][j] + damp * jump_left
        beside = []
        for j in range(2):
            turned = [sroll(trace_z[j][i], 4) for i in range(2)]
            beside.append([jnp.where(low_c, lroll(t, 1), lroll(t, -1)) for t in turned])
        for i in range(2):
            for j in range(2):
                jump = jnp.where(flags[2], beside[j][1 - i], beside[j][i]) - trace_z[j][i]
                waves[2][i][j][v] = flux_z[j][i] + sign * jump
                acc_ref[v, i, j] = acc[i][j] + damp * jump
    for d in range(3):
        matrix = [[jac_ref[25 * d + 5 * o + i] for i in range(5)] for o in range(5)]
        for i in range(2):
            for j in range(2):
                for v, value in enumerate(mix(matrix, waves[d][i][j])):
                    acc_ref[v, i, j] = acc_ref[v, i, j] - value


def restrict_kernel(
    acc_ref, flag_ref, face_ref, smooth_ref, rxo, rxe, ryo, rye, rhs_ref, c_ref, xo, xe, yo, ye
):
    rhs = [[[acc_ref[v, i, j] for j in range(2)] for i in range(2)] for v in range(5)]
    for d, axis in ((0, "gx"), (1, "gy")):
        is_even = parity(axis)
        low, step = axis_low(d)
        flag = flag_ref[d]
        flag = jnp.where(low, sroll(flag, -step), flag) != 0
        even, odd = ((rxe, rxo), (rye, ryo))[d]
        at = (lambda n, m: (n, m)) if d == 0 else (lambda n, m: (m, n))
        right, left = [], []
        for v in range(5):
            value = jnp.where(is_even, even[v], odd[v])
            swapped = jnp.where(low, sroll(value, -step), sroll(value, step))
            right.append(jnp.where(flag, swapped, value))
            left.append(jnp.where(is_even, odd[v], even[v]))
        upper = [[face_ref[2 * d, 5 * o + i] for i in range(5)] for o in range(5)]
        lower = [[face_ref[2 * d + 1, 5 * o + i] for i in range(5)] for o in range(5)]
        for v, value in enumerate(mix(upper, right)):
            for m, part in enumerate((sroll(value, step), value)):
                i, j = at(1, m)
                rhs[v][i][j] = rhs[v][i][j] - jnp.where(low, 0.0, part)
        for v, value in enumerate(mix(lower, left)):
            for m, part in enumerate((value, sroll(value, -step))):
                i, j = at(0, m)
                rhs[v][i][j] = rhs[v][i][j] + jnp.where(low, part, 0.0)
    c = coarse_smooth(smooth_ref, rhs)
    for v in range(5):
        for i in range(2):
            for j in range(2):
                rhs_ref[v, i, j] = rhs[v][i][j]
                c_ref[v, i, j] = c[v][i][j]
    coarse_faces(c, flag_ref, xo, xe, yo, ye)


def coarse_step(c_ref, rhs_ref, smooth_ref, flag_ref, jac_ref, damp_ref, rxo, rxe, ryo, rye):
    damp = 0.5 * damp_ref[...]
    c = [[[c_ref[v, i, j] for j in range(2)] for i in range(2)] for v in range(5)]
    acc = [[[rhs_ref[v, i, j] - 2.0 * c[v][i][j] for j in range(2)] for i in range(2)] for v in range(5)]
    for d, axis in ((0, "gx"), (1, "gy")):
        is_even = parity(axis)
        low, step = axis_low(d)
        flag = flag_ref[d] != 0
        matrix = [[jac_ref[25 * d + 5 * o + i] for i in range(5)] for o in range(5)]
        even, odd = ((rxe, rxo), (rye, ryo))[d]
        at = (lambda n, m: (n, m)) if d == 0 else (lambda n, m: (m, n))
        waves = [[[None] * 5, [None] * 5] for _ in range(2)]
        for v in range(5):
            got_right = jnp.where(is_even, even[v], odd[v])
            got_left = jnp.where(is_even, odd[v], even[v])
            lo = [c[v][at(0, m)[0]][at(0, m)[1]] for m in range(2)]
            hi = [c[v][at(1, m)[0]][at(1, m)[1]] for m in range(2)]
            right = [
                jnp.where(low, sroll(lo[0], -step), sroll(got_right, step)),
                jnp.where(low, sroll(lo[1], -step), got_right),
            ]
            right = [jnp.where(flag, right[1 - m], right[m]) for m in range(2)]
            left = [sroll(jnp.where(flag, hi[1 - m], hi[m]), step) for m in range(2)]
            left = [jnp.where(low, got_left, left[0]), jnp.where(low, sroll(got_left, -step), left[1])]
            for m in range(2):
                waves[1][m][v] = 0.5 * (right[m] - lo[m])
                waves[0][m][v] = 0.5 * (hi[m] - left[m])
                i, j = at(1, m)
                acc[v][i][j] = acc[v][i][j] + damp * (right[m] - hi[m])
                i, j = at(0, m)
                acc[v][i][j] = acc[v][i][j] + damp * (left[m] - lo[m])
        for n in range(2):
            for m in range(2):
                i, j = at(n, m)
                for v, value in enumerate(mix(matrix, waves[n][m])):
                    acc[v][i][j] = acc[v][i][j] - value
    low = c_low()
    flag = jnp.where(low, lroll(flag_ref[2], 1), flag_ref[2]) != 0
    half = jnp.where(low, 0.5, -0.5).astype(F32)
    matrix = [[jac_ref[50 + 5 * o + i] for i in range(5)] for o in range(5)]
    turned = [[[sroll(c[v][i][j], 4) for j in range(2)] for i in range(2)] for v in range(5)]
    beside = [
        [[jnp.where(low, lroll(t, 1), lroll(t, -1)) for t in turned[v][i]] for i in range(2)] for v in range(5)
    ]
    for i in range(2):
        for j in range(2):
            wave = []
            for v in range(5):
                next_to = jnp.where(flag, beside[v][1 - i][j], beside[v][i][j])
                wave.append(half * (turned[v][i][j] - next_to))
                acc[v][i][j] = acc[v][i][j] + damp * (next_to - c[v][i][j])
            for v, value in enumerate(mix(matrix, wave)):
                acc[v][i][j] = acc[v][i][j] - value
    change = coarse_smooth(smooth_ref, acc)
    return [[[c[v][i][j] + change[v][i][j] for j in range(2)] for i in range(2)] for v in range(5)]


def coarse_kernel(
    c_ref, rhs_ref, smooth_ref, flag_ref, jac_ref, damp_ref, rxo, rxe, ryo, rye, out_ref, xo, xe, yo, ye
):
    c = coarse_step(c_ref, rhs_ref, smooth_ref, flag_ref, jac_ref, damp_ref, rxo, rxe, ryo, rye)
    for v in range(5):
        for i in range(2):
            for j in range(2):
                out_ref[v, i, j] = c[v][i][j]
    coarse_faces(c, flag_ref, xo, xe, yo, ye)


def spread(first, second):
    return first, NEAR * first + FAR * second, FAR * first + NEAR * second, second


def last_kernel(
    c_ref, rhs_ref, smooth_ref, flag_ref, jac_ref, damp_ref, rxo, rxe, ryo, rye, second_ref, out_hbm, out_ref, sems
):
    c = coarse_step(c_ref, rhs_ref, smooth_ref, flag_ref, jac_ref, damp_ref, rxo, rxe, ryo, rye)
    low = c_low()
    copies = []
    for v in range(5):
        by_c = [[None, None], [None, None]]
        for i in range(2):
            for j in range(2):
                value = c[v][i][j]
                inner = FAR * value + NEAR * sroll(value, 4)
                by_c[i][j] = (jnp.where(low, value, inner), jnp.where(low, inner, value))
        for q in range(2):
            lines = [spread(by_c[i][0][q], by_c[i][1][q]) for i in range(2)]
            for b in range(4):
                for a, value in enumerate(spread(lines[0][b], lines[1][b])):
                    out_ref[v, a, b, q] = second_ref[v, a, b, q] + value
        copy = pltpu.make_async_copy(out_ref.at[v], out_hbm.at[v], sems.at[v])
        copy.start()
        copies.append(copy)
    for copy in copies:
        copy.wait()


FINE = (5, 4, 4, 2, 8, 128)
FINE_MESSAGE = (5, 4, 8, 128)
COARSE = (5, 2, 2, 8, 128)
COARSE_MESSAGE = (5, 8, 128)


def vmem(shape, dtype=F32):
    return pltpu.VMEM(shape, dtype)


def here(array):
    return pltpu.with_memory_space_constraint(array, pltpu.VMEM)


def call(kernel, args, outs, in_hbm=(), out_hbm=(), scratch=(), flops=0):
    in_specs = [
        pl.BlockSpec(memory_space=pltpu.HBM if k in in_hbm else pltpu.VMEM) for k in range(len(args))
    ]
    out_specs = [
        pl.BlockSpec(memory_space=pltpu.HBM if k in out_hbm else pltpu.VMEM) for k in range(len(outs))
    ]
    args = [pltpu.with_memory_space_constraint(a, pltpu.HBM) if k in in_hbm else here(a) for k, a in enumerate(args)]
    return pl.pallas_call(
        kernel,
        out_shape=outs,
        in_specs=in_specs,
        out_specs=out_specs,
        scratch_shapes=scratch,
        compiler_params=pltpu.CompilerParams(vmem_limit_bytes=8 * 2**20),
        cost_estimate=pl.CostEstimate(flops=flops, bytes_accessed=4 * 2**20, transcendentals=0),
    )(*args)


def partners(axis):
    size = lax.axis_size(axis)
    even = [(i, i ^ 1) for i in range(size)]
    odd = [(i, (i - 1) % size if i % 2 == 0 else (i + 1) % size) for i in range(size)]
    return even, odd


def exchange(xo, xe, yo, ye):
    even_x, odd_x = partners("gx")
    even_y, odd_y = partners("gy")
    xo = lax.ppermute(xo, "gx", odd_x)
    xe = lax.ppermute(xe, "gx", even_x)
    yo = lax.ppermute(yo, "gy", odd_y)
    ye = lax.ppermute(ye, "gy", even_y)
    return xo, xe, yo, ye


def body(source, jacobian, damping, orient, smoother, coarse_smoother):
    source = source.reshape(FINE)
    smoother = smoother.reshape(25, 4, 4, 16, 128)
    coarse_smoother = coarse_smoother.reshape(25, 2, 16, 128)
    jacobian = jacobian.reshape(75, 4, 128)
    damping = damping.reshape(4, 128)
    orient = orient.reshape(3, 4, 128)
    fine_messages = [vmem(FINE_MESSAGE)] * 4
    coarse_messages = [vmem(COARSE_MESSAGE)] * 4

    source, smoother, first, flag, *sent = call(
        first_kernel,
        (source, smoother, orient),
        [vmem(FINE), vmem(smoother.shape, smoother.dtype), vmem(FINE), vmem((3, 8, 128), jnp.int32)] + fine_messages,
        in_hbm=(0, 1, 2),
        scratch=[pltpu.SemaphoreType.DMA((2, 4)), pltpu.VMEM((3, 4, 128), jnp.int32), pltpu.SemaphoreType.DMA],
        flops=2 * 25 * 64 * 512,
    )
    got = exchange(*sent)
    acc, jac8, damp8, face = call(
        first_volume_kernel,
        (source, first, flag, jacobian, damping),
        [vmem(FINE), vmem((75, 8, 128)), vmem((8, 128)), vmem((4, 25, 8, 128))],
        flops=9 * 2**20,
    )
    second, *sent = call(
        second_kernel,
        (acc, first, smoother, flag, face, *got),
        [vmem(FINE)] + coarse_messages,
        scratch=[pltpu.VMEM((4, 5, 4, 2, 8, 128), F32)],
        flops=3 * 2**20,
    )
    got = exchange(*sent)
    (acc,) = call(restricted_volume_kernel, (source, second, flag, jac8, damp8), [vmem(COARSE)], flops=4 * 2**20)
    rhs, coarse, *sent = call(
        restrict_kernel,
        (acc, flag, face, coarse_smoother, *got),
        [vmem(COARSE), vmem(COARSE)] + coarse_messages,
        flops=2**20,
    )
    got = exchange(*sent)
    coarse, *sent = call(
        coarse_kernel,
        (coarse, rhs, coarse_smoother, flag, jac8, damp8, *got),
        [vmem(COARSE)] + coarse_messages,
        flops=2**20,
    )
    got = exchange(*sent)
    (out,) = call(
        last_kernel,
        (coarse, rhs, coarse_smoother, flag, jac8, damp8, *got, second),
        [jax.ShapeDtypeStruct(FINE, F32)],
        out_hbm=(0,),
        scratch=[pltpu.VMEM(FINE, F32), pltpu.SemaphoreType.DMA((5,))],
        flops=2**20,
    )
    return out.reshape(5, 4, 4, 4, 2, 2, 128)


def solution(mesh):
    in_specs = (
        P(None, None, None, None, "gx", "gy", None),
        P(None, None, None, "gx", "gy", None),
        P("gx", "gy", None),
        P(None, "gx", "gy", None),
        P(None, None, None, None, None, "gx", "gy", None),
        P(None, None, None, None, None, "gx", "gy", None),
    )
    out_specs = P(None, None, None, None, "gx", "gy", None)
    return jax.shard_map(body, mesh=mesh, in_specs=in_specs, out_specs=out_specs, check_vma=False)
```

```python
import functools
import math

import jax
import jax.numpy as jnp
import numpy as np
from jax import lax
from jax.experimental import pallas as pl
from jax.experimental.pallas import tpu as pltpu
from jax.sharding import PartitionSpec as P


F32 = jnp.float32
OMEGA = 0.8
H4 = 3.0
ROOT = 1.0 / math.sqrt(5.0)
NEAR = (1.0 + ROOT) / 2.0
FAR = (1.0 - ROOT) / 2.0


def lobatto_slopes():
    points = np.array([-1.0, -ROOT, ROOT, 1.0])
    weights = np.ones(4)
    for i in range(4):
        for j in range(4):
            if i != j:
                weights[i] = weights[i] / (points[i] - points[j])
    slopes = np.zeros((4, 4))
    for i in range(4):
        for j in range(4):
            if i != j:
                slopes[i, j] = weights[j] / weights[i] / (points[i] - points[j])
        slopes[i, i] = -np.sum(slopes[i])
    return slopes


D4 = lobatto_slopes()
PD = np.array([[1.0, NEAR, FAR, 0.0], [0.0, FAR, NEAR, 1.0]]) @ D4


def sum_of(terms):
    total = None
    for weight, value in terms:
        total = weight * value if total is None else total + weight * value
    return total


def rows():
    return lax.broadcasted_iota(jnp.int32, (8, 128), 0)


def x_low():
    return (rows() & 2) == 0


def y_low():
    return (rows() & 1) == 0


def c_low():
    return (rows() & 4) == 0


def sroll(value, shift):
    return pltpu.roll(value, shift % 8, 0)


def lroll(value, shift):
    return pltpu.roll(value, shift % 128, 1)


def twice(value):
    return jnp.concatenate([value, value], axis=0)


def axis_low(direction):
    return (x_low(), 2) if direction == 0 else (y_low(), 1)


def pack_low(first, second, direction):
    low, step = axis_low(direction)
    return jnp.where(low, first, sroll(second, step))


def pack_high(first, second, direction):
    low, step = axis_low(direction)
    return jnp.where(low, sroll(first, -step), second)


def slopes_along(u0, u1, u2, u3):
    e0, o0, e1, o1 = u0 + u3, u0 - u3, u1 + u2, u1 - u2
    diff = e1 - e0
    even_a = float((D4[0, 1] + D4[0, 2]) / 2.0) * diff
    even_b = float((D4[1, 2] - 0.0) / 2.0) * diff
    odd_a = float((D4[0, 0] - D4[0, 3]) / 2.0) * o0 + float((D4[0, 1] - D4[0, 2]) / 2.0) * o1
    odd_b = float((D4[1, 0] - D4[1, 3]) / 2.0) * o0 - float(D4[1, 2] / 2.0) * o1
    return even_a + odd_a, even_b + odd_b, odd_b - even_b, odd_a - even_a


def mix(matrix, fields):
    out = []
    for o in range(5):
        total = matrix[o][0] * fields[0]
        for i in range(1, 5):
            total = total + matrix[o][i] * fields[i]
        out.append(total)
    return out


def is_black():
    return lax.rem(lax.axis_index("gx") + lax.axis_index("gy"), 2) == 1


def received(refs, index):
    return jnp.where(is_black(), refs[0][index], refs[1][index])


def fine_faces(u_ref, flag_ref, x_low_ref, x_high_ref, y_low_ref, y_high_ref):
    fx, fy = flag_ref[0] != 0, flag_ref[1] != 0
    for v in range(5):
        for n in range(4):
            x_low_ref[v, n] = pack_low(u_ref[v, 0, n, 0], u_ref[v, 0, n, 1], 0)
            h = [jnp.where(fx, u_ref[v, 3, 3 - n, q], u_ref[v, 3, n, q]) for q in range(2)]
            x_high_ref[v, n] = pack_high(h[0], h[1], 0)
            y_low_ref[v, n] = pack_low(u_ref[v, n, 0, 0], u_ref[v, n, 0, 1], 1)
            h = [jnp.where(fy, u_ref[v, 3 - n, 3, q], u_ref[v, n, 3, q]) for q in range(2)]
            y_high_ref[v, n] = pack_high(h[0], h[1], 1)


def restrict_c(first, second):
    low = c_low()
    middle = jnp.where(low, second, first)
    return jnp.where(low, first, second) + FAR * middle + NEAR * sroll(middle, 4)


def restrict_four(values):
    return values[0] + NEAR * values[1] + FAR * values[2], values[3] + NEAR * values[2] + FAR * values[1]


def put_coarse_faces(v, lows, highs, flag_ref, faces):
    for d in range(2):
        flag = flag_ref[d] != 0
        low, high = lows[d], highs[d]
        turned = [jnp.where(flag, high[1 - m], high[m]) for m in range(2)]
        faces[2 * d][v] = pack_low(*low, d)
        faces[2 * d + 1][v] = pack_high(*turned, d)


def restricted_faces(u_ref, flag_ref, faces):
    for v in range(5):
        line = {}
        for a in range(4):
            for b in range(4):
                if a in (0, 3) or b in (0, 3):
                    line[a, b] = restrict_c(u_ref[v, a, b, 0], u_ref[v, a, b, 1])
        lows = [restrict_four([line[0, n] for n in range(4)]), restrict_four([line[n, 0] for n in range(4)])]
        highs = [restrict_four([line[3, n] for n in range(4)]), restrict_four([line[n, 3] for n in range(4)])]
        put_coarse_faces(v, lows, highs, flag_ref, faces)


def first_kernel(
    src_hbm, smooth_hbm, orient_hbm, src_ref, smooth_ref, u_ref, flag_ref, f0, f1, f2, f3, sems, orient_ref, orient_sem
):
    faces = (f0, f1, f2, f3)
    orient_copy = pltpu.make_async_copy(orient_hbm, orient_ref, orient_sem)
    orient_copy.start()
    copies = []
    for slot, a in enumerate((0, 3, 1, 2)):
        pair = (
            pltpu.make_async_copy(src_hbm.at[:, a], src_ref.at[:, a], sems.at[0, slot]),
            pltpu.make_async_copy(smooth_hbm.at[:, a], smooth_ref.at[:, a], sems.at[1, slot]),
        )
        for one in pair:
            one.start()
        copies.append((a, pair))
    orient_copy.wait()
    for d in range(3):
        flag_ref[d] = twice(orient_ref[d])
    for a, pair in copies:
        for one in pair:
            one.wait()

        def one_line(b, carry, a=a):
            src = [[src_ref[v, a, b, q] for q in range(2)] for v in range(5)]
            for o in range(5):
                total = [None, None]
                for i in range(5):
                    block = smooth_ref[5 * o + i, a, b].astype(F32)
                    for q in range(2):
                        term = block[8 * q : 8 * q + 8] * src[i][q]
                        total[q] = term if i == 0 else total[q] + term
                for q in range(2):
                    u_ref[o, a, b, q] = OMEGA * total[q]
            return carry

        lax.fori_loop(0, 4, one_line, 0)
    fine_faces(u_ref, flag_ref, *faces)


def prepare_tables(jac_ref, damp_ref, jac8_ref, damp8_ref, face_ref):
    damp = twice(damp_ref[...])
    damp8_ref[...] = damp
    for d in range(3):
        for k in range(25):
            value = twice(jac_ref[25 * d + k])
            jac8_ref[25 * d + k] = value
            if d < 2:
                low, step = axis_low(d)
                diagonal = k % 6 == 0
                upper = H4 * (value - damp if diagonal else value)
                lower = H4 * (value + damp if diagonal else value)
                face_ref[2 * d, k] = jnp.where(low, sroll(upper, -step), upper)
                face_ref[2 * d + 1, k] = jnp.where(low, lower, sroll(lower, step))


def volume(src_ref, u_ref, flag_ref, jac_ref, damp_ref, acc_ref):
    damp = H4 * damp_ref[...]

    def jacobian(d):
        return [[jac_ref[25 * d + 5 * o + i] for i in range(5)] for o in range(5)]

    def along(direction):
        low, step = axis_low(direction)
        flag = flag_ref[direction] != 0
        flag_before = sroll(flag_ref[direction], step) != 0

        def at(v, n, other, q):
            return (v, n, other, q) if direction == 0 else (v, other, n, q)

        def step_fn(j, carry):
            other, q = j // 2, j % 2
            u = [[u_ref[at(v, n, other, q)] for n in range(4)] for v in range(5)]
            waves = []
            jumps = []
            for v in range(5):
                back_low, back_high = u_ref[at(v, 0, 3 - other, q)], u_ref[at(v, 3, 3 - other, q)]
                right = sroll(jnp.where(flag_before, back_low, u[v][0]), -step)
                left = sroll(jnp.where(flag, back_high, u[v][3]), step)
                jump_right = jnp.where(low, right, 0.0) - u[v][3]
                jump_left = jnp.where(low, 0.0, left) - u[v][0]
                w = list(slopes_along(*u[v]))
                w[3] = w[3] + H4 * jump_right
                w[0] = w[0] - H4 * jump_left
                waves.append(w)
                jumps.append((damp * jump_left, None, None, damp * jump_right))
            matrix = jacobian(direction)
            for n in range(4):
                flux = mix(matrix, [waves[v][n] for v in range(5)])
                for v in range(5):
                    if direction == 0:
                        total = src_ref[at(v, n, other, q)] - 2.0 * u[v][n]
                    else:
                        total = acc_ref[at(v, n, other, q)]
                    total = total - flux[v]
                    if jumps[v][n] is not None:
                        total = total + jumps[v][n]
                    acc_ref[at(v, n, other, q)] = total
            return carry

        lax.fori_loop(0, 8, step_fn, 0)

    along(0)
    along(1)

    low = c_low()
    flag = jnp.where(low, lroll(flag_ref[2], 1), flag_ref[2]) != 0
    damp_z = damp
    coef = [
        [jnp.where(low, float(D4[2 * p, c]), float(D4[2 * p + 1, c ^ 1])).astype(F32) for c in range(4)]
        for p in range(2)
    ]

    def step_z(j, carry):
        a0, b = j // 4, j % 4
        here = (a0, 3 - a0)
        u = [[[u_ref[v, a, b, q] for q in range(2)] for v in range(5)] for a in here]
        turned = [[[sroll(u[s][v][q], 4) for q in range(2)] for v in range(5)] for s in range(2)]
        beside = []
        for s in range(2):
            line = []
            for v in range(5):
                face = jnp.where(low, turned[s][v][1], turned[s][v][0])
                line.append(jnp.where(low, lroll(face, 1), lroll(face, -1)))
            beside.append(line)
        matrix = jacobian(2)
        for s in range(2):
            waves = [[], []]
            jumps = []
            for v in range(5):
                own = jnp.where(low, u[s][v][0], u[s][v][1])
                jump = jnp.where(flag, beside[1 - s][v], beside[s][v]) - own
                jumps.append(damp_z * jump)
                lifted = H4 * jump
                for p in range(2):
                    w = coef[p][0] * u[s][v][0] + coef[p][1] * turned[s][v][0]
                    w = w + (coef[p][2] * u[s][v][1] + coef[p][3] * turned[s][v][1])
                    w = w - jnp.where(low, lifted, 0.0) if p == 0 else w + jnp.where(low, 0.0, lifted)
                    waves[p].append(w)
            for p in range(2):
                flux = mix(matrix, waves[p])
                for v in range(5):
                    part = jnp.where(low, jumps[v], 0.0) if p == 0 else jnp.where(low, 0.0, jumps[v])
                    acc_ref[v, here[s], b, p] = acc_ref[v, here[s], b, p] - flux[v] + part
        return carry

    lax.fori_loop(0, 8, step_z, 0)


def first_volume_kernel(src_ref, u_ref, flag_ref, jac_ref, damp_ref, acc_ref, jac8_ref, damp8_ref, face_ref):
    prepare_tables(jac_ref, damp_ref, jac8_ref, damp8_ref, face_ref)
    volume(src_ref, u_ref, flag_ref, jac8_ref, damp8_ref, acc_ref)


def both_colours(refs):
    return [(refs[k], refs[4 + k]) for k in range(4)], refs[8:]


def remote_parts(got, flag_ref, face_ref, part_ref):
    for d in range(2):
        low, step = axis_low(d)
        flag = flag_ref[d]
        flag = jnp.where(low, sroll(flag, -step), flag) != 0
        from_right, from_left = got[2 * d], got[2 * d + 1]
        matrix = [[face_ref[2 * d, 5 * o + i] for i in range(5)] for o in range(5)]
        for n in range(4):
            right = [
                jnp.where(flag, received(from_right, (v, 3 - n)), received(from_right, (v, n))) for v in range(5)
            ]
            for v, value in enumerate(mix(matrix, right)):
                part_ref[2 * d, v, n, 0] = jnp.where(low, 0.0, -sroll(value, step))
                part_ref[2 * d, v, n, 1] = jnp.where(low, 0.0, -value)
        matrix = [[face_ref[2 * d + 1, 5 * o + i] for i in range(5)] for o in range(5)]
        for n in range(4):
            left = [received(from_left, (v, n)) for v in range(5)]
            for v, value in enumerate(mix(matrix, left)):
                part_ref[2 * d + 1, v, n, 0] = jnp.where(low, value, 0.0)
                part_ref[2 * d + 1, v, n, 1] = jnp.where(low, sroll(value, -step), 0.0)


def whole(acc_ref, part_ref, v, a, b, q):
    total = acc_ref[v, a, b, q]
    if a == 3:
        total = total + part_ref[0, v, b, q]
    if a == 0:
        total = total + part_ref[1, v, b, q]
    if b == 3:
        total = total + part_ref[2, v, a, q]
    if b == 0:
        total = total + part_ref[3, v, a, q]
    return total


def second_kernel(
    acc_ref, u_ref, smooth_ref, flag_ref, face_ref, *refs
):
    got, (out_ref, *faces, part_ref) = both_colours(refs)
    remote_parts(got, flag_ref, face_ref, part_ref)
    for a in range(4):
        for b in range(4):
            left = [[whole(acc_ref, part_ref, v, a, b, q) for q in range(2)] for v in range(5)]
            for o in range(5):
                total = [None, None]
                for i in range(5):
                    block = smooth_ref[5 * o + i, a, b].astype(F32)
                    for q in range(2):
                        term = block[8 * q : 8 * q + 8] * left[i][q]
                        total[q] = term if i == 0 else total[q] + term
                for q in range(2):
                    out_ref[o, a, b, q] = u_ref[o, a, b, q] + OMEGA * total[q]
    restricted_faces(out_ref, flag_ref, faces)


def coarse_smooth(smooth_ref, fields):
    out = [[[None, None], [None, None]] for _ in range(5)]
    for i in range(2):
        for o in range(5):
            total = [None, None]
            for k in range(5):
                block = smooth_ref[5 * o + k, i].astype(F32)
                for j in range(2):
                    term = block[8 * j : 8 * j + 8] * fields[k][i][j]
                    total[j] = term if k == 0 else total[j] + term
            for j in range(2):
                out[o][i][j] = OMEGA * total[j]
    return out


def coarse_faces(field, flag_ref, faces):
    for v in range(5):
        c = field[v]
        lows = [[c[0][0], c[0][1]], [c[0][0], c[1][0]]]
        highs = [[c[1][0], c[1][1]], [c[0][1], c[1][1]]]
        put_coarse_faces(v, lows, highs, flag_ref, faces)


def restricted_volume_kernel(src_ref, u_ref, flag_ref, jac_ref, damp_ref, acc_ref):
    damp = H4 * damp_ref[...]
    low_c = c_low()
    slope = [
        jnp.where(low_c, float(PD[0, c]), float(PD[1, c ^ 1])).astype(F32) for c in range(4)
    ]
    flags = [flag_ref[0] != 0, flag_ref[1] != 0, jnp.where(low_c, lroll(flag_ref[2], 1), flag_ref[2]) != 0]
    sign = jnp.where(low_c, -H4, H4).astype(F32)
    waves = [[[[None] * 5 for _ in range(2)] for _ in range(2)] for _ in range(3)]

    def slopes_four(values):
        return [sum_of([(float(PD[i, n]), values[n]) for n in range(4)]) for i in range(2)]

    for v in range(5):
        line, slope_c, ends = {}, {}, {}
        for a in range(4):
            for b in range(4):
                first, second = u_ref[v, a, b, 0], u_ref[v, a, b, 1]
                line[a, b] = restrict_c(first, second)
                slope_c[a, b] = (slope[0] * first + slope[1] * sroll(first, 4)) + (
                    slope[2] * second + slope[3] * sroll(second, 4)
                )
                ends[a, b] = jnp.where(low_c, first, second)

        def along_b(table):
            return [restrict_four([table[a, b] for b in range(4)]) for a in range(4)]

        def both(table):
            by_b = along_b(table)
            return [restrict_four([by_b[a][j] for a in range(4)]) for j in range(2)]

        by_b = along_b(line)
        by_a = [restrict_four([line[a, b] for a in range(4)]) for b in range(4)]
        flux_z = both(slope_c)
        trace_z = both(ends)
        sources = both({(a, b): restrict_c(src_ref[v, a, b, 0], src_ref[v, a, b, 1]) for a in range(4) for b in range(4)})
        acc = [[None, None], [None, None]]
        for j in range(2):
            value = restrict_four([by_b[a][j] for a in range(4)])
            flux = slopes_four([by_b[a][j] for a in range(4)])
            for i in range(2):
                acc[i][j] = sources[j][i] - 2.0 * value[i]
                waves[0][i][j][v] = flux[i]
        for i in range(2):
            flux = slopes_four([by_a[b][i] for b in range(4)])
            for j in range(2):
                waves[1][i][j][v] = flux[j]
        for d, lo, hi in ((0, by_b[0], by_b[3]), (1, by_a[0], by_a[3])):
            low, step = axis_low(d)
            flag = flags[d]
            flag_before = sroll(flag_ref[d], step) != 0
            for m in range(2):
                right = sroll(jnp.where(flag_before, lo[1 - m], lo[m]), -step)
                left = sroll(jnp.where(flag, hi[1 - m], hi[m]), step)
                jump_right = jnp.where(low, right, 0.0) - hi[m]
                jump_left = jnp.where(low, 0.0, left) - lo[m]
                i, j = (1, m) if d == 0 else (m, 1)
                waves[d][i][j][v] = waves[d][i][j][v] + H4 * jump_right
                acc[i][j] = acc[i][j] + damp * jump_right
                i, j = (0, m) if d == 0 else (m, 0)
                waves[d][i][j][v] = waves[d][i][j][v] - H4 * jump_left
                acc[i][j] = acc[i][j] + damp * jump_left
        beside = []
        for j in range(2):
            turned = [sroll(trace_z[j][i], 4) for i in range(2)]
            beside.append([jnp.where(low_c, lroll(t, 1), lroll(t, -1)) for t in turned])
        for i in range(2):
            for j in range(2):
                jump = jnp.where(flags[2], beside[j][1 - i], beside[j][i]) - trace_z[j][i]
                waves[2][i][j][v] = flux_z[j][i] + sign * jump
                acc_ref[v, i, j] = acc[i][j] + damp * jump
    for d in range(3):
        matrix = [[jac_ref[25 * d + 5 * o + i] for i in range(5)] for o in range(5)]
        for i in range(2):
            for j in range(2):
                for v, value in enumerate(mix(matrix, waves[d][i][j])):
                    acc_ref[v, i, j] = acc_ref[v, i, j] - value


def restrict_kernel(
    acc_ref, flag_ref, face_ref, smooth_ref, *refs
):
    got, (rhs_ref, c_ref, *faces) = both_colours(refs)
    rhs = [[[acc_ref[v, i, j] for j in range(2)] for i in range(2)] for v in range(5)]
    for d in range(2):
        low, step = axis_low(d)
        flag = flag_ref[d]
        flag = jnp.where(low, sroll(flag, -step), flag) != 0
        at = (lambda n, m: (n, m)) if d == 0 else (lambda n, m: (m, n))
        right, left = [], []
        for v in range(5):
            value = received(got[2 * d], v)
            swapped = jnp.where(low, sroll(value, -step), sroll(value, step))
            right.append(jnp.where(flag, swapped, value))
            left.append(received(got[2 * d + 1], v))
        upper = [[face_ref[2 * d, 5 * o + i] for i in range(5)] for o in range(5)]
        lower = [[face_ref[2 * d + 1, 5 * o + i] for i in range(5)] for o in range(5)]
        for v, value in enumerate(mix(upper, right)):
            for m, part in enumerate((sroll(value, step), value)):
                i, j = at(1, m)
                rhs[v][i][j] = rhs[v][i][j] - jnp.where(low, 0.0, part)
        for v, value in enumerate(mix(lower, left)):
            for m, part in enumerate((value, sroll(value, -step))):
                i, j = at(0, m)
                rhs[v][i][j] = rhs[v][i][j] + jnp.where(low, part, 0.0)
    c = coarse_smooth(smooth_ref, rhs)
    for v in range(5):
        for i in range(2):
            for j in range(2):
                rhs_ref[v, i, j] = rhs[v][i][j]
                c_ref[v, i, j] = c[v][i][j]
    coarse_faces(c, flag_ref, faces)


def coarse_step(c_ref, rhs_ref, smooth_ref, flag_ref, jac_ref, damp_ref, got):
    damp = 0.5 * damp_ref[...]
    c = [[[c_ref[v, i, j] for j in range(2)] for i in range(2)] for v in range(5)]
    acc = [[[rhs_ref[v, i, j] - 2.0 * c[v][i][j] for j in range(2)] for i in range(2)] for v in range(5)]
    for d in range(2):
        low, step = axis_low(d)
        flag = flag_ref[d] != 0
        matrix = [[jac_ref[25 * d + 5 * o + i] for i in range(5)] for o in range(5)]
        at = (lambda n, m: (n, m)) if d == 0 else (lambda n, m: (m, n))
        waves = [[[None] * 5, [None] * 5] for _ in range(2)]
        for v in range(5):
            got_right = received(got[2 * d], v)
            got_left = received(got[2 * d + 1], v)
            lo = [c[v][at(0, m)[0]][at(0, m)[1]] for m in range(2)]
            hi = [c[v][at(1, m)[0]][at(1, m)[1]] for m in range(2)]
            right = [
                jnp.where(low, sroll(lo[0], -step), sroll(got_right, step)),
                jnp.where(low, sroll(lo[1], -step), got_right),
            ]
            right = [jnp.where(flag, right[1 - m], right[m]) for m in range(2)]
            left = [sroll(jnp.where(flag, hi[1 - m], hi[m]), step) for m in range(2)]
            left = [jnp.where(low, got_left, left[0]), jnp.where(low, sroll(got_left, -step), left[1])]
            for m in range(2):
                waves[1][m][v] = 0.5 * (right[m] - lo[m])
                waves[0][m][v] = 0.5 * (hi[m] - left[m])
                i, j = at(1, m)
                acc[v][i][j] = acc[v][i][j] + damp * (right[m] - hi[m])
                i, j = at(0, m)
                acc[v][i][j] = acc[v][i][j] + damp * (left[m] - lo[m])
        for n in range(2):
            for m in range(2):
                i, j = at(n, m)
                for v, value in enumerate(mix(matrix, waves[n][m])):
                    acc[v][i][j] = acc[v][i][j] - value
    low = c_low()
    flag = jnp.where(low, lroll(flag_ref[2], 1), flag_ref[2]) != 0
    half = jnp.where(low, 0.5, -0.5).astype(F32)
    matrix = [[jac_ref[50 + 5 * o + i] for i in range(5)] for o in range(5)]
    turned = [[[sroll(c[v][i][j], 4) for j in range(2)] for i in range(2)] for v in range(5)]
    beside = [
        [[jnp.where(low, lroll(t, 1), lroll(t, -1)) for t in turned[v][i]] for i in range(2)] for v in range(5)
    ]
    for i in range(2):
        for j in range(2):
            wave = []
            for v in range(5):
                next_to = jnp.where(flag, beside[v][1 - i][j], beside[v][i][j])
                wave.append(half * (turned[v][i][j] - next_to))
                acc[v][i][j] = acc[v][i][j] + damp * (next_to - c[v][i][j])
            for v, value in enumerate(mix(matrix, wave)):
                acc[v][i][j] = acc[v][i][j] - value
    change = coarse_smooth(smooth_ref, acc)
    return [[[c[v][i][j] + change[v][i][j] for j in range(2)] for i in range(2)] for v in range(5)]


def coarse_kernel(c_ref, rhs_ref, smooth_ref, flag_ref, jac_ref, damp_ref, *refs):
    got, (out_ref, *faces) = both_colours(refs)
    c = coarse_step(c_ref, rhs_ref, smooth_ref, flag_ref, jac_ref, damp_ref, got)
    for v in range(5):
        for i in range(2):
            for j in range(2):
                out_ref[v, i, j] = c[v][i][j]
    coarse_faces(c, flag_ref, faces)


def spread(first, second):
    return first, NEAR * first + FAR * second, FAR * first + NEAR * second, second


def last_kernel(c_ref, rhs_ref, smooth_ref, flag_ref, jac_ref, damp_ref, *refs):
    got, (second_ref, out_hbm, out_ref, sems) = both_colours(refs)
    c = coarse_step(c_ref, rhs_ref, smooth_ref, flag_ref, jac_ref, damp_ref, got)
    low = c_low()
    copies = []
    for v in range(5):
        by_c = [[None, None], [None, None]]
        for i in range(2):
            for j in range(2):
                value = c[v][i][j]
                inner = FAR * value + NEAR * sroll(value, 4)
                by_c[i][j] = (jnp.where(low, value, inner), jnp.where(low, inner, value))
        for q in range(2):
            lines = [spread(by_c[i][0][q], by_c[i][1][q]) for i in range(2)]
            for b in range(4):
                for a, value in enumerate(spread(lines[0][b], lines[1][b])):
                    out_ref[v, a, b, q] = second_ref[v, a, b, q] + value
        copy = pltpu.make_async_copy(out_ref.at[v], out_hbm.at[v], sems.at[v])
        copy.start()
        copies.append(copy)
    for copy in copies:
        copy.wait()


FINE = (5, 4, 4, 2, 8, 128)
FINE_MESSAGE = (5, 4, 8, 128)
COARSE = (5, 2, 2, 8, 128)
COARSE_MESSAGE = (5, 8, 128)


def vmem(shape, dtype=F32):
    return pltpu.VMEM(shape, dtype)


def here(array):
    return pltpu.with_memory_space_constraint(array, pltpu.VMEM)


def call(kernel, args, outs, in_hbm=(), out_hbm=(), scratch=(), flops=0):
    in_specs = [
        pl.BlockSpec(memory_space=pltpu.HBM if k in in_hbm else pltpu.VMEM) for k in range(len(args))
    ]
    out_specs = [
        pl.BlockSpec(memory_space=pltpu.HBM if k in out_hbm else pltpu.VMEM) for k in range(len(outs))
    ]
    args = [pltpu.with_memory_space_constraint(a, pltpu.HBM) if k in in_hbm else here(a) for k, a in enumerate(args)]
    return pl.pallas_call(
        kernel,
        out_shape=outs,
        in_specs=in_specs,
        out_specs=out_specs,
        scratch_shapes=scratch,
        compiler_params=pltpu.CompilerParams(vmem_limit_bytes=8 * 2**20),
        cost_estimate=pl.CostEstimate(flops=flops, bytes_accessed=4 * 2**20, transcendentals=0),
    )(*args)


def half_ring(dx, dy, colour):
    nx, ny = lax.axis_size("gx"), lax.axis_size("gy")
    return [
        (i * ny + j, (i + dx) % nx * ny + (j + dy) % ny) for i in range(nx) for j in range(ny) if (i + j) % 2 == colour
    ]


def exchange(*faces):
    steps = ((-1, 0), (1, 0), (0, -1), (0, 1))

    def send(faces, colour):
        return [lax.ppermute(face, ("gx", "gy"), half_ring(dx, dy, colour)) for face, (dx, dy) in zip(faces, steps)]

    white = send(faces, 0)
    *white, f0, f1, f2, f3 = lax.optimization_barrier((*white, *faces))
    return white + send((f0, f1, f2, f3), 1)


def body(source, jacobian, damping, orient, smoother, coarse_smoother):
    source = source.reshape(FINE)
    smoother = smoother.reshape(25, 4, 4, 16, 128)
    coarse_smoother = coarse_smoother.reshape(25, 2, 16, 128)
    jacobian = jacobian.reshape(75, 4, 128)
    damping = damping.reshape(4, 128)
    orient = orient.reshape(3, 4, 128)
    fine_messages = [vmem(FINE_MESSAGE)] * 4
    coarse_messages = [vmem(COARSE_MESSAGE)] * 4

    source, smoother, first, flag, *sent = call(
        first_kernel,
        (source, smoother, orient),
        [vmem(FINE), vmem(smoother.shape, smoother.dtype), vmem(FINE), vmem((3, 8, 128), jnp.int32)] + fine_messages,
        in_hbm=(0, 1, 2),
        scratch=[pltpu.SemaphoreType.DMA((2, 4)), pltpu.VMEM((3, 4, 128), jnp.int32), pltpu.SemaphoreType.DMA],
        flops=2 * 25 * 64 * 512,
    )
    got = exchange(*sent)
    acc, jac8, damp8, face = call(
        first_volume_kernel,
        (source, first, flag, jacobian, damping),
        [vmem(FINE), vmem((75, 8, 128)), vmem((8, 128)), vmem((4, 25, 8, 128))],
        flops=9 * 2**20,
    )
    second, *sent = call(
        second_kernel,
        (acc, first, smoother, flag, face, *got),
        [vmem(FINE)] + coarse_messages,
        scratch=[pltpu.VMEM((4, 5, 4, 2, 8, 128), F32)],
        flops=3 * 2**20,
    )
    got = exchange(*sent)
    (acc,) = call(restricted_volume_kernel, (source, second, flag, jac8, damp8), [vmem(COARSE)], flops=4 * 2**20)
    rhs, coarse, *sent = call(
        restrict_kernel,
        (acc, flag, face, coarse_smoother, *got),
        [vmem(COARSE), vmem(COARSE)] + coarse_messages,
        flops=2**20,
    )
    got = exchange(*sent)
    coarse, *sent = call(
        coarse_kernel,
        (coarse, rhs, coarse_smoother, flag, jac8, damp8, *got),
        [vmem(COARSE)] + coarse_messages,
        flops=2**20,
    )
    got = exchange(*sent)
    (out,) = call(
        last_kernel,
        (coarse, rhs, coarse_smoother, flag, jac8, damp8, *got, second),
        [jax.ShapeDtypeStruct(FINE, F32)],
        out_hbm=(0,),
        scratch=[pltpu.VMEM(FINE, F32), pltpu.SemaphoreType.DMA((5,))],
        flops=2**20,
    )
    return out.reshape(5, 4, 4, 4, 2, 2, 128)


def solution(mesh):
    in_specs = (
        P(None, None, None, None, "gx", "gy", None),
        P(None, None, None, "gx", "gy", None),
        P("gx", "gy", None),
        P(None, "gx", "gy", None),
        P(None, None, None, None, None, "gx", "gy", None),
        P(None, None, None, None, None, "gx", "gy", None),
    )
    out_specs = P(None, None, None, None, "gx", "gy", None)
    return jax.shard_map(body, mesh=mesh, in_specs=in_specs, out_specs=out_specs, check_vma=False)
```

```python
import functools
import math

import jax
import jax.numpy as jnp
import numpy as np
from jax import lax
from jax.experimental import pallas as pl
from jax.experimental.pallas import tpu as pltpu
from jax.sharding import PartitionSpec as P


F32 = jnp.float32
OMEGA = 0.8
H4 = 3.0
ROOT = 1.0 / math.sqrt(5.0)
NEAR = (1.0 + ROOT) / 2.0
FAR = (1.0 - ROOT) / 2.0


def lobatto_slopes():
    points = np.array([-1.0, -ROOT, ROOT, 1.0])
    weights = np.ones(4)
    for i in range(4):
        for j in range(4):
            if i != j:
                weights[i] = weights[i] / (points[i] - points[j])
    slopes = np.zeros((4, 4))
    for i in range(4):
        for j in range(4):
            if i != j:
                slopes[i, j] = weights[j] / weights[i] / (points[i] - points[j])
        slopes[i, i] = -np.sum(slopes[i])
    return slopes


D4 = lobatto_slopes()
PD = np.array([[1.0, NEAR, FAR, 0.0], [0.0, FAR, NEAR, 1.0]]) @ D4


def sum_of(terms):
    total = None
    for weight, value in terms:
        total = weight * value if total is None else total + weight * value
    return total


def rows():
    return lax.broadcasted_iota(jnp.int32, (8, 128), 0)


def x_low():
    return (rows() & 2) == 0


def y_low():
    return (rows() & 1) == 0


def c_low():
    return (rows() & 4) == 0


def sroll(value, shift):
    return pltpu.roll(value, shift % 8, 0)


def lroll(value, shift):
    return pltpu.roll(value, shift % 128, 1)


def twice(value):
    return jnp.concatenate([value, value], axis=0)


def axis_low(direction):
    return (x_low(), 2) if direction == 0 else (y_low(), 1)


def pack_low(first, second, direction):
    low, step = axis_low(direction)
    return jnp.where(low, first, sroll(second, step))


def pack_high(first, second, direction):
    low, step = axis_low(direction)
    return jnp.where(low, sroll(first, -step), second)


def slopes_along(u0, u1, u2, u3):
    e0, o0, e1, o1 = u0 + u3, u0 - u3, u1 + u2, u1 - u2
    diff = e1 - e0
    even_a = float((D4[0, 1] + D4[0, 2]) / 2.0) * diff
    even_b = float((D4[1, 2] - 0.0) / 2.0) * diff
    odd_a = float((D4[0, 0] - D4[0, 3]) / 2.0) * o0 + float((D4[0, 1] - D4[0, 2]) / 2.0) * o1
    odd_b = float((D4[1, 0] - D4[1, 3]) / 2.0) * o0 - float(D4[1, 2] / 2.0) * o1
    return even_a + odd_a, even_b + odd_b, odd_b - even_b, odd_a - even_a


def mix(matrix, fields):
    out = []
    for o in range(5):
        total = matrix[o][0] * fields[0]
        for i in range(1, 5):
            total = total + matrix[o][i] * fields[i]
        out.append(total)
    return out


def parity(axis):
    return lax.rem(lax.axis_index(axis), 2) == 0


def put_pair(even_ref, odd_ref, index, low_face, high_face, is_even):
    even_ref[index] = jnp.where(is_even, high_face, low_face)
    odd_ref[index] = jnp.where(is_even, low_face, high_face)


def block_views(even_ref, odd_ref):
    x, y = lax.rem(lax.axis_index("gx"), 2), lax.rem(lax.axis_index("gy"), 2)
    return (
        odd_ref.at[x + 2 * (1 - y)],
        even_ref.at[(1 - x) + 2 * y],
        odd_ref.at[(1 - x) + 2 * y],
        even_ref.at[x + 2 * (1 - y)],
    )


def fine_faces(u_ref, flag_ref, xo, xe, yo, ye):
    even_x, even_y = parity("gx"), parity("gy")
    fx, fy = flag_ref[0] != 0, flag_ref[1] != 0
    for v in range(5):
        for n in range(4):
            low = pack_low(u_ref[v, 0, n, 0], u_ref[v, 0, n, 1], 0)
            h = [jnp.where(fx, u_ref[v, 3, 3 - n, q], u_ref[v, 3, n, q]) for q in range(2)]
            put_pair(xe, xo, (v, n), low, pack_high(h[0], h[1], 0), even_x)
            low = pack_low(u_ref[v, n, 0, 0], u_ref[v, n, 0, 1], 1)
            h = [jnp.where(fy, u_ref[v, 3 - n, 3, q], u_ref[v, n, 3, q]) for q in range(2)]
            put_pair(ye, yo, (v, n), low, pack_high(h[0], h[1], 1), even_y)


def restrict_c(first, second):
    low = c_low()
    middle = jnp.where(low, second, first)
    return jnp.where(low, first, second) + FAR * middle + NEAR * sroll(middle, 4)


def restrict_four(values):
    return values[0] + NEAR * values[1] + FAR * values[2], values[3] + NEAR * values[2] + FAR * values[1]


def put_coarse_faces(v, lows, highs, flag_ref, pairs):
    for d, axis in ((0, "gx"), (1, "gy")):
        flag = flag_ref[d] != 0
        low, high = lows[d], highs[d]
        turned = [jnp.where(flag, high[1 - m], high[m]) for m in range(2)]
        even_ref, odd_ref = pairs[d]
        put_pair(even_ref, odd_ref, v, pack_low(*low, d), pack_high(*turned, d), parity(axis))


def restricted_faces(u_ref, flag_ref, xo, xe, yo, ye):
    for v in range(5):
        line = {}
        for a in range(4):
            for b in range(4):
                if a in (0, 3) or b in (0, 3):
                    line[a, b] = restrict_c(u_ref[v, a, b, 0], u_ref[v, a, b, 1])
        lows = [restrict_four([line[0, n] for n in range(4)]), restrict_four([line[n, 0] for n in range(4)])]
        highs = [restrict_four([line[3, n] for n in range(4)]), restrict_four([line[n, 3] for n in range(4)])]
        put_coarse_faces(v, lows, highs, flag_ref, ((xe, xo), (ye, yo)))


def first_kernel(
    src_hbm, smooth_hbm, orient_hbm, src_ref, smooth_ref, u_ref, flag_ref, xo, xe, yo, ye, sems, orient_ref, orient_sem
):
    orient_copy = pltpu.make_async_copy(orient_hbm, orient_ref, orient_sem)
    orient_copy.start()
    copies = []
    for slot, a in enumerate((0, 3, 1, 2)):
        pair = (
            pltpu.make_async_copy(src_hbm.at[:, a], src_ref.at[:, a], sems.at[0, slot]),
            pltpu.make_async_copy(smooth_hbm.at[:, a], smooth_ref.at[:, a], sems.at[1, slot]),
        )
        for one in pair:
            one.start()
        copies.append((a, pair))
    orient_copy.wait()
    for d in range(3):
        flag_ref[d] = twice(orient_ref[d])
    for a, pair in copies:
        for one in pair:
            one.wait()

        def one_line(b, carry, a=a):
            src = [[src_ref[v, a, b, q] for q in range(2)] for v in range(5)]
            for o in range(5):
                total = [None, None]
                for i in range(5):
                    block = smooth_ref[5 * o + i, a, b].astype(F32)
                    for q in range(2):
                        term = block[8 * q : 8 * q + 8] * src[i][q]
                        total[q] = term if i == 0 else total[q] + term
                for q in range(2):
                    u_ref[o, a, b, q] = OMEGA * total[q]
            return carry

        lax.fori_loop(0, 4, one_line, 0)
    fine_faces(u_ref, flag_ref, xo, xe, yo, ye)


def prepare_tables(jac_ref, damp_ref, jac8_ref, damp8_ref, face_ref):
    damp = twice(damp_ref[...])
    damp8_ref[...] = damp
    for d in range(3):
        for k in range(25):
            value = twice(jac_ref[25 * d + k])
            jac8_ref[25 * d + k] = value
            if d < 2:
                low, step = axis_low(d)
                diagonal = k % 6 == 0
                upper = H4 * (value - damp if diagonal else value)
                lower = H4 * (value + damp if diagonal else value)
                face_ref[2 * d, k] = jnp.where(low, sroll(upper, -step), upper)
                face_ref[2 * d + 1, k] = jnp.where(low, lower, sroll(lower, step))


def volume(src_ref, u_ref, flag_ref, jac_ref, damp_ref, acc_ref):
    damp = H4 * damp_ref[...]

    def jacobian(d):
        return [[jac_ref[25 * d + 5 * o + i] for i in range(5)] for o in range(5)]

    def along(direction):
        low, step = axis_low(direction)
        flag = flag_ref[direction] != 0
        flag_before = sroll(flag_ref[direction], step) != 0

        def at(v, n, other, q):
            return (v, n, other, q) if direction == 0 else (v, other, n, q)

        def step_fn(j, carry):
            other, q = j // 2, j % 2
            u = [[u_ref[at(v, n, other, q)] for n in range(4)] for v in range(5)]
            waves = []
            jumps = []
            for v in range(5):
                back_low, back_high = u_ref[at(v, 0, 3 - other, q)], u_ref[at(v, 3, 3 - other, q)]
                right = sroll(jnp.where(flag_before, back_low, u[v][0]), -step)
                left = sroll(jnp.where(flag, back_high, u[v][3]), step)
                jump_right = jnp.where(low, right, 0.0) - u[v][3]
                jump_left = jnp.where(low, 0.0, left) - u[v][0]
                w = list(slopes_along(*u[v]))
                w[3] = w[3] + H4 * jump_right
                w[0] = w[0] - H4 * jump_left
                waves.append(w)
                jumps.append((damp * jump_left, None, None, damp * jump_right))
            matrix = jacobian(direction)
            for n in range(4):
                flux = mix(matrix, [waves[v][n] for v in range(5)])
                for v in range(5):
                    if direction == 0:
                        total = src_ref[at(v, n, other, q)] - 2.0 * u[v][n]
                    else:
                        total = acc_ref[at(v, n, other, q)]
                    total = total - flux[v]
                    if jumps[v][n] is not None:
                        total = total + jumps[v][n]
                    acc_ref[at(v, n, other, q)] = total
            return carry

        lax.fori_loop(0, 8, step_fn, 0)

    along(0)
    along(1)

    low = c_low()
    flag = jnp.where(low, lroll(flag_ref[2], 1), flag_ref[2]) != 0
    damp_z = damp
    coef = [
        [jnp.where(low, float(D4[2 * p, c]), float(D4[2 * p + 1, c ^ 1])).astype(F32) for c in range(4)]
        for p in range(2)
    ]

    def step_z(j, carry):
        a0, b = j // 4, j % 4
        here = (a0, 3 - a0)
        u = [[[u_ref[v, a, b, q] for q in range(2)] for v in range(5)] for a in here]
        turned = [[[sroll(u[s][v][q], 4) for q in range(2)] for v in range(5)] for s in range(2)]
        beside = []
        for s in range(2):
            line = []
            for v in range(5):
                face = jnp.where(low, turned[s][v][1], turned[s][v][0])
                line.append(jnp.where(low, lroll(face, 1), lroll(face, -1)))
            beside.append(line)
        matrix = jacobian(2)
        for s in range(2):
            waves = [[], []]
            jumps = []
            for v in range(5):
                own = jnp.where(low, u[s][v][0], u[s][v][1])
                jump = jnp.where(flag, beside[1 - s][v], beside[s][v]) - own
                jumps.append(damp_z * jump)
                lifted = H4 * jump
                for p in range(2):
                    w = coef[p][0] * u[s][v][0] + coef[p][1] * turned[s][v][0]
                    w = w + (coef[p][2] * u[s][v][1] + coef[p][3] * turned[s][v][1])
                    w = w - jnp.where(low, lifted, 0.0) if p == 0 else w + jnp.where(low, 0.0, lifted)
                    waves[p].append(w)
            for p in range(2):
                flux = mix(matrix, waves[p])
                for v in range(5):
                    part = jnp.where(low, jumps[v], 0.0) if p == 0 else jnp.where(low, 0.0, jumps[v])
                    acc_ref[v, here[s], b, p] = acc_ref[v, here[s], b, p] - flux[v] + part
        return carry

    lax.fori_loop(0, 8, step_z, 0)


def first_volume_kernel(src_ref, u_ref, flag_ref, jac_ref, damp_ref, acc_ref, jac8_ref, damp8_ref, face_ref):
    prepare_tables(jac_ref, damp_ref, jac8_ref, damp8_ref, face_ref)
    volume(src_ref, u_ref, flag_ref, jac8_ref, damp8_ref, acc_ref)


def remote_parts(even_refs, odd_refs, flag_ref, face_ref, part_ref):
    for d, axis in ((0, "gx"), (1, "gy")):
        is_even = parity(axis)
        low, step = axis_low(d)
        flag = flag_ref[d]
        flag = jnp.where(low, sroll(flag, -step), flag) != 0
        even, odd = even_refs[d], odd_refs[d]
        matrix = [[face_ref[2 * d, 5 * o + i] for i in range(5)] for o in range(5)]
        for n in range(4):
            take = lambda v, m: jnp.where(is_even, even[v, m], odd[v, m])
            right = [jnp.where(flag, take(v, 3 - n), take(v, n)) for v in range(5)]
            for v, value in enumerate(mix(matrix, right)):
                part_ref[2 * d, v, n, 0] = jnp.where(low, 0.0, -sroll(value, step))
                part_ref[2 * d, v, n, 1] = jnp.where(low, 0.0, -value)
        matrix = [[face_ref[2 * d + 1, 5 * o + i] for i in range(5)] for o in range(5)]
        for n in range(4):
            left = [jnp.where(is_even, odd[v, n], even[v, n]) for v in range(5)]
            for v, value in enumerate(mix(matrix, left)):
                part_ref[2 * d + 1, v, n, 0] = jnp.where(low, value, 0.0)
                part_ref[2 * d + 1, v, n, 1] = jnp.where(low, sroll(value, -step), 0.0)


def whole(acc_ref, part_ref, v, a, b, q):
    total = acc_ref[v, a, b, q]
    if a == 3:
        total = total + part_ref[0, v, b, q]
    if a == 0:
        total = total + part_ref[1, v, b, q]
    if b == 3:
        total = total + part_ref[2, v, a, q]
    if b == 0:
        total = total + part_ref[3, v, a, q]
    return total


def second_kernel(
    acc_ref, u_ref, smooth_ref, flag_ref, face_ref, rxo, rxe, ryo, rye, out_ref, even_ref, odd_ref, part_ref
):
    remote_parts((rxe, rye), (rxo, ryo), flag_ref, face_ref, part_ref)
    for a in range(4):
        for b in range(4):
            left = [[whole(acc_ref, part_ref, v, a, b, q) for q in range(2)] for v in range(5)]
            for o in range(5):
                total = [None, None]
                for i in range(5):
                    block = smooth_ref[5 * o + i, a, b].astype(F32)
                    for q in range(2):
                        term = block[8 * q : 8 * q + 8] * left[i][q]
                        total[q] = term if i == 0 else total[q] + term
                for q in range(2):
                    out_ref[o, a, b, q] = u_ref[o, a, b, q] + OMEGA * total[q]
    restricted_faces(out_ref, flag_ref, *block_views(even_ref, odd_ref))


def coarse_smooth(smooth_ref, fields):
    out = [[[None, None], [None, None]] for _ in range(5)]
    for i in range(2):
        for o in range(5):
            total = [None, None]
            for k in range(5):
                block = smooth_ref[5 * o + k, i].astype(F32)
                for j in range(2):
                    term = block[8 * j : 8 * j + 8] * fields[k][i][j]
                    total[j] = term if k == 0 else total[j] + term
            for j in range(2):
                out[o][i][j] = OMEGA * total[j]
    return out


def coarse_faces(field, flag_ref, xo, xe, yo, ye):
    for v in range(5):
        c = field[v]
        lows = [[c[0][0], c[0][1]], [c[0][0], c[1][0]]]
        highs = [[c[1][0], c[1][1]], [c[0][1], c[1][1]]]
        put_coarse_faces(v, lows, highs, flag_ref, ((xe, xo), (ye, yo)))


def restricted_volume_kernel(src_ref, u_ref, flag_ref, jac_ref, damp_ref, acc_ref):
    damp = H4 * damp_ref[...]
    low_c = c_low()
    slope = [
        jnp.where(low_c, float(PD[0, c]), float(PD[1, c ^ 1])).astype(F32) for c in range(4)
    ]
    flags = [flag_ref[0] != 0, flag_ref[1] != 0, jnp.where(low_c, lroll(flag_ref[2], 1), flag_ref[2]) != 0]
    sign = jnp.where(low_c, -H4, H4).astype(F32)
    waves = [[[[None] * 5 for _ in range(2)] for _ in range(2)] for _ in range(3)]

    def slopes_four(values):
        return [sum_of([(float(PD[i, n]), values[n]) for n in range(4)]) for i in range(2)]

    for v in range(5):
        line, slope_c, ends = {}, {}, {}
        for a in range(4):
            for b in range(4):
                first, second = u_ref[v, a, b, 0], u_ref[v, a, b, 1]
                line[a, b] = restrict_c(first, second)
                slope_c[a, b] = (slope[0] * first + slope[1] * sroll(first, 4)) + (
                    slope[2] * second + slope[3] * sroll(second, 4)
                )
                ends[a, b] = jnp.where(low_c, first, second)

        def along_b(table):
            return [restrict_four([table[a, b] for b in range(4)]) for a in range(4)]

        def both(table):
            by_b = along_b(table)
            return [restrict_four([by_b[a][j] for a in range(4)]) for j in range(2)]

        by_b = along_b(line)
        by_a = [restrict_four([line[a, b] for a in range(4)]) for b in range(4)]
        flux_z = both(slope_c)
        trace_z = both(ends)
        sources = both({(a, b): restrict_c(src_ref[v, a, b, 0], src_ref[v, a, b, 1]) for a in range(4) for b in range(4)})
        acc = [[None, None], [None, None]]
        for j in range(2):
            value = restrict_four([by_b[a][j] for a in range(4)])
            flux = slopes_four([by_b[a][j] for a in range(4)])
            for i in range(2):
                acc[i][j] = sources[j][i] - 2.0 * value[i]
                waves[0][i][j][v] = flux[i]
        for i in range(2):
            flux = slopes_four([by_a[b][i] for b in range(4)])
            for j in range(2):
                waves[1][i][j][v] = flux[j]
        for d, lo, hi in ((0, by_b[0], by_b[3]), (1, by_a[0], by_a[3])):
            low, step = axis_low(d)
            flag = flags[d]
            flag_before = sroll(flag_ref[d], step) != 0
            for m in range(2):
                right = sroll(jnp.where(flag_before, lo[1 - m], lo[m]), -step)
                left = sroll(jnp.where(flag, hi[1 - m], hi[m]), step)
                jump_right = jnp.where(low, right, 0.0) - hi[m]
                jump_left = jnp.where(low, 0.0, left) - lo[m]
                i, j = (1, m) if d == 0 else (m, 1)
                waves[d][i][j][v] = waves[d][i][j][v] + H4 * jump_right
                acc[i][j] = acc[i][j] + damp * jump_right
                i, j = (0, m) if d == 0 else (m, 0)
                waves[d][i][j][v] = waves[d][i][j][v] - H4 * jump_left
                acc[i][j] = acc[i][j] + damp * jump_left
        beside = []
        for j in range(2):
            turned = [sroll(trace_z[j][i], 4) for i in range(2)]
            beside.append([jnp.where(low_c, lroll(t, 1), lroll(t, -1)) for t in turned])
        for i in range(2):
            for j in range(2):
                jump = jnp.where(flags[2], beside[j][1 - i], beside[j][i]) - trace_z[j][i]
                waves[2][i][j][v] = flux_z[j][i] + sign * jump
                acc_ref[v, i, j] = acc[i][j] + damp * jump
    for d in range(3):
        matrix = [[jac_ref[25 * d + 5 * o + i] for i in range(5)] for o in range(5)]
        for i in range(2):
            for j in range(2):
                for v, value in enumerate(mix(matrix, waves[d][i][j])):
                    acc_ref[v, i, j] = acc_ref[v, i, j] - value


def restrict_kernel(
    acc_ref, flag_ref, face_ref, smooth_ref, got_even, got_odd, rhs_ref, c_ref, even_ref, odd_ref
):
    rxo, rxe, ryo, rye = block_views(got_even, got_odd)
    rhs = [[[acc_ref[v, i, j] for j in range(2)] for i in range(2)] for v in range(5)]
    for d, axis in ((0, "gx"), (1, "gy")):
        is_even = parity(axis)
        low, step = axis_low(d)
        flag = flag_ref[d]
        flag = jnp.where(low, sroll(flag, -step), flag) != 0
        even, odd = ((rxe, rxo), (rye, ryo))[d]
        at = (lambda n, m: (n, m)) if d == 0 else (lambda n, m: (m, n))
        right, left = [], []
        for v in range(5):
            value = jnp.where(is_even, even[v], odd[v])
            swapped = jnp.where(low, sroll(value, -step), sroll(value, step))
            right.append(jnp.where(flag, swapped, value))
            left.append(jnp.where(is_even, odd[v], even[v]))
        upper = [[face_ref[2 * d, 5 * o + i] for i in range(5)] for o in range(5)]
        lower = [[face_ref[2 * d + 1, 5 * o + i] for i in range(5)] for o in range(5)]
        for v, value in enumerate(mix(upper, right)):
            for m, part in enumerate((sroll(value, step), value)):
                i, j = at(1, m)
                rhs[v][i][j] = rhs[v][i][j] - jnp.where(low, 0.0, part)
        for v, value in enumerate(mix(lower, left)):
            for m, part in enumerate((value, sroll(value, -step))):
                i, j = at(0, m)
                rhs[v][i][j] = rhs[v][i][j] + jnp.where(low, part, 0.0)
    c = coarse_smooth(smooth_ref, rhs)
    for v in range(5):
        for i in range(2):
            for j in range(2):
                rhs_ref[v, i, j] = rhs[v][i][j]
                c_ref[v, i, j] = c[v][i][j]
    coarse_faces(c, flag_ref, *block_views(even_ref, odd_ref))


def coarse_step(c_ref, rhs_ref, smooth_ref, flag_ref, jac_ref, damp_ref, rxo, rxe, ryo, rye):
    damp = 0.5 * damp_ref[...]
    c = [[[c_ref[v, i, j] for j in range(2)] for i in range(2)] for v in range(5)]
    acc = [[[rhs_ref[v, i, j] - 2.0 * c[v][i][j] for j in range(2)] for i in range(2)] for v in range(5)]
    for d, axis in ((0, "gx"), (1, "gy")):
        is_even = parity(axis)
        low, step = axis_low(d)
        flag = flag_ref[d] != 0
        matrix = [[jac_ref[25 * d + 5 * o + i] for i in range(5)] for o in range(5)]
        even, odd = ((rxe, rxo), (rye, ryo))[d]
        at = (lambda n, m: (n, m)) if d == 0 else (lambda n, m: (m, n))
        waves = [[[None] * 5, [None] * 5] for _ in range(2)]
        for v in range(5):
            got_right = jnp.where(is_even, even[v], odd[v])
            got_left = jnp.where(is_even, odd[v], even[v])
            lo = [c[v][at(0, m)[0]][at(0, m)[1]] for m in range(2)]
            hi = [c[v][at(1, m)[0]][at(1, m)[1]] for m in range(2)]
            right = [
                jnp.where(low, sroll(lo[0], -step), sroll(got_right, step)),
                jnp.where(low, sroll(lo[1], -step), got_right),
            ]
            right = [jnp.where(flag, right[1 - m], right[m]) for m in range(2)]
            left = [sroll(jnp.where(flag, hi[1 - m], hi[m]), step) for m in range(2)]
            left = [jnp.where(low, got_left, left[0]), jnp.where(low, sroll(got_left, -step), left[1])]
            for m in range(2):
                waves[1][m][v] = 0.5 * (right[m] - lo[m])
                waves[0][m][v] = 0.5 * (hi[m] - left[m])
                i, j = at(1, m)
                acc[v][i][j] = acc[v][i][j] + damp * (right[m] - hi[m])
                i, j = at(0, m)
                acc[v][i][j] = acc[v][i][j] + damp * (left[m] - lo[m])
        for n in range(2):
            for m in range(2):
                i, j = at(n, m)
                for v, value in enumerate(mix(matrix, waves[n][m])):
                    acc[v][i][j] = acc[v][i][j] - value
    low = c_low()
    flag = jnp.where(low, lroll(flag_ref[2], 1), flag_ref[2]) != 0
    half = jnp.where(low, 0.5, -0.5).astype(F32)
    matrix = [[jac_ref[50 + 5 * o + i] for i in range(5)] for o in range(5)]
    turned = [[[sroll(c[v][i][j], 4) for j in range(2)] for i in range(2)] for v in range(5)]
    beside = [
        [[jnp.where(low, lroll(t, 1), lroll(t, -1)) for t in turned[v][i]] for i in range(2)] for v in range(5)
    ]
    for i in range(2):
        for j in range(2):
            wave = []
            for v in range(5):
                next_to = jnp.where(flag, beside[v][1 - i][j], beside[v][i][j])
                wave.append(half * (turned[v][i][j] - next_to))
                acc[v][i][j] = acc[v][i][j] + damp * (next_to - c[v][i][j])
            for v, value in enumerate(mix(matrix, wave)):
                acc[v][i][j] = acc[v][i][j] - value
    change = coarse_smooth(smooth_ref, acc)
    return [[[c[v][i][j] + change[v][i][j] for j in range(2)] for i in range(2)] for v in range(5)]


def coarse_kernel(
    c_ref, rhs_ref, smooth_ref, flag_ref, jac_ref, damp_ref, got_even, got_odd, out_ref, even_ref, odd_ref
):
    rxo, rxe, ryo, rye = block_views(got_even, got_odd)
    c = coarse_step(c_ref, rhs_ref, smooth_ref, flag_ref, jac_ref, damp_ref, rxo, rxe, ryo, rye)
    for v in range(5):
        for i in range(2):
            for j in range(2):
                out_ref[v, i, j] = c[v][i][j]
    coarse_faces(c, flag_ref, *block_views(even_ref, odd_ref))


def spread(first, second):
    return first, NEAR * first + FAR * second, FAR * first + NEAR * second, second


def last_kernel(
    c_ref, rhs_ref, smooth_ref, flag_ref, jac_ref, damp_ref, got_even, got_odd, second_ref, out_hbm, out_ref, sems
):
    rxo, rxe, ryo, rye = block_views(got_even, got_odd)
    c = coarse_step(c_ref, rhs_ref, smooth_ref, flag_ref, jac_ref, damp_ref, rxo, rxe, ryo, rye)
    low = c_low()
    copies = []
    for v in range(5):
        by_c = [[None, None], [None, None]]
        for i in range(2):
            for j in range(2):
                value = c[v][i][j]
                inner = FAR * value + NEAR * sroll(value, 4)
                by_c[i][j] = (jnp.where(low, value, inner), jnp.where(low, inner, value))
        for q in range(2):
            lines = [spread(by_c[i][0][q], by_c[i][1][q]) for i in range(2)]
            for b in range(4):
                for a, value in enumerate(spread(lines[0][b], lines[1][b])):
                    out_ref[v, a, b, q] = second_ref[v, a, b, q] + value
        copy = pltpu.make_async_copy(out_ref.at[v], out_hbm.at[v], sems.at[v])
        copy.start()
        copies.append(copy)
    for copy in copies:
        copy.wait()


FINE = (5, 4, 4, 2, 8, 128)
FINE_MESSAGE = (5, 4, 8, 128)
COARSE = (5, 2, 2, 8, 128)
COARSE_MESSAGE = (4, 5, 8, 128)


def vmem(shape, dtype=F32):
    return pltpu.VMEM(shape, dtype)


def here(array):
    return pltpu.with_memory_space_constraint(array, pltpu.VMEM)


def call(kernel, args, outs, in_hbm=(), out_hbm=(), scratch=(), flops=0):
    in_specs = [
        pl.BlockSpec(memory_space=pltpu.HBM if k in in_hbm else pltpu.VMEM) for k in range(len(args))
    ]
    out_specs = [
        pl.BlockSpec(memory_space=pltpu.HBM if k in out_hbm else pltpu.VMEM) for k in range(len(outs))
    ]
    args = [pltpu.with_memory_space_constraint(a, pltpu.HBM) if k in in_hbm else here(a) for k, a in enumerate(args)]
    return pl.pallas_call(
        kernel,
        out_shape=outs,
        in_specs=in_specs,
        out_specs=out_specs,
        scratch_shapes=scratch,
        compiler_params=pltpu.CompilerParams(vmem_limit_bytes=8 * 2**20),
        cost_estimate=pl.CostEstimate(flops=flops, bytes_accessed=4 * 2**20, transcendentals=0),
    )(*args)


def partners(axis):
    size = lax.axis_size(axis)
    even = [(i, i ^ 1) for i in range(size)]
    odd = [(i, (i - 1) % size if i % 2 == 0 else (i + 1) % size) for i in range(size)]
    return even, odd


def exchange(xo, xe, yo, ye):
    even_x, odd_x = partners("gx")
    even_y, odd_y = partners("gy")
    xo = lax.ppermute(xo, "gx", odd_x)
    xe = lax.ppermute(xe, "gx", even_x)
    yo = lax.ppermute(yo, "gy", odd_y)
    ye = lax.ppermute(ye, "gy", even_y)
    return xo, xe, yo, ye


def blocks(first):
    nx, ny = lax.axis_size("gx"), lax.axis_size("gy")
    return [
        [(i + a) % nx * ny + (j + b) % ny for b in range(2) for a in range(2)]
        for i in range(first, nx, 2)
        for j in range(first, ny, 2)
    ]


def block_exchange(even, odd):
    odd = lax.all_to_all(odd, ("gx", "gy"), 0, 0, axis_index_groups=blocks(1), tiled=True)
    even = lax.all_to_all(even, ("gx", "gy"), 0, 0, axis_index_groups=blocks(0), tiled=True)
    return even, odd


def body(source, jacobian, damping, orient, smoother, coarse_smoother):
    source = source.reshape(FINE)
    smoother = smoother.reshape(25, 4, 4, 16, 128)
    coarse_smoother = coarse_smoother.reshape(25, 2, 16, 128)
    jacobian = jacobian.reshape(75, 4, 128)
    damping = damping.reshape(4, 128)
    orient = orient.reshape(3, 4, 128)
    fine_messages = [vmem(FINE_MESSAGE)] * 4
    coarse_messages = [vmem(COARSE_MESSAGE)] * 2

    source, smoother, first, flag, *sent = call(
        first_kernel,
        (source, smoother, orient),
        [vmem(FINE), vmem(smoother.shape, smoother.dtype), vmem(FINE), vmem((3, 8, 128), jnp.int32)] + fine_messages,
        in_hbm=(0, 1, 2),
        scratch=[pltpu.SemaphoreType.DMA((2, 4)), pltpu.VMEM((3, 4, 128), jnp.int32), pltpu.SemaphoreType.DMA],
        flops=2 * 25 * 64 * 512,
    )
    got = exchange(*sent)
    acc, jac8, damp8, face = call(
        first_volume_kernel,
        (source, first, flag, jacobian, damping),
        [vmem(FINE), vmem((75, 8, 128)), vmem((8, 128)), vmem((4, 25, 8, 128))],
        flops=9 * 2**20,
    )
    second, *sent = call(
        second_kernel,
        (acc, first, smoother, flag, face, *got),
        [vmem(FINE)] + coarse_messages,
        scratch=[pltpu.VMEM((4, 5, 4, 2, 8, 128), F32)],
        flops=3 * 2**20,
    )
    got = block_exchange(*sent)
    (acc,) = call(restricted_volume_kernel, (source, second, flag, jac8, damp8), [vmem(COARSE)], flops=4 * 2**20)
    rhs, coarse, *sent = call(
        restrict_kernel,
        (acc, flag, face, coarse_smoother, *got),
        [vmem(COARSE), vmem(COARSE)] + coarse_messages,
        flops=2**20,
    )
    got = block_exchange(*sent)
    coarse, *sent = call(
        coarse_kernel,
        (coarse, rhs, coarse_smoother, flag, jac8, damp8, *got),
        [vmem(COARSE)] + coarse_messages,
        flops=2**20,
    )
    got = block_exchange(*sent)
    (out,) = call(
        last_kernel,
        (coarse, rhs, coarse_smoother, flag, jac8, damp8, *got, second),
        [jax.ShapeDtypeStruct(FINE, F32)],
        out_hbm=(0,),
        scratch=[pltpu.VMEM(FINE, F32), pltpu.SemaphoreType.DMA((5,))],
        flops=2**20,
    )
    return out.reshape(5, 4, 4, 4, 2, 2, 128)


def solution(mesh):
    in_specs = (
        P(None, None, None, None, "gx", "gy", None),
        P(None, None, None, "gx", "gy", None),
        P("gx", "gy", None),
        P(None, "gx", "gy", None),
        P(None, None, None, None, None, "gx", "gy", None),
        P(None, None, None, None, None, "gx", "gy", None),
    )
    out_specs = P(None, None, None, None, "gx", "gy", None)
    return jax.shard_map(body, mesh=mesh, in_specs=in_specs, out_specs=out_specs, check_vma=False)
```

```python
import functools
import math

import jax
import jax.numpy as jnp
import numpy as np
from jax import lax
from jax.experimental import pallas as pl
from jax.experimental.pallas import tpu as pltpu
from jax.sharding import PartitionSpec as P


F32 = jnp.float32
OMEGA = 0.8
H4 = 3.0
ROOT = 1.0 / math.sqrt(5.0)
NEAR = (1.0 + ROOT) / 2.0
FAR = (1.0 - ROOT) / 2.0


def lobatto_slopes():
    points = np.array([-1.0, -ROOT, ROOT, 1.0])
    weights = np.ones(4)
    for i in range(4):
        for j in range(4):
            if i != j:
                weights[i] = weights[i] / (points[i] - points[j])
    slopes = np.zeros((4, 4))
    for i in range(4):
        for j in range(4):
            if i != j:
                slopes[i, j] = weights[j] / weights[i] / (points[i] - points[j])
        slopes[i, i] = -np.sum(slopes[i])
    return slopes


D4 = lobatto_slopes()
PD = np.array([[1.0, NEAR, FAR, 0.0], [0.0, FAR, NEAR, 1.0]]) @ D4


def sum_of(terms):
    total = None
    for weight, value in terms:
        total = weight * value if total is None else total + weight * value
    return total


def rows():
    return lax.broadcasted_iota(jnp.int32, (8, 128), 0)


def x_low():
    return (rows() & 2) == 0


def y_low():
    return (rows() & 1) == 0


def c_low():
    return (rows() & 4) == 0


def sroll(value, shift):
    return pltpu.roll(value, shift % 8, 0)


def lroll(value, shift):
    return pltpu.roll(value, shift % 128, 1)


def twice(value):
    return jnp.concatenate([value, value], axis=0)


def axis_low(direction):
    return (x_low(), 2) if direction == 0 else (y_low(), 1)


def pack_low(first, second, direction):
    low, step = axis_low(direction)
    return jnp.where(low, first, sroll(second, step))


def pack_high(first, second, direction):
    low, step = axis_low(direction)
    return jnp.where(low, sroll(first, -step), second)


def slopes_along(u0, u1, u2, u3):
    e0, o0, e1, o1 = u0 + u3, u0 - u3, u1 + u2, u1 - u2
    diff = e1 - e0
    even_a = float((D4[0, 1] + D4[0, 2]) / 2.0) * diff
    even_b = float((D4[1, 2] - 0.0) / 2.0) * diff
    odd_a = float((D4[0, 0] - D4[0, 3]) / 2.0) * o0 + float((D4[0, 1] - D4[0, 2]) / 2.0) * o1
    odd_b = float((D4[1, 0] - D4[1, 3]) / 2.0) * o0 - float(D4[1, 2] / 2.0) * o1
    return even_a + odd_a, even_b + odd_b, odd_b - even_b, odd_a - even_a


def mix(matrix, fields):
    out = []
    for o in range(5):
        total = matrix[o][0] * fields[0]
        for i in range(1, 5):
            total = total + matrix[o][i] * fields[i]
        out.append(total)
    return out


def parity(axis):
    return lax.rem(lax.axis_index(axis), 2) == 0


def put_pair(even_ref, odd_ref, index, low_face, high_face, is_even):
    even_ref[index] = jnp.where(is_even, high_face, low_face)
    odd_ref[index] = jnp.where(is_even, low_face, high_face)


def fine_faces(u_ref, flag_ref, xo, xe, yo, ye):
    even_x, even_y = parity("gx"), parity("gy")
    fx, fy = flag_ref[0] != 0, flag_ref[1] != 0
    for v in range(5):
        for n in range(4):
            low = pack_low(u_ref[v, 0, n, 0], u_ref[v, 0, n, 1], 0)
            h = [jnp.where(fx, u_ref[v, 3, 3 - n, q], u_ref[v, 3, n, q]) for q in range(2)]
            put_pair(xe, xo, (v, n), low, pack_high(h[0], h[1], 0), even_x)
            low = pack_low(u_ref[v, n, 0, 0], u_ref[v, n, 0, 1], 1)
            h = [jnp.where(fy, u_ref[v, 3 - n, 3, q], u_ref[v, n, 3, q]) for q in range(2)]
            put_pair(ye, yo, (v, n), low, pack_high(h[0], h[1], 1), even_y)


def restrict_c(first, second):
    low = c_low()
    middle = jnp.where(low, second, first)
    return jnp.where(low, first, second) + FAR * middle + NEAR * sroll(middle, 4)


def restrict_four(values):
    return values[0] + NEAR * values[1] + FAR * values[2], values[3] + NEAR * values[2] + FAR * values[1]


def put_coarse_faces(v, lows, highs, flag_ref, pairs):
    for d, axis in ((0, "gx"), (1, "gy")):
        flag = flag_ref[d] != 0
        low, high = lows[d], highs[d]
        turned = [jnp.where(flag, high[1 - m], high[m]) for m in range(2)]
        even_ref, odd_ref = pairs[d]
        put_pair(even_ref, odd_ref, v, pack_low(*low, d), pack_high(*turned, d), parity(axis))


def restricted_faces(u_ref, flag_ref, xo, xe, yo, ye):
    for v in range(5):
        line = {}
        for a in range(4):
            for b in range(4):
                if a in (0, 3) or b in (0, 3):
                    line[a, b] = restrict_c(u_ref[v, a, b, 0], u_ref[v, a, b, 1])
        lows = [restrict_four([line[0, n] for n in range(4)]), restrict_four([line[n, 0] for n in range(4)])]
        highs = [restrict_four([line[3, n] for n in range(4)]), restrict_four([line[n, 3] for n in range(4)])]
        put_coarse_faces(v, lows, highs, flag_ref, ((xe, xo), (ye, yo)))


def first_kernel(
    src_hbm, smooth_hbm, orient_hbm, src_ref, smooth_ref, u_ref, flag_ref, xo, xe, yo, ye, sems, orient_ref, orient_sem
):
    orient_copy = pltpu.make_async_copy(orient_hbm, orient_ref, orient_sem)
    orient_copy.start()
    copies = []
    for slot, a in enumerate((0, 3, 1, 2)):
        pair = (
            pltpu.make_async_copy(src_hbm.at[:, a], src_ref.at[:, a], sems.at[0, slot]),
            pltpu.make_async_copy(smooth_hbm.at[:, a], smooth_ref.at[:, a], sems.at[1, slot]),
        )
        for one in pair:
            one.start()
        copies.append((a, pair))
    orient_copy.wait()
    for d in range(3):
        flag_ref[d] = twice(orient_ref[d])
    for a, pair in copies:
        for one in pair:
            one.wait()

        for b in range(4):
            src = [[src_ref[v, a, b, q] for q in range(2)] for v in range(5)]
            for o in range(5):
                total = [None, None]
                for i in range(5):
                    block = smooth_ref[5 * o + i, a, b].astype(F32)
                    for q in range(2):
                        term = block[8 * q : 8 * q + 8] * src[i][q]
                        total[q] = term if i == 0 else total[q] + term
                for q in range(2):
                    u_ref[o, a, b, q] = OMEGA * total[q]
    fine_faces(u_ref, flag_ref, xo, xe, yo, ye)


def prepare_tables(jac_ref, damp_ref, jac8_ref, damp8_ref, face_ref):
    damp = twice(damp_ref[...])
    damp8_ref[...] = damp
    for d in range(3):
        for k in range(25):
            value = twice(jac_ref[25 * d + k])
            jac8_ref[25 * d + k] = value
            if d < 2:
                low, step = axis_low(d)
                diagonal = k % 6 == 0
                upper = H4 * (value - damp if diagonal else value)
                lower = H4 * (value + damp if diagonal else value)
                face_ref[2 * d, k] = jnp.where(low, sroll(upper, -step), upper)
                face_ref[2 * d + 1, k] = jnp.where(low, lower, sroll(lower, step))


def volume(src_ref, u_ref, flag_ref, jac_ref, damp_ref, acc_ref):
    damp = H4 * damp_ref[...]

    def jacobian(d):
        return [[jac_ref[25 * d + 5 * o + i] for i in range(5)] for o in range(5)]

    def along(direction):
        low, step = axis_low(direction)
        flag = flag_ref[direction] != 0
        flag_before = sroll(flag_ref[direction], step) != 0

        def at(v, n, other, q):
            return (v, n, other, q) if direction == 0 else (v, other, n, q)

        def step_fn(j, carry):
            other, q = j // 2, j % 2
            u = [[u_ref[at(v, n, other, q)] for n in range(4)] for v in range(5)]
            waves = []
            jumps = []
            for v in range(5):
                back_low, back_high = u_ref[at(v, 0, 3 - other, q)], u_ref[at(v, 3, 3 - other, q)]
                right = sroll(jnp.where(flag_before, back_low, u[v][0]), -step)
                left = sroll(jnp.where(flag, back_high, u[v][3]), step)
                jump_right = jnp.where(low, right, 0.0) - u[v][3]
                jump_left = jnp.where(low, 0.0, left) - u[v][0]
                w = list(slopes_along(*u[v]))
                w[3] = w[3] + H4 * jump_right
                w[0] = w[0] - H4 * jump_left
                waves.append(w)
                jumps.append((damp * jump_left, None, None, damp * jump_right))
            matrix = jacobian(direction)
            for n in range(4):
                flux = mix(matrix, [waves[v][n] for v in range(5)])
                for v in range(5):
                    if direction == 0:
                        total = src_ref[at(v, n, other, q)] - 2.0 * u[v][n]
                    else:
                        total = acc_ref[at(v, n, other, q)]
                    total = total - flux[v]
                    if jumps[v][n] is not None:
                        total = total + jumps[v][n]
                    acc_ref[at(v, n, other, q)] = total
            return carry

        lax.fori_loop(0, 8, step_fn, 0)

    along(0)
    along(1)

    low = c_low()
    flag = jnp.where(low, lroll(flag_ref[2], 1), flag_ref[2]) != 0
    damp_z = damp
    coef = [
        [jnp.where(low, float(D4[2 * p, c]), float(D4[2 * p + 1, c ^ 1])).astype(F32) for c in range(4)]
        for p in range(2)
    ]

    def step_z(j, carry):
        a0, b = j // 4, j % 4
        here = (a0, 3 - a0)
        u = [[[u_ref[v, a, b, q] for q in range(2)] for v in range(5)] for a in here]
        turned = [[[sroll(u[s][v][q], 4) for q in range(2)] for v in range(5)] for s in range(2)]
        beside = []
        for s in range(2):
            line = []
            for v in range(5):
                face = jnp.where(low, turned[s][v][1], turned[s][v][0])
                line.append(jnp.where(low, lroll(face, 1), lroll(face, -1)))
            beside.append(line)
        matrix = jacobian(2)
        for s in range(2):
            waves = [[], []]
            jumps = []
            for v in range(5):
                own = jnp.where(low, u[s][v][0], u[s][v][1])
                jump = jnp.where(flag, beside[1 - s][v], beside[s][v]) - own
                jumps.append(damp_z * jump)
                lifted = H4 * jump
                for p in range(2):
                    w = coef[p][0] * u[s][v][0] + coef[p][1] * turned[s][v][0]
                    w = w + (coef[p][2] * u[s][v][1] + coef[p][3] * turned[s][v][1])
                    w = w - jnp.where(low, lifted, 0.0) if p == 0 else w + jnp.where(low, 0.0, lifted)
                    waves[p].append(w)
            for p in range(2):
                flux = mix(matrix, waves[p])
                for v in range(5):
                    part = jnp.where(low, jumps[v], 0.0) if p == 0 else jnp.where(low, 0.0, jumps[v])
                    acc_ref[v, here[s], b, p] = acc_ref[v, here[s], b, p] - flux[v] + part
        return carry

    lax.fori_loop(0, 8, step_z, 0)


def first_volume_kernel(src_ref, u_ref, flag_ref, jac_ref, damp_ref, acc_ref, jac8_ref, damp8_ref, face_ref):
    prepare_tables(jac_ref, damp_ref, jac8_ref, damp8_ref, face_ref)
    volume(src_ref, u_ref, flag_ref, jac8_ref, damp8_ref, acc_ref)


def remote_parts(even_refs, odd_refs, flag_ref, face_ref, part_ref):
    for d, axis in ((0, "gx"), (1, "gy")):
        is_even = parity(axis)
        low, step = axis_low(d)
        flag = flag_ref[d]
        flag = jnp.where(low, sroll(flag, -step), flag) != 0
        even, odd = even_refs[d], odd_refs[d]
        matrix = [[face_ref[2 * d, 5 * o + i] for i in range(5)] for o in range(5)]
        for n in range(4):
            take = lambda v, m: jnp.where(is_even, even[v, m], odd[v, m])
            right = [jnp.where(flag, take(v, 3 - n), take(v, n)) for v in range(5)]
            for v, value in enumerate(mix(matrix, right)):
                part_ref[2 * d, v, n, 0] = jnp.where(low, 0.0, -sroll(value, step))
                part_ref[2 * d, v, n, 1] = jnp.where(low, 0.0, -value)
        matrix = [[face_ref[2 * d + 1, 5 * o + i] for i in range(5)] for o in range(5)]
        for n in range(4):
            left = [jnp.where(is_even, odd[v, n], even[v, n]) for v in range(5)]
            for v, value in enumerate(mix(matrix, left)):
                part_ref[2 * d + 1, v, n, 0] = jnp.where(low, value, 0.0)
                part_ref[2 * d + 1, v, n, 1] = jnp.where(low, sroll(value, -step), 0.0)


def whole(acc_ref, part_ref, v, a, b, q):
    total = acc_ref[v, a, b, q]
    if a == 3:
        total = total + part_ref[0, v, b, q]
    if a == 0:
        total = total + part_ref[1, v, b, q]
    if b == 3:
        total = total + part_ref[2, v, a, q]
    if b == 0:
        total = total + part_ref[3, v, a, q]
    return total


def second_kernel(
    acc_ref, u_ref, smooth_ref, flag_ref, face_ref, rxo, rxe, ryo, rye, out_ref, xo, xe, yo, ye, part_ref
):
    remote_parts((rxe, rye), (rxo, ryo), flag_ref, face_ref, part_ref)
    for a in range(4):
        for b in range(4):
            left = [[whole(acc_ref, part_ref, v, a, b, q) for q in range(2)] for v in range(5)]
            for o in range(5):
                total = [None, None]
                for i in range(5):
                    block = smooth_ref[5 * o + i, a, b].astype(F32)
                    for q in range(2):
                        term = block[8 * q : 8 * q + 8] * left[i][q]
                        total[q] = term if i == 0 else total[q] + term
                for q in range(2):
                    out_ref[o, a, b, q] = u_ref[o, a, b, q] + OMEGA * total[q]
    restricted_faces(out_ref, flag_ref, xo, xe, yo, ye)


def coarse_smooth(smooth_ref, fields):
    out = [[[None, None], [None, None]] for _ in range(5)]
    for i in range(2):
        for o in range(5):
            total = [None, None]
            for k in range(5):
                block = smooth_ref[5 * o + k, i].astype(F32)
                for j in range(2):
                    term = block[8 * j : 8 * j + 8] * fields[k][i][j]
                    total[j] = term if k == 0 else total[j] + term
            for j in range(2):
                out[o][i][j] = OMEGA * total[j]
    return out


def coarse_faces(field, flag_ref, xo, xe, yo, ye):
    for v in range(5):
        c = field[v]
        lows = [[c[0][0], c[0][1]], [c[0][0], c[1][0]]]
        highs = [[c[1][0], c[1][1]], [c[0][1], c[1][1]]]
        put_coarse_faces(v, lows, highs, flag_ref, ((xe, xo), (ye, yo)))


def restricted_volume_kernel(src_ref, u_ref, flag_ref, jac_ref, damp_ref, acc_ref):
    damp = H4 * damp_ref[...]
    low_c = c_low()
    slope = [
        jnp.where(low_c, float(PD[0, c]), float(PD[1, c ^ 1])).astype(F32) for c in range(4)
    ]
    flags = [flag_ref[0] != 0, flag_ref[1] != 0, jnp.where(low_c, lroll(flag_ref[2], 1), flag_ref[2]) != 0]
    sign = jnp.where(low_c, -H4, H4).astype(F32)
    waves = [[[[None] * 5 for _ in range(2)] for _ in range(2)] for _ in range(3)]

    def slopes_four(values):
        return [sum_of([(float(PD[i, n]), values[n]) for n in range(4)]) for i in range(2)]

    for v in range(5):
        line, slope_c, ends = {}, {}, {}
        for a in range(4):
            for b in range(4):
                first, second = u_ref[v, a, b, 0], u_ref[v, a, b, 1]
                line[a, b] = restrict_c(first, second)
                slope_c[a, b] = (slope[0] * first + slope[1] * sroll(first, 4)) + (
                    slope[2] * second + slope[3] * sroll(second, 4)
                )
                ends[a, b] = jnp.where(low_c, first, second)

        def along_b(table):
            return [restrict_four([table[a, b] for b in range(4)]) for a in range(4)]

        def both(table):
            by_b = along_b(table)
            return [restrict_four([by_b[a][j] for a in range(4)]) for j in range(2)]

        by_b = along_b(line)
        by_a = [restrict_four([line[a, b] for a in range(4)]) for b in range(4)]
        flux_z = both(slope_c)
        trace_z = both(ends)
        sources = both({(a, b): restrict_c(src_ref[v, a, b, 0], src_ref[v, a, b, 1]) for a in range(4) for b in range(4)})
        acc = [[None, None], [None, None]]
        for j in range(2):
            value = restrict_four([by_b[a][j] for a in range(4)])
            flux = slopes_four([by_b[a][j] for a in range(4)])
            for i in range(2):
                acc[i][j] = sources[j][i] - 2.0 * value[i]
                waves[0][i][j][v] = flux[i]
        for i in range(2):
            flux = slopes_four([by_a[b][i] for b in range(4)])
            for j in range(2):
                waves[1][i][j][v] = flux[j]
        for d, lo, hi in ((0, by_b[0], by_b[3]), (1, by_a[0], by_a[3])):
            low, step = axis_low(d)
            flag = flags[d]
            flag_before = sroll(flag_ref[d], step) != 0
            for m in range(2):
                right = sroll(jnp.where(flag_before, lo[1 - m], lo[m]), -step)
                left = sroll(jnp.where(flag, hi[1 - m], hi[m]), step)
                jump_right = jnp.where(low, right, 0.0) - hi[m]
                jump_left = jnp.where(low, 0.0, left) - lo[m]
                i, j = (1, m) if d == 0 else (m, 1)
                waves[d][i][j][v] = waves[d][i][j][v] + H4 * jump_right
                acc[i][j] = acc[i][j] + damp * jump_right
                i, j = (0, m) if d == 0 else (m, 0)
                waves[d][i][j][v] = waves[d][i][j][v] - H4 * jump_left
                acc[i][j] = acc[i][j] + damp * jump_left
        beside = []
        for j in range(2):
            turned = [sroll(trace_z[j][i], 4) for i in range(2)]
            beside.append([jnp.where(low_c, lroll(t, 1), lroll(t, -1)) for t in turned])
        for i in range(2):
            for j in range(2):
                jump = jnp.where(flags[2], beside[j][1 - i], beside[j][i]) - trace_z[j][i]
                waves[2][i][j][v] = flux_z[j][i] + sign * jump
                acc_ref[v, i, j] = acc[i][j] + damp * jump
    for d in range(3):
        matrix = [[jac_ref[25 * d + 5 * o + i] for i in range(5)] for o in range(5)]
        for i in range(2):
            for j in range(2):
                for v, value in enumerate(mix(matrix, waves[d][i][j])):
                    acc_ref[v, i, j] = acc_ref[v, i, j] - value


def add_remote(field, scale, flag_ref, face_ref, rxo, rxe, ryo, rye):
    for d, axis in ((0, "gx"), (1, "gy")):
        is_even = parity(axis)
        low, step = axis_low(d)
        flag = flag_ref[d]
        flag = jnp.where(low, sroll(flag, -step), flag) != 0
        even, odd = ((rxe, rxo), (rye, ryo))[d]
        at = (lambda n, m: (n, m)) if d == 0 else (lambda n, m: (m, n))
        right, left = [], []
        for v in range(5):
            value = scale * jnp.where(is_even, even[v], odd[v])
            swapped = jnp.where(low, sroll(value, -step), sroll(value, step))
            right.append(jnp.where(flag, swapped, value))
            left.append(scale * jnp.where(is_even, odd[v], even[v]))
        upper = [[face_ref[2 * d, 5 * o + i] for i in range(5)] for o in range(5)]
        lower = [[face_ref[2 * d + 1, 5 * o + i] for i in range(5)] for o in range(5)]
        for v, value in enumerate(mix(upper, right)):
            for m, part in enumerate((sroll(value, step), value)):
                i, j = at(1, m)
                field[v][i][j] = field[v][i][j] - jnp.where(low, 0.0, part)
        for v, value in enumerate(mix(lower, left)):
            for m, part in enumerate((value, sroll(value, -step))):
                i, j = at(0, m)
                field[v][i][j] = field[v][i][j] + jnp.where(low, part, 0.0)


def restrict_kernel(
    acc_ref, flag_ref, face_ref, smooth_ref, rxo, rxe, ryo, rye, rhs_ref, c_ref, xo, xe, yo, ye
):
    rhs = [[[acc_ref[v, i, j] for j in range(2)] for i in range(2)] for v in range(5)]
    add_remote(rhs, 1.0, flag_ref, face_ref, rxo, rxe, ryo, rye)
    c = coarse_smooth(smooth_ref, rhs)
    for v in range(5):
        for i in range(2):
            for j in range(2):
                rhs_ref[v, i, j] = rhs[v][i][j]
                c_ref[v, i, j] = c[v][i][j]
    coarse_faces(c, flag_ref, xo, xe, yo, ye)


def coarse_local_kernel(c_ref, rhs_ref, smooth_ref, flag_ref, jac_ref, damp_ref, out_ref):
    damp = 0.5 * damp_ref[...]
    c = [[[c_ref[v, i, j] for j in range(2)] for i in range(2)] for v in range(5)]
    acc = [[[rhs_ref[v, i, j] - 2.0 * c[v][i][j] for j in range(2)] for i in range(2)] for v in range(5)]
    for d in range(2):
        low, step = axis_low(d)
        flag = flag_ref[d] != 0
        flag_before = sroll(flag_ref[d], step) != 0
        matrix = [[jac_ref[25 * d + 5 * o + i] for i in range(5)] for o in range(5)]
        at = (lambda n, m: (n, m)) if d == 0 else (lambda n, m: (m, n))
        waves = [[[None] * 5, [None] * 5] for _ in range(2)]
        for v in range(5):
            lo = [c[v][at(0, m)[0]][at(0, m)[1]] for m in range(2)]
            hi = [c[v][at(1, m)[0]][at(1, m)[1]] for m in range(2)]
            for m in range(2):
                right = jnp.where(low, sroll(jnp.where(flag_before, lo[1 - m], lo[m]), -step), 0.0)
                left = jnp.where(low, 0.0, sroll(jnp.where(flag, hi[1 - m], hi[m]), step))
                waves[1][m][v] = 0.5 * (right - lo[m])
                waves[0][m][v] = 0.5 * (hi[m] - left)
                i, j = at(1, m)
                acc[v][i][j] = acc[v][i][j] + damp * (right - hi[m])
                i, j = at(0, m)
                acc[v][i][j] = acc[v][i][j] + damp * (left - lo[m])
        for n in range(2):
            for m in range(2):
                i, j = at(n, m)
                for v, value in enumerate(mix(matrix, waves[n][m])):
                    acc[v][i][j] = acc[v][i][j] - value
    low = c_low()
    flag = jnp.where(low, lroll(flag_ref[2], 1), flag_ref[2]) != 0
    half = jnp.where(low, 0.5, -0.5).astype(F32)
    matrix = [[jac_ref[50 + 5 * o + i] for i in range(5)] for o in range(5)]
    turned = [[[sroll(c[v][i][j], 4) for j in range(2)] for i in range(2)] for v in range(5)]
    beside = [
        [[jnp.where(low, lroll(t, 1), lroll(t, -1)) for t in turned[v][i]] for i in range(2)] for v in range(5)
    ]
    for i in range(2):
        for j in range(2):
            wave = []
            for v in range(5):
                next_to = jnp.where(flag, beside[v][1 - i][j], beside[v][i][j])
                wave.append(half * (turned[v][i][j] - next_to))
                acc[v][i][j] = acc[v][i][j] + damp * (next_to - c[v][i][j])
            for v, value in enumerate(mix(matrix, wave)):
                acc[v][i][j] = acc[v][i][j] - value
    change = coarse_smooth(smooth_ref, acc)
    for v in range(5):
        for i in range(2):
            for j in range(2):
                out_ref[v, i, j] = c[v][i][j] + change[v][i][j]


def coarse_step(c_ref, smooth_ref, flag_ref, face_ref, rxo, rxe, ryo, rye):
    rest = [[[0.0, 0.0], [0.0, 0.0]] for _ in range(5)]
    add_remote(rest, 1.0 / 6.0, flag_ref, face_ref, rxo, rxe, ryo, rye)
    change = coarse_smooth(smooth_ref, rest)
    return [[[c_ref[v, i, j] + change[v][i][j] for j in range(2)] for i in range(2)] for v in range(5)]


def coarse_kernel(c_ref, smooth_ref, flag_ref, face_ref, rxo, rxe, ryo, rye, out_ref, xo, xe, yo, ye):
    c = coarse_step(c_ref, smooth_ref, flag_ref, face_ref, rxo, rxe, ryo, rye)
    for v in range(5):
        for i in range(2):
            for j in range(2):
                out_ref[v, i, j] = c[v][i][j]
    coarse_faces(c, flag_ref, xo, xe, yo, ye)


def spread(first, second):
    return first, NEAR * first + FAR * second, FAR * first + NEAR * second, second


def last_kernel(
    c_ref, smooth_ref, flag_ref, face_ref, rxo, rxe, ryo, rye, second_ref, out_hbm, out_ref, sems
):
    c = coarse_step(c_ref, smooth_ref, flag_ref, face_ref, rxo, rxe, ryo, rye)
    low = c_low()
    copies = []
    for v in range(5):
        by_c = [[None, None], [None, None]]
        for i in range(2):
            for j in range(2):
                value = c[v][i][j]
                inner = FAR * value + NEAR * sroll(value, 4)
                by_c[i][j] = (jnp.where(low, value, inner), jnp.where(low, inner, value))
        for q in range(2):
            lines = [spread(by_c[i][0][q], by_c[i][1][q]) for i in range(2)]
            for b in range(4):
                for a, value in enumerate(spread(lines[0][b], lines[1][b])):
                    out_ref[v, a, b, q] = second_ref[v, a, b, q] + value
        copy = pltpu.make_async_copy(out_ref.at[v], out_hbm.at[v], sems.at[v])
        copy.start()
        copies.append(copy)
    for copy in copies:
        copy.wait()


FINE = (5, 4, 4, 2, 8, 128)
FINE_MESSAGE = (5, 4, 8, 128)
COARSE = (5, 2, 2, 8, 128)
COARSE_MESSAGE = (5, 8, 128)


def vmem(shape, dtype=F32):
    return pltpu.VMEM(shape, dtype)


def here(array):
    return pltpu.with_memory_space_constraint(array, pltpu.VMEM)


def call(kernel, args, outs, in_hbm=(), out_hbm=(), scratch=(), flops=0):
    in_specs = [
        pl.BlockSpec(memory_space=pltpu.HBM if k in in_hbm else pltpu.VMEM) for k in range(len(args))
    ]
    out_specs = [
        pl.BlockSpec(memory_space=pltpu.HBM if k in out_hbm else pltpu.VMEM) for k in range(len(outs))
    ]
    args = [pltpu.with_memory_space_constraint(a, pltpu.HBM) if k in in_hbm else here(a) for k, a in enumerate(args)]
    return pl.pallas_call(
        kernel,
        out_shape=outs,
        in_specs=in_specs,
        out_specs=out_specs,
        scratch_shapes=scratch,
        compiler_params=pltpu.CompilerParams(vmem_limit_bytes=8 * 2**20),
        cost_estimate=pl.CostEstimate(flops=flops, bytes_accessed=4 * 2**20, transcendentals=0),
    )(*args)


def partners(axis):
    size = lax.axis_size(axis)
    even = [(i, i ^ 1) for i in range(size)]
    odd = [(i, (i - 1) % size if i % 2 == 0 else (i + 1) % size) for i in range(size)]
    return even, odd


def exchange(xo, xe, yo, ye):
    even_x, odd_x = partners("gx")
    even_y, odd_y = partners("gy")
    xo = lax.ppermute(xo, "gx", odd_x)
    xe = lax.ppermute(xe, "gx", even_x)
    yo = lax.ppermute(yo, "gy", odd_y)
    ye = lax.ppermute(ye, "gy", even_y)
    return xo, xe, yo, ye


def local_sweep(coarse, *rest):
    (out,) = call(coarse_local_kernel, (coarse, *rest), [vmem(COARSE)], flops=4 * 2**20)
    return out


def body(source, jacobian, damping, orient, smoother, coarse_smoother):
    source = source.reshape(FINE)
    smoother = smoother.reshape(25, 4, 4, 16, 128)
    coarse_smoother = coarse_smoother.reshape(25, 2, 16, 128)
    jacobian = jacobian.reshape(75, 4, 128)
    damping = damping.reshape(4, 128)
    orient = orient.reshape(3, 4, 128)
    fine_messages = [vmem(FINE_MESSAGE)] * 4
    coarse_messages = [vmem(COARSE_MESSAGE)] * 4

    source, smoother, first, flag, *sent = call(
        first_kernel,
        (source, smoother, orient),
        [vmem(FINE), vmem(smoother.shape, smoother.dtype), vmem(FINE), vmem((3, 8, 128), jnp.int32)] + fine_messages,
        in_hbm=(0, 1, 2),
        scratch=[pltpu.SemaphoreType.DMA((2, 4)), pltpu.VMEM((3, 4, 128), jnp.int32), pltpu.SemaphoreType.DMA],
        flops=2 * 25 * 64 * 512,
    )
    got = exchange(*sent)
    acc, jac8, damp8, face = call(
        first_volume_kernel,
        (source, first, flag, jacobian, damping),
        [vmem(FINE), vmem((75, 8, 128)), vmem((8, 128)), vmem((4, 25, 8, 128))],
        flops=9 * 2**20,
    )
    second, *sent = call(
        second_kernel,
        (acc, first, smoother, flag, face, *got),
        [vmem(FINE)] + coarse_messages,
        scratch=[pltpu.VMEM((4, 5, 4, 2, 8, 128), F32)],
        flops=3 * 2**20,
    )
    got = exchange(*sent)
    (acc,) = call(restricted_volume_kernel, (source, second, flag, jac8, damp8), [vmem(COARSE)], flops=4 * 2**20)
    rhs, coarse, *sent = call(
        restrict_kernel,
        (acc, flag, face, coarse_smoother, *got),
        [vmem(COARSE), vmem(COARSE)] + coarse_messages,
        flops=2**20,
    )
    got = exchange(*sent)
    coarse = local_sweep(coarse, rhs, coarse_smoother, flag, jac8, damp8)
    coarse, *sent = call(
        coarse_kernel,
        (coarse, coarse_smoother, flag, face, *got),
        [vmem(COARSE)] + coarse_messages,
        flops=2**20,
    )
    got = exchange(*sent)
    coarse = local_sweep(coarse, rhs, coarse_smoother, flag, jac8, damp8)
    (out,) = call(
        last_kernel,
        (coarse, coarse_smoother, flag, face, *got, second),
        [jax.ShapeDtypeStruct(FINE, F32)],
        out_hbm=(0,),
        scratch=[pltpu.VMEM(FINE, F32), pltpu.SemaphoreType.DMA((5,))],
        flops=2**20,
    )
    return out.reshape(5, 4, 4, 4, 2, 2, 128)


def solution(mesh):
    in_specs = (
        P(None, None, None, None, "gx", "gy", None),
        P(None, None, None, "gx", "gy", None),
        P("gx", "gy", None),
        P(None, "gx", "gy", None),
        P(None, None, None, None, None, "gx", "gy", None),
        P(None, None, None, None, None, "gx", "gy", None),
    )
    out_specs = P(None, None, None, None, "gx", "gy", None)
    return jax.shard_map(body, mesh=mesh, in_specs=in_specs, out_specs=out_specs, check_vma=False)
```

```python
import functools
import math

import jax
import jax.numpy as jnp
import numpy as np
from jax import lax
from jax.experimental import pallas as pl
from jax.experimental.pallas import tpu as pltpu
from jax.sharding import PartitionSpec as P


F32 = jnp.float32
OMEGA = 0.8
H4 = 3.0
ROOT = 1.0 / math.sqrt(5.0)
NEAR = (1.0 + ROOT) / 2.0
FAR = (1.0 - ROOT) / 2.0


def lobatto_slopes():
    points = np.array([-1.0, -ROOT, ROOT, 1.0])
    weights = np.ones(4)
    for i in range(4):
        for j in range(4):
            if i != j:
                weights[i] = weights[i] / (points[i] - points[j])
    slopes = np.zeros((4, 4))
    for i in range(4):
        for j in range(4):
            if i != j:
                slopes[i, j] = weights[j] / weights[i] / (points[i] - points[j])
        slopes[i, i] = -np.sum(slopes[i])
    return slopes


D4 = lobatto_slopes()
PD = np.array([[1.0, NEAR, FAR, 0.0], [0.0, FAR, NEAR, 1.0]]) @ D4


def sum_of(terms):
    total = None
    for weight, value in terms:
        total = weight * value if total is None else total + weight * value
    return total


def rows():
    return lax.broadcasted_iota(jnp.int32, (8, 128), 0)


def x_low():
    return (rows() & 2) == 0


def y_low():
    return (rows() & 1) == 0


def c_low():
    return (rows() & 4) == 0


def sroll(value, shift):
    return pltpu.roll(value, shift % 8, 0)


def lroll(value, shift):
    return pltpu.roll(value, shift % 128, 1)


def twice(value):
    return jnp.concatenate([value, value], axis=0)


def axis_low(direction):
    return (x_low(), 2) if direction == 0 else (y_low(), 1)


def pack_low(first, second, direction):
    low, step = axis_low(direction)
    return jnp.where(low, first, sroll(second, step))


def pack_high(first, second, direction):
    low, step = axis_low(direction)
    return jnp.where(low, sroll(first, -step), second)


def slopes_along(u0, u1, u2, u3):
    e0, o0, e1, o1 = u0 + u3, u0 - u3, u1 + u2, u1 - u2
    diff = e1 - e0
    even_a = float((D4[0, 1] + D4[0, 2]) / 2.0) * diff
    even_b = float((D4[1, 2] - 0.0) / 2.0) * diff
    odd_a = float((D4[0, 0] - D4[0, 3]) / 2.0) * o0 + float((D4[0, 1] - D4[0, 2]) / 2.0) * o1
    odd_b = float((D4[1, 0] - D4[1, 3]) / 2.0) * o0 - float(D4[1, 2] / 2.0) * o1
    return even_a + odd_a, even_b + odd_b, odd_b - even_b, odd_a - even_a


def mix(matrix, fields):
    out = []
    for o in range(5):
        total = matrix[o][0] * fields[0]
        for i in range(1, 5):
            total = total + matrix[o][i] * fields[i]
        out.append(total)
    return out


def parity(axis):
    return lax.rem(lax.axis_index(axis), 2) == 0


def put_pair(even_ref, odd_ref, index, low_face, high_face, is_even):
    even_ref[index] = jnp.where(is_even, high_face, low_face)
    odd_ref[index] = jnp.where(is_even, low_face, high_face)


def fine_x_faces(u_ref, flag_ref, xo, xe):
    even_x, fx = parity("gx"), flag_ref[0] != 0
    for v in range(5):
        for n in range(4):
            low = pack_low(u_ref[v, 0, n, 0], u_ref[v, 0, n, 1], 0)
            h = [jnp.where(fx, u_ref[v, 3, 3 - n, q], u_ref[v, 3, n, q]) for q in range(2)]
            put_pair(xe, xo, (v, n), low, pack_high(h[0], h[1], 0), even_x)


def fine_y_faces(u_ref, flag_ref, yo, ye):
    even_y, fy = parity("gy"), flag_ref[1] != 0
    for v in range(5):
        for n in range(4):
            low = pack_low(u_ref[v, n, 0, 0], u_ref[v, n, 0, 1], 1)
            h = [jnp.where(fy, u_ref[v, 3 - n, 3, q], u_ref[v, n, 3, q]) for q in range(2)]
            put_pair(ye, yo, (v, n), low, pack_high(h[0], h[1], 1), even_y)


def restrict_c(first, second):
    low = c_low()
    middle = jnp.where(low, second, first)
    return jnp.where(low, first, second) + FAR * middle + NEAR * sroll(middle, 4)


def restrict_four(values):
    return values[0] + NEAR * values[1] + FAR * values[2], values[3] + NEAR * values[2] + FAR * values[1]


def put_coarse_faces(v, lows, highs, flag_ref, pairs):
    for d, axis in ((0, "gx"), (1, "gy")):
        flag = flag_ref[d] != 0
        low, high = lows[d], highs[d]
        turned = [jnp.where(flag, high[1 - m], high[m]) for m in range(2)]
        even_ref, odd_ref = pairs[d]
        put_pair(even_ref, odd_ref, v, pack_low(*low, d), pack_high(*turned, d), parity(axis))


def restricted_faces(u_ref, flag_ref, xo, xe, yo, ye):
    for v in range(5):
        line = {}
        for a in range(4):
            for b in range(4):
                if a in (0, 3) or b in (0, 3):
                    line[a, b] = restrict_c(u_ref[v, a, b, 0], u_ref[v, a, b, 1])
        lows = [restrict_four([line[0, n] for n in range(4)]), restrict_four([line[n, 0] for n in range(4)])]
        highs = [restrict_four([line[3, n] for n in range(4)]), restrict_four([line[n, 3] for n in range(4)])]
        put_coarse_faces(v, lows, highs, flag_ref, ((xe, xo), (ye, yo)))


def first_plane(src_ref, smooth_ref, u_ref, a, at):
    for b in range(4):
        src = [[src_ref[v, at, b, q] for q in range(2)] for v in range(5)]
        for o in range(5):
            total = [None, None]
            for i in range(5):
                block = smooth_ref[5 * o + i, at, b].astype(F32)
                for q in range(2):
                    term = block[8 * q : 8 * q + 8] * src[i][q]
                    total[q] = term if i == 0 else total[q] + term
            for q in range(2):
                u_ref[o, a, b, q] = OMEGA * total[q]


def x_planes_kernel(
    src_hbm, smooth_hbm, orient_hbm, jac_hbm, damp_hbm,
    xo, xe, u_ref, flag_ref, jac8_ref, damp8_ref, face_ref,
    src_ref, smooth_ref, orient_ref, jac_ref, damp_ref, sems, small_sems,
):
    copies = []
    for slot, a in enumerate((0, 3)):
        pair = (
            pltpu.make_async_copy(src_hbm.at[:, a], src_ref.at[:, slot], sems.at[0, slot]),
            pltpu.make_async_copy(smooth_hbm.at[:, a], smooth_ref.at[:, slot], sems.at[1, slot]),
        )
        for one in pair:
            one.start()
        copies.append((a, pair))
    small = [
        pltpu.make_async_copy(hbm, ref, small_sems.at[k])
        for k, (hbm, ref) in enumerate(((orient_hbm, orient_ref), (damp_hbm, damp_ref), (jac_hbm, jac_ref)))
    ]
    for one in small:
        one.start()
    for one in small:
        one.wait()
    for d in range(3):
        flag_ref[d] = twice(orient_ref[d])
    prepare_tables(jac_ref, damp_ref, jac8_ref, damp8_ref, face_ref)
    for slot, (a, pair) in enumerate(copies):
        for one in pair:
            one.wait()
        first_plane(src_ref, smooth_ref, u_ref, a, slot)
    fine_x_faces(u_ref, flag_ref, xo, xe)


def inner_planes_kernel(src_ref, smooth_ref, outer_ref, flag_ref, yo, ye, u_ref):
    for a in (1, 2):
        first_plane(src_ref, smooth_ref, u_ref, a, a)
    fine_y_faces(u_ref, flag_ref, yo, ye)


def prepare_tables(jac_ref, damp_ref, jac8_ref, damp8_ref, face_ref):
    damp = twice(damp_ref[...])
    damp8_ref[...] = damp
    for d in range(3):
        for k in range(25):
            value = twice(jac_ref[25 * d + k])
            jac8_ref[25 * d + k] = value
            if d < 2:
                low, step = axis_low(d)
                diagonal = k % 6 == 0
                upper = H4 * (value - damp if diagonal else value)
                lower = H4 * (value + damp if diagonal else value)
                face_ref[2 * d, k] = jnp.where(low, sroll(upper, -step), upper)
                face_ref[2 * d + 1, k] = jnp.where(low, lower, sroll(lower, step))


def volume(src_ref, u_ref, flag_ref, jac_ref, damp_ref, acc_ref):
    damp = H4 * damp_ref[...]

    def jacobian(d):
        return [[jac_ref[25 * d + 5 * o + i] for i in range(5)] for o in range(5)]

    def along(direction):
        low, step = axis_low(direction)
        flag = flag_ref[direction] != 0
        flag_before = sroll(flag_ref[direction], step) != 0

        def at(v, n, other, q):
            return (v, n, other, q) if direction == 0 else (v, other, n, q)

        def step_fn(j, carry):
            other, q = j // 2, j % 2
            u = [[u_ref[at(v, n, other, q)] for n in range(4)] for v in range(5)]
            waves = []
            jumps = []
            for v in range(5):
                back_low, back_high = u_ref[at(v, 0, 3 - other, q)], u_ref[at(v, 3, 3 - other, q)]
                right = sroll(jnp.where(flag_before, back_low, u[v][0]), -step)
                left = sroll(jnp.where(flag, back_high, u[v][3]), step)
                jump_right = jnp.where(low, right, 0.0) - u[v][3]
                jump_left = jnp.where(low, 0.0, left) - u[v][0]
                w = list(slopes_along(*u[v]))
                w[3] = w[3] + H4 * jump_right
                w[0] = w[0] - H4 * jump_left
                waves.append(w)
                jumps.append((damp * jump_left, None, None, damp * jump_right))
            matrix = jacobian(direction)
            for n in range(4):
                flux = mix(matrix, [waves[v][n] for v in range(5)])
                for v in range(5):
                    if direction == 0:
                        total = src_ref[at(v, n, other, q)] - 2.0 * u[v][n]
                    else:
                        total = acc_ref[at(v, n, other, q)]
                    total = total - flux[v]
                    if jumps[v][n] is not None:
                        total = total + jumps[v][n]
                    acc_ref[at(v, n, other, q)] = total
            return carry

        lax.fori_loop(0, 8, step_fn, 0)

    along(0)
    along(1)

    low = c_low()
    flag = jnp.where(low, lroll(flag_ref[2], 1), flag_ref[2]) != 0
    damp_z = damp
    coef = [
        [jnp.where(low, float(D4[2 * p, c]), float(D4[2 * p + 1, c ^ 1])).astype(F32) for c in range(4)]
        for p in range(2)
    ]

    def step_z(j, carry):
        a0, b = j // 4, j % 4
        here = (a0, 3 - a0)
        u = [[[u_ref[v, a, b, q] for q in range(2)] for v in range(5)] for a in here]
        turned = [[[sroll(u[s][v][q], 4) for q in range(2)] for v in range(5)] for s in range(2)]
        beside = []
        for s in range(2):
            line = []
            for v in range(5):
                face = jnp.where(low, turned[s][v][1], turned[s][v][0])
                line.append(jnp.where(low, lroll(face, 1), lroll(face, -1)))
            beside.append(line)
        matrix = jacobian(2)
        for s in range(2):
            waves = [[], []]
            jumps = []
            for v in range(5):
                own = jnp.where(low, u[s][v][0], u[s][v][1])
                jump = jnp.where(flag, beside[1 - s][v], beside[s][v]) - own
                jumps.append(damp_z * jump)
                lifted = H4 * jump
                for p in range(2):
                    w = coef[p][0] * u[s][v][0] + coef[p][1] * turned[s][v][0]
                    w = w + (coef[p][2] * u[s][v][1] + coef[p][3] * turned[s][v][1])
                    w = w - jnp.where(low, lifted, 0.0) if p == 0 else w + jnp.where(low, 0.0, lifted)
                    waves[p].append(w)
            for p in range(2):
                flux = mix(matrix, waves[p])
                for v in range(5):
                    part = jnp.where(low, jumps[v], 0.0) if p == 0 else jnp.where(low, 0.0, jumps[v])
                    acc_ref[v, here[s], b, p] = acc_ref[v, here[s], b, p] - flux[v] + part
        return carry

    lax.fori_loop(0, 8, step_z, 0)


def volume_kernel(src_ref, u_ref, flag_ref, jac8_ref, damp8_ref, acc_ref):
    volume(src_ref, u_ref, flag_ref, jac8_ref, damp8_ref, acc_ref)


def remote_parts(even_refs, odd_refs, flag_ref, face_ref, part_ref):
    for d, axis in ((0, "gx"), (1, "gy")):
        is_even = parity(axis)
        low, step = axis_low(d)
        flag = flag_ref[d]
        flag = jnp.where(low, sroll(flag, -step), flag) != 0
        even, odd = even_refs[d], odd_refs[d]
        matrix = [[face_ref[2 * d, 5 * o + i] for i in range(5)] for o in range(5)]
        for n in range(4):
            take = lambda v, m: jnp.where(is_even, even[v, m], odd[v, m])
            right = [jnp.where(flag, take(v, 3 - n), take(v, n)) for v in range(5)]
            for v, value in enumerate(mix(matrix, right)):
                part_ref[2 * d, v, n, 0] = jnp.where(low, 0.0, -sroll(value, step))
                part_ref[2 * d, v, n, 1] = jnp.where(low, 0.0, -value)
        matrix = [[face_ref[2 * d + 1, 5 * o + i] for i in range(5)] for o in range(5)]
        for n in range(4):
            left = [jnp.where(is_even, odd[v, n], even[v, n]) for v in range(5)]
            for v, value in enumerate(mix(matrix, left)):
                part_ref[2 * d + 1, v, n, 0] = jnp.where(low, value, 0.0)
                part_ref[2 * d + 1, v, n, 1] = jnp.where(low, sroll(value, -step), 0.0)


def whole(acc_ref, part_ref, v, a, b, q):
    total = acc_ref[v, a, b, q]
    if a == 3:
        total = total + part_ref[0, v, b, q]
    if a == 0:
        total = total + part_ref[1, v, b, q]
    if b == 3:
        total = total + part_ref[2, v, a, q]
    if b == 0:
        total = total + part_ref[3, v, a, q]
    return total


def second_kernel(
    acc_ref, u_ref, smooth_ref, flag_ref, face_ref, rxo, rxe, ryo, rye, out_ref, xo, xe, yo, ye, part_ref
):
    remote_parts((rxe, rye), (rxo, ryo), flag_ref, face_ref, part_ref)
    for a in range(4):
        for b in range(4):
            left = [[whole(acc_ref, part_ref, v, a, b, q) for q in range(2)] for v in range(5)]
            for o in range(5):
                total = [None, None]
                for i in range(5):
                    block = smooth_ref[5 * o + i, a, b].astype(F32)
                    for q in range(2):
                        term = block[8 * q : 8 * q + 8] * left[i][q]
                        total[q] = term if i == 0 else total[q] + term
                for q in range(2):
                    out_ref[o, a, b, q] = u_ref[o, a, b, q] + OMEGA * total[q]
    restricted_faces(out_ref, flag_ref, xo, xe, yo, ye)


def coarse_smooth(smooth_ref, fields):
    out = [[[None, None], [None, None]] for _ in range(5)]
    for i in range(2):
        for o in range(5):
            total = [None, None]
            for k in range(5):
                block = smooth_ref[5 * o + k, i].astype(F32)
                for j in range(2):
                    term = block[8 * j : 8 * j + 8] * fields[k][i][j]
                    total[j] = term if k == 0 else total[j] + term
            for j in range(2):
                out[o][i][j] = OMEGA * total[j]
    return out


def coarse_faces(field, flag_ref, xo, xe, yo, ye):
    for v in range(5):
        c = field[v]
        lows = [[c[0][0], c[0][1]], [c[0][0], c[1][0]]]
        highs = [[c[1][0], c[1][1]], [c[0][1], c[1][1]]]
        put_coarse_faces(v, lows, highs, flag_ref, ((xe, xo), (ye, yo)))


def restricted_volume_kernel(src_ref, u_ref, flag_ref, jac_ref, damp_ref, acc_ref):
    damp = H4 * damp_ref[...]
    low_c = c_low()
    slope = [
        jnp.where(low_c, float(PD[0, c]), float(PD[1, c ^ 1])).astype(F32) for c in range(4)
    ]
    flags = [flag_ref[0] != 0, flag_ref[1] != 0, jnp.where(low_c, lroll(flag_ref[2], 1), flag_ref[2]) != 0]
    sign = jnp.where(low_c, -H4, H4).astype(F32)
    waves = [[[[None] * 5 for _ in range(2)] for _ in range(2)] for _ in range(3)]

    def slopes_four(values):
        return [sum_of([(float(PD[i, n]), values[n]) for n in range(4)]) for i in range(2)]

    for v in range(5):
        line, slope_c, ends = {}, {}, {}
        for a in range(4):
            for b in range(4):
                first, second = u_ref[v, a, b, 0], u_ref[v, a, b, 1]
                line[a, b] = restrict_c(first, second)
                slope_c[a, b] = (slope[0] * first + slope[1] * sroll(first, 4)) + (
                    slope[2] * second + slope[3] * sroll(second, 4)
                )
                ends[a, b] = jnp.where(low_c, first, second)

        def along_b(table):
            return [restrict_four([table[a, b] for b in range(4)]) for a in range(4)]

        def both(table):
            by_b = along_b(table)
            return [restrict_four([by_b[a][j] for a in range(4)]) for j in range(2)]

        by_b = along_b(line)
        by_a = [restrict_four([line[a, b] for a in range(4)]) for b in range(4)]
        flux_z = both(slope_c)
        trace_z = both(ends)
        sources = both({(a, b): restrict_c(src_ref[v, a, b, 0], src_ref[v, a, b, 1]) for a in range(4) for b in range(4)})
        acc = [[None, None], [None, None]]
        for j in range(2):
            value = restrict_four([by_b[a][j] for a in range(4)])
            flux = slopes_four([by_b[a][j] for a in range(4)])
            for i in range(2):
                acc[i][j] = sources[j][i] - 2.0 * value[i]
                waves[0][i][j][v] = flux[i]
        for i in range(2):
            flux = slopes_four([by_a[b][i] for b in range(4)])
            for j in range(2):
                waves[1][i][j][v] = flux[j]
        for d, lo, hi in ((0, by_b[0], by_b[3]), (1, by_a[0], by_a[3])):
            low, step = axis_low(d)
            flag = flags[d]
            flag_before = sroll(flag_ref[d], step) != 0
            for m in range(2):
                right = sroll(jnp.where(flag_before, lo[1 - m], lo[m]), -step)
                left = sroll(jnp.where(flag, hi[1 - m], hi[m]), step)
                jump_right = jnp.where(low, right, 0.0) - hi[m]
                jump_left = jnp.where(low, 0.0, left) - lo[m]
                i, j = (1, m) if d == 0 else (m, 1)
                waves[d][i][j][v] = waves[d][i][j][v] + H4 * jump_right
                acc[i][j] = acc[i][j] + damp * jump_right
                i, j = (0, m) if d == 0 else (m, 0)
                waves[d][i][j][v] = waves[d][i][j][v] - H4 * jump_left
                acc[i][j] = acc[i][j] + damp * jump_left
        beside = []
        for j in range(2):
            turned = [sroll(trace_z[j][i], 4) for i in range(2)]
            beside.append([jnp.where(low_c, lroll(t, 1), lroll(t, -1)) for t in turned])
        for i in range(2):
            for j in range(2):
                jump = jnp.where(flags[2], beside[j][1 - i], beside[j][i]) - trace_z[j][i]
                waves[2][i][j][v] = flux_z[j][i] + sign * jump
                acc_ref[v, i, j] = acc[i][j] + damp * jump
    for d in range(3):
        matrix = [[jac_ref[25 * d + 5 * o + i] for i in range(5)] for o in range(5)]
        for i in range(2):
            for j in range(2):
                for v, value in enumerate(mix(matrix, waves[d][i][j])):
                    acc_ref[v, i, j] = acc_ref[v, i, j] - value


def add_remote(field, scale, flag_ref, face_ref, rxo, rxe, ryo, rye):
    for d, axis in ((0, "gx"), (1, "gy")):
        is_even = parity(axis)
        low, step = axis_low(d)
        flag = flag_ref[d]
        flag = jnp.where(low, sroll(flag, -step), flag) != 0
        even, odd = ((rxe, rxo), (rye, ryo))[d]
        at = (lambda n, m: (n, m)) if d == 0 else (lambda n, m: (m, n))
        right, left = [], []
        for v in range(5):
            value = scale * jnp.where(is_even, even[v], odd[v])
            swapped = jnp.where(low, sroll(value, -step), sroll(value, step))
            right.append(jnp.where(flag, swapped, value))
            left.append(scale * jnp.where(is_even, odd[v], even[v]))
        upper = [[face_ref[2 * d, 5 * o + i] for i in range(5)] for o in range(5)]
        lower = [[face_ref[2 * d + 1, 5 * o + i] for i in range(5)] for o in range(5)]
        for v, value in enumerate(mix(upper, right)):
            for m, part in enumerate((sroll(value, step), value)):
                i, j = at(1, m)
                field[v][i][j] = field[v][i][j] - jnp.where(low, 0.0, part)
        for v, value in enumerate(mix(lower, left)):
            for m, part in enumerate((value, sroll(value, -step))):
                i, j = at(0, m)
                field[v][i][j] = field[v][i][j] + jnp.where(low, part, 0.0)


def restrict_kernel(
    acc_ref, flag_ref, face_ref, smooth_ref, rxo, rxe, ryo, rye, rhs_ref, c_ref, xo, xe, yo, ye
):
    rhs = [[[acc_ref[v, i, j] for j in range(2)] for i in range(2)] for v in range(5)]
    add_remote(rhs, 1.0, flag_ref, face_ref, rxo, rxe, ryo, rye)
    c = coarse_smooth(smooth_ref, rhs)
    for v in range(5):
        for i in range(2):
            for j in range(2):
                rhs_ref[v, i, j] = rhs[v][i][j]
                c_ref[v, i, j] = c[v][i][j]
    coarse_faces(c, flag_ref, xo, xe, yo, ye)


def coarse_local_kernel(c_ref, rhs_ref, smooth_ref, flag_ref, jac_ref, damp_ref, out_ref):
    damp = 0.5 * damp_ref[...]
    c = [[[c_ref[v, i, j] for j in range(2)] for i in range(2)] for v in range(5)]
    acc = [[[rhs_ref[v, i, j] - 2.0 * c[v][i][j] for j in range(2)] for i in range(2)] for v in range(5)]
    for d in range(2):
        low, step = axis_low(d)
        flag = flag_ref[d] != 0
        flag_before = sroll(flag_ref[d], step) != 0
        matrix = [[jac_ref[25 * d + 5 * o + i] for i in range(5)] for o in range(5)]
        at = (lambda n, m: (n, m)) if d == 0 else (lambda n, m: (m, n))
        waves = [[[None] * 5, [None] * 5] for _ in range(2)]
        for v in range(5):
            lo = [c[v][at(0, m)[0]][at(0, m)[1]] for m in range(2)]
            hi = [c[v][at(1, m)[0]][at(1, m)[1]] for m in range(2)]
            for m in range(2):
                right = jnp.where(low, sroll(jnp.where(flag_before, lo[1 - m], lo[m]), -step), 0.0)
                left = jnp.where(low, 0.0, sroll(jnp.where(flag, hi[1 - m], hi[m]), step))
                waves[1][m][v] = 0.5 * (right - lo[m])
                waves[0][m][v] = 0.5 * (hi[m] - left)
                i, j = at(1, m)
                acc[v][i][j] = acc[v][i][j] + damp * (right - hi[m])
                i, j = at(0, m)
                acc[v][i][j] = acc[v][i][j] + damp * (left - lo[m])
        for n in range(2):
            for m in range(2):
                i, j = at(n, m)
                for v, value in enumerate(mix(matrix, waves[n][m])):
                    acc[v][i][j] = acc[v][i][j] - value
    low = c_low()
    flag = jnp.where(low, lroll(flag_ref[2], 1), flag_ref[2]) != 0
    half = jnp.where(low, 0.5, -0.5).astype(F32)
    matrix = [[jac_ref[50 + 5 * o + i] for i in range(5)] for o in range(5)]
    turned = [[[sroll(c[v][i][j], 4) for j in range(2)] for i in range(2)] for v in range(5)]
    beside = [
        [[jnp.where(low, lroll(t, 1), lroll(t, -1)) for t in turned[v][i]] for i in range(2)] for v in range(5)
    ]
    for i in range(2):
        for j in range(2):
            wave = []
            for v in range(5):
                next_to = jnp.where(flag, beside[v][1 - i][j], beside[v][i][j])
                wave.append(half * (turned[v][i][j] - next_to))
                acc[v][i][j] = acc[v][i][j] + damp * (next_to - c[v][i][j])
            for v, value in enumerate(mix(matrix, wave)):
                acc[v][i][j] = acc[v][i][j] - value
    change = coarse_smooth(smooth_ref, acc)
    for v in range(5):
        for i in range(2):
            for j in range(2):
                out_ref[v, i, j] = c[v][i][j] + change[v][i][j]


def coarse_step(c_ref, smooth_ref, flag_ref, face_ref, rxo, rxe, ryo, rye):
    rest = [[[0.0, 0.0], [0.0, 0.0]] for _ in range(5)]
    add_remote(rest, 1.0 / 6.0, flag_ref, face_ref, rxo, rxe, ryo, rye)
    change = coarse_smooth(smooth_ref, rest)
    return [[[c_ref[v, i, j] + change[v][i][j] for j in range(2)] for i in range(2)] for v in range(5)]


def coarse_kernel(c_ref, smooth_ref, flag_ref, face_ref, rxo, rxe, ryo, rye, out_ref, xo, xe, yo, ye):
    c = coarse_step(c_ref, smooth_ref, flag_ref, face_ref, rxo, rxe, ryo, rye)
    for v in range(5):
        for i in range(2):
            for j in range(2):
                out_ref[v, i, j] = c[v][i][j]
    coarse_faces(c, flag_ref, xo, xe, yo, ye)


def spread(first, second):
    return first, NEAR * first + FAR * second, FAR * first + NEAR * second, second


def last_kernel(
    c_ref, smooth_ref, flag_ref, face_ref, rxo, rxe, ryo, rye, second_ref, out_hbm, out_ref, sems
):
    c = coarse_step(c_ref, smooth_ref, flag_ref, face_ref, rxo, rxe, ryo, rye)
    low = c_low()
    copies = []
    for v in range(5):
        by_c = [[None, None], [None, None]]
        for i in range(2):
            for j in range(2):
                value = c[v][i][j]
                inner = FAR * value + NEAR * sroll(value, 4)
                by_c[i][j] = (jnp.where(low, value, inner), jnp.where(low, inner, value))
        for q in range(2):
            lines = [spread(by_c[i][0][q], by_c[i][1][q]) for i in range(2)]
            for b in range(4):
                for a, value in enumerate(spread(lines[0][b], lines[1][b])):
                    out_ref[v, a, b, q] = second_ref[v, a, b, q] + value
        copy = pltpu.make_async_copy(out_ref.at[v], out_hbm.at[v], sems.at[v])
        copy.start()
        copies.append(copy)
    for copy in copies:
        copy.wait()


FINE = (5, 4, 4, 2, 8, 128)
FINE_MESSAGE = (5, 4, 8, 128)
COARSE = (5, 2, 2, 8, 128)
COARSE_MESSAGE = (5, 8, 128)


def vmem(shape, dtype=F32):
    return pltpu.VMEM(shape, dtype)


def here(array):
    return pltpu.with_memory_space_constraint(array, pltpu.VMEM)


def call(kernel, args, outs, in_hbm=(), out_hbm=(), scratch=(), aliases=None, flops=0):
    in_specs = [
        pl.BlockSpec(memory_space=pltpu.HBM if k in in_hbm else pltpu.VMEM) for k in range(len(args))
    ]
    out_specs = [
        pl.BlockSpec(memory_space=pltpu.HBM if k in out_hbm else pltpu.VMEM) for k in range(len(outs))
    ]
    args = [pltpu.with_memory_space_constraint(a, pltpu.HBM) if k in in_hbm else here(a) for k, a in enumerate(args)]
    return pl.pallas_call(
        kernel,
        out_shape=outs,
        in_specs=in_specs,
        out_specs=out_specs,
        scratch_shapes=scratch,
        input_output_aliases=aliases or {},
        compiler_params=pltpu.CompilerParams(vmem_limit_bytes=8 * 2**20),
        cost_estimate=pl.CostEstimate(flops=flops, bytes_accessed=4 * 2**20, transcendentals=0),
    )(*args)


def partners(axis):
    size = lax.axis_size(axis)
    even = [(i, i ^ 1) for i in range(size)]
    odd = [(i, (i - 1) % size if i % 2 == 0 else (i + 1) % size) for i in range(size)]
    return even, odd


def exchange_x(xo, xe):
    even, odd = partners("gx")
    return lax.ppermute(xo, "gx", odd), lax.ppermute(xe, "gx", even)


def exchange_y(yo, ye):
    even, odd = partners("gy")
    return lax.ppermute(yo, "gy", odd), lax.ppermute(ye, "gy", even)


def exchange(xo, xe, yo, ye):
    return *exchange_x(xo, xe), *exchange_y(yo, ye)


def local_sweep(coarse, *rest):
    (out,) = call(coarse_local_kernel, (coarse, *rest), [vmem(COARSE)], flops=4 * 2**20)
    return out


def body(source, jacobian, damping, orient, smoother, coarse_smoother):
    source = source.reshape(FINE)
    smoother = smoother.reshape(25, 4, 4, 16, 128)
    coarse_smoother = coarse_smoother.reshape(25, 2, 16, 128)
    jacobian = jacobian.reshape(75, 4, 128)
    damping = damping.reshape(4, 128)
    orient = orient.reshape(3, 4, 128)
    fine_message = vmem(FINE_MESSAGE)
    coarse_messages = [vmem(COARSE_MESSAGE)] * 4

    xo, xe, outer, flag, jac8, damp8, face = call(
        x_planes_kernel,
        (source, smoother, orient, jacobian, damping),
        [
            fine_message,
            fine_message,
            vmem(FINE),
            vmem((3, 8, 128), jnp.int32),
            vmem((75, 8, 128)),
            vmem((8, 128)),
            vmem((4, 25, 8, 128)),
        ],
        in_hbm=(0, 1, 2, 3, 4),
        scratch=[
            pltpu.VMEM((5, 2, 4, 2, 8, 128), F32),
            pltpu.VMEM((25, 2, 4, 16, 128), smoother.dtype),
            pltpu.VMEM((3, 4, 128), jnp.int32),
            pltpu.VMEM((75, 4, 128), F32),
            pltpu.VMEM((4, 128), F32),
            pltpu.SemaphoreType.DMA((2, 2)),
            pltpu.SemaphoreType.DMA((3,)),
        ],
        flops=2 * 25 * 64 * 512,
    )
    got_x = exchange_x(xo, xe)
    yo, ye, first = call(
        inner_planes_kernel,
        (source, smoother, outer, flag),
        [fine_message, fine_message, vmem(FINE)],
        aliases={2: 2},
        flops=2 * 25 * 64 * 512,
    )
    got = (*got_x, *exchange_y(yo, ye))
    (acc,) = call(volume_kernel, (source, first, flag, jac8, damp8), [vmem(FINE)], flops=9 * 2**20)
    second, *sent = call(
        second_kernel,
        (acc, first, smoother, flag, face, *got),
        [vmem(FINE)] + coarse_messages,
        scratch=[pltpu.VMEM((4, 5, 4, 2, 8, 128), F32)],
        flops=3 * 2**20,
    )
    got = exchange(*sent)
    (acc,) = call(restricted_volume_kernel, (source, second, flag, jac8, damp8), [vmem(COARSE)], flops=4 * 2**20)
    rhs, coarse, *sent = call(
        restrict_kernel,
        (acc, flag, face, coarse_smoother, *got),
        [vmem(COARSE), vmem(COARSE)] + coarse_messages,
        flops=2**20,
    )
    got = exchange(*sent)
    coarse = local_sweep(coarse, rhs, coarse_smoother, flag, jac8, damp8)
    coarse, *sent = call(
        coarse_kernel,
        (coarse, coarse_smoother, flag, face, *got),
        [vmem(COARSE)] + coarse_messages,
        flops=2**20,
    )
    got = exchange(*sent)
    coarse = local_sweep(coarse, rhs, coarse_smoother, flag, jac8, damp8)
    (out,) = call(
        last_kernel,
        (coarse, coarse_smoother, flag, face, *got, second),
        [jax.ShapeDtypeStruct(FINE, F32)],
        out_hbm=(0,),
        scratch=[pltpu.VMEM(FINE, F32), pltpu.SemaphoreType.DMA((5,))],
        flops=2**20,
    )
    return out.reshape(5, 4, 4, 4, 2, 2, 128)


def solution(mesh):
    in_specs = (
        P(None, None, None, None, "gx", "gy", None),
        P(None, None, None, "gx", "gy", None),
        P("gx", "gy", None),
        P(None, "gx", "gy", None),
        P(None, None, None, None, None, "gx", "gy", None),
        P(None, None, None, None, None, "gx", "gy", None),
    )
    out_specs = P(None, None, None, None, "gx", "gy", None)
    return jax.shard_map(body, mesh=mesh, in_specs=in_specs, out_specs=out_specs, check_vma=False)
```

```python
import functools
import math

import jax
import jax.numpy as jnp
import numpy as np
from jax import lax
from jax.experimental import pallas as pl
from jax.experimental.pallas import tpu as pltpu
from jax.sharding import PartitionSpec as P


F32 = jnp.float32
OMEGA = 0.8
H4 = 3.0
ROOT = 1.0 / math.sqrt(5.0)
NEAR = (1.0 + ROOT) / 2.0
FAR = (1.0 - ROOT) / 2.0


def lobatto_slopes():
    points = np.array([-1.0, -ROOT, ROOT, 1.0])
    weights = np.ones(4)
    for i in range(4):
        for j in range(4):
            if i != j:
                weights[i] = weights[i] / (points[i] - points[j])
    slopes = np.zeros((4, 4))
    for i in range(4):
        for j in range(4):
            if i != j:
                slopes[i, j] = weights[j] / weights[i] / (points[i] - points[j])
        slopes[i, i] = -np.sum(slopes[i])
    return slopes


D4 = lobatto_slopes()
PD = np.array([[1.0, NEAR, FAR, 0.0], [0.0, FAR, NEAR, 1.0]]) @ D4


def sum_of(terms):
    total = None
    for weight, value in terms:
        total = weight * value if total is None else total + weight * value
    return total


def rows():
    return lax.broadcasted_iota(jnp.int32, (8, 128), 0)


def x_low():
    return (rows() & 2) == 0


def y_low():
    return (rows() & 1) == 0


def c_low():
    return (rows() & 4) == 0


def sroll(value, shift):
    return pltpu.roll(value, shift % 8, 0)


def lroll(value, shift):
    return pltpu.roll(value, shift % 128, 1)


def twice(value):
    return jnp.concatenate([value, value], axis=0)


def axis_low(direction):
    return (x_low(), 2) if direction == 0 else (y_low(), 1)


def pack_low(first, second, direction):
    low, step = axis_low(direction)
    return jnp.where(low, first, sroll(second, step))


def pack_high(first, second, direction):
    low, step = axis_low(direction)
    return jnp.where(low, sroll(first, -step), second)


def slopes_along(u0, u1, u2, u3):
    e0, o0, e1, o1 = u0 + u3, u0 - u3, u1 + u2, u1 - u2
    diff = e1 - e0
    even_a = float((D4[0, 1] + D4[0, 2]) / 2.0) * diff
    even_b = float((D4[1, 2] - 0.0) / 2.0) * diff
    odd_a = float((D4[0, 0] - D4[0, 3]) / 2.0) * o0 + float((D4[0, 1] - D4[0, 2]) / 2.0) * o1
    odd_b = float((D4[1, 0] - D4[1, 3]) / 2.0) * o0 - float(D4[1, 2] / 2.0) * o1
    return even_a + odd_a, even_b + odd_b, odd_b - even_b, odd_a - even_a


def mix(matrix, fields):
    out = []
    for o in range(5):
        total = matrix[o][0] * fields[0]
        for i in range(1, 5):
            total = total + matrix[o][i] * fields[i]
        out.append(total)
    return out


def parity(axis):
    return lax.rem(lax.axis_index(axis), 2) == 0


def put_pair(even_ref, odd_ref, index, low_face, high_face, is_even):
    even_ref[index] = jnp.where(is_even, high_face, low_face)
    odd_ref[index] = jnp.where(is_even, low_face, high_face)


def fine_faces(u_ref, flag_ref, xo, xe, yo, ye):
    even_x, even_y = parity("gx"), parity("gy")
    fx, fy = flag_ref[0] != 0, flag_ref[1] != 0
    for v in range(5):
        for n in range(4):
            low = pack_low(u_ref[v, 0, n, 0], u_ref[v, 0, n, 1], 0)
            h = [jnp.where(fx, u_ref[v, 3, 3 - n, q], u_ref[v, 3, n, q]) for q in range(2)]
            put_pair(xe, xo, (v, n), low, pack_high(h[0], h[1], 0), even_x)
            low = pack_low(u_ref[v, n, 0, 0], u_ref[v, n, 0, 1], 1)
            h = [jnp.where(fy, u_ref[v, 3 - n, 3, q], u_ref[v, n, 3, q]) for q in range(2)]
            put_pair(ye, yo, (v, n), low, pack_high(h[0], h[1], 1), even_y)


def restrict_c(first, second):
    low = c_low()
    middle = jnp.where(low, second, first)
    return jnp.where(low, first, second) + FAR * middle + NEAR * sroll(middle, 4)


def restrict_four(values):
    return values[0] + NEAR * values[1] + FAR * values[2], values[3] + NEAR * values[2] + FAR * values[1]


def put_coarse_faces(v, lows, highs, flag_ref, pairs):
    for d, axis in ((0, "gx"), (1, "gy")):
        flag = flag_ref[d] != 0
        low, high = lows[d], highs[d]
        turned = [jnp.where(flag, high[1 - m], high[m]) for m in range(2)]
        even_ref, odd_ref = pairs[d]
        put_pair(even_ref, odd_ref, v, pack_low(*low, d), pack_high(*turned, d), parity(axis))


def restricted_faces(u_ref, flag_ref, xo, xe, yo, ye):
    for v in range(5):
        line = {}
        for a in range(4):
            for b in range(4):
                if a in (0, 3) or b in (0, 3):
                    line[a, b] = restrict_c(u_ref[v, a, b, 0], u_ref[v, a, b, 1])
        lows = [restrict_four([line[0, n] for n in range(4)]), restrict_four([line[n, 0] for n in range(4)])]
        highs = [restrict_four([line[3, n] for n in range(4)]), restrict_four([line[n, 3] for n in range(4)])]
        put_coarse_faces(v, lows, highs, flag_ref, ((xe, xo), (ye, yo)))


def smoothed(smooth_ref, fields, a, b):
    out = []
    for o in range(5):
        total = [None, None]
        for i in range(5):
            block = smooth_ref[5 * o + i, a, b].astype(F32)
            for q in range(2):
                term = block[8 * q : 8 * q + 8] * fields[i][q]
                total[q] = term if i == 0 else total[q] + term
        out.append([OMEGA * total[q] for q in range(2)])
    return out


def first_line(src_ref, smooth_ref, u_ref, a, b):
    value = smoothed(smooth_ref, [[src_ref[v, a, b, q] for q in range(2)] for v in range(5)], a, b)
    for v in range(5):
        for q in range(2):
            u_ref[v, a, b, q] = value[v][q]


def line_copies(src_hbm, smooth_hbm, src_ref, smooth_ref, sems, slot, a, b):
    return (
        pltpu.make_async_copy(src_hbm.at[:, a, b], src_ref.at[:, a, b], sems.at[0, slot]),
        pltpu.make_async_copy(smooth_hbm.at[:, a, b], smooth_ref.at[:, a, b], sems.at[1, slot]),
    )


def first_kernel(
    src_hbm, smooth_hbm, orient_hbm, src_ref, smooth_ref, u_ref, flag_ref, xo, xe, yo, ye, sems, orient_ref, orient_sem
):
    every, inner = slice(0, 4), slice(1, 3)
    orient_copy = pltpu.make_async_copy(orient_hbm, orient_ref, orient_sem)
    orient_copy.start()
    copies = []
    for slot, (a, b) in enumerate(((0, every), (3, every), (inner, 0), (inner, 3))):
        pair = line_copies(src_hbm, smooth_hbm, src_ref, smooth_ref, sems, slot, a, b)
        for one in pair:
            one.start()
        copies.append(pair)
    orient_copy.wait()
    for d in range(3):
        flag_ref[d] = twice(orient_ref[d])
    lines = [[(0, b) for b in range(4)], [(3, b) for b in range(4)], [(1, 0), (2, 0)], [(1, 3), (2, 3)]]
    for pair, group in zip(copies, lines):
        for one in pair:
            one.wait()
        for a, b in group:
            first_line(src_ref, smooth_ref, u_ref, a, b)
    fine_faces(u_ref, flag_ref, xo, xe, yo, ye)


def prepare_tables(jac_ref, damp_ref, jac8_ref, damp8_ref, face_ref):
    damp = twice(damp_ref[...])
    damp8_ref[...] = damp
    for d in range(3):
        for k in range(25):
            value = twice(jac_ref[25 * d + k])
            jac8_ref[25 * d + k] = value
            if d < 2:
                low, step = axis_low(d)
                diagonal = k % 6 == 0
                upper = H4 * (value - damp if diagonal else value)
                lower = H4 * (value + damp if diagonal else value)
                face_ref[2 * d, k] = jnp.where(low, sroll(upper, -step), upper)
                face_ref[2 * d + 1, k] = jnp.where(low, lower, sroll(lower, step))


def volume(src_ref, u_ref, flag_ref, jac_ref, damp_ref, acc_ref, finish_lines):
    damp = H4 * damp_ref[...]

    def jacobian(d):
        return [[jac_ref[25 * d + 5 * o + i] for i in range(5)] for o in range(5)]

    def along(direction, others):
        low, step = axis_low(direction)
        flag = flag_ref[direction] != 0
        flag_before = sroll(flag_ref[direction], step) != 0

        def at(v, n, other, q):
            return (v, n, other, q) if direction == 0 else (v, other, n, q)

        def step_fn(j, carry):
            other, q = others(j // 2), j % 2
            u = [[u_ref[at(v, n, other, q)] for n in range(4)] for v in range(5)]
            waves = []
            jumps = []
            for v in range(5):
                back_low, back_high = u_ref[at(v, 0, 3 - other, q)], u_ref[at(v, 3, 3 - other, q)]
                right = sroll(jnp.where(flag_before, back_low, u[v][0]), -step)
                left = sroll(jnp.where(flag, back_high, u[v][3]), step)
                jump_right = jnp.where(low, right, 0.0) - u[v][3]
                jump_left = jnp.where(low, 0.0, left) - u[v][0]
                w = list(slopes_along(*u[v]))
                w[3] = w[3] + H4 * jump_right
                w[0] = w[0] - H4 * jump_left
                waves.append(w)
                jumps.append((damp * jump_left, None, None, damp * jump_right))
            matrix = jacobian(direction)
            for n in range(4):
                flux = mix(matrix, [waves[v][n] for v in range(5)])
                for v in range(5):
                    if direction == 1:
                        total = src_ref[at(v, n, other, q)] - 2.0 * u[v][n]
                    else:
                        total = acc_ref[at(v, n, other, q)]
                    total = total - flux[v]
                    if jumps[v][n] is not None:
                        total = total + jumps[v][n]
                    acc_ref[at(v, n, other, q)] = total
            return carry

        return step_fn

    low = c_low()
    flag = jnp.where(low, lroll(flag_ref[2], 1), flag_ref[2]) != 0
    damp_z = damp
    coef = [
        [jnp.where(low, float(D4[2 * p, c]), float(D4[2 * p + 1, c ^ 1])).astype(F32) for c in range(4)]
        for p in range(2)
    ]

    def step_z(j, carry):
        a0, b = j // 4, j % 4
        here = (a0, 3 - a0)
        u = [[[u_ref[v, a, b, q] for q in range(2)] for v in range(5)] for a in here]
        turned = [[[sroll(u[s][v][q], 4) for q in range(2)] for v in range(5)] for s in range(2)]
        beside = []
        for s in range(2):
            line = []
            for v in range(5):
                face = jnp.where(low, turned[s][v][1], turned[s][v][0])
                line.append(jnp.where(low, lroll(face, 1), lroll(face, -1)))
            beside.append(line)
        matrix = jacobian(2)
        for s in range(2):
            waves = [[], []]
            jumps = []
            for v in range(5):
                own = jnp.where(low, u[s][v][0], u[s][v][1])
                jump = jnp.where(flag, beside[1 - s][v], beside[s][v]) - own
                jumps.append(damp_z * jump)
                lifted = H4 * jump
                for p in range(2):
                    w = coef[p][0] * u[s][v][0] + coef[p][1] * turned[s][v][0]
                    w = w + (coef[p][2] * u[s][v][1] + coef[p][3] * turned[s][v][1])
                    w = w - jnp.where(low, lifted, 0.0) if p == 0 else w + jnp.where(low, 0.0, lifted)
                    waves[p].append(w)
            for p in range(2):
                flux = mix(matrix, waves[p])
                for v in range(5):
                    part = jnp.where(low, jumps[v], 0.0) if p == 0 else jnp.where(low, 0.0, jumps[v])
                    acc_ref[v, here[s], b, p] = acc_ref[v, here[s], b, p] - flux[v] + part
        return carry

    lax.fori_loop(0, 4, along(1, lambda k: 3 * k), 0)
    lax.fori_loop(0, 4, step_z, 0)
    finish_lines()
    lax.fori_loop(0, 4, along(1, lambda k: 1 + k), 0)
    lax.fori_loop(4, 8, step_z, 0)
    lax.fori_loop(0, 8, along(0, lambda k: k), 0)


def first_volume_kernel(
    src_hbm, smooth_hbm, src_in, smooth_in, u_in, flag_ref, jac_ref, damp_ref,
    src_ref, smooth_ref, u_ref, acc_ref, jac8_ref, damp8_ref, face_ref, second_ref, sems,
):
    inner = slice(1, 3)
    copies = line_copies(src_hbm, smooth_hbm, src_ref, smooth_ref, sems, 0, inner, inner)
    for one in copies:
        one.start()
    prepare_tables(jac_ref, damp_ref, jac8_ref, damp8_ref, face_ref)
    lines = [(a, b) for a in (1, 2) for b in (1, 2)]

    def finish_lines():
        for one in copies:
            one.wait()
        for a, b in lines:
            first_line(src_ref, smooth_ref, u_ref, a, b)

    volume(src_ref, u_ref, flag_ref, jac8_ref, damp8_ref, acc_ref, finish_lines)
    for a, b in lines:
        change = smoothed(smooth_ref, [[acc_ref[v, a, b, q] for q in range(2)] for v in range(5)], a, b)
        for v in range(5):
            for q in range(2):
                second_ref[v, a, b, q] = u_ref[v, a, b, q] + change[v][q]


def remote_parts(even_refs, odd_refs, flag_ref, face_ref, part_ref):
    for d, axis in ((0, "gx"), (1, "gy")):
        is_even = parity(axis)
        low, step = axis_low(d)
        flag = flag_ref[d]
        flag = jnp.where(low, sroll(flag, -step), flag) != 0
        even, odd = even_refs[d], odd_refs[d]
        matrix = [[face_ref[2 * d, 5 * o + i] for i in range(5)] for o in range(5)]
        for n in range(4):
            take = lambda v, m: jnp.where(is_even, even[v, m], odd[v, m])
            right = [jnp.where(flag, take(v, 3 - n), take(v, n)) for v in range(5)]
            for v, value in enumerate(mix(matrix, right)):
                part_ref[2 * d, v, n, 0] = jnp.where(low, 0.0, -sroll(value, step))
                part_ref[2 * d, v, n, 1] = jnp.where(low, 0.0, -value)
        matrix = [[face_ref[2 * d + 1, 5 * o + i] for i in range(5)] for o in range(5)]
        for n in range(4):
            left = [jnp.where(is_even, odd[v, n], even[v, n]) for v in range(5)]
            for v, value in enumerate(mix(matrix, left)):
                part_ref[2 * d + 1, v, n, 0] = jnp.where(low, value, 0.0)
                part_ref[2 * d + 1, v, n, 1] = jnp.where(low, sroll(value, -step), 0.0)


def whole(acc_ref, part_ref, v, a, b, q):
    total = acc_ref[v, a, b, q]
    if a == 3:
        total = total + part_ref[0, v, b, q]
    if a == 0:
        total = total + part_ref[1, v, b, q]
    if b == 3:
        total = total + part_ref[2, v, a, q]
    if b == 0:
        total = total + part_ref[3, v, a, q]
    return total


def second_kernel(
    acc_ref, u_ref, smooth_ref, flag_ref, face_ref, rxo, rxe, ryo, rye, inner_ref, out_ref, xo, xe, yo, ye, part_ref
):
    remote_parts((rxe, rye), (rxo, ryo), flag_ref, face_ref, part_ref)
    for a in range(4):
        for b in range(4):
            if a in (1, 2) and b in (1, 2):
                continue
            left = [[whole(acc_ref, part_ref, v, a, b, q) for q in range(2)] for v in range(5)]
            change = smoothed(smooth_ref, left, a, b)
            for v in range(5):
                for q in range(2):
                    out_ref[v, a, b, q] = u_ref[v, a, b, q] + change[v][q]
    restricted_faces(out_ref, flag_ref, xo, xe, yo, ye)


def coarse_smooth(smooth_ref, fields):
    out = [[[None, None], [None, None]] for _ in range(5)]
    for i in range(2):
        for o in range(5):
            total = [None, None]
            for k in range(5):
                block = smooth_ref[5 * o + k, i].astype(F32)
                for j in range(2):
                    term = block[8 * j : 8 * j + 8] * fields[k][i][j]
                    total[j] = term if k == 0 else total[j] + term
            for j in range(2):
                out[o][i][j] = OMEGA * total[j]
    return out


def coarse_faces(field, flag_ref, xo, xe, yo, ye):
    for v in range(5):
        c = field[v]
        lows = [[c[0][0], c[0][1]], [c[0][0], c[1][0]]]
        highs = [[c[1][0], c[1][1]], [c[0][1], c[1][1]]]
        put_coarse_faces(v, lows, highs, flag_ref, ((xe, xo), (ye, yo)))


def restricted_volume_kernel(src_ref, u_ref, flag_ref, jac_ref, damp_ref, acc_ref):
    damp = H4 * damp_ref[...]
    low_c = c_low()
    slope = [
        jnp.where(low_c, float(PD[0, c]), float(PD[1, c ^ 1])).astype(F32) for c in range(4)
    ]
    flags = [flag_ref[0] != 0, flag_ref[1] != 0, jnp.where(low_c, lroll(flag_ref[2], 1), flag_ref[2]) != 0]
    sign = jnp.where(low_c, -H4, H4).astype(F32)
    waves = [[[[None] * 5 for _ in range(2)] for _ in range(2)] for _ in range(3)]

    def slopes_four(values):
        return [sum_of([(float(PD[i, n]), values[n]) for n in range(4)]) for i in range(2)]

    for v in range(5):
        line, slope_c, ends = {}, {}, {}
        for a in range(4):
            for b in range(4):
                first, second = u_ref[v, a, b, 0], u_ref[v, a, b, 1]
                line[a, b] = restrict_c(first, second)
                slope_c[a, b] = (slope[0] * first + slope[1] * sroll(first, 4)) + (
                    slope[2] * second + slope[3] * sroll(second, 4)
                )
                ends[a, b] = jnp.where(low_c, first, second)

        def along_b(table):
            return [restrict_four([table[a, b] for b in range(4)]) for a in range(4)]

        def both(table):
            by_b = along_b(table)
            return [restrict_four([by_b[a][j] for a in range(4)]) for j in range(2)]

        by_b = along_b(line)
        by_a = [restrict_four([line[a, b] for a in range(4)]) for b in range(4)]
        flux_z = both(slope_c)
        trace_z = both(ends)
        sources = both({(a, b): restrict_c(src_ref[v, a, b, 0], src_ref[v, a, b, 1]) for a in range(4) for b in range(4)})
        acc = [[None, None], [None, None]]
        for j in range(2):
            value = restrict_four([by_b[a][j] for a in range(4)])
            flux = slopes_four([by_b[a][j] for a in range(4)])
            for i in range(2):
                acc[i][j] = sources[j][i] - 2.0 * value[i]
                waves[0][i][j][v] = flux[i]
        for i in range(2):
            flux = slopes_four([by_a[b][i] for b in range(4)])
            for j in range(2):
                waves[1][i][j][v] = flux[j]
        for d, lo, hi in ((0, by_b[0], by_b[3]), (1, by_a[0], by_a[3])):
            low, step = axis_low(d)
            flag = flags[d]
            flag_before = sroll(flag_ref[d], step) != 0
            for m in range(2):
                right = sroll(jnp.where(flag_before, lo[1 - m], lo[m]), -step)
                left = sroll(jnp.where(flag, hi[1 - m], hi[m]), step)
                jump_right = jnp.where(low, right, 0.0) - hi[m]
                jump_left = jnp.where(low, 0.0, left) - lo[m]
                i, j = (1, m) if d == 0 else (m, 1)
                waves[d][i][j][v] = waves[d][i][j][v] + H4 * jump_right
                acc[i][j] = acc[i][j] + damp * jump_right
                i, j = (0, m) if d == 0 else (m, 0)
                waves[d][i][j][v] = waves[d][i][j][v] - H4 * jump_left
                acc[i][j] = acc[i][j] + damp * jump_left
        beside = []
        for j in range(2):
            turned = [sroll(trace_z[j][i], 4) for i in range(2)]
            beside.append([jnp.where(low_c, lroll(t, 1), lroll(t, -1)) for t in turned])
        for i in range(2):
            for j in range(2):
                jump = jnp.where(flags[2], beside[j][1 - i], beside[j][i]) - trace_z[j][i]
                waves[2][i][j][v] = flux_z[j][i] + sign * jump
                acc_ref[v, i, j] = acc[i][j] + damp * jump
    for d in range(3):
        matrix = [[jac_ref[25 * d + 5 * o + i] for i in range(5)] for o in range(5)]
        for i in range(2):
            for j in range(2):
                for v, value in enumerate(mix(matrix, waves[d][i][j])):
                    acc_ref[v, i, j] = acc_ref[v, i, j] - value


def add_remote(field, scale, flag_ref, face_ref, rxo, rxe, ryo, rye):
    for d, axis in ((0, "gx"), (1, "gy")):
        is_even = parity(axis)
        low, step = axis_low(d)
        flag = flag_ref[d]
        flag = jnp.where(low, sroll(flag, -step), flag) != 0
        even, odd = ((rxe, rxo), (rye, ryo))[d]
        at = (lambda n, m: (n, m)) if d == 0 else (lambda n, m: (m, n))
        right, left = [], []
        for v in range(5):
            value = scale * jnp.where(is_even, even[v], odd[v])
            swapped = jnp.where(low, sroll(value, -step), sroll(value, step))
            right.append(jnp.where(flag, swapped, value))
            left.append(scale * jnp.where(is_even, odd[v], even[v]))
        upper = [[face_ref[2 * d, 5 * o + i] for i in range(5)] for o in range(5)]
        lower = [[face_ref[2 * d + 1, 5 * o + i] for i in range(5)] for o in range(5)]
        for v, value in enumerate(mix(upper, right)):
            for m, part in enumerate((sroll(value, step), value)):
                i, j = at(1, m)
                field[v][i][j] = field[v][i][j] - jnp.where(low, 0.0, part)
        for v, value in enumerate(mix(lower, left)):
            for m, part in enumerate((value, sroll(value, -step))):
                i, j = at(0, m)
                field[v][i][j] = field[v][i][j] + jnp.where(low, part, 0.0)


def restrict_kernel(
    acc_ref, flag_ref, face_ref, smooth_ref, rxo, rxe, ryo, rye, rhs_ref, c_ref, xo, xe, yo, ye
):
    rhs = [[[acc_ref[v, i, j] for j in range(2)] for i in range(2)] for v in range(5)]
    add_remote(rhs, 1.0, flag_ref, face_ref, rxo, rxe, ryo, rye)
    c = coarse_smooth(smooth_ref, rhs)
    for v in range(5):
        for i in range(2):
            for j in range(2):
                rhs_ref[v, i, j] = rhs[v][i][j]
                c_ref[v, i, j] = c[v][i][j]
    coarse_faces(c, flag_ref, xo, xe, yo, ye)


def coarse_local_kernel(c_ref, rhs_ref, smooth_ref, flag_ref, jac_ref, damp_ref, out_ref):
    damp = 0.5 * damp_ref[...]
    c = [[[c_ref[v, i, j] for j in range(2)] for i in range(2)] for v in range(5)]
    acc = [[[rhs_ref[v, i, j] - 2.0 * c[v][i][j] for j in range(2)] for i in range(2)] for v in range(5)]
    for d in range(2):
        low, step = axis_low(d)
        flag = flag_ref[d] != 0
        flag_before = sroll(flag_ref[d], step) != 0
        matrix = [[jac_ref[25 * d + 5 * o + i] for i in range(5)] for o in range(5)]
        at = (lambda n, m: (n, m)) if d == 0 else (lambda n, m: (m, n))
        waves = [[[None] * 5, [None] * 5] for _ in range(2)]
        for v in range(5):
            lo = [c[v][at(0, m)[0]][at(0, m)[1]] for m in range(2)]
            hi = [c[v][at(1, m)[0]][at(1, m)[1]] for m in range(2)]
            for m in range(2):
                right = jnp.where(low, sroll(jnp.where(flag_before, lo[1 - m], lo[m]), -step), 0.0)
                left = jnp.where(low, 0.0, sroll(jnp.where(flag, hi[1 - m], hi[m]), step))
                waves[1][m][v] = 0.5 * (right - lo[m])
                waves[0][m][v] = 0.5 * (hi[m] - left)
                i, j = at(1, m)
                acc[v][i][j] = acc[v][i][j] + damp * (right - hi[m])
                i, j = at(0, m)
                acc[v][i][j] = acc[v][i][j] + damp * (left - lo[m])
        for n in range(2):
            for m in range(2):
                i, j = at(n, m)
                for v, value in enumerate(mix(matrix, waves[n][m])):
                    acc[v][i][j] = acc[v][i][j] - value
    low = c_low()
    flag = jnp.where(low, lroll(flag_ref[2], 1), flag_ref[2]) != 0
    half = jnp.where(low, 0.5, -0.5).astype(F32)
    matrix = [[jac_ref[50 + 5 * o + i] for i in range(5)] for o in range(5)]
    turned = [[[sroll(c[v][i][j], 4) for j in range(2)] for i in range(2)] for v in range(5)]
    beside = [
        [[jnp.where(low, lroll(t, 1), lroll(t, -1)) for t in turned[v][i]] for i in range(2)] for v in range(5)
    ]
    for i in range(2):
        for j in range(2):
            wave = []
            for v in range(5):
                next_to = jnp.where(flag, beside[v][1 - i][j], beside[v][i][j])
                wave.append(half * (turned[v][i][j] - next_to))
                acc[v][i][j] = acc[v][i][j] + damp * (next_to - c[v][i][j])
            for v, value in enumerate(mix(matrix, wave)):
                acc[v][i][j] = acc[v][i][j] - value
    change = coarse_smooth(smooth_ref, acc)
    for v in range(5):
        for i in range(2):
            for j in range(2):
                out_ref[v, i, j] = c[v][i][j] + change[v][i][j]


def coarse_step(c_ref, smooth_ref, flag_ref, face_ref, rxo, rxe, ryo, rye):
    rest = [[[0.0, 0.0], [0.0, 0.0]] for _ in range(5)]
    add_remote(rest, 1.0 / 6.0, flag_ref, face_ref, rxo, rxe, ryo, rye)
    change = coarse_smooth(smooth_ref, rest)
    return [[[c_ref[v, i, j] + change[v][i][j] for j in range(2)] for i in range(2)] for v in range(5)]


def coarse_kernel(c_ref, smooth_ref, flag_ref, face_ref, rxo, rxe, ryo, rye, out_ref, xo, xe, yo, ye):
    c = coarse_step(c_ref, smooth_ref, flag_ref, face_ref, rxo, rxe, ryo, rye)
    for v in range(5):
        for i in range(2):
            for j in range(2):
                out_ref[v, i, j] = c[v][i][j]
    coarse_faces(c, flag_ref, xo, xe, yo, ye)


def spread(first, second):
    return first, NEAR * first + FAR * second, FAR * first + NEAR * second, second


def last_kernel(
    c_ref, smooth_ref, flag_ref, face_ref, rxo, rxe, ryo, rye, second_ref, out_hbm, out_ref, sems
):
    c = coarse_step(c_ref, smooth_ref, flag_ref, face_ref, rxo, rxe, ryo, rye)
    low = c_low()
    copies = []
    for v in range(5):
        by_c = [[None, None], [None, None]]
        for i in range(2):
            for j in range(2):
                value = c[v][i][j]
                inner = FAR * value + NEAR * sroll(value, 4)
                by_c[i][j] = (jnp.where(low, value, inner), jnp.where(low, inner, value))
        for q in range(2):
            lines = [spread(by_c[i][0][q], by_c[i][1][q]) for i in range(2)]
            for b in range(4):
                for a, value in enumerate(spread(lines[0][b], lines[1][b])):
                    out_ref[v, a, b, q] = second_ref[v, a, b, q] + value
        copy = pltpu.make_async_copy(out_ref.at[v], out_hbm.at[v], sems.at[v])
        copy.start()
        copies.append(copy)
    for copy in copies:
        copy.wait()


FINE = (5, 4, 4, 2, 8, 128)
FINE_MESSAGE = (5, 4, 8, 128)
COARSE = (5, 2, 2, 8, 128)
COARSE_MESSAGE = (5, 8, 128)


def vmem(shape, dtype=F32):
    return pltpu.VMEM(shape, dtype)


def here(array):
    return pltpu.with_memory_space_constraint(array, pltpu.VMEM)


def call(kernel, args, outs, in_hbm=(), out_hbm=(), scratch=(), aliases=None, flops=0):
    in_specs = [
        pl.BlockSpec(memory_space=pltpu.HBM if k in in_hbm else pltpu.VMEM) for k in range(len(args))
    ]
    out_specs = [
        pl.BlockSpec(memory_space=pltpu.HBM if k in out_hbm else pltpu.VMEM) for k in range(len(outs))
    ]
    args = [pltpu.with_memory_space_constraint(a, pltpu.HBM) if k in in_hbm else here(a) for k, a in enumerate(args)]
    return pl.pallas_call(
        kernel,
        out_shape=outs,
        in_specs=in_specs,
        out_specs=out_specs,
        scratch_shapes=scratch,
        input_output_aliases=aliases or {},
        compiler_params=pltpu.CompilerParams(vmem_limit_bytes=8 * 2**20),
        cost_estimate=pl.CostEstimate(flops=flops, bytes_accessed=4 * 2**20, transcendentals=0),
    )(*args)


def partners(axis):
    size = lax.axis_size(axis)
    even = [(i, i ^ 1) for i in range(size)]
    odd = [(i, (i - 1) % size if i % 2 == 0 else (i + 1) % size) for i in range(size)]
    return even, odd


def exchange(xo, xe, yo, ye):
    even_x, odd_x = partners("gx")
    even_y, odd_y = partners("gy")
    xo = lax.ppermute(xo, "gx", odd_x)
    xe = lax.ppermute(xe, "gx", even_x)
    yo = lax.ppermute(yo, "gy", odd_y)
    ye = lax.ppermute(ye, "gy", even_y)
    return xo, xe, yo, ye


def local_sweep(coarse, *rest):
    (out,) = call(coarse_local_kernel, (coarse, *rest), [vmem(COARSE)], flops=4 * 2**20)
    return out


def body(source, jacobian, damping, orient, smoother, coarse_smoother):
    source = source.reshape(FINE)
    smoother = smoother.reshape(25, 4, 4, 16, 128)
    coarse_smoother = coarse_smoother.reshape(25, 2, 16, 128)
    jacobian = jacobian.reshape(75, 4, 128)
    damping = damping.reshape(4, 128)
    orient = orient.reshape(3, 4, 128)
    fine_messages = [vmem(FINE_MESSAGE)] * 4
    coarse_messages = [vmem(COARSE_MESSAGE)] * 4

    held = vmem(smoother.shape, smoother.dtype)
    source_in, smoother_in = source, smoother
    source, smoother, first, flag, *sent = call(
        first_kernel,
        (source_in, smoother_in, orient),
        [vmem(FINE), held, vmem(FINE), vmem((3, 8, 128), jnp.int32)] + fine_messages,
        in_hbm=(0, 1, 2),
        scratch=[pltpu.SemaphoreType.DMA((2, 4)), pltpu.VMEM((3, 4, 128), jnp.int32), pltpu.SemaphoreType.DMA],
        flops=2 * 25 * 64 * 512,
    )
    got = exchange(*sent)
    source, smoother, first, acc, jac8, damp8, face, second = call(
        first_volume_kernel,
        (source_in, smoother_in, source, smoother, first, flag, jacobian, damping),
        [vmem(FINE), held, vmem(FINE), vmem(FINE), vmem((75, 8, 128)), vmem((8, 128)), vmem((4, 25, 8, 128)), vmem(FINE)],
        in_hbm=(0, 1),
        aliases={2: 0, 3: 1, 4: 2},
        scratch=[pltpu.SemaphoreType.DMA((2, 1))],
        flops=9 * 2**20,
    )
    second, *sent = call(
        second_kernel,
        (acc, first, smoother, flag, face, *got, second),
        [vmem(FINE)] + coarse_messages,
        aliases={9: 0},
        scratch=[pltpu.VMEM((4, 5, 4, 2, 8, 128), F32)],
        flops=3 * 2**20,
    )
    got = exchange(*sent)
    (acc,) = call(restricted_volume_kernel, (source, second, flag, jac8, damp8), [vmem(COARSE)], flops=4 * 2**20)
    rhs, coarse, *sent = call(
        restrict_kernel,
        (acc, flag, face, coarse_smoother, *got),
        [vmem(COARSE), vmem(COARSE)] + coarse_messages,
        flops=2**20,
    )
    got = exchange(*sent)
    coarse = local_sweep(coarse, rhs, coarse_smoother, flag, jac8, damp8)
    coarse, *sent = call(
        coarse_kernel,
        (coarse, coarse_smoother, flag, face, *got),
        [vmem(COARSE)] + coarse_messages,
        flops=2**20,
    )
    got = exchange(*sent)
    coarse = local_sweep(coarse, rhs, coarse_smoother, flag, jac8, damp8)
    (out,) = call(
        last_kernel,
        (coarse, coarse_smoother, flag, face, *got, second),
        [jax.ShapeDtypeStruct(FINE, F32)],
        out_hbm=(0,),
        scratch=[pltpu.VMEM(FINE, F32), pltpu.SemaphoreType.DMA((5,))],
        flops=2**20,
    )
    return out.reshape(5, 4, 4, 4, 2, 2, 128)


def solution(mesh):
    in_specs = (
        P(None, None, None, None, "gx", "gy", None),
        P(None, None, None, "gx", "gy", None),
        P("gx", "gy", None),
        P(None, "gx", "gy", None),
        P(None, None, None, None, None, "gx", "gy", None),
        P(None, None, None, None, None, "gx", "gy", None),
    )
    out_specs = P(None, None, None, None, "gx", "gy", None)
    return jax.shard_map(body, mesh=mesh, in_specs=in_specs, out_specs=out_specs, check_vma=False)
```

```python
import functools
import math

import jax
import jax.numpy as jnp
import numpy as np
from jax import lax
from jax.experimental import pallas as pl
from jax.experimental.pallas import tpu as pltpu
from jax.sharding import PartitionSpec as P


F32 = jnp.float32
OMEGA = 0.8
H4 = 3.0
ROOT = 1.0 / math.sqrt(5.0)
NEAR = (1.0 + ROOT) / 2.0
FAR = (1.0 - ROOT) / 2.0


def lobatto_slopes():
    points = np.array([-1.0, -ROOT, ROOT, 1.0])
    weights = np.ones(4)
    for i in range(4):
        for j in range(4):
            if i != j:
                weights[i] = weights[i] / (points[i] - points[j])
    slopes = np.zeros((4, 4))
    for i in range(4):
        for j in range(4):
            if i != j:
                slopes[i, j] = weights[j] / weights[i] / (points[i] - points[j])
        slopes[i, i] = -np.sum(slopes[i])
    return slopes


D4 = lobatto_slopes()
PD = np.array([[1.0, NEAR, FAR, 0.0], [0.0, FAR, NEAR, 1.0]]) @ D4


def sum_of(terms):
    total = None
    for weight, value in terms:
        total = weight * value if total is None else total + weight * value
    return total


def rows():
    return lax.broadcasted_iota(jnp.int32, (8, 128), 0)


def x_low():
    return (rows() & 2) == 0


def y_low():
    return (rows() & 1) == 0


def c_low():
    return (rows() & 4) == 0


def sroll(value, shift):
    return pltpu.roll(value, shift % 8, 0)


def lroll(value, shift):
    return pltpu.roll(value, shift % 128, 1)


def twice(value):
    return jnp.concatenate([value, value], axis=0)


def axis_low(direction):
    return (x_low(), 2) if direction == 0 else (y_low(), 1)


def pack_low(first, second, direction):
    low, step = axis_low(direction)
    return jnp.where(low, first, sroll(second, step))


def pack_high(first, second, direction):
    low, step = axis_low(direction)
    return jnp.where(low, sroll(first, -step), second)


def slopes_along(u0, u1, u2, u3):
    e0, o0, e1, o1 = u0 + u3, u0 - u3, u1 + u2, u1 - u2
    diff = e1 - e0
    even_a = float((D4[0, 1] + D4[0, 2]) / 2.0) * diff
    even_b = float((D4[1, 2] - 0.0) / 2.0) * diff
    odd_a = float((D4[0, 0] - D4[0, 3]) / 2.0) * o0 + float((D4[0, 1] - D4[0, 2]) / 2.0) * o1
    odd_b = float((D4[1, 0] - D4[1, 3]) / 2.0) * o0 - float(D4[1, 2] / 2.0) * o1
    return even_a + odd_a, even_b + odd_b, odd_b - even_b, odd_a - even_a


def mix(matrix, fields):
    out = []
    for o in range(5):
        total = matrix[o][0] * fields[0]
        for i in range(1, 5):
            total = total + matrix[o][i] * fields[i]
        out.append(total)
    return out


def parity(axis):
    return lax.rem(lax.axis_index(axis), 2) == 0


def put_pair(even_ref, odd_ref, index, low_face, high_face, is_even):
    even_ref[index] = jnp.where(is_even, high_face, low_face)
    odd_ref[index] = jnp.where(is_even, low_face, high_face)


def fine_faces(u_ref, flag_ref, xo, xe, yo, ye):
    even_x, even_y = parity("gx"), parity("gy")
    fx, fy = flag_ref[0] != 0, flag_ref[1] != 0
    for v in range(5):
        for n in range(4):
            low = pack_low(u_ref[v, 0, n, 0], u_ref[v, 0, n, 1], 0)
            h = [jnp.where(fx, u_ref[v, 3, 3 - n, q], u_ref[v, 3, n, q]) for q in range(2)]
            put_pair(xe, xo, (v, n), low, pack_high(h[0], h[1], 0), even_x)
            low = pack_low(u_ref[v, n, 0, 0], u_ref[v, n, 0, 1], 1)
            h = [jnp.where(fy, u_ref[v, 3 - n, 3, q], u_ref[v, n, 3, q]) for q in range(2)]
            put_pair(ye, yo, (v, n), low, pack_high(h[0], h[1], 1), even_y)


def restrict_c(first, second):
    low = c_low()
    middle = jnp.where(low, second, first)
    return jnp.where(low, first, second) + FAR * middle + NEAR * sroll(middle, 4)


def restrict_four(values):
    return values[0] + NEAR * values[1] + FAR * values[2], values[3] + NEAR * values[2] + FAR * values[1]


def put_coarse_faces(v, lows, highs, flag_ref, pairs):
    for d, axis in ((0, "gx"), (1, "gy")):
        flag = flag_ref[d] != 0
        low, high = lows[d], highs[d]
        turned = [jnp.where(flag, high[1 - m], high[m]) for m in range(2)]
        even_ref, odd_ref = pairs[d]
        put_pair(even_ref, odd_ref, v, pack_low(*low, d), pack_high(*turned, d), parity(axis))


def restricted_faces(u_ref, flag_ref, xo, xe, yo, ye):
    for v in range(5):
        line = {}
        for a in range(4):
            for b in range(4):
                if a in (0, 3) or b in (0, 3):
                    line[a, b] = restrict_c(u_ref[v, a, b, 0], u_ref[v, a, b, 1])
        lows = [restrict_four([line[0, n] for n in range(4)]), restrict_four([line[n, 0] for n in range(4)])]
        highs = [restrict_four([line[3, n] for n in range(4)]), restrict_four([line[n, 3] for n in range(4)])]
        put_coarse_faces(v, lows, highs, flag_ref, ((xe, xo), (ye, yo)))


def smoothed(smooth_ref, fields, a, b):
    out = []
    for o in range(5):
        total = [None, None]
        for i in range(5):
            block = smooth_ref[5 * o + i, a, b].astype(F32)
            for q in range(2):
                term = block[8 * q : 8 * q + 8] * fields[i][q]
                total[q] = term if i == 0 else total[q] + term
        out.append([OMEGA * total[q] for q in range(2)])
    return out


def first_kernel(
    src_hbm, smooth_hbm, orient_hbm, src_ref, smooth_ref, u_ref, flag_ref, xo, xe, yo, ye,
    src_sems, smooth_sems, orient_ref, orient_sem,
):
    orient_copy = pltpu.make_async_copy(orient_hbm, orient_ref, orient_sem)
    src_copies = [pltpu.make_async_copy(src_hbm.at[v], src_ref.at[v], src_sems.at[v]) for v in range(5)]
    smooth_copies = [pltpu.make_async_copy(smooth_hbm.at[k], smooth_ref.at[k], smooth_sems.at[k]) for k in range(25)]
    for one in (*src_copies, *smooth_copies, orient_copy):
        one.start()
    for one in src_copies:
        one.wait()
    for o in range(5):
        for one in smooth_copies[5 * o : 5 * o + 5]:
            one.wait()
        for a in range(4):
            for b in range(4):
                total = [None, None]
                for i in range(5):
                    block = smooth_ref[5 * o + i, a, b].astype(F32)
                    for q in range(2):
                        term = block[8 * q : 8 * q + 8] * src_ref[i, a, b, q]
                        total[q] = term if i == 0 else total[q] + term
                for q in range(2):
                    u_ref[o, a, b, q] = OMEGA * total[q]
    orient_copy.wait()
    for d in range(3):
        flag_ref[d] = twice(orient_ref[d])
    fine_faces(u_ref, flag_ref, xo, xe, yo, ye)


def prepare_tables(jac_ref, damp_ref, jac8_ref, damp8_ref, face_ref):
    damp = twice(damp_ref[...])
    damp8_ref[...] = damp
    for d in range(3):
        for k in range(25):
            value = twice(jac_ref[25 * d + k])
            jac8_ref[25 * d + k] = value
            if d < 2:
                low, step = axis_low(d)
                diagonal = k % 6 == 0
                upper = H4 * (value - damp if diagonal else value)
                lower = H4 * (value + damp if diagonal else value)
                face_ref[2 * d, k] = jnp.where(low, sroll(upper, -step), upper)
                face_ref[2 * d + 1, k] = jnp.where(low, lower, sroll(lower, step))


def volume(src_ref, u_ref, flag_ref, jac_ref, damp_ref, acc_ref):
    damp = H4 * damp_ref[...]

    def jacobian(d):
        return [[jac_ref[25 * d + 5 * o + i] for i in range(5)] for o in range(5)]

    def along(direction):
        low, step = axis_low(direction)
        flag = flag_ref[direction] != 0
        flag_before = sroll(flag_ref[direction], step) != 0

        def at(v, n, other, q):
            return (v, n, other, q) if direction == 0 else (v, other, n, q)

        def step_fn(j, carry):
            other, q = j // 2, j % 2
            u = [[u_ref[at(v, n, other, q)] for n in range(4)] for v in range(5)]
            waves = []
            jumps = []
            for v in range(5):
                back_low, back_high = u_ref[at(v, 0, 3 - other, q)], u_ref[at(v, 3, 3 - other, q)]
                right = sroll(jnp.where(flag_before, back_low, u[v][0]), -step)
                left = sroll(jnp.where(flag, back_high, u[v][3]), step)
                jump_right = jnp.where(low, right, 0.0) - u[v][3]
                jump_left = jnp.where(low, 0.0, left) - u[v][0]
                w = list(slopes_along(*u[v]))
                w[3] = w[3] + H4 * jump_right
                w[0] = w[0] - H4 * jump_left
                waves.append(w)
                jumps.append((damp * jump_left, None, None, damp * jump_right))
            matrix = jacobian(direction)
            for n in range(4):
                flux = mix(matrix, [waves[v][n] for v in range(5)])
                for v in range(5):
                    if direction == 1:
                        total = src_ref[at(v, n, other, q)] - 2.0 * u[v][n]
                    else:
                        total = acc_ref[at(v, n, other, q)]
                    total = total - flux[v]
                    if jumps[v][n] is not None:
                        total = total + jumps[v][n]
                    acc_ref[at(v, n, other, q)] = total
            return carry

        return step_fn

    low = c_low()
    flag = jnp.where(low, lroll(flag_ref[2], 1), flag_ref[2]) != 0
    damp_z = damp
    coef = [
        [jnp.where(low, float(D4[2 * p, c]), float(D4[2 * p + 1, c ^ 1])).astype(F32) for c in range(4)]
        for p in range(2)
    ]

    def step_z(j, carry):
        a0, b = j // 4, j % 4
        here = (a0, 3 - a0)
        u = [[[u_ref[v, a, b, q] for q in range(2)] for v in range(5)] for a in here]
        turned = [[[sroll(u[s][v][q], 4) for q in range(2)] for v in range(5)] for s in range(2)]
        beside = []
        for s in range(2):
            line = []
            for v in range(5):
                face = jnp.where(low, turned[s][v][1], turned[s][v][0])
                line.append(jnp.where(low, lroll(face, 1), lroll(face, -1)))
            beside.append(line)
        matrix = jacobian(2)
        for s in range(2):
            waves = [[], []]
            jumps = []
            for v in range(5):
                own = jnp.where(low, u[s][v][0], u[s][v][1])
                jump = jnp.where(flag, beside[1 - s][v], beside[s][v]) - own
                jumps.append(damp_z * jump)
                lifted = H4 * jump
                for p in range(2):
                    w = coef[p][0] * u[s][v][0] + coef[p][1] * turned[s][v][0]
                    w = w + (coef[p][2] * u[s][v][1] + coef[p][3] * turned[s][v][1])
                    w = w - jnp.where(low, lifted, 0.0) if p == 0 else w + jnp.where(low, 0.0, lifted)
                    waves[p].append(w)
            for p in range(2):
                flux = mix(matrix, waves[p])
                for v in range(5):
                    part = jnp.where(low, jumps[v], 0.0) if p == 0 else jnp.where(low, 0.0, jumps[v])
                    acc_ref[v, here[s], b, p] = acc_ref[v, here[s], b, p] - flux[v] + part
        return carry

    lax.fori_loop(0, 8, along(1), 0)
    lax.fori_loop(0, 8, step_z, 0)
    lax.fori_loop(0, 8, along(0), 0)


def first_volume_kernel(
    src_ref, smooth_ref, u_ref, flag_ref, jac_ref, damp_ref, acc_ref, jac8_ref, damp8_ref, face_ref, second_ref
):
    prepare_tables(jac_ref, damp_ref, jac8_ref, damp8_ref, face_ref)
    volume(src_ref, u_ref, flag_ref, jac8_ref, damp8_ref, acc_ref)
    for a in (1, 2):
        for b in (1, 2):
            change = smoothed(smooth_ref, [[acc_ref[v, a, b, q] for q in range(2)] for v in range(5)], a, b)
            for v in range(5):
                for q in range(2):
                    second_ref[v, a, b, q] = u_ref[v, a, b, q] + change[v][q]


def remote_parts(even_refs, odd_refs, flag_ref, face_ref, part_ref):
    for d, axis in ((0, "gx"), (1, "gy")):
        is_even = parity(axis)
        low, step = axis_low(d)
        flag = flag_ref[d]
        flag = jnp.where(low, sroll(flag, -step), flag) != 0
        even, odd = even_refs[d], odd_refs[d]
        matrix = [[face_ref[2 * d, 5 * o + i] for i in range(5)] for o in range(5)]
        for n in range(4):
            take = lambda v, m: jnp.where(is_even, even[v, m], odd[v, m])
            right = [jnp.where(flag, take(v, 3 - n), take(v, n)) for v in range(5)]
            for v, value in enumerate(mix(matrix, right)):
                part_ref[2 * d, v, n, 0] = jnp.where(low, 0.0, -sroll(value, step))
                part_ref[2 * d, v, n, 1] = jnp.where(low, 0.0, -value)
        matrix = [[face_ref[2 * d + 1, 5 * o + i] for i in range(5)] for o in range(5)]
        for n in range(4):
            left = [jnp.where(is_even, odd[v, n], even[v, n]) for v in range(5)]
            for v, value in enumerate(mix(matrix, left)):
                part_ref[2 * d + 1, v, n, 0] = jnp.where(low, value, 0.0)
                part_ref[2 * d + 1, v, n, 1] = jnp.where(low, sroll(value, -step), 0.0)


def whole(acc_ref, part_ref, v, a, b, q):
    total = acc_ref[v, a, b, q]
    if a == 3:
        total = total + part_ref[0, v, b, q]
    if a == 0:
        total = total + part_ref[1, v, b, q]
    if b == 3:
        total = total + part_ref[2, v, a, q]
    if b == 0:
        total = total + part_ref[3, v, a, q]
    return total


def second_kernel(
    acc_ref, u_ref, smooth_ref, flag_ref, face_ref, rxo, rxe, ryo, rye, inner_ref, out_ref, xo, xe, yo, ye, part_ref
):
    remote_parts((rxe, rye), (rxo, ryo), flag_ref, face_ref, part_ref)
    for a in range(4):
        for b in range(4):
            if a in (1, 2) and b in (1, 2):
                continue
            left = [[whole(acc_ref, part_ref, v, a, b, q) for q in range(2)] for v in range(5)]
            change = smoothed(smooth_ref, left, a, b)
            for v in range(5):
                for q in range(2):
                    out_ref[v, a, b, q] = u_ref[v, a, b, q] + change[v][q]
    restricted_faces(out_ref, flag_ref, xo, xe, yo, ye)


def coarse_smooth(smooth_ref, fields):
    out = [[[None, None], [None, None]] for _ in range(5)]
    for i in range(2):
        for o in range(5):
            total = [None, None]
            for k in range(5):
                block = smooth_ref[5 * o + k, i].astype(F32)
                for j in range(2):
                    term = block[8 * j : 8 * j + 8] * fields[k][i][j]
                    total[j] = term if k == 0 else total[j] + term
            for j in range(2):
                out[o][i][j] = OMEGA * total[j]
    return out


def coarse_faces(field, flag_ref, xo, xe, yo, ye):
    for v in range(5):
        c = field[v]
        lows = [[c[0][0], c[0][1]], [c[0][0], c[1][0]]]
        highs = [[c[1][0], c[1][1]], [c[0][1], c[1][1]]]
        put_coarse_faces(v, lows, highs, flag_ref, ((xe, xo), (ye, yo)))


def restricted_volume_kernel(src_ref, u_ref, flag_ref, jac_ref, damp_ref, acc_ref):
    damp = H4 * damp_ref[...]
    low_c = c_low()
    slope = [
        jnp.where(low_c, float(PD[0, c]), float(PD[1, c ^ 1])).astype(F32) for c in range(4)
    ]
    flags = [flag_ref[0] != 0, flag_ref[1] != 0, jnp.where(low_c, lroll(flag_ref[2], 1), flag_ref[2]) != 0]
    sign = jnp.where(low_c, -H4, H4).astype(F32)
    waves = [[[[None] * 5 for _ in range(2)] for _ in range(2)] for _ in range(3)]

    def slopes_four(values):
        return [sum_of([(float(PD[i, n]), values[n]) for n in range(4)]) for i in range(2)]

    for v in range(5):
        line, slope_c, ends = {}, {}, {}
        for a in range(4):
            for b in range(4):
                first, second = u_ref[v, a, b, 0], u_ref[v, a, b, 1]
                line[a, b] = restrict_c(first, second)
                slope_c[a, b] = (slope[0] * first + slope[1] * sroll(first, 4)) + (
                    slope[2] * second + slope[3] * sroll(second, 4)
                )
                ends[a, b] = jnp.where(low_c, first, second)

        def along_b(table):
            return [restrict_four([table[a, b] for b in range(4)]) for a in range(4)]

        def both(table):
            by_b = along_b(table)
            return [restrict_four([by_b[a][j] for a in range(4)]) for j in range(2)]

        by_b = along_b(line)
        by_a = [restrict_four([line[a, b] for a in range(4)]) for b in range(4)]
        flux_z = both(slope_c)
        trace_z = both(ends)
        sources = both({(a, b): restrict_c(src_ref[v, a, b, 0], src_ref[v, a, b, 1]) for a in range(4) for b in range(4)})
        acc = [[None, None], [None, None]]
        for j in range(2):
            value = restrict_four([by_b[a][j] for a in range(4)])
            flux = slopes_four([by_b[a][j] for a in range(4)])
            for i in range(2):
                acc[i][j] = sources[j][i] - 2.0 * value[i]
                waves[0][i][j][v] = flux[i]
        for i in range(2):
            flux = slopes_four([by_a[b][i] for b in range(4)])
            for j in range(2):
                waves[1][i][j][v] = flux[j]
        for d, lo, hi in ((0, by_b[0], by_b[3]), (1, by_a[0], by_a[3])):
            low, step = axis_low(d)
            flag = flags[d]
            flag_before = sroll(flag_ref[d], step) != 0
            for m in range(2):
                right = sroll(jnp.where(flag_before, lo[1 - m], lo[m]), -step)
                left = sroll(jnp.where(flag, hi[1 - m], hi[m]), step)
                jump_right = jnp.where(low, right, 0.0) - hi[m]
                jump_left = jnp.where(low, 0.0, left) - lo[m]
                i, j = (1, m) if d == 0 else (m, 1)
                waves[d][i][j][v] = waves[d][i][j][v] + H4 * jump_right
                acc[i][j] = acc[i][j] + damp * jump_right
                i, j = (0, m) if d == 0 else (m, 0)
                waves[d][i][j][v] = waves[d][i][j][v] - H4 * jump_left
                acc[i][j] = acc[i][j] + damp * jump_left
        beside = []
        for j in range(2):
            turned = [sroll(trace_z[j][i], 4) for i in range(2)]
            beside.append([jnp.where(low_c, lroll(t, 1), lroll(t, -1)) for t in turned])
        for i in range(2):
            for j in range(2):
                jump = jnp.where(flags[2], beside[j][1 - i], beside[j][i]) - trace_z[j][i]
                waves[2][i][j][v] = flux_z[j][i] + sign * jump
                acc_ref[v, i, j] = acc[i][j] + damp * jump
    for d in range(3):
        matrix = [[jac_ref[25 * d + 5 * o + i] for i in range(5)] for o in range(5)]
        for i in range(2):
            for j in range(2):
                for v, value in enumerate(mix(matrix, waves[d][i][j])):
                    acc_ref[v, i, j] = acc_ref[v, i, j] - value


def add_remote(field, scale, flag_ref, face_ref, rxo, rxe, ryo, rye):
    for d, axis in ((0, "gx"), (1, "gy")):
        is_even = parity(axis)
        low, step = axis_low(d)
        flag = flag_ref[d]
        flag = jnp.where(low, sroll(flag, -step), flag) != 0
        even, odd = ((rxe, rxo), (rye, ryo))[d]
        at = (lambda n, m: (n, m)) if d == 0 else (lambda n, m: (m, n))
        right, left = [], []
        for v in range(5):
            value = scale * jnp.where(is_even, even[v], odd[v])
            swapped = jnp.where(low, sroll(value, -step), sroll(value, step))
            right.append(jnp.where(flag, swapped, value))
            left.append(scale * jnp.where(is_even, odd[v], even[v]))
        upper = [[face_ref[2 * d, 5 * o + i] for i in range(5)] for o in range(5)]
        lower = [[face_ref[2 * d + 1, 5 * o + i] for i in range(5)] for o in range(5)]
        for v, value in enumerate(mix(upper, right)):
            for m, part in enumerate((sroll(value, step), value)):
                i, j = at(1, m)
                field[v][i][j] = field[v][i][j] - jnp.where(low, 0.0, part)
        for v, value in enumerate(mix(lower, left)):
            for m, part in enumerate((value, sroll(value, -step))):
                i, j = at(0, m)
                field[v][i][j] = field[v][i][j] + jnp.where(low, part, 0.0)


def restrict_kernel(
    acc_ref, flag_ref, face_ref, smooth_ref, rxo, rxe, ryo, rye, rhs_ref, c_ref, xo, xe, yo, ye
):
    rhs = [[[acc_ref[v, i, j] for j in range(2)] for i in range(2)] for v in range(5)]
    add_remote(rhs, 1.0, flag_ref, face_ref, rxo, rxe, ryo, rye)
    c = coarse_smooth(smooth_ref, rhs)
    for v in range(5):
        for i in range(2):
            for j in range(2):
                rhs_ref[v, i, j] = rhs[v][i][j]
                c_ref[v, i, j] = c[v][i][j]
    coarse_faces(c, flag_ref, xo, xe, yo, ye)


def coarse_local_kernel(c_ref, rhs_ref, smooth_ref, flag_ref, jac_ref, damp_ref, out_ref):
    damp = 0.5 * damp_ref[...]
    c = [[[c_ref[v, i, j] for j in range(2)] for i in range(2)] for v in range(5)]
    acc = [[[rhs_ref[v, i, j] - 2.0 * c[v][i][j] for j in range(2)] for i in range(2)] for v in range(5)]
    for d in range(2):
        low, step = axis_low(d)
        flag = flag_ref[d] != 0
        flag_before = sroll(flag_ref[d], step) != 0
        matrix = [[jac_ref[25 * d + 5 * o + i] for i in range(5)] for o in range(5)]
        at = (lambda n, m: (n, m)) if d == 0 else (lambda n, m: (m, n))
        waves = [[[None] * 5, [None] * 5] for _ in range(2)]
        for v in range(5):
            lo = [c[v][at(0, m)[0]][at(0, m)[1]] for m in range(2)]
            hi = [c[v][at(1, m)[0]][at(1, m)[1]] for m in range(2)]
            for m in range(2):
                right = jnp.where(low, sroll(jnp.where(flag_before, lo[1 - m], lo[m]), -step), 0.0)
                left = jnp.where(low, 0.0, sroll(jnp.where(flag, hi[1 - m], hi[m]), step))
                waves[1][m][v] = 0.5 * (right - lo[m])
                waves[0][m][v] = 0.5 * (hi[m] - left)
                i, j = at(1, m)
                acc[v][i][j] = acc[v][i][j] + damp * (right - hi[m])
                i, j = at(0, m)
                acc[v][i][j] = acc[v][i][j] + damp * (left - lo[m])
        for n in range(2):
            for m in range(2):
                i, j = at(n, m)
                for v, value in enumerate(mix(matrix, waves[n][m])):
                    acc[v][i][j] = acc[v][i][j] - value
    low = c_low()
    flag = jnp.where(low, lroll(flag_ref[2], 1), flag_ref[2]) != 0
    half = jnp.where(low, 0.5, -0.5).astype(F32)
    matrix = [[jac_ref[50 + 5 * o + i] for i in range(5)] for o in range(5)]
    turned = [[[sroll(c[v][i][j], 4) for j in range(2)] for i in range(2)] for v in range(5)]
    beside = [
        [[jnp.where(low, lroll(t, 1), lroll(t, -1)) for t in turned[v][i]] for i in range(2)] for v in range(5)
    ]
    for i in range(2):
        for j in range(2):
            wave = []
            for v in range(5):
                next_to = jnp.where(flag, beside[v][1 - i][j], beside[v][i][j])
                wave.append(half * (turned[v][i][j] - next_to))
                acc[v][i][j] = acc[v][i][j] + damp * (next_to - c[v][i][j])
            for v, value in enumerate(mix(matrix, wave)):
                acc[v][i][j] = acc[v][i][j] - value
    change = coarse_smooth(smooth_ref, acc)
    for v in range(5):
        for i in range(2):
            for j in range(2):
                out_ref[v, i, j] = c[v][i][j] + change[v][i][j]


def coarse_step(c_ref, smooth_ref, flag_ref, face_ref, rxo, rxe, ryo, rye):
    rest = [[[0.0, 0.0], [0.0, 0.0]] for _ in range(5)]
    add_remote(rest, 1.0 / 6.0, flag_ref, face_ref, rxo, rxe, ryo, rye)
    change = coarse_smooth(smooth_ref, rest)
    return [[[c_ref[v, i, j] + change[v][i][j] for j in range(2)] for i in range(2)] for v in range(5)]


def coarse_kernel(c_ref, smooth_ref, flag_ref, face_ref, rxo, rxe, ryo, rye, out_ref, xo, xe, yo, ye):
    c = coarse_step(c_ref, smooth_ref, flag_ref, face_ref, rxo, rxe, ryo, rye)
    for v in range(5):
        for i in range(2):
            for j in range(2):
                out_ref[v, i, j] = c[v][i][j]
    coarse_faces(c, flag_ref, xo, xe, yo, ye)


def spread(first, second):
    return first, NEAR * first + FAR * second, FAR * first + NEAR * second, second


def last_kernel(
    c_ref, smooth_ref, flag_ref, face_ref, rxo, rxe, ryo, rye, second_ref, out_hbm, out_ref, sems
):
    c = coarse_step(c_ref, smooth_ref, flag_ref, face_ref, rxo, rxe, ryo, rye)
    low = c_low()
    copies = []
    for v in range(5):
        by_c = [[None, None], [None, None]]
        for i in range(2):
            for j in range(2):
                value = c[v][i][j]
                inner = FAR * value + NEAR * sroll(value, 4)
                by_c[i][j] = (jnp.where(low, value, inner), jnp.where(low, inner, value))
        for q in range(2):
            lines = [spread(by_c[i][0][q], by_c[i][1][q]) for i in range(2)]
            for b in range(4):
                for a, value in enumerate(spread(lines[0][b], lines[1][b])):
                    out_ref[v, a, b, q] = second_ref[v, a, b, q] + value
        copy = pltpu.make_async_copy(out_ref.at[v], out_hbm.at[v], sems.at[v])
        copy.start()
        copies.append(copy)
    for copy in copies:
        copy.wait()


FINE = (5, 4, 4, 2, 8, 128)
FINE_MESSAGE = (5, 4, 8, 128)
COARSE = (5, 2, 2, 8, 128)
COARSE_MESSAGE = (5, 8, 128)


def vmem(shape, dtype=F32):
    return pltpu.VMEM(shape, dtype)


def here(array):
    return pltpu.with_memory_space_constraint(array, pltpu.VMEM)


def call(kernel, args, outs, in_hbm=(), out_hbm=(), scratch=(), aliases=None, flops=0):
    in_specs = [
        pl.BlockSpec(memory_space=pltpu.HBM if k in in_hbm else pltpu.VMEM) for k in range(len(args))
    ]
    out_specs = [
        pl.BlockSpec(memory_space=pltpu.HBM if k in out_hbm else pltpu.VMEM) for k in range(len(outs))
    ]
    args = [pltpu.with_memory_space_constraint(a, pltpu.HBM) if k in in_hbm else here(a) for k, a in enumerate(args)]
    return pl.pallas_call(
        kernel,
        out_shape=outs,
        in_specs=in_specs,
        out_specs=out_specs,
        scratch_shapes=scratch,
        input_output_aliases=aliases or {},
        compiler_params=pltpu.CompilerParams(vmem_limit_bytes=8 * 2**20),
        cost_estimate=pl.CostEstimate(flops=flops, bytes_accessed=4 * 2**20, transcendentals=0),
    )(*args)


def partners(axis):
    size = lax.axis_size(axis)
    even = [(i, i ^ 1) for i in range(size)]
    odd = [(i, (i - 1) % size if i % 2 == 0 else (i + 1) % size) for i in range(size)]
    return even, odd


def exchange(xo, xe, yo, ye):
    even_x, odd_x = partners("gx")
    even_y, odd_y = partners("gy")
    xo = lax.ppermute(xo, "gx", odd_x)
    xe = lax.ppermute(xe, "gx", even_x)
    yo = lax.ppermute(yo, "gy", odd_y)
    ye = lax.ppermute(ye, "gy", even_y)
    return xo, xe, yo, ye


def local_sweep(coarse, *rest):
    (out,) = call(coarse_local_kernel, (coarse, *rest), [vmem(COARSE)], flops=4 * 2**20)
    return out


def body(source, jacobian, damping, orient, smoother, coarse_smoother):
    source = source.reshape(FINE)
    smoother = smoother.reshape(25, 4, 4, 16, 128)
    coarse_smoother = coarse_smoother.reshape(25, 2, 16, 128)
    jacobian = jacobian.reshape(75, 4, 128)
    damping = damping.reshape(4, 128)
    orient = orient.reshape(3, 4, 128)
    fine_messages = [vmem(FINE_MESSAGE)] * 4
    coarse_messages = [vmem(COARSE_MESSAGE)] * 4

    source, smoother, first, flag, *sent = call(
        first_kernel,
        (source, smoother, orient),
        [vmem(FINE), vmem(smoother.shape, smoother.dtype), vmem(FINE), vmem((3, 8, 128), jnp.int32)] + fine_messages,
        in_hbm=(0, 1, 2),
        scratch=[
            pltpu.SemaphoreType.DMA((5,)),
            pltpu.SemaphoreType.DMA((25,)),
            pltpu.VMEM((3, 4, 128), jnp.int32),
            pltpu.SemaphoreType.DMA,
        ],
        flops=2 * 25 * 64 * 512,
    )
    got = exchange(*sent)
    acc, jac8, damp8, face, second = call(
        first_volume_kernel,
        (source, smoother, first, flag, jacobian, damping),
        [vmem(FINE), vmem((75, 8, 128)), vmem((8, 128)), vmem((4, 25, 8, 128)), vmem(FINE)],
        flops=9 * 2**20,
    )
    second, *sent = call(
        second_kernel,
        (acc, first, smoother, flag, face, *got, second),
        [vmem(FINE)] + coarse_messages,
        aliases={9: 0},
        scratch=[pltpu.VMEM((4, 5, 4, 2, 8, 128), F32)],
        flops=3 * 2**20,
    )
    got = exchange(*sent)
    (acc,) = call(restricted_volume_kernel, (source, second, flag, jac8, damp8), [vmem(COARSE)], flops=4 * 2**20)
    rhs, coarse, *sent = call(
        restrict_kernel,
        (acc, flag, face, coarse_smoother, *got),
        [vmem(COARSE), vmem(COARSE)] + coarse_messages,
        flops=2**20,
    )
    got = exchange(*sent)
    coarse = local_sweep(coarse, rhs, coarse_smoother, flag, jac8, damp8)
    coarse, *sent = call(
        coarse_kernel,
        (coarse, coarse_smoother, flag, face, *got),
        [vmem(COARSE)] + coarse_messages,
        flops=2**20,
    )
    got = exchange(*sent)
    coarse = local_sweep(coarse, rhs, coarse_smoother, flag, jac8, damp8)
    (out,) = call(
        last_kernel,
        (coarse, coarse_smoother, flag, face, *got, second),
        [jax.ShapeDtypeStruct(FINE, F32)],
        out_hbm=(0,),
        scratch=[pltpu.VMEM(FINE, F32), pltpu.SemaphoreType.DMA((5,))],
        flops=2**20,
    )
    return out.reshape(5, 4, 4, 4, 2, 2, 128)


def solution(mesh):
    in_specs = (
        P(None, None, None, None, "gx", "gy", None),
        P(None, None, None, "gx", "gy", None),
        P("gx", "gy", None),
        P(None, "gx", "gy", None),
        P(None, None, None, None, None, "gx", "gy", None),
        P(None, None, None, None, None, "gx", "gy", None),
    )
    out_specs = P(None, None, None, None, "gx", "gy", None)
    return jax.shard_map(body, mesh=mesh, in_specs=in_specs, out_specs=out_specs, check_vma=False)
```

```python
import functools
import math

import jax
import jax.numpy as jnp
import numpy as np
from jax import lax
from jax.experimental import pallas as pl
from jax.experimental.pallas import tpu as pltpu
from jax.sharding import PartitionSpec as P


F32 = jnp.float32
OMEGA = 0.8
H4 = 3.0
ROOT = 1.0 / math.sqrt(5.0)
NEAR = (1.0 + ROOT) / 2.0
FAR = (1.0 - ROOT) / 2.0


def lobatto_slopes():
    points = np.array([-1.0, -ROOT, ROOT, 1.0])
    weights = np.ones(4)
    for i in range(4):
        for j in range(4):
            if i != j:
                weights[i] = weights[i] / (points[i] - points[j])
    slopes = np.zeros((4, 4))
    for i in range(4):
        for j in range(4):
            if i != j:
                slopes[i, j] = weights[j] / weights[i] / (points[i] - points[j])
        slopes[i, i] = -np.sum(slopes[i])
    return slopes


D4 = lobatto_slopes()
PD = np.array([[1.0, NEAR, FAR, 0.0], [0.0, FAR, NEAR, 1.0]]) @ D4


def sum_of(terms):
    total = None
    for weight, value in terms:
        total = weight * value if total is None else total + weight * value
    return total


def rows():
    return lax.broadcasted_iota(jnp.int32, (8, 128), 0)


def x_low():
    return (rows() & 2) == 0


def y_low():
    return (rows() & 1) == 0


def c_low():
    return (rows() & 4) == 0


def sroll(value, shift):
    return pltpu.roll(value, shift % 8, 0)


def lroll(value, shift):
    return pltpu.roll(value, shift % 128, 1)


def twice(value):
    return jnp.concatenate([value, value], axis=0)


def axis_low(direction):
    return (x_low(), 2) if direction == 0 else (y_low(), 1)


def pack_low(first, second, direction):
    low, step = axis_low(direction)
    return jnp.where(low, first, sroll(second, step))


def pack_high(first, second, direction):
    low, step = axis_low(direction)
    return jnp.where(low, sroll(first, -step), second)


def slopes_along(u0, u1, u2, u3):
    e0, o0, e1, o1 = u0 + u3, u0 - u3, u1 + u2, u1 - u2
    diff = e1 - e0
    even_a = float((D4[0, 1] + D4[0, 2]) / 2.0) * diff
    even_b = float((D4[1, 2] - 0.0) / 2.0) * diff
    odd_a = float((D4[0, 0] - D4[0, 3]) / 2.0) * o0 + float((D4[0, 1] - D4[0, 2]) / 2.0) * o1
    odd_b = float((D4[1, 0] - D4[1, 3]) / 2.0) * o0 - float(D4[1, 2] / 2.0) * o1
    return even_a + odd_a, even_b + odd_b, odd_b - even_b, odd_a - even_a


def mix(matrix, fields):
    out = []
    for o in range(5):
        total = matrix[o][0] * fields[0]
        for i in range(1, 5):
            total = total + matrix[o][i] * fields[i]
        out.append(total)
    return out


def parity(axis):
    return lax.rem(lax.axis_index(axis), 2) == 0


def put_pair(even_ref, odd_ref, index, low_face, high_face, is_even):
    even_ref[index] = jnp.where(is_even, high_face, low_face)
    odd_ref[index] = jnp.where(is_even, low_face, high_face)


def fine_faces(u_ref, flag_ref, xo, xe, yo, ye):
    even_x, even_y = parity("gx"), parity("gy")
    fx, fy = flag_ref[0] != 0, flag_ref[1] != 0
    for v in range(5):
        for n in range(4):
            low = pack_low(u_ref[v, 0, n, 0], u_ref[v, 0, n, 1], 0)
            h = [jnp.where(fx, u_ref[v, 3, 3 - n, q], u_ref[v, 3, n, q]) for q in range(2)]
            put_pair(xe, xo, (v, n), low, pack_high(h[0], h[1], 0), even_x)
            low = pack_low(u_ref[v, n, 0, 0], u_ref[v, n, 0, 1], 1)
            h = [jnp.where(fy, u_ref[v, 3 - n, 3, q], u_ref[v, n, 3, q]) for q in range(2)]
            put_pair(ye, yo, (v, n), low, pack_high(h[0], h[1], 1), even_y)


def restrict_c(first, second):
    low = c_low()
    middle = jnp.where(low, second, first)
    return jnp.where(low, first, second) + FAR * middle + NEAR * sroll(middle, 4)


def restrict_four(values):
    return values[0] + NEAR * values[1] + FAR * values[2], values[3] + NEAR * values[2] + FAR * values[1]


def put_coarse_faces(v, lows, highs, flag_ref, pairs):
    for d, axis in ((0, "gx"), (1, "gy")):
        flag = flag_ref[d] != 0
        low, high = lows[d], highs[d]
        turned = [jnp.where(flag, high[1 - m], high[m]) for m in range(2)]
        even_ref, odd_ref = pairs[d]
        put_pair(even_ref, odd_ref, v, pack_low(*low, d), pack_high(*turned, d), parity(axis))


def restricted_faces(u_ref, flag_ref, xo, xe, yo, ye):
    for v in range(5):
        line = {}
        for a in range(4):
            for b in range(4):
                if a in (0, 3) or b in (0, 3):
                    line[a, b] = restrict_c(u_ref[v, a, b, 0], u_ref[v, a, b, 1])
        lows = [restrict_four([line[0, n] for n in range(4)]), restrict_four([line[n, 0] for n in range(4)])]
        highs = [restrict_four([line[3, n] for n in range(4)]), restrict_four([line[n, 3] for n in range(4)])]
        put_coarse_faces(v, lows, highs, flag_ref, ((xe, xo), (ye, yo)))


def smoothed(smooth_ref, fields, a, b):
    out = []
    for o in range(5):
        total = [None, None]
        for i in range(5):
            block = smooth_ref[5 * o + i, a, b].astype(F32)
            for q in range(2):
                term = block[8 * q : 8 * q + 8] * fields[i][q]
                total[q] = term if i == 0 else total[q] + term
        out.append([OMEGA * total[q] for q in range(2)])
    return out


def first_line(src_ref, smooth_ref, u_ref, a, b):
    value = smoothed(smooth_ref, [[src_ref[v, a, b, q] for q in range(2)] for v in range(5)], a, b)
    for v in range(5):
        for q in range(2):
            u_ref[v, a, b, q] = value[v][q]


def line_copy(smooth_hbm, smooth_ref, sem, a, b):
    return pltpu.make_async_copy(smooth_hbm.at[:, a, b], smooth_ref.at[:, a, b], sem)


def first_kernel(
    src_hbm, smooth_hbm, orient_hbm, src_ref, smooth_ref, u_ref, flag_ref, xo, xe, yo, ye, sems, orient_ref, orient_sem
):
    every, inner = slice(0, 4), slice(1, 3)
    src_copy = pltpu.make_async_copy(src_hbm, src_ref, sems.at[4])
    src_copy.start()
    copies = [
        line_copy(smooth_hbm, smooth_ref, sems.at[slot], a, b)
        for slot, (a, b) in enumerate(((0, every), (3, every), (inner, 0), (inner, 3)))
    ]
    for one in copies:
        one.start()
    orient_copy = pltpu.make_async_copy(orient_hbm, orient_ref, orient_sem)
    orient_copy.start()
    orient_copy.wait()
    for d in range(3):
        flag_ref[d] = twice(orient_ref[d])
    lines = [[(0, b) for b in range(4)], [(3, b) for b in range(4)], [(1, 0), (2, 0)], [(1, 3), (2, 3)]]
    src_copy.wait()
    for one, group in zip(copies, lines):
        one.wait()
        for a, b in group:
            first_line(src_ref, smooth_ref, u_ref, a, b)
    fine_faces(u_ref, flag_ref, xo, xe, yo, ye)


def prepare_tables(jac_ref, damp_ref, jac8_ref, damp8_ref, face_ref):
    damp = twice(damp_ref[...])
    damp8_ref[...] = damp
    for d in range(3):
        for k in range(25):
            value = twice(jac_ref[25 * d + k])
            jac8_ref[25 * d + k] = value
            if d < 2:
                low, step = axis_low(d)
                diagonal = k % 6 == 0
                upper = H4 * (value - damp if diagonal else value)
                lower = H4 * (value + damp if diagonal else value)
                face_ref[2 * d, k] = jnp.where(low, sroll(upper, -step), upper)
                face_ref[2 * d + 1, k] = jnp.where(low, lower, sroll(lower, step))


def volume(src_ref, u_ref, flag_ref, jac_ref, damp_ref, acc_ref, finish_lines):
    damp = H4 * damp_ref[...]

    def jacobian(d):
        return [[jac_ref[25 * d + 5 * o + i] for i in range(5)] for o in range(5)]

    def along(direction, others):
        low, step = axis_low(direction)
        flag = flag_ref[direction] != 0
        flag_before = sroll(flag_ref[direction], step) != 0

        def at(v, n, other, q):
            return (v, n, other, q) if direction == 0 else (v, other, n, q)

        def step_fn(j, carry):
            other, q = others(j // 2), j % 2
            u = [[u_ref[at(v, n, other, q)] for n in range(4)] for v in range(5)]
            waves = []
            jumps = []
            for v in range(5):
                back_low, back_high = u_ref[at(v, 0, 3 - other, q)], u_ref[at(v, 3, 3 - other, q)]
                right = sroll(jnp.where(flag_before, back_low, u[v][0]), -step)
                left = sroll(jnp.where(flag, back_high, u[v][3]), step)
                jump_right = jnp.where(low, right, 0.0) - u[v][3]
                jump_left = jnp.where(low, 0.0, left) - u[v][0]
                w = list(slopes_along(*u[v]))
                w[3] = w[3] + H4 * jump_right
                w[0] = w[0] - H4 * jump_left
                waves.append(w)
                jumps.append((damp * jump_left, None, None, damp * jump_right))
            matrix = jacobian(direction)
            for n in range(4):
                flux = mix(matrix, [waves[v][n] for v in range(5)])
                for v in range(5):
                    if direction == 1:
                        total = src_ref[at(v, n, other, q)] - 2.0 * u[v][n]
                    else:
                        total = acc_ref[at(v, n, other, q)]
                    total = total - flux[v]
                    if jumps[v][n] is not None:
                        total = total + jumps[v][n]
                    acc_ref[at(v, n, other, q)] = total
            return carry

        return step_fn

    low = c_low()
    flag = jnp.where(low, lroll(flag_ref[2], 1), flag_ref[2]) != 0
    damp_z = damp
    coef = [
        [jnp.where(low, float(D4[2 * p, c]), float(D4[2 * p + 1, c ^ 1])).astype(F32) for c in range(4)]
        for p in range(2)
    ]

    def step_z(j, carry):
        a0, b = j // 4, j % 4
        here = (a0, 3 - a0)
        u = [[[u_ref[v, a, b, q] for q in range(2)] for v in range(5)] for a in here]
        turned = [[[sroll(u[s][v][q], 4) for q in range(2)] for v in range(5)] for s in range(2)]
        beside = []
        for s in range(2):
            line = []
            for v in range(5):
                face = jnp.where(low, turned[s][v][1], turned[s][v][0])
                line.append(jnp.where(low, lroll(face, 1), lroll(face, -1)))
            beside.append(line)
        matrix = jacobian(2)
        for s in range(2):
            waves = [[], []]
            jumps = []
            for v in range(5):
                own = jnp.where(low, u[s][v][0], u[s][v][1])
                jump = jnp.where(flag, beside[1 - s][v], beside[s][v]) - own
                jumps.append(damp_z * jump)
                lifted = H4 * jump
                for p in range(2):
                    w = coef[p][0] * u[s][v][0] + coef[p][1] * turned[s][v][0]
                    w = w + (coef[p][2] * u[s][v][1] + coef[p][3] * turned[s][v][1])
                    w = w - jnp.where(low, lifted, 0.0) if p == 0 else w + jnp.where(low, 0.0, lifted)
                    waves[p].append(w)
            for p in range(2):
                flux = mix(matrix, waves[p])
                for v in range(5):
                    part = jnp.where(low, jumps[v], 0.0) if p == 0 else jnp.where(low, 0.0, jumps[v])
                    acc_ref[v, here[s], b, p] = acc_ref[v, here[s], b, p] - flux[v] + part
        return carry

    lax.fori_loop(0, 4, along(1, lambda k: 3 * k), 0)
    lax.fori_loop(0, 4, step_z, 0)
    finish_lines()
    lax.fori_loop(0, 4, along(1, lambda k: 1 + k), 0)
    lax.fori_loop(4, 8, step_z, 0)
    lax.fori_loop(0, 8, along(0, lambda k: k), 0)


def first_volume_kernel(
    smooth_hbm, src_ref, smooth_in, u_in, flag_ref, jac_ref, damp_ref,
    smooth_ref, u_ref, acc_ref, jac8_ref, damp8_ref, face_ref, second_ref, sem,
):
    inner = slice(1, 3)
    copy = line_copy(smooth_hbm, smooth_ref, sem, inner, inner)
    copy.start()
    prepare_tables(jac_ref, damp_ref, jac8_ref, damp8_ref, face_ref)
    lines = [(a, b) for a in (1, 2) for b in (1, 2)]

    def finish_lines():
        copy.wait()
        for a, b in lines:
            first_line(src_ref, smooth_ref, u_ref, a, b)

    volume(src_ref, u_ref, flag_ref, jac8_ref, damp8_ref, acc_ref, finish_lines)
    for a, b in lines:
        change = smoothed(smooth_ref, [[acc_ref[v, a, b, q] for q in range(2)] for v in range(5)], a, b)
        for v in range(5):
            for q in range(2):
                second_ref[v, a, b, q] = u_ref[v, a, b, q] + change[v][q]


def remote_parts(even_refs, odd_refs, flag_ref, face_ref, part_ref):
    for d, axis in ((0, "gx"), (1, "gy")):
        is_even = parity(axis)
        low, step = axis_low(d)
        flag = flag_ref[d]
        flag = jnp.where(low, sroll(flag, -step), flag) != 0
        even, odd = even_refs[d], odd_refs[d]
        matrix = [[face_ref[2 * d, 5 * o + i] for i in range(5)] for o in range(5)]
        for n in range(4):
            take = lambda v, m: jnp.where(is_even, even[v, m], odd[v, m])
            right = [jnp.where(flag, take(v, 3 - n), take(v, n)) for v in range(5)]
            for v, value in enumerate(mix(matrix, right)):
                part_ref[2 * d, v, n, 0] = jnp.where(low, 0.0, -sroll(value, step))
                part_ref[2 * d, v, n, 1] = jnp.where(low, 0.0, -value)
        matrix = [[face_ref[2 * d + 1, 5 * o + i] for i in range(5)] for o in range(5)]
        for n in range(4):
            left = [jnp.where(is_even, odd[v, n], even[v, n]) for v in range(5)]
            for v, value in enumerate(mix(matrix, left)):
                part_ref[2 * d + 1, v, n, 0] = jnp.where(low, value, 0.0)
                part_ref[2 * d + 1, v, n, 1] = jnp.where(low, sroll(value, -step), 0.0)


def whole(acc_ref, part_ref, v, a, b, q):
    total = acc_ref[v, a, b, q]
    if a == 3:
        total = total + part_ref[0, v, b, q]
    if a == 0:
        total = total + part_ref[1, v, b, q]
    if b == 3:
        total = total + part_ref[2, v, a, q]
    if b == 0:
        total = total + part_ref[3, v, a, q]
    return total


def second_kernel(
    acc_ref, u_ref, smooth_ref, flag_ref, face_ref, rxo, rxe, ryo, rye, inner_ref, out_ref, xo, xe, yo, ye, part_ref
):
    remote_parts((rxe, rye), (rxo, ryo), flag_ref, face_ref, part_ref)
    for a in range(4):
        for b in range(4):
            if a in (1, 2) and b in (1, 2):
                continue
            left = [[whole(acc_ref, part_ref, v, a, b, q) for q in range(2)] for v in range(5)]
            change = smoothed(smooth_ref, left, a, b)
            for v in range(5):
                for q in range(2):
                    out_ref[v, a, b, q] = u_ref[v, a, b, q] + change[v][q]
    restricted_faces(out_ref, flag_ref, xo, xe, yo, ye)


def coarse_smooth(smooth_ref, fields):
    out = [[[None, None], [None, None]] for _ in range(5)]
    for i in range(2):
        for o in range(5):
            total = [None, None]
            for k in range(5):
                block = smooth_ref[5 * o + k, i].astype(F32)
                for j in range(2):
                    term = block[8 * j : 8 * j + 8] * fields[k][i][j]
                    total[j] = term if k == 0 else total[j] + term
            for j in range(2):
                out[o][i][j] = OMEGA * total[j]
    return out


def coarse_faces(field, flag_ref, xo, xe, yo, ye):
    for v in range(5):
        c = field[v]
        lows = [[c[0][0], c[0][1]], [c[0][0], c[1][0]]]
        highs = [[c[1][0], c[1][1]], [c[0][1], c[1][1]]]
        put_coarse_faces(v, lows, highs, flag_ref, ((xe, xo), (ye, yo)))


def restricted_volume_kernel(src_ref, u_ref, flag_ref, jac_ref, damp_ref, acc_ref):
    damp = H4 * damp_ref[...]
    low_c = c_low()
    slope = [
        jnp.where(low_c, float(PD[0, c]), float(PD[1, c ^ 1])).astype(F32) for c in range(4)
    ]
    flags = [flag_ref[0] != 0, flag_ref[1] != 0, jnp.where(low_c, lroll(flag_ref[2], 1), flag_ref[2]) != 0]
    sign = jnp.where(low_c, -H4, H4).astype(F32)
    waves = [[[[None] * 5 for _ in range(2)] for _ in range(2)] for _ in range(3)]

    def slopes_four(values):
        return [sum_of([(float(PD[i, n]), values[n]) for n in range(4)]) for i in range(2)]

    for v in range(5):
        line, slope_c, ends = {}, {}, {}
        for a in range(4):
            for b in range(4):
                first, second = u_ref[v, a, b, 0], u_ref[v, a, b, 1]
                line[a, b] = restrict_c(first, second)
                slope_c[a, b] = (slope[0] * first + slope[1] * sroll(first, 4)) + (
                    slope[2] * second + slope[3] * sroll(second, 4)
                )
                ends[a, b] = jnp.where(low_c, first, second)

        def along_b(table):
            return [restrict_four([table[a, b] for b in range(4)]) for a in range(4)]

        def both(table):
            by_b = along_b(table)
            return [restrict_four([by_b[a][j] for a in range(4)]) for j in range(2)]

        by_b = along_b(line)
        by_a = [restrict_four([line[a, b] for a in range(4)]) for b in range(4)]
        flux_z = both(slope_c)
        trace_z = both(ends)
        sources = both({(a, b): restrict_c(src_ref[v, a, b, 0], src_ref[v, a, b, 1]) for a in range(4) for b in range(4)})
        acc = [[None, None], [None, None]]
        for j in range(2):
            value = restrict_four([by_b[a][j] for a in range(4)])
            flux = slopes_four([by_b[a][j] for a in range(4)])
            for i in range(2):
                acc[i][j] = sources[j][i] - 2.0 * value[i]
                waves[0][i][j][v] = flux[i]
        for i in range(2):
            flux = slopes_four([by_a[b][i] for b in range(4)])
            for j in range(2):
                waves[1][i][j][v] = flux[j]
        for d, lo, hi in ((0, by_b[0], by_b[3]), (1, by_a[0], by_a[3])):
            low, step = axis_low(d)
            flag = flags[d]
            flag_before = sroll(flag_ref[d], step) != 0
            for m in range(2):
                right = sroll(jnp.where(flag_before, lo[1 - m], lo[m]), -step)
                left = sroll(jnp.where(flag, hi[1 - m], hi[m]), step)
                jump_right = jnp.where(low, right, 0.0) - hi[m]
                jump_left = jnp.where(low, 0.0, left) - lo[m]
                i, j = (1, m) if d == 0 else (m, 1)
                waves[d][i][j][v] = waves[d][i][j][v] + H4 * jump_right
                acc[i][j] = acc[i][j] + damp * jump_right
                i, j = (0, m) if d == 0 else (m, 0)
                waves[d][i][j][v] = waves[d][i][j][v] - H4 * jump_left
                acc[i][j] = acc[i][j] + damp * jump_left
        beside = []
        for j in range(2):
            turned = [sroll(trace_z[j][i], 4) for i in range(2)]
            beside.append([jnp.where(low_c, lroll(t, 1), lroll(t, -1)) for t in turned])
        for i in range(2):
            for j in range(2):
                jump = jnp.where(flags[2], beside[j][1 - i], beside[j][i]) - trace_z[j][i]
                waves[2][i][j][v] = flux_z[j][i] + sign * jump
                acc_ref[v, i, j] = acc[i][j] + damp * jump
    for d in range(3):
        matrix = [[jac_ref[25 * d + 5 * o + i] for i in range(5)] for o in range(5)]
        for i in range(2):
            for j in range(2):
                for v, value in enumerate(mix(matrix, waves[d][i][j])):
                    acc_ref[v, i, j] = acc_ref[v, i, j] - value


def add_remote(field, scale, flag_ref, face_ref, rxo, rxe, ryo, rye):
    for d, axis in ((0, "gx"), (1, "gy")):
        is_even = parity(axis)
        low, step = axis_low(d)
        flag = flag_ref[d]
        flag = jnp.where(low, sroll(flag, -step), flag) != 0
        even, odd = ((rxe, rxo), (rye, ryo))[d]
        at = (lambda n, m: (n, m)) if d == 0 else (lambda n, m: (m, n))
        right, left = [], []
        for v in range(5):
            value = scale * jnp.where(is_even, even[v], odd[v])
            swapped = jnp.where(low, sroll(value, -step), sroll(value, step))
            right.append(jnp.where(flag, swapped, value))
            left.append(scale * jnp.where(is_even, odd[v], even[v]))
        upper = [[face_ref[2 * d, 5 * o + i] for i in range(5)] for o in range(5)]
        lower = [[face_ref[2 * d + 1, 5 * o + i] for i in range(5)] for o in range(5)]
        for v, value in enumerate(mix(upper, right)):
            for m, part in enumerate((sroll(value, step), value)):
                i, j = at(1, m)
                field[v][i][j] = field[v][i][j] - jnp.where(low, 0.0, part)
        for v, value in enumerate(mix(lower, left)):
            for m, part in enumerate((value, sroll(value, -step))):
                i, j = at(0, m)
                field[v][i][j] = field[v][i][j] + jnp.where(low, part, 0.0)


def restrict_kernel(
    acc_ref, flag_ref, face_ref, smooth_ref, rxo, rxe, ryo, rye, rhs_ref, c_ref, xo, xe, yo, ye
):
    rhs = [[[acc_ref[v, i, j] for j in range(2)] for i in range(2)] for v in range(5)]
    add_remote(rhs, 1.0, flag_ref, face_ref, rxo, rxe, ryo, rye)
    c = coarse_smooth(smooth_ref, rhs)
    for v in range(5):
        for i in range(2):
            for j in range(2):
                rhs_ref[v, i, j] = rhs[v][i][j]
                c_ref[v, i, j] = c[v][i][j]
    coarse_faces(c, flag_ref, xo, xe, yo, ye)


def coarse_local_kernel(c_ref, rhs_ref, smooth_ref, flag_ref, jac_ref, damp_ref, out_ref):
    damp = 0.5 * damp_ref[...]
    c = [[[c_ref[v, i, j] for j in range(2)] for i in range(2)] for v in range(5)]
    acc = [[[rhs_ref[v, i, j] - 2.0 * c[v][i][j] for j in range(2)] for i in range(2)] for v in range(5)]
    for d in range(2):
        low, step = axis_low(d)
        flag = flag_ref[d] != 0
        flag_before = sroll(flag_ref[d], step) != 0
        matrix = [[jac_ref[25 * d + 5 * o + i] for i in range(5)] for o in range(5)]
        at = (lambda n, m: (n, m)) if d == 0 else (lambda n, m: (m, n))
        waves = [[[None] * 5, [None] * 5] for _ in range(2)]
        for v in range(5):
            lo = [c[v][at(0, m)[0]][at(0, m)[1]] for m in range(2)]
            hi = [c[v][at(1, m)[0]][at(1, m)[1]] for m in range(2)]
            for m in range(2):
                right = jnp.where(low, sroll(jnp.where(flag_before, lo[1 - m], lo[m]), -step), 0.0)
                left = jnp.where(low, 0.0, sroll(jnp.where(flag, hi[1 - m], hi[m]), step))
                waves[1][m][v] = 0.5 * (right - lo[m])
                waves[0][m][v] = 0.5 * (hi[m] - left)
                i, j = at(1, m)
                acc[v][i][j] = acc[v][i][j] + damp * (right - hi[m])
                i, j = at(0, m)
                acc[v][i][j] = acc[v][i][j] + damp * (left - lo[m])
        for n in range(2):
            for m in range(2):
                i, j = at(n, m)
                for v, value in enumerate(mix(matrix, waves[n][m])):
                    acc[v][i][j] = acc[v][i][j] - value
    low = c_low()
    flag = jnp.where(low, lroll(flag_ref[2], 1), flag_ref[2]) != 0
    half = jnp.where(low, 0.5, -0.5).astype(F32)
    matrix = [[jac_ref[50 + 5 * o + i] for i in range(5)] for o in range(5)]
    turned = [[[sroll(c[v][i][j], 4) for j in range(2)] for i in range(2)] for v in range(5)]
    beside = [
        [[jnp.where(low, lroll(t, 1), lroll(t, -1)) for t in turned[v][i]] for i in range(2)] for v in range(5)
    ]
    for i in range(2):
        for j in range(2):
            wave = []
            for v in range(5):
                next_to = jnp.where(flag, beside[v][1 - i][j], beside[v][i][j])
                wave.append(half * (turned[v][i][j] - next_to))
                acc[v][i][j] = acc[v][i][j] + damp * (next_to - c[v][i][j])
            for v, value in enumerate(mix(matrix, wave)):
                acc[v][i][j] = acc[v][i][j] - value
    change = coarse_smooth(smooth_ref, acc)
    for v in range(5):
        for i in range(2):
            for j in range(2):
                out_ref[v, i, j] = c[v][i][j] + change[v][i][j]


def coarse_step(c_ref, smooth_ref, flag_ref, face_ref, rxo, rxe, ryo, rye):
    rest = [[[0.0, 0.0], [0.0, 0.0]] for _ in range(5)]
    add_remote(rest, 1.0 / 6.0, flag_ref, face_ref, rxo, rxe, ryo, rye)
    change = coarse_smooth(smooth_ref, rest)
    return [[[c_ref[v, i, j] + change[v][i][j] for j in range(2)] for i in range(2)] for v in range(5)]


def coarse_kernel(c_ref, smooth_ref, flag_ref, face_ref, rxo, rxe, ryo, rye, out_ref, xo, xe, yo, ye):
    c = coarse_step(c_ref, smooth_ref, flag_ref, face_ref, rxo, rxe, ryo, rye)
    for v in range(5):
        for i in range(2):
            for j in range(2):
                out_ref[v, i, j] = c[v][i][j]
    coarse_faces(c, flag_ref, xo, xe, yo, ye)


def spread(first, second):
    return first, NEAR * first + FAR * second, FAR * first + NEAR * second, second


def last_kernel(
    c_ref, smooth_ref, flag_ref, face_ref, rxo, rxe, ryo, rye, second_ref, out_hbm, out_ref, sems
):
    c = coarse_step(c_ref, smooth_ref, flag_ref, face_ref, rxo, rxe, ryo, rye)
    low = c_low()
    copies = []
    for v in range(5):
        by_c = [[None, None], [None, None]]
        for i in range(2):
            for j in range(2):
                value = c[v][i][j]
                inner = FAR * value + NEAR * sroll(value, 4)
                by_c[i][j] = (jnp.where(low, value, inner), jnp.where(low, inner, value))
        for q in range(2):
            lines = [spread(by_c[i][0][q], by_c[i][1][q]) for i in range(2)]
            for b in range(4):
                for a, value in enumerate(spread(lines[0][b], lines[1][b])):
                    out_ref[v, a, b, q] = second_ref[v, a, b, q] + value
        copy = pltpu.make_async_copy(out_ref.at[v], out_hbm.at[v], sems.at[v])
        copy.start()
        copies.append(copy)
    for copy in copies:
        copy.wait()


FINE = (5, 4, 4, 2, 8, 128)
FINE_MESSAGE = (5, 4, 8, 128)
COARSE = (5, 2, 2, 8, 128)
COARSE_MESSAGE = (5, 8, 128)


def vmem(shape, dtype=F32):
    return pltpu.VMEM(shape, dtype)


def here(array):
    return pltpu.with_memory_space_constraint(array, pltpu.VMEM)


def call(kernel, args, outs, in_hbm=(), out_hbm=(), scratch=(), aliases=None, flops=0):
    in_specs = [
        pl.BlockSpec(memory_space=pltpu.HBM if k in in_hbm else pltpu.VMEM) for k in range(len(args))
    ]
    out_specs = [
        pl.BlockSpec(memory_space=pltpu.HBM if k in out_hbm else pltpu.VMEM) for k in range(len(outs))
    ]
    args = [pltpu.with_memory_space_constraint(a, pltpu.HBM) if k in in_hbm else here(a) for k, a in enumerate(args)]
    return pl.pallas_call(
        kernel,
        out_shape=outs,
        in_specs=in_specs,
        out_specs=out_specs,
        scratch_shapes=scratch,
        input_output_aliases=aliases or {},
        compiler_params=pltpu.CompilerParams(vmem_limit_bytes=8 * 2**20),
        cost_estimate=pl.CostEstimate(flops=flops, bytes_accessed=4 * 2**20, transcendentals=0),
    )(*args)


def partners(axis):
    size = lax.axis_size(axis)
    even = [(i, i ^ 1) for i in range(size)]
    odd = [(i, (i - 1) % size if i % 2 == 0 else (i + 1) % size) for i in range(size)]
    return even, odd


def exchange(xo, xe, yo, ye):
    even_x, odd_x = partners("gx")
    even_y, odd_y = partners("gy")
    xo = lax.ppermute(xo, "gx", odd_x)
    xe = lax.ppermute(xe, "gx", even_x)
    yo = lax.ppermute(yo, "gy", odd_y)
    ye = lax.ppermute(ye, "gy", even_y)
    return xo, xe, yo, ye


def local_sweep(coarse, *rest):
    (out,) = call(coarse_local_kernel, (coarse, *rest), [vmem(COARSE)], flops=4 * 2**20)
    return out


def body(source, jacobian, damping, orient, smoother, coarse_smoother):
    source = source.reshape(FINE)
    smoother = smoother.reshape(25, 4, 4, 16, 128)
    coarse_smoother = coarse_smoother.reshape(25, 2, 16, 128)
    jacobian = jacobian.reshape(75, 4, 128)
    damping = damping.reshape(4, 128)
    orient = orient.reshape(3, 4, 128)
    fine_messages = [vmem(FINE_MESSAGE)] * 4
    coarse_messages = [vmem(COARSE_MESSAGE)] * 4

    held = vmem(smoother.shape, smoother.dtype)
    smoother_in = smoother
    source, smoother, first, flag, *sent = call(
        first_kernel,
        (source, smoother_in, orient),
        [vmem(FINE), held, vmem(FINE), vmem((3, 8, 128), jnp.int32)] + fine_messages,
        in_hbm=(0, 1, 2),
        scratch=[pltpu.SemaphoreType.DMA((5,)), pltpu.VMEM((3, 4, 128), jnp.int32), pltpu.SemaphoreType.DMA],
        flops=2 * 25 * 64 * 512,
    )
    got = exchange(*sent)
    smoother, first, acc, jac8, damp8, face, second = call(
        first_volume_kernel,
        (smoother_in, source, smoother, first, flag, jacobian, damping),
        [held, vmem(FINE), vmem(FINE), vmem((75, 8, 128)), vmem((8, 128)), vmem((4, 25, 8, 128)), vmem(FINE)],
        in_hbm=(0,),
        aliases={2: 0, 3: 1},
        scratch=[pltpu.SemaphoreType.DMA],
        flops=9 * 2**20,
    )
    second, *sent = call(
        second_kernel,
        (acc, first, smoother, flag, face, *got, second),
        [vmem(FINE)] + coarse_messages,
        aliases={9: 0},
        scratch=[pltpu.VMEM((4, 5, 4, 2, 8, 128), F32)],
        flops=3 * 2**20,
    )
    got = exchange(*sent)
    (acc,) = call(restricted_volume_kernel, (source, second, flag, jac8, damp8), [vmem(COARSE)], flops=4 * 2**20)
    rhs, coarse, *sent = call(
        restrict_kernel,
        (acc, flag, face, coarse_smoother, *got),
        [vmem(COARSE), vmem(COARSE)] + coarse_messages,
        flops=2**20,
    )
    got = exchange(*sent)
    coarse = local_sweep(coarse, rhs, coarse_smoother, flag, jac8, damp8)
    coarse, *sent = call(
        coarse_kernel,
        (coarse, coarse_smoother, flag, face, *got),
        [vmem(COARSE)] + coarse_messages,
        flops=2**20,
    )
    got = exchange(*sent)
    coarse = local_sweep(coarse, rhs, coarse_smoother, flag, jac8, damp8)
    (out,) = call(
        last_kernel,
        (coarse, coarse_smoother, flag, face, *got, second),
        [jax.ShapeDtypeStruct(FINE, F32)],
        out_hbm=(0,),
        scratch=[pltpu.VMEM(FINE, F32), pltpu.SemaphoreType.DMA((5,))],
        flops=2**20,
    )
    return out.reshape(5, 4, 4, 4, 2, 2, 128)


def solution(mesh):
    in_specs = (
        P(None, None, None, None, "gx", "gy", None),
        P(None, None, None, "gx", "gy", None),
        P("gx", "gy", None),
        P(None, "gx", "gy", None),
        P(None, None, None, None, None, "gx", "gy", None),
        P(None, None, None, None, None, "gx", "gy", None),
    )
    out_specs = P(None, None, None, None, "gx", "gy", None)
    return jax.shard_map(body, mesh=mesh, in_specs=in_specs, out_specs=out_specs, check_vma=False)
```

```python
import functools
import math

import jax
import jax.numpy as jnp
import numpy as np
from jax import lax
from jax.experimental import pallas as pl
from jax.experimental.pallas import tpu as pltpu
from jax.sharding import PartitionSpec as P


F32 = jnp.float32
OMEGA = 0.8
H4 = 3.0
ROOT = 1.0 / math.sqrt(5.0)
NEAR = (1.0 + ROOT) / 2.0
FAR = (1.0 - ROOT) / 2.0


def lobatto_slopes():
    points = np.array([-1.0, -ROOT, ROOT, 1.0])
    weights = np.ones(4)
    for i in range(4):
        for j in range(4):
            if i != j:
                weights[i] = weights[i] / (points[i] - points[j])
    slopes = np.zeros((4, 4))
    for i in range(4):
        for j in range(4):
            if i != j:
                slopes[i, j] = weights[j] / weights[i] / (points[i] - points[j])
        slopes[i, i] = -np.sum(slopes[i])
    return slopes


D4 = lobatto_slopes()
PD = np.array([[1.0, NEAR, FAR, 0.0], [0.0, FAR, NEAR, 1.0]]) @ D4


def sum_of(terms):
    total = None
    for weight, value in terms:
        total = weight * value if total is None else total + weight * value
    return total


def rows():
    return lax.broadcasted_iota(jnp.int32, (8, 128), 0)


def x_low():
    return (rows() & 2) == 0


def y_low():
    return (rows() & 1) == 0


def c_low():
    return (rows() & 4) == 0


def sroll(value, shift):
    return pltpu.roll(value, shift % 8, 0)


def lroll(value, shift):
    return pltpu.roll(value, shift % 128, 1)


def twice(value):
    return jnp.concatenate([value, value], axis=0)


def axis_low(direction):
    return (x_low(), 2) if direction == 0 else (y_low(), 1)


def pack_low(first, second, direction):
    low, step = axis_low(direction)
    return jnp.where(low, first, sroll(second, step))


def pack_high(first, second, direction):
    low, step = axis_low(direction)
    return jnp.where(low, sroll(first, -step), second)


def slopes_along(u0, u1, u2, u3):
    e0, o0, e1, o1 = u0 + u3, u0 - u3, u1 + u2, u1 - u2
    diff = e1 - e0
    even_a = float((D4[0, 1] + D4[0, 2]) / 2.0) * diff
    even_b = float((D4[1, 2] - 0.0) / 2.0) * diff
    odd_a = float((D4[0, 0] - D4[0, 3]) / 2.0) * o0 + float((D4[0, 1] - D4[0, 2]) / 2.0) * o1
    odd_b = float((D4[1, 0] - D4[1, 3]) / 2.0) * o0 - float(D4[1, 2] / 2.0) * o1
    return even_a + odd_a, even_b + odd_b, odd_b - even_b, odd_a - even_a


def mix(matrix, fields):
    out = []
    for o in range(5):
        total = matrix[o][0] * fields[0]
        for i in range(1, 5):
            total = total + matrix[o][i] * fields[i]
        out.append(total)
    return out


def parity(axis):
    return lax.rem(lax.axis_index(axis), 2) == 0


def put_pair(even_ref, odd_ref, index, low_face, high_face, is_even):
    even_ref[index] = jnp.where(is_even, high_face, low_face)
    odd_ref[index] = jnp.where(is_even, low_face, high_face)


def fine_faces(u_ref, flag_ref, xo, xe, yo, ye):
    even_x, even_y = parity("gx"), parity("gy")
    fx, fy = flag_ref[0] != 0, flag_ref[1] != 0
    for v in range(5):
        for n in range(4):
            low = pack_low(u_ref[v, 0, n, 0], u_ref[v, 0, n, 1], 0)
            h = [jnp.where(fx, u_ref[v, 3, 3 - n, q], u_ref[v, 3, n, q]) for q in range(2)]
            put_pair(xe, xo, (v, n), low, pack_high(h[0], h[1], 0), even_x)
            low = pack_low(u_ref[v, n, 0, 0], u_ref[v, n, 0, 1], 1)
            h = [jnp.where(fy, u_ref[v, 3 - n, 3, q], u_ref[v, n, 3, q]) for q in range(2)]
            put_pair(ye, yo, (v, n), low, pack_high(h[0], h[1], 1), even_y)


def restrict_c(first, second):
    low = c_low()
    middle = jnp.where(low, second, first)
    return jnp.where(low, first, second) + FAR * middle + NEAR * sroll(middle, 4)


def restrict_four(values):
    return values[0] + NEAR * values[1] + FAR * values[2], values[3] + NEAR * values[2] + FAR * values[1]


def put_coarse_faces(v, lows, highs, flag_ref, pairs):
    for d, axis in ((0, "gx"), (1, "gy")):
        flag = flag_ref[d] != 0
        low, high = lows[d], highs[d]
        turned = [jnp.where(flag, high[1 - m], high[m]) for m in range(2)]
        even_ref, odd_ref = pairs[d]
        put_pair(even_ref, odd_ref, v, pack_low(*low, d), pack_high(*turned, d), parity(axis))


def restricted_faces(u_ref, flag_ref, xo, xe, yo, ye):
    for v in range(5):
        line = {}
        for a in range(4):
            for b in range(4):
                if a in (0, 3) or b in (0, 3):
                    line[a, b] = restrict_c(u_ref[v, a, b, 0], u_ref[v, a, b, 1])
        lows = [restrict_four([line[0, n] for n in range(4)]), restrict_four([line[n, 0] for n in range(4)])]
        highs = [restrict_four([line[3, n] for n in range(4)]), restrict_four([line[n, 3] for n in range(4)])]
        put_coarse_faces(v, lows, highs, flag_ref, ((xe, xo), (ye, yo)))


def smoothed(smooth_ref, fields, a, b):
    out = []
    for o in range(5):
        total = [None, None]
        for i in range(5):
            block = smooth_ref[5 * o + i, a, b].astype(F32)
            for q in range(2):
                term = block[8 * q : 8 * q + 8] * fields[i][q]
                total[q] = term if i == 0 else total[q] + term
        out.append([OMEGA * total[q] for q in range(2)])
    return out


def first_line(src_ref, smooth_ref, u_ref, a, b):
    value = smoothed(smooth_ref, [[src_ref[v, a, b, q] for q in range(2)] for v in range(5)], a, b)
    for v in range(5):
        for q in range(2):
            u_ref[v, a, b, q] = value[v][q]


def line_copy(smooth_hbm, smooth_ref, sem, a, b):
    return pltpu.make_async_copy(smooth_hbm.at[:, a, b], smooth_ref.at[:, a, b], sem)


def first_kernel(
    src_hbm, smooth_hbm, orient_hbm, src_ref, smooth_ref, u_ref, flag_ref, xo, yo, xe, ye, sems, orient_ref, orient_sem
):
    every, inner = slice(0, 4), slice(1, 3)
    src_copy = pltpu.make_async_copy(src_hbm, src_ref, sems.at[4])
    src_copy.start()
    copies = [
        line_copy(smooth_hbm, smooth_ref, sems.at[slot], a, b)
        for slot, (a, b) in enumerate(((0, every), (3, every), (inner, 0), (inner, 3)))
    ]
    for one in copies:
        one.start()
    orient_copy = pltpu.make_async_copy(orient_hbm, orient_ref, orient_sem)
    orient_copy.start()
    orient_copy.wait()
    for d in range(3):
        flag_ref[d] = twice(orient_ref[d])
    lines = [[(0, b) for b in range(4)], [(3, b) for b in range(4)], [(1, 0), (2, 0)], [(1, 3), (2, 3)]]
    src_copy.wait()
    for one, group in zip(copies, lines):
        one.wait()
        for a, b in group:
            first_line(src_ref, smooth_ref, u_ref, a, b)
    fine_faces(u_ref, flag_ref, xo, xe, yo, ye)


def prepare_tables(jac_ref, damp_ref, jac8_ref, damp8_ref, face_ref):
    damp = twice(damp_ref[...])
    damp8_ref[...] = damp
    for d in range(3):
        for k in range(25):
            value = twice(jac_ref[25 * d + k])
            jac8_ref[25 * d + k] = value
            if d < 2:
                low, step = axis_low(d)
                diagonal = k % 6 == 0
                upper = H4 * (value - damp if diagonal else value)
                lower = H4 * (value + damp if diagonal else value)
                face_ref[2 * d, k] = jnp.where(low, sroll(upper, -step), upper)
                face_ref[2 * d + 1, k] = jnp.where(low, lower, sroll(lower, step))


def volume(src_ref, u_ref, flag_ref, jac_ref, damp_ref, acc_ref, finish_lines):
    damp = H4 * damp_ref[...]

    def jacobian(d):
        return [[jac_ref[25 * d + 5 * o + i] for i in range(5)] for o in range(5)]

    def along(direction, others):
        low, step = axis_low(direction)
        flag = flag_ref[direction] != 0
        flag_before = sroll(flag_ref[direction], step) != 0

        def at(v, n, other, q):
            return (v, n, other, q) if direction == 0 else (v, other, n, q)

        def step_fn(j, carry):
            other, q = others(j // 2), j % 2
            u = [[u_ref[at(v, n, other, q)] for n in range(4)] for v in range(5)]
            waves = []
            jumps = []
            for v in range(5):
                back_low, back_high = u_ref[at(v, 0, 3 - other, q)], u_ref[at(v, 3, 3 - other, q)]
                right = sroll(jnp.where(flag_before, back_low, u[v][0]), -step)
                left = sroll(jnp.where(flag, back_high, u[v][3]), step)
                jump_right = jnp.where(low, right, 0.0) - u[v][3]
                jump_left = jnp.where(low, 0.0, left) - u[v][0]
                w = list(slopes_along(*u[v]))
                w[3] = w[3] + H4 * jump_right
                w[0] = w[0] - H4 * jump_left
                waves.append(w)
                jumps.append((damp * jump_left, None, None, damp * jump_right))
            matrix = jacobian(direction)
            for n in range(4):
                flux = mix(matrix, [waves[v][n] for v in range(5)])
                for v in range(5):
                    if direction == 1:
                        total = src_ref[at(v, n, other, q)] - 2.0 * u[v][n]
                    else:
                        total = acc_ref[at(v, n, other, q)]
                    total = total - flux[v]
                    if jumps[v][n] is not None:
                        total = total + jumps[v][n]
                    acc_ref[at(v, n, other, q)] = total
            return carry

        return step_fn

    low = c_low()
    flag = jnp.where(low, lroll(flag_ref[2], 1), flag_ref[2]) != 0
    damp_z = damp
    coef = [
        [jnp.where(low, float(D4[2 * p, c]), float(D4[2 * p + 1, c ^ 1])).astype(F32) for c in range(4)]
        for p in range(2)
    ]

    def step_z(j, carry):
        a0, b = j // 4, j % 4
        here = (a0, 3 - a0)
        u = [[[u_ref[v, a, b, q] for q in range(2)] for v in range(5)] for a in here]
        turned = [[[sroll(u[s][v][q], 4) for q in range(2)] for v in range(5)] for s in range(2)]
        beside = []
        for s in range(2):
            line = []
            for v in range(5):
                face = jnp.where(low, turned[s][v][1], turned[s][v][0])
                line.append(jnp.where(low, lroll(face, 1), lroll(face, -1)))
            beside.append(line)
        matrix = jacobian(2)
        for s in range(2):
            waves = [[], []]
            jumps = []
            for v in range(5):
                own = jnp.where(low, u[s][v][0], u[s][v][1])
                jump = jnp.where(flag, beside[1 - s][v], beside[s][v]) - own
                jumps.append(damp_z * jump)
                lifted = H4 * jump
                for p in range(2):
                    w = coef[p][0] * u[s][v][0] + coef[p][1] * turned[s][v][0]
                    w = w + (coef[p][2] * u[s][v][1] + coef[p][3] * turned[s][v][1])
                    w = w - jnp.where(low, lifted, 0.0) if p == 0 else w + jnp.where(low, 0.0, lifted)
                    waves[p].append(w)
            for p in range(2):
                flux = mix(matrix, waves[p])
                for v in range(5):
                    part = jnp.where(low, jumps[v], 0.0) if p == 0 else jnp.where(low, 0.0, jumps[v])
                    acc_ref[v, here[s], b, p] = acc_ref[v, here[s], b, p] - flux[v] + part
        return carry

    lax.fori_loop(0, 4, along(1, lambda k: 3 * k), 0)
    lax.fori_loop(0, 4, step_z, 0)
    finish_lines()
    lax.fori_loop(0, 4, along(1, lambda k: 1 + k), 0)
    lax.fori_loop(4, 8, step_z, 0)
    lax.fori_loop(0, 8, along(0, lambda k: k), 0)


def first_volume_kernel(
    smooth_hbm, src_ref, smooth_in, u_in, flag_ref, jac_ref, damp_ref,
    smooth_ref, u_ref, acc_ref, jac8_ref, damp8_ref, face_ref, second_ref, sem,
):
    inner = slice(1, 3)
    copy = line_copy(smooth_hbm, smooth_ref, sem, inner, inner)
    copy.start()
    prepare_tables(jac_ref, damp_ref, jac8_ref, damp8_ref, face_ref)
    lines = [(a, b) for a in (1, 2) for b in (1, 2)]

    def finish_lines():
        copy.wait()
        for a, b in lines:
            first_line(src_ref, smooth_ref, u_ref, a, b)

    volume(src_ref, u_ref, flag_ref, jac8_ref, damp8_ref, acc_ref, finish_lines)
    for a, b in lines:
        change = smoothed(smooth_ref, [[acc_ref[v, a, b, q] for q in range(2)] for v in range(5)], a, b)
        for v in range(5):
            for q in range(2):
                second_ref[v, a, b, q] = u_ref[v, a, b, q] + change[v][q]


def remote_parts(even_refs, odd_refs, flag_ref, face_ref, part_ref):
    for d, axis in ((0, "gx"), (1, "gy")):
        is_even = parity(axis)
        low, step = axis_low(d)
        flag = flag_ref[d]
        flag = jnp.where(low, sroll(flag, -step), flag) != 0
        even, odd = even_refs[d], odd_refs[d]
        matrix = [[face_ref[2 * d, 5 * o + i] for i in range(5)] for o in range(5)]
        for n in range(4):
            take = lambda v, m: jnp.where(is_even, even[v, m], odd[v, m])
            right = [jnp.where(flag, take(v, 3 - n), take(v, n)) for v in range(5)]
            for v, value in enumerate(mix(matrix, right)):
                part_ref[2 * d, v, n, 0] = jnp.where(low, 0.0, -sroll(value, step))
                part_ref[2 * d, v, n, 1] = jnp.where(low, 0.0, -value)
        matrix = [[face_ref[2 * d + 1, 5 * o + i] for i in range(5)] for o in range(5)]
        for n in range(4):
            left = [jnp.where(is_even, odd[v, n], even[v, n]) for v in range(5)]
            for v, value in enumerate(mix(matrix, left)):
                part_ref[2 * d + 1, v, n, 0] = jnp.where(low, value, 0.0)
                part_ref[2 * d + 1, v, n, 1] = jnp.where(low, sroll(value, -step), 0.0)


def whole(acc_ref, part_ref, v, a, b, q):
    total = acc_ref[v, a, b, q]
    if a == 3:
        total = total + part_ref[0, v, b, q]
    if a == 0:
        total = total + part_ref[1, v, b, q]
    if b == 3:
        total = total + part_ref[2, v, a, q]
    if b == 0:
        total = total + part_ref[3, v, a, q]
    return total


def second_kernel(
    acc_ref, u_ref, smooth_ref, flag_ref, face_ref, rxo, rxe, ryo, rye, inner_ref, out_ref, xo, xe, yo, ye, part_ref
):
    remote_parts((rxe, rye), (rxo, ryo), flag_ref, face_ref, part_ref)
    for a in range(4):
        for b in range(4):
            if a in (1, 2) and b in (1, 2):
                continue
            left = [[whole(acc_ref, part_ref, v, a, b, q) for q in range(2)] for v in range(5)]
            change = smoothed(smooth_ref, left, a, b)
            for v in range(5):
                for q in range(2):
                    out_ref[v, a, b, q] = u_ref[v, a, b, q] + change[v][q]
    restricted_faces(out_ref, flag_ref, xo, xe, yo, ye)


def coarse_smooth(smooth_ref, fields):
    out = [[[None, None], [None, None]] for _ in range(5)]
    for i in range(2):
        for o in range(5):
            total = [None, None]
            for k in range(5):
                block = smooth_ref[5 * o + k, i].astype(F32)
                for j in range(2):
                    term = block[8 * j : 8 * j + 8] * fields[k][i][j]
                    total[j] = term if k == 0 else total[j] + term
            for j in range(2):
                out[o][i][j] = OMEGA * total[j]
    return out


def coarse_faces(field, flag_ref, xo, xe, yo, ye):
    for v in range(5):
        c = field[v]
        lows = [[c[0][0], c[0][1]], [c[0][0], c[1][0]]]
        highs = [[c[1][0], c[1][1]], [c[0][1], c[1][1]]]
        put_coarse_faces(v, lows, highs, flag_ref, ((xe, xo), (ye, yo)))


def restricted_volume_kernel(src_ref, u_ref, flag_ref, jac_ref, damp_ref, acc_ref):
    damp = H4 * damp_ref[...]
    low_c = c_low()
    slope = [
        jnp.where(low_c, float(PD[0, c]), float(PD[1, c ^ 1])).astype(F32) for c in range(4)
    ]
    flags = [flag_ref[0] != 0, flag_ref[1] != 0, jnp.where(low_c, lroll(flag_ref[2], 1), flag_ref[2]) != 0]
    sign = jnp.where(low_c, -H4, H4).astype(F32)
    waves = [[[[None] * 5 for _ in range(2)] for _ in range(2)] for _ in range(3)]

    def slopes_four(values):
        return [sum_of([(float(PD[i, n]), values[n]) for n in range(4)]) for i in range(2)]

    for v in range(5):
        line, slope_c, ends = {}, {}, {}
        for a in range(4):
            for b in range(4):
                first, second = u_ref[v, a, b, 0], u_ref[v, a, b, 1]
                line[a, b] = restrict_c(first, second)
                slope_c[a, b] = (slope[0] * first + slope[1] * sroll(first, 4)) + (
                    slope[2] * second + slope[3] * sroll(second, 4)
                )
                ends[a, b] = jnp.where(low_c, first, second)

        def along_b(table):
            return [restrict_four([table[a, b] for b in range(4)]) for a in range(4)]

        def both(table):
            by_b = along_b(table)
            return [restrict_four([by_b[a][j] for a in range(4)]) for j in range(2)]

        by_b = along_b(line)
        by_a = [restrict_four([line[a, b] for a in range(4)]) for b in range(4)]
        flux_z = both(slope_c)
        trace_z = both(ends)
        sources = both({(a, b): restrict_c(src_ref[v, a, b, 0], src_ref[v, a, b, 1]) for a in range(4) for b in range(4)})
        acc = [[None, None], [None, None]]
        for j in range(2):
            value = restrict_four([by_b[a][j] for a in range(4)])
            flux = slopes_four([by_b[a][j] for a in range(4)])
            for i in range(2):
                acc[i][j] = sources[j][i] - 2.0 * value[i]
                waves[0][i][j][v] = flux[i]
        for i in range(2):
            flux = slopes_four([by_a[b][i] for b in range(4)])
            for j in range(2):
                waves[1][i][j][v] = flux[j]
        for d, lo, hi in ((0, by_b[0], by_b[3]), (1, by_a[0], by_a[3])):
            low, step = axis_low(d)
            flag = flags[d]
            flag_before = sroll(flag_ref[d], step) != 0
            for m in range(2):
                right = sroll(jnp.where(flag_before, lo[1 - m], lo[m]), -step)
                left = sroll(jnp.where(flag, hi[1 - m], hi[m]), step)
                jump_right = jnp.where(low, right, 0.0) - hi[m]
                jump_left = jnp.where(low, 0.0, left) - lo[m]
                i, j = (1, m) if d == 0 else (m, 1)
                waves[d][i][j][v] = waves[d][i][j][v] + H4 * jump_right
                acc[i][j] = acc[i][j] + damp * jump_right
                i, j = (0, m) if d == 0 else (m, 0)
                waves[d][i][j][v] = waves[d][i][j][v] - H4 * jump_left
                acc[i][j] = acc[i][j] + damp * jump_left
        beside = []
        for j in range(2):
            turned = [sroll(trace_z[j][i], 4) for i in range(2)]
            beside.append([jnp.where(low_c, lroll(t, 1), lroll(t, -1)) for t in turned])
        for i in range(2):
            for j in range(2):
                jump = jnp.where(flags[2], beside[j][1 - i], beside[j][i]) - trace_z[j][i]
                waves[2][i][j][v] = flux_z[j][i] + sign * jump
                acc_ref[v, i, j] = acc[i][j] + damp * jump
    for d in range(3):
        matrix = [[jac_ref[25 * d + 5 * o + i] for i in range(5)] for o in range(5)]
        for i in range(2):
            for j in range(2):
                for v, value in enumerate(mix(matrix, waves[d][i][j])):
                    acc_ref[v, i, j] = acc_ref[v, i, j] - value


def add_remote(field, scale, flag_ref, face_ref, rxo, rxe, ryo, rye):
    for d, axis in ((0, "gx"), (1, "gy")):
        is_even = parity(axis)
        low, step = axis_low(d)
        flag = flag_ref[d]
        flag = jnp.where(low, sroll(flag, -step), flag) != 0
        even, odd = ((rxe, rxo), (rye, ryo))[d]
        at = (lambda n, m: (n, m)) if d == 0 else (lambda n, m: (m, n))
        right, left = [], []
        for v in range(5):
            value = scale * jnp.where(is_even, even[v], odd[v])
            swapped = jnp.where(low, sroll(value, -step), sroll(value, step))
            right.append(jnp.where(flag, swapped, value))
            left.append(scale * jnp.where(is_even, odd[v], even[v]))
        upper = [[face_ref[2 * d, 5 * o + i] for i in range(5)] for o in range(5)]
        lower = [[face_ref[2 * d + 1, 5 * o + i] for i in range(5)] for o in range(5)]
        for v, value in enumerate(mix(upper, right)):
            for m, part in enumerate((sroll(value, step), value)):
                i, j = at(1, m)
                field[v][i][j] = field[v][i][j] - jnp.where(low, 0.0, part)
        for v, value in enumerate(mix(lower, left)):
            for m, part in enumerate((value, sroll(value, -step))):
                i, j = at(0, m)
                field[v][i][j] = field[v][i][j] + jnp.where(low, part, 0.0)


def restrict_kernel(
    acc_ref, flag_ref, face_ref, smooth_ref, rxo, rxe, ryo, rye, rhs_ref, c_ref, xo, xe, yo, ye
):
    rhs = [[[acc_ref[v, i, j] for j in range(2)] for i in range(2)] for v in range(5)]
    add_remote(rhs, 1.0, flag_ref, face_ref, rxo, rxe, ryo, rye)
    c = coarse_smooth(smooth_ref, rhs)
    for v in range(5):
        for i in range(2):
            for j in range(2):
                rhs_ref[v, i, j] = rhs[v][i][j]
                c_ref[v, i, j] = c[v][i][j]
    coarse_faces(c, flag_ref, xo, xe, yo, ye)


def coarse_local_kernel(c_ref, rhs_ref, smooth_ref, flag_ref, jac_ref, damp_ref, out_ref):
    damp = 0.5 * damp_ref[...]
    c = [[[c_ref[v, i, j] for j in range(2)] for i in range(2)] for v in range(5)]
    acc = [[[rhs_ref[v, i, j] - 2.0 * c[v][i][j] for j in range(2)] for i in range(2)] for v in range(5)]
    for d in range(2):
        low, step = axis_low(d)
        flag = flag_ref[d] != 0
        flag_before = sroll(flag_ref[d], step) != 0
        matrix = [[jac_ref[25 * d + 5 * o + i] for i in range(5)] for o in range(5)]
        at = (lambda n, m: (n, m)) if d == 0 else (lambda n, m: (m, n))
        waves = [[[None] * 5, [None] * 5] for _ in range(2)]
        for v in range(5):
            lo = [c[v][at(0, m)[0]][at(0, m)[1]] for m in range(2)]
            hi = [c[v][at(1, m)[0]][at(1, m)[1]] for m in range(2)]
            for m in range(2):
                right = jnp.where(low, sroll(jnp.where(flag_before, lo[1 - m], lo[m]), -step), 0.0)
                left = jnp.where(low, 0.0, sroll(jnp.where(flag, hi[1 - m], hi[m]), step))
                waves[1][m][v] = 0.5 * (right - lo[m])
                waves[0][m][v] = 0.5 * (hi[m] - left)
                i, j = at(1, m)
                acc[v][i][j] = acc[v][i][j] + damp * (right - hi[m])
                i, j = at(0, m)
                acc[v][i][j] = acc[v][i][j] + damp * (left - lo[m])
        for n in range(2):
            for m in range(2):
                i, j = at(n, m)
                for v, value in enumerate(mix(matrix, waves[n][m])):
                    acc[v][i][j] = acc[v][i][j] - value
    low = c_low()
    flag = jnp.where(low, lroll(flag_ref[2], 1), flag_ref[2]) != 0
    half = jnp.where(low, 0.5, -0.5).astype(F32)
    matrix = [[jac_ref[50 + 5 * o + i] for i in range(5)] for o in range(5)]
    turned = [[[sroll(c[v][i][j], 4) for j in range(2)] for i in range(2)] for v in range(5)]
    beside = [
        [[jnp.where(low, lroll(t, 1), lroll(t, -1)) for t in turned[v][i]] for i in range(2)] for v in range(5)
    ]
    for i in range(2):
        for j in range(2):
            wave = []
            for v in range(5):
                next_to = jnp.where(flag, beside[v][1 - i][j], beside[v][i][j])
                wave.append(half * (turned[v][i][j] - next_to))
                acc[v][i][j] = acc[v][i][j] + damp * (next_to - c[v][i][j])
            for v, value in enumerate(mix(matrix, wave)):
                acc[v][i][j] = acc[v][i][j] - value
    change = coarse_smooth(smooth_ref, acc)
    for v in range(5):
        for i in range(2):
            for j in range(2):
                out_ref[v, i, j] = c[v][i][j] + change[v][i][j]


def coarse_step(c_ref, smooth_ref, flag_ref, face_ref, rxo, rxe, ryo, rye):
    rest = [[[0.0, 0.0], [0.0, 0.0]] for _ in range(5)]
    add_remote(rest, 1.0 / 6.0, flag_ref, face_ref, rxo, rxe, ryo, rye)
    change = coarse_smooth(smooth_ref, rest)
    return [[[c_ref[v, i, j] + change[v][i][j] for j in range(2)] for i in range(2)] for v in range(5)]


def coarse_kernel(c_ref, smooth_ref, flag_ref, face_ref, rxo, rxe, ryo, rye, out_ref, xo, xe, yo, ye):
    c = coarse_step(c_ref, smooth_ref, flag_ref, face_ref, rxo, rxe, ryo, rye)
    for v in range(5):
        for i in range(2):
            for j in range(2):
                out_ref[v, i, j] = c[v][i][j]
    coarse_faces(c, flag_ref, xo, xe, yo, ye)


def spread(first, second):
    return first, NEAR * first + FAR * second, FAR * first + NEAR * second, second


def last_kernel(
    c_ref, smooth_ref, flag_ref, face_ref, rxo, rxe, ryo, rye, second_ref, out_hbm, out_ref, sems
):
    c = coarse_step(c_ref, smooth_ref, flag_ref, face_ref, rxo, rxe, ryo, rye)
    low = c_low()
    copies = []
    for v in range(5):
        by_c = [[None, None], [None, None]]
        for i in range(2):
            for j in range(2):
                value = c[v][i][j]
                inner = FAR * value + NEAR * sroll(value, 4)
                by_c[i][j] = (jnp.where(low, value, inner), jnp.where(low, inner, value))
        for q in range(2):
            lines = [spread(by_c[i][0][q], by_c[i][1][q]) for i in range(2)]
            for b in range(4):
                for a, value in enumerate(spread(lines[0][b], lines[1][b])):
                    out_ref[v, a, b, q] = second_ref[v, a, b, q] + value
        copy = pltpu.make_async_copy(out_ref.at[v], out_hbm.at[v], sems.at[v])
        copy.start()
        copies.append(copy)
    for copy in copies:
        copy.wait()


FINE = (5, 4, 4, 2, 8, 128)
FINE_MESSAGE = (5, 4, 8, 128)
COARSE = (5, 2, 2, 8, 128)
COARSE_MESSAGE = (5, 8, 128)


def vmem(shape, dtype=F32):
    return pltpu.VMEM(shape, dtype)


def here(array):
    return pltpu.with_memory_space_constraint(array, pltpu.VMEM)


def call(kernel, args, outs, in_hbm=(), out_hbm=(), scratch=(), aliases=None, flops=0):
    in_specs = [
        pl.BlockSpec(memory_space=pltpu.HBM if k in in_hbm else pltpu.VMEM) for k in range(len(args))
    ]
    out_specs = [
        pl.BlockSpec(memory_space=pltpu.HBM if k in out_hbm else pltpu.VMEM) for k in range(len(outs))
    ]
    args = [pltpu.with_memory_space_constraint(a, pltpu.HBM) if k in in_hbm else here(a) for k, a in enumerate(args)]
    return pl.pallas_call(
        kernel,
        out_shape=outs,
        in_specs=in_specs,
        out_specs=out_specs,
        scratch_shapes=scratch,
        input_output_aliases=aliases or {},
        compiler_params=pltpu.CompilerParams(vmem_limit_bytes=8 * 2**20),
        cost_estimate=pl.CostEstimate(flops=flops, bytes_accessed=4 * 2**20, transcendentals=0),
    )(*args)


def partners(axis):
    size = lax.axis_size(axis)
    even = [(i, i ^ 1) for i in range(size)]
    odd = [(i, (i - 1) % size if i % 2 == 0 else (i + 1) % size) for i in range(size)]
    return even, odd


def exchange(xo, xe, yo, ye):
    even_x, odd_x = partners("gx")
    even_y, odd_y = partners("gy")
    xo = lax.ppermute(xo, "gx", odd_x)
    xe = lax.ppermute(xe, "gx", even_x)
    yo = lax.ppermute(yo, "gy", odd_y)
    ye = lax.ppermute(ye, "gy", even_y)
    return xo, xe, yo, ye


def local_sweep(coarse, *rest):
    (out,) = call(coarse_local_kernel, (coarse, *rest), [vmem(COARSE)], flops=4 * 2**20)
    return out


def body(source, jacobian, damping, orient, smoother, coarse_smoother):
    source = source.reshape(FINE)
    smoother = smoother.reshape(25, 4, 4, 16, 128)
    coarse_smoother = coarse_smoother.reshape(25, 2, 16, 128)
    jacobian = jacobian.reshape(75, 4, 128)
    damping = damping.reshape(4, 128)
    orient = orient.reshape(3, 4, 128)
    fine_messages = [vmem(FINE_MESSAGE)] * 4
    coarse_messages = [vmem(COARSE_MESSAGE)] * 4

    held = vmem(smoother.shape, smoother.dtype)
    smoother_in = smoother
    source, smoother, first, flag, xo, yo, xe, ye = call(
        first_kernel,
        (source, smoother_in, orient),
        [vmem(FINE), held, vmem(FINE), vmem((3, 8, 128), jnp.int32)] + fine_messages,
        in_hbm=(0, 1, 2),
        scratch=[pltpu.SemaphoreType.DMA((5,)), pltpu.VMEM((3, 4, 128), jnp.int32), pltpu.SemaphoreType.DMA],
        flops=2 * 25 * 64 * 512,
    )
    got = exchange(xo, xe, yo, ye)
    smoother, first, acc, jac8, damp8, face, second = call(
        first_volume_kernel,
        (smoother_in, source, smoother, first, flag, jacobian, damping),
        [held, vmem(FINE), vmem(FINE), vmem((75, 8, 128)), vmem((8, 128)), vmem((4, 25, 8, 128)), vmem(FINE)],
        in_hbm=(0,),
        aliases={2: 0, 3: 1},
        scratch=[pltpu.SemaphoreType.DMA],
        flops=9 * 2**20,
    )
    second, *sent = call(
        second_kernel,
        (acc, first, smoother, flag, face, *got, second),
        [vmem(FINE)] + coarse_messages,
        aliases={9: 0},
        scratch=[pltpu.VMEM((4, 5, 4, 2, 8, 128), F32)],
        flops=3 * 2**20,
    )
    got = exchange(*sent)
    (acc,) = call(restricted_volume_kernel, (source, second, flag, jac8, damp8), [vmem(COARSE)], flops=4 * 2**20)
    rhs, coarse, *sent = call(
        restrict_kernel,
        (acc, flag, face, coarse_smoother, *got),
        [vmem(COARSE), vmem(COARSE)] + coarse_messages,
        flops=2**20,
    )
    got = exchange(*sent)
    coarse = local_sweep(coarse, rhs, coarse_smoother, flag, jac8, damp8)
    coarse, *sent = call(
        coarse_kernel,
        (coarse, coarse_smoother, flag, face, *got),
        [vmem(COARSE)] + coarse_messages,
        flops=2**20,
    )
    got = exchange(*sent)
    coarse = local_sweep(coarse, rhs, coarse_smoother, flag, jac8, damp8)
    (out,) = call(
        last_kernel,
        (coarse, coarse_smoother, flag, face, *got, second),
        [jax.ShapeDtypeStruct(FINE, F32)],
        out_hbm=(0,),
        scratch=[pltpu.VMEM(FINE, F32), pltpu.SemaphoreType.DMA((5,))],
        flops=2**20,
    )
    return out.reshape(5, 4, 4, 4, 2, 2, 128)


def solution(mesh):
    in_specs = (
        P(None, None, None, None, "gx", "gy", None),
        P(None, None, None, "gx", "gy", None),
        P("gx", "gy", None),
        P(None, "gx", "gy", None),
        P(None, None, None, None, None, "gx", "gy", None),
        P(None, None, None, None, None, "gx", "gy", None),
    )
    out_specs = P(None, None, None, None, "gx", "gy", None)
    return jax.shard_map(body, mesh=mesh, in_specs=in_specs, out_specs=out_specs, check_vma=False)
```

```python
import functools
import math

import jax
import jax.numpy as jnp
import numpy as np
from jax import lax
from jax.experimental import pallas as pl
from jax.experimental.pallas import tpu as pltpu
from jax.sharding import PartitionSpec as P


F32 = jnp.float32
OMEGA = 0.8
H4 = 3.0
ROOT = 1.0 / math.sqrt(5.0)
NEAR = (1.0 + ROOT) / 2.0
FAR = (1.0 - ROOT) / 2.0


def lobatto_slopes():
    points = np.array([-1.0, -ROOT, ROOT, 1.0])
    weights = np.ones(4)
    for i in range(4):
        for j in range(4):
            if i != j:
                weights[i] = weights[i] / (points[i] - points[j])
    slopes = np.zeros((4, 4))
    for i in range(4):
        for j in range(4):
            if i != j:
                slopes[i, j] = weights[j] / weights[i] / (points[i] - points[j])
        slopes[i, i] = -np.sum(slopes[i])
    return slopes


D4 = lobatto_slopes()
PD = np.array([[1.0, NEAR, FAR, 0.0], [0.0, FAR, NEAR, 1.0]]) @ D4


def sum_of(terms):
    total = None
    for weight, value in terms:
        total = weight * value if total is None else total + weight * value
    return total


def rows():
    return lax.broadcasted_iota(jnp.int32, (8, 128), 0)


def x_low():
    return (rows() & 2) == 0


def y_low():
    return (rows() & 1) == 0


def c_low():
    return (rows() & 4) == 0


def sroll(value, shift):
    return pltpu.roll(value, shift % 8, 0)


def lroll(value, shift):
    return pltpu.roll(value, shift % 128, 1)


def twice(value):
    return jnp.concatenate([value, value], axis=0)


def axis_low(direction):
    return (x_low(), 2) if direction == 0 else (y_low(), 1)


def pack_low(first, second, direction):
    low, step = axis_low(direction)
    return jnp.where(low, first, sroll(second, step))


def pack_high(first, second, direction):
    low, step = axis_low(direction)
    return jnp.where(low, sroll(first, -step), second)


def slopes_along(u0, u1, u2, u3):
    e0, o0, e1, o1 = u0 + u3, u0 - u3, u1 + u2, u1 - u2
    diff = e1 - e0
    even_a = float((D4[0, 1] + D4[0, 2]) / 2.0) * diff
    even_b = float((D4[1, 2] - 0.0) / 2.0) * diff
    odd_a = float((D4[0, 0] - D4[0, 3]) / 2.0) * o0 + float((D4[0, 1] - D4[0, 2]) / 2.0) * o1
    odd_b = float((D4[1, 0] - D4[1, 3]) / 2.0) * o0 - float(D4[1, 2] / 2.0) * o1
    return even_a + odd_a, even_b + odd_b, odd_b - even_b, odd_a - even_a


def mix(matrix, fields):
    out = []
    for o in range(5):
        total = matrix[o][0] * fields[0]
        for i in range(1, 5):
            total = total + matrix[o][i] * fields[i]
        out.append(total)
    return out


def parity(axis):
    return lax.rem(lax.axis_index(axis), 2) == 0


def put_pair(even_ref, odd_ref, index, low_face, high_face, is_even):
    even_ref[index] = jnp.where(is_even, high_face, low_face)
    odd_ref[index] = jnp.where(is_even, low_face, high_face)


def fine_faces(u_ref, flag_ref, xo, xe, yo, ye):
    even_x, even_y = parity("gx"), parity("gy")
    fx, fy = flag_ref[0] != 0, flag_ref[1] != 0
    for v in range(5):
        for n in range(4):
            low = pack_low(u_ref[v, 0, n, 0], u_ref[v, 0, n, 1], 0)
            h = [jnp.where(fx, u_ref[v, 3, 3 - n, q], u_ref[v, 3, n, q]) for q in range(2)]
            put_pair(xe, xo, (v, n), low, pack_high(h[0], h[1], 0), even_x)
            low = pack_low(u_ref[v, n, 0, 0], u_ref[v, n, 0, 1], 1)
            h = [jnp.where(fy, u_ref[v, 3 - n, 3, q], u_ref[v, n, 3, q]) for q in range(2)]
            put_pair(ye, yo, (v, n), low, pack_high(h[0], h[1], 1), even_y)


def restrict_c(first, second):
    low = c_low()
    middle = jnp.where(low, second, first)
    return jnp.where(low, first, second) + FAR * middle + NEAR * sroll(middle, 4)


def restrict_four(values):
    return values[0] + NEAR * values[1] + FAR * values[2], values[3] + NEAR * values[2] + FAR * values[1]


def put_coarse_faces(v, lows, highs, flag_ref, pairs):
    for d, axis in ((0, "gx"), (1, "gy")):
        flag = flag_ref[d] != 0
        low, high = lows[d], highs[d]
        turned = [jnp.where(flag, high[1 - m], high[m]) for m in range(2)]
        even_ref, odd_ref = pairs[d]
        put_pair(even_ref, odd_ref, v, pack_low(*low, d), pack_high(*turned, d), parity(axis))


def restricted_faces(u_ref, flag_ref, xo, xe, yo, ye):
    for v in range(5):
        line = {}
        for a in range(4):
            for b in range(4):
                if a in (0, 3) or b in (0, 3):
                    line[a, b] = restrict_c(u_ref[v, a, b, 0], u_ref[v, a, b, 1])
        lows = [restrict_four([line[0, n] for n in range(4)]), restrict_four([line[n, 0] for n in range(4)])]
        highs = [restrict_four([line[3, n] for n in range(4)]), restrict_four([line[n, 3] for n in range(4)])]
        put_coarse_faces(v, lows, highs, flag_ref, ((xe, xo), (ye, yo)))


def smoothed(smooth_ref, fields, a, b):
    out = []
    for o in range(5):
        total = [None, None]
        for i in range(5):
            block = smooth_ref[5 * o + i, a, b].astype(F32)
            for q in range(2):
                term = block[8 * q : 8 * q + 8] * fields[i][q]
                total[q] = term if i == 0 else total[q] + term
        out.append([OMEGA * total[q] for q in range(2)])
    return out


def first_line(src_ref, smooth_ref, u_ref, a, b):
    value = smoothed(smooth_ref, [[src_ref[v, a, b, q] for q in range(2)] for v in range(5)], a, b)
    for v in range(5):
        for q in range(2):
            u_ref[v, a, b, q] = value[v][q]


def line_copy(smooth_hbm, smooth_ref, sem, a, b):
    return pltpu.make_async_copy(smooth_hbm.at[:, a, b], smooth_ref.at[:, a, b], sem)


def first_kernel(
    src_hbm, smooth_hbm, orient_hbm, src_ref, smooth_ref, u_ref, flag_ref, xo, xe, yo, ye, sems, orient_ref, orient_sem
):
    every, inner = slice(0, 4), slice(1, 3)
    src_copy = pltpu.make_async_copy(src_hbm, src_ref, sems.at[4])
    src_copy.start()
    copies = [
        line_copy(smooth_hbm, smooth_ref, sems.at[slot], a, b)
        for slot, (a, b) in enumerate(((0, every), (3, every), (inner, 0), (inner, 3)))
    ]
    for one in copies:
        one.start()
    orient_copy = pltpu.make_async_copy(orient_hbm, orient_ref, orient_sem)
    orient_copy.start()
    orient_copy.wait()
    for d in range(3):
        flag_ref[d] = twice(orient_ref[d])
    lines = [[(0, b) for b in range(4)], [(3, b) for b in range(4)], [(1, 0), (2, 0)], [(1, 3), (2, 3)]]
    src_copy.wait()
    for one, group in zip(copies, lines):
        one.wait()
        for a, b in group:
            first_line(src_ref, smooth_ref, u_ref, a, b)
    fine_faces(u_ref, flag_ref, xo, xe, yo, ye)


def prepare_tables(jac_ref, damp_ref, jac8_ref, damp8_ref, face_ref):
    damp = twice(damp_ref[...])
    damp8_ref[...] = damp
    for d in range(3):
        for k in range(25):
            value = twice(jac_ref[25 * d + k])
            jac8_ref[25 * d + k] = value
            if d < 2:
                low, step = axis_low(d)
                diagonal = k % 6 == 0
                upper = H4 * (value - damp if diagonal else value)
                lower = H4 * (value + damp if diagonal else value)
                face_ref[2 * d, k] = jnp.where(low, sroll(upper, -step), upper)
                face_ref[2 * d + 1, k] = jnp.where(low, lower, sroll(lower, step))


def volume(src_ref, u_ref, flag_ref, jac_ref, damp_ref, acc_ref, finish_lines):
    damp = H4 * damp_ref[...]

    def jacobian(d):
        return [[jac_ref[25 * d + 5 * o + i] for i in range(5)] for o in range(5)]

    def along(direction, others):
        low, step = axis_low(direction)
        flag = flag_ref[direction] != 0
        flag_before = sroll(flag_ref[direction], step) != 0

        def at(v, n, other, q):
            return (v, n, other, q) if direction == 0 else (v, other, n, q)

        def step_fn(j, carry):
            other, q = others(j // 2), j % 2
            u = [[u_ref[at(v, n, other, q)] for n in range(4)] for v in range(5)]
            waves = []
            jumps = []
            for v in range(5):
                back_low, back_high = u_ref[at(v, 0, 3 - other, q)], u_ref[at(v, 3, 3 - other, q)]
                right = sroll(jnp.where(flag_before, back_low, u[v][0]), -step)
                left = sroll(jnp.where(flag, back_high, u[v][3]), step)
                jump_right = jnp.where(low, right, 0.0) - u[v][3]
                jump_left = jnp.where(low, 0.0, left) - u[v][0]
                w = list(slopes_along(*u[v]))
                w[3] = w[3] + H4 * jump_right
                w[0] = w[0] - H4 * jump_left
                waves.append(w)
                jumps.append((damp * jump_left, None, None, damp * jump_right))
            matrix = jacobian(direction)
            for n in range(4):
                flux = mix(matrix, [waves[v][n] for v in range(5)])
                for v in range(5):
                    if direction == 1:
                        total = src_ref[at(v, n, other, q)] - 2.0 * u[v][n]
                    else:
                        total = acc_ref[at(v, n, other, q)]
                    total = total - flux[v]
                    if jumps[v][n] is not None:
                        total = total + jumps[v][n]
                    acc_ref[at(v, n, other, q)] = total
            return carry

        return step_fn

    low = c_low()
    flag = jnp.where(low, lroll(flag_ref[2], 1), flag_ref[2]) != 0
    damp_z = damp
    coef = [
        [jnp.where(low, float(D4[2 * p, c]), float(D4[2 * p + 1, c ^ 1])).astype(F32) for c in range(4)]
        for p in range(2)
    ]

    def step_z(j, carry):
        a0, b = j // 4, j % 4
        here = (a0, 3 - a0)
        u = [[[u_ref[v, a, b, q] for q in range(2)] for v in range(5)] for a in here]
        turned = [[[sroll(u[s][v][q], 4) for q in range(2)] for v in range(5)] for s in range(2)]
        beside = []
        for s in range(2):
            line = []
            for v in range(5):
                face = jnp.where(low, turned[s][v][1], turned[s][v][0])
                line.append(jnp.where(low, lroll(face, 1), lroll(face, -1)))
            beside.append(line)
        matrix = jacobian(2)
        for s in range(2):
            waves = [[], []]
            jumps = []
            for v in range(5):
                own = jnp.where(low, u[s][v][0], u[s][v][1])
                jump = jnp.where(flag, beside[1 - s][v], beside[s][v]) - own
                jumps.append(damp_z * jump)
                lifted = H4 * jump
                for p in range(2):
                    w = coef[p][0] * u[s][v][0] + coef[p][1] * turned[s][v][0]
                    w = w + (coef[p][2] * u[s][v][1] + coef[p][3] * turned[s][v][1])
                    w = w - jnp.where(low, lifted, 0.0) if p == 0 else w + jnp.where(low, 0.0, lifted)
                    waves[p].append(w)
            for p in range(2):
                flux = mix(matrix, waves[p])
                for v in range(5):
                    part = jnp.where(low, jumps[v], 0.0) if p == 0 else jnp.where(low, 0.0, jumps[v])
                    acc_ref[v, here[s], b, p] = acc_ref[v, here[s], b, p] - flux[v] + part
        return carry

    lax.fori_loop(0, 4, along(1, lambda k: 3 * k), 0)
    lax.fori_loop(0, 4, step_z, 0)
    finish_lines()
    lax.fori_loop(0, 4, along(1, lambda k: 1 + k), 0)
    lax.fori_loop(4, 8, step_z, 0)
    lax.fori_loop(0, 8, along(0, lambda k: k), 0)


def first_volume_kernel(
    smooth_hbm, src_ref, smooth_in, u_in, flag_ref, jac_ref, damp_ref,
    smooth_ref, u_ref, acc_ref, jac8_ref, damp8_ref, face_ref, second_ref, sem,
):
    inner = slice(1, 3)
    copy = line_copy(smooth_hbm, smooth_ref, sem, inner, inner)
    copy.start()
    prepare_tables(jac_ref, damp_ref, jac8_ref, damp8_ref, face_ref)
    lines = [(a, b) for a in (1, 2) for b in (1, 2)]

    def finish_lines():
        copy.wait()
        for a, b in lines:
            first_line(src_ref, smooth_ref, u_ref, a, b)

    volume(src_ref, u_ref, flag_ref, jac8_ref, damp8_ref, acc_ref, finish_lines)
    for a, b in lines:
        change = smoothed(smooth_ref, [[acc_ref[v, a, b, q] for q in range(2)] for v in range(5)], a, b)
        for v in range(5):
            for q in range(2):
                second_ref[v, a, b, q] = u_ref[v, a, b, q] + change[v][q]


def remote_parts(even_refs, odd_refs, flag_ref, face_ref, part_ref):
    for d, axis in ((0, "gx"), (1, "gy")):
        is_even = parity(axis)
        low, step = axis_low(d)
        flag = flag_ref[d]
        flag = jnp.where(low, sroll(flag, -step), flag) != 0
        even, odd = even_refs[d], odd_refs[d]
        matrix = [[face_ref[2 * d, 5 * o + i] for i in range(5)] for o in range(5)]
        for n in range(4):
            take = lambda v, m: jnp.where(is_even, even[v, m], odd[v, m])
            right = [jnp.where(flag, take(v, 3 - n), take(v, n)) for v in range(5)]
            for v, value in enumerate(mix(matrix, right)):
                part_ref[2 * d, v, n, 0] = jnp.where(low, 0.0, -sroll(value, step))
                part_ref[2 * d, v, n, 1] = jnp.where(low, 0.0, -value)
        matrix = [[face_ref[2 * d + 1, 5 * o + i] for i in range(5)] for o in range(5)]
        for n in range(4):
            left = [jnp.where(is_even, odd[v, n], even[v, n]) for v in range(5)]
            for v, value in enumerate(mix(matrix, left)):
                part_ref[2 * d + 1, v, n, 0] = jnp.where(low, value, 0.0)
                part_ref[2 * d + 1, v, n, 1] = jnp.where(low, sroll(value, -step), 0.0)


def whole(acc_ref, part_ref, v, a, b, q):
    total = acc_ref[v, a, b, q]
    if a == 3:
        total = total + part_ref[0, v, b, q]
    if a == 0:
        total = total + part_ref[1, v, b, q]
    if b == 3:
        total = total + part_ref[2, v, a, q]
    if b == 0:
        total = total + part_ref[3, v, a, q]
    return total


def second_kernel(
    acc_ref, u_ref, smooth_ref, flag_ref, face_ref, rxo, ryo, rxe, rye, inner_ref, out_ref, xo, xe, yo, ye, part_ref
):
    remote_parts((rxe, rye), (rxo, ryo), flag_ref, face_ref, part_ref)
    for a in range(4):
        for b in range(4):
            if a in (1, 2) and b in (1, 2):
                continue
            left = [[whole(acc_ref, part_ref, v, a, b, q) for q in range(2)] for v in range(5)]
            change = smoothed(smooth_ref, left, a, b)
            for v in range(5):
                for q in range(2):
                    out_ref[v, a, b, q] = u_ref[v, a, b, q] + change[v][q]
    restricted_faces(out_ref, flag_ref, xo, xe, yo, ye)


def coarse_smooth(smooth_ref, fields):
    out = [[[None, None], [None, None]] for _ in range(5)]
    for i in range(2):
        for o in range(5):
            total = [None, None]
            for k in range(5):
                block = smooth_ref[5 * o + k, i].astype(F32)
                for j in range(2):
                    term = block[8 * j : 8 * j + 8] * fields[k][i][j]
                    total[j] = term if k == 0 else total[j] + term
            for j in range(2):
                out[o][i][j] = OMEGA * total[j]
    return out


def coarse_faces(field, flag_ref, xo, xe, yo, ye):
    for v in range(5):
        c = field[v]
        lows = [[c[0][0], c[0][1]], [c[0][0], c[1][0]]]
        highs = [[c[1][0], c[1][1]], [c[0][1], c[1][1]]]
        put_coarse_faces(v, lows, highs, flag_ref, ((xe, xo), (ye, yo)))


def restricted_volume_kernel(src_ref, u_ref, flag_ref, jac_ref, damp_ref, acc_ref):
    damp = H4 * damp_ref[...]
    low_c = c_low()
    slope = [
        jnp.where(low_c, float(PD[0, c]), float(PD[1, c ^ 1])).astype(F32) for c in range(4)
    ]
    flags = [flag_ref[0] != 0, flag_ref[1] != 0, jnp.where(low_c, lroll(flag_ref[2], 1), flag_ref[2]) != 0]
    sign = jnp.where(low_c, -H4, H4).astype(F32)
    waves = [[[[None] * 5 for _ in range(2)] for _ in range(2)] for _ in range(3)]

    def slopes_four(values):
        return [sum_of([(float(PD[i, n]), values[n]) for n in range(4)]) for i in range(2)]

    for v in range(5):
        line, slope_c, ends = {}, {}, {}
        for a in range(4):
            for b in range(4):
                first, second = u_ref[v, a, b, 0], u_ref[v, a, b, 1]
                line[a, b] = restrict_c(first, second)
                slope_c[a, b] = (slope[0] * first + slope[1] * sroll(first, 4)) + (
                    slope[2] * second + slope[3] * sroll(second, 4)
                )
                ends[a, b] = jnp.where(low_c, first, second)

        def along_b(table):
            return [restrict_four([table[a, b] for b in range(4)]) for a in range(4)]

        def both(table):
            by_b = along_b(table)
            return [restrict_four([by_b[a][j] for a in range(4)]) for j in range(2)]

        by_b = along_b(line)
        by_a = [restrict_four([line[a, b] for a in range(4)]) for b in range(4)]
        flux_z = both(slope_c)
        trace_z = both(ends)
        sources = both({(a, b): restrict_c(src_ref[v, a, b, 0], src_ref[v, a, b, 1]) for a in range(4) for b in range(4)})
        acc = [[None, None], [None, None]]
        for j in range(2):
            value = restrict_four([by_b[a][j] for a in range(4)])
            flux = slopes_four([by_b[a][j] for a in range(4)])
            for i in range(2):
                acc[i][j] = sources[j][i] - 2.0 * value[i]
                waves[0][i][j][v] = flux[i]
        for i in range(2):
            flux = slopes_four([by_a[b][i] for b in range(4)])
            for j in range(2):
                waves[1][i][j][v] = flux[j]
        for d, lo, hi in ((0, by_b[0], by_b[3]), (1, by_a[0], by_a[3])):
            low, step = axis_low(d)
            flag = flags[d]
            flag_before = sroll(flag_ref[d], step) != 0
            for m in range(2):
                right = sroll(jnp.where(flag_before, lo[1 - m], lo[m]), -step)
                left = sroll(jnp.where(flag, hi[1 - m], hi[m]), step)
                jump_right = jnp.where(low, right, 0.0) - hi[m]
                jump_left = jnp.where(low, 0.0, left) - lo[m]
                i, j = (1, m) if d == 0 else (m, 1)
                waves[d][i][j][v] = waves[d][i][j][v] + H4 * jump_right
                acc[i][j] = acc[i][j] + damp * jump_right
                i, j = (0, m) if d == 0 else (m, 0)
                waves[d][i][j][v] = waves[d][i][j][v] - H4 * jump_left
                acc[i][j] = acc[i][j] + damp * jump_left
        beside = []
        for j in range(2):
            turned = [sroll(trace_z[j][i], 4) for i in range(2)]
            beside.append([jnp.where(low_c, lroll(t, 1), lroll(t, -1)) for t in turned])
        for i in range(2):
            for j in range(2):
                jump = jnp.where(flags[2], beside[j][1 - i], beside[j][i]) - trace_z[j][i]
                waves[2][i][j][v] = flux_z[j][i] + sign * jump
                acc_ref[v, i, j] = acc[i][j] + damp * jump
    for d in range(3):
        matrix = [[jac_ref[25 * d + 5 * o + i] for i in range(5)] for o in range(5)]
        for i in range(2):
            for j in range(2):
                for v, value in enumerate(mix(matrix, waves[d][i][j])):
                    acc_ref[v, i, j] = acc_ref[v, i, j] - value


def add_remote(field, scale, flag_ref, face_ref, rxo, rxe, ryo, rye):
    for d, axis in ((0, "gx"), (1, "gy")):
        is_even = parity(axis)
        low, step = axis_low(d)
        flag = flag_ref[d]
        flag = jnp.where(low, sroll(flag, -step), flag) != 0
        even, odd = ((rxe, rxo), (rye, ryo))[d]
        at = (lambda n, m: (n, m)) if d == 0 else (lambda n, m: (m, n))
        right, left = [], []
        for v in range(5):
            value = scale * jnp.where(is_even, even[v], odd[v])
            swapped = jnp.where(low, sroll(value, -step), sroll(value, step))
            right.append(jnp.where(flag, swapped, value))
            left.append(scale * jnp.where(is_even, odd[v], even[v]))
        upper = [[face_ref[2 * d, 5 * o + i] for i in range(5)] for o in range(5)]
        lower = [[face_ref[2 * d + 1, 5 * o + i] for i in range(5)] for o in range(5)]
        for v, value in enumerate(mix(upper, right)):
            for m, part in enumerate((sroll(value, step), value)):
                i, j = at(1, m)
                field[v][i][j] = field[v][i][j] - jnp.where(low, 0.0, part)
        for v, value in enumerate(mix(lower, left)):
            for m, part in enumerate((value, sroll(value, -step))):
                i, j = at(0, m)
                field[v][i][j] = field[v][i][j] + jnp.where(low, part, 0.0)


def restrict_kernel(
    acc_ref, flag_ref, face_ref, smooth_ref, rxo, rxe, ryo, rye, rhs_ref, c_ref, xo, xe, yo, ye
):
    rhs = [[[acc_ref[v, i, j] for j in range(2)] for i in range(2)] for v in range(5)]
    add_remote(rhs, 1.0, flag_ref, face_ref, rxo, rxe, ryo, rye)
    c = coarse_smooth(smooth_ref, rhs)
    for v in range(5):
        for i in range(2):
            for j in range(2):
                rhs_ref[v, i, j] = rhs[v][i][j]
                c_ref[v, i, j] = c[v][i][j]
    coarse_faces(c, flag_ref, xo, xe, yo, ye)


def coarse_local_kernel(c_ref, rhs_ref, smooth_ref, flag_ref, jac_ref, damp_ref, out_ref):
    damp = 0.5 * damp_ref[...]
    c = [[[c_ref[v, i, j] for j in range(2)] for i in range(2)] for v in range(5)]
    acc = [[[rhs_ref[v, i, j] - 2.0 * c[v][i][j] for j in range(2)] for i in range(2)] for v in range(5)]
    for d in range(2):
        low, step = axis_low(d)
        flag = flag_ref[d] != 0
        flag_before = sroll(flag_ref[d], step) != 0
        matrix = [[jac_ref[25 * d + 5 * o + i] for i in range(5)] for o in range(5)]
        at = (lambda n, m: (n, m)) if d == 0 else (lambda n, m: (m, n))
        waves = [[[None] * 5, [None] * 5] for _ in range(2)]
        for v in range(5):
            lo = [c[v][at(0, m)[0]][at(0, m)[1]] for m in range(2)]
            hi = [c[v][at(1, m)[0]][at(1, m)[1]] for m in range(2)]
            for m in range(2):
                right = jnp.where(low, sroll(jnp.where(flag_before, lo[1 - m], lo[m]), -step), 0.0)
                left = jnp.where(low, 0.0, sroll(jnp.where(flag, hi[1 - m], hi[m]), step))
                waves[1][m][v] = 0.5 * (right - lo[m])
                waves[0][m][v] = 0.5 * (hi[m] - left)
                i, j = at(1, m)
                acc[v][i][j] = acc[v][i][j] + damp * (right - hi[m])
                i, j = at(0, m)
                acc[v][i][j] = acc[v][i][j] + damp * (left - lo[m])
        for n in range(2):
            for m in range(2):
                i, j = at(n, m)
                for v, value in enumerate(mix(matrix, waves[n][m])):
                    acc[v][i][j] = acc[v][i][j] - value
    low = c_low()
    flag = jnp.where(low, lroll(flag_ref[2], 1), flag_ref[2]) != 0
    half = jnp.where(low, 0.5, -0.5).astype(F32)
    matrix = [[jac_ref[50 + 5 * o + i] for i in range(5)] for o in range(5)]
    turned = [[[sroll(c[v][i][j], 4) for j in range(2)] for i in range(2)] for v in range(5)]
    beside = [
        [[jnp.where(low, lroll(t, 1), lroll(t, -1)) for t in turned[v][i]] for i in range(2)] for v in range(5)
    ]
    for i in range(2):
        for j in range(2):
            wave = []
            for v in range(5):
                next_to = jnp.where(flag, beside[v][1 - i][j], beside[v][i][j])
                wave.append(half * (turned[v][i][j] - next_to))
                acc[v][i][j] = acc[v][i][j] + damp * (next_to - c[v][i][j])
            for v, value in enumerate(mix(matrix, wave)):
                acc[v][i][j] = acc[v][i][j] - value
    change = coarse_smooth(smooth_ref, acc)
    for v in range(5):
        for i in range(2):
            for j in range(2):
                out_ref[v, i, j] = c[v][i][j] + change[v][i][j]


def coarse_step(c_ref, smooth_ref, flag_ref, face_ref, rxo, rxe, ryo, rye):
    rest = [[[0.0, 0.0], [0.0, 0.0]] for _ in range(5)]
    add_remote(rest, 1.0 / 6.0, flag_ref, face_ref, rxo, rxe, ryo, rye)
    change = coarse_smooth(smooth_ref, rest)
    return [[[c_ref[v, i, j] + change[v][i][j] for j in range(2)] for i in range(2)] for v in range(5)]


def coarse_kernel(c_ref, smooth_ref, flag_ref, face_ref, rxo, rxe, ryo, rye, out_ref, xo, xe, yo, ye):
    c = coarse_step(c_ref, smooth_ref, flag_ref, face_ref, rxo, rxe, ryo, rye)
    for v in range(5):
        for i in range(2):
            for j in range(2):
                out_ref[v, i, j] = c[v][i][j]
    coarse_faces(c, flag_ref, xo, xe, yo, ye)


def spread(first, second):
    return first, NEAR * first + FAR * second, FAR * first + NEAR * second, second


def last_kernel(
    c_ref, smooth_ref, flag_ref, face_ref, rxo, rxe, ryo, rye, second_ref, out_hbm, out_ref, sems
):
    c = coarse_step(c_ref, smooth_ref, flag_ref, face_ref, rxo, rxe, ryo, rye)
    low = c_low()
    copies = []
    for v in range(5):
        by_c = [[None, None], [None, None]]
        for i in range(2):
            for j in range(2):
                value = c[v][i][j]
                inner = FAR * value + NEAR * sroll(value, 4)
                by_c[i][j] = (jnp.where(low, value, inner), jnp.where(low, inner, value))
        for q in range(2):
            lines = [spread(by_c[i][0][q], by_c[i][1][q]) for i in range(2)]
            for b in range(4):
                for a, value in enumerate(spread(lines[0][b], lines[1][b])):
                    out_ref[v, a, b, q] = second_ref[v, a, b, q] + value
        copy = pltpu.make_async_copy(out_ref.at[v], out_hbm.at[v], sems.at[v])
        copy.start()
        copies.append(copy)
    for copy in copies:
        copy.wait()


FINE = (5, 4, 4, 2, 8, 128)
FINE_MESSAGE = (5, 4, 8, 128)
COARSE = (5, 2, 2, 8, 128)
COARSE_MESSAGE = (5, 8, 128)


def vmem(shape, dtype=F32):
    return pltpu.VMEM(shape, dtype)


def here(array):
    return pltpu.with_memory_space_constraint(array, pltpu.VMEM)


def call(kernel, args, outs, in_hbm=(), out_hbm=(), scratch=(), aliases=None, flops=0):
    in_specs = [
        pl.BlockSpec(memory_space=pltpu.HBM if k in in_hbm else pltpu.VMEM) for k in range(len(args))
    ]
    out_specs = [
        pl.BlockSpec(memory_space=pltpu.HBM if k in out_hbm else pltpu.VMEM) for k in range(len(outs))
    ]
    args = [pltpu.with_memory_space_constraint(a, pltpu.HBM) if k in in_hbm else here(a) for k, a in enumerate(args)]
    return pl.pallas_call(
        kernel,
        out_shape=outs,
        in_specs=in_specs,
        out_specs=out_specs,
        scratch_shapes=scratch,
        input_output_aliases=aliases or {},
        compiler_params=pltpu.CompilerParams(vmem_limit_bytes=8 * 2**20),
        cost_estimate=pl.CostEstimate(flops=flops, bytes_accessed=4 * 2**20, transcendentals=0),
    )(*args)


def partners(axis):
    size = lax.axis_size(axis)
    even = [(i, i ^ 1) for i in range(size)]
    odd = [(i, (i - 1) % size if i % 2 == 0 else (i + 1) % size) for i in range(size)]
    return even, odd


def exchange(xo, xe, yo, ye):
    even_x, odd_x = partners("gx")
    even_y, odd_y = partners("gy")
    xo = lax.ppermute(xo, "gx", odd_x)
    xe = lax.ppermute(xe, "gx", even_x)
    yo = lax.ppermute(yo, "gy", odd_y)
    ye = lax.ppermute(ye, "gy", even_y)
    return xo, xe, yo, ye


def local_sweep(coarse, *rest):
    (out,) = call(coarse_local_kernel, (coarse, *rest), [vmem(COARSE)], flops=4 * 2**20)
    return out


def body(source, jacobian, damping, orient, smoother, coarse_smoother):
    source = source.reshape(FINE)
    smoother = smoother.reshape(25, 4, 4, 16, 128)
    coarse_smoother = coarse_smoother.reshape(25, 2, 16, 128)
    jacobian = jacobian.reshape(75, 4, 128)
    damping = damping.reshape(4, 128)
    orient = orient.reshape(3, 4, 128)
    fine_messages = [vmem(FINE_MESSAGE)] * 4
    coarse_messages = [vmem(COARSE_MESSAGE)] * 4

    held = vmem(smoother.shape, smoother.dtype)
    smoother_in = smoother
    source, smoother, first, flag, *sent = call(
        first_kernel,
        (source, smoother_in, orient),
        [vmem(FINE), held, vmem(FINE), vmem((3, 8, 128), jnp.int32)] + fine_messages,
        in_hbm=(0, 1, 2),
        scratch=[pltpu.SemaphoreType.DMA((5,)), pltpu.VMEM((3, 4, 128), jnp.int32), pltpu.SemaphoreType.DMA],
        flops=2 * 25 * 64 * 512,
    )
    rxo, rxe, ryo, rye = exchange(*sent)
    smoother, first, acc, jac8, damp8, face, second = call(
        first_volume_kernel,
        (smoother_in, source, smoother, first, flag, jacobian, damping),
        [held, vmem(FINE), vmem(FINE), vmem((75, 8, 128)), vmem((8, 128)), vmem((4, 25, 8, 128)), vmem(FINE)],
        in_hbm=(0,),
        aliases={2: 0, 3: 1},
        scratch=[pltpu.SemaphoreType.DMA],
        flops=9 * 2**20,
    )
    second, *sent = call(
        second_kernel,
        (acc, first, smoother, flag, face, rxo, ryo, rxe, rye, second),
        [vmem(FINE)] + coarse_messages,
        aliases={9: 0},
        scratch=[pltpu.VMEM((4, 5, 4, 2, 8, 128), F32)],
        flops=3 * 2**20,
    )
    got = exchange(*sent)
    (acc,) = call(restricted_volume_kernel, (source, second, flag, jac8, damp8), [vmem(COARSE)], flops=4 * 2**20)
    rhs, coarse, *sent = call(
        restrict_kernel,
        (acc, flag, face, coarse_smoother, *got),
        [vmem(COARSE), vmem(COARSE)] + coarse_messages,
        flops=2**20,
    )
    got = exchange(*sent)
    coarse = local_sweep(coarse, rhs, coarse_smoother, flag, jac8, damp8)
    coarse, *sent = call(
        coarse_kernel,
        (coarse, coarse_smoother, flag, face, *got),
        [vmem(COARSE)] + coarse_messages,
        flops=2**20,
    )
    got = exchange(*sent)
    coarse = local_sweep(coarse, rhs, coarse_smoother, flag, jac8, damp8)
    (out,) = call(
        last_kernel,
        (coarse, coarse_smoother, flag, face, *got, second),
        [jax.ShapeDtypeStruct(FINE, F32)],
        out_hbm=(0,),
        scratch=[pltpu.VMEM(FINE, F32), pltpu.SemaphoreType.DMA((5,))],
        flops=2**20,
    )
    return out.reshape(5, 4, 4, 4, 2, 2, 128)


def solution(mesh):
    in_specs = (
        P(None, None, None, None, "gx", "gy", None),
        P(None, None, None, "gx", "gy", None),
        P("gx", "gy", None),
        P(None, "gx", "gy", None),
        P(None, None, None, None, None, "gx", "gy", None),
        P(None, None, None, None, None, "gx", "gy", None),
    )
    out_specs = P(None, None, None, None, "gx", "gy", None)
    return jax.shard_map(body, mesh=mesh, in_specs=in_specs, out_specs=out_specs, check_vma=False)
```

```python
import functools
import math

import jax
import jax.numpy as jnp
import numpy as np
from jax import lax
from jax.experimental import pallas as pl
from jax.experimental.pallas import tpu as pltpu
from jax.sharding import PartitionSpec as P


F32 = jnp.float32
OMEGA = 0.8
H4 = 3.0
ROOT = 1.0 / math.sqrt(5.0)
NEAR = (1.0 + ROOT) / 2.0
FAR = (1.0 - ROOT) / 2.0


def lobatto_slopes():
    points = np.array([-1.0, -ROOT, ROOT, 1.0])
    weights = np.ones(4)
    for i in range(4):
        for j in range(4):
            if i != j:
                weights[i] = weights[i] / (points[i] - points[j])
    slopes = np.zeros((4, 4))
    for i in range(4):
        for j in range(4):
            if i != j:
                slopes[i, j] = weights[j] / weights[i] / (points[i] - points[j])
        slopes[i, i] = -np.sum(slopes[i])
    return slopes


D4 = lobatto_slopes()
PD = np.array([[1.0, NEAR, FAR, 0.0], [0.0, FAR, NEAR, 1.0]]) @ D4


def sum_of(terms):
    total = None
    for weight, value in terms:
        total = weight * value if total is None else total + weight * value
    return total


def rows():
    return lax.broadcasted_iota(jnp.int32, (8, 128), 0)


def x_low():
    return (rows() & 2) == 0


def y_low():
    return (rows() & 1) == 0


def c_low():
    return (rows() & 4) == 0


def sroll(value, shift):
    return pltpu.roll(value, shift % 8, 0)


def lroll(value, shift):
    return pltpu.roll(value, shift % 128, 1)


def twice(value):
    return jnp.concatenate([value, value], axis=0)


def axis_low(direction):
    return (x_low(), 2) if direction == 0 else (y_low(), 1)


def pack_low(first, second, direction):
    low, step = axis_low(direction)
    return jnp.where(low, first, sroll(second, step))


def pack_high(first, second, direction):
    low, step = axis_low(direction)
    return jnp.where(low, sroll(first, -step), second)


def slopes_along(u0, u1, u2, u3):
    e0, o0, e1, o1 = u0 + u3, u0 - u3, u1 + u2, u1 - u2
    diff = e1 - e0
    even_a = float((D4[0, 1] + D4[0, 2]) / 2.0) * diff
    even_b = float((D4[1, 2] - 0.0) / 2.0) * diff
    odd_a = float((D4[0, 0] - D4[0, 3]) / 2.0) * o0 + float((D4[0, 1] - D4[0, 2]) / 2.0) * o1
    odd_b = float((D4[1, 0] - D4[1, 3]) / 2.0) * o0 - float(D4[1, 2] / 2.0) * o1
    return even_a + odd_a, even_b + odd_b, odd_b - even_b, odd_a - even_a


def mix(matrix, fields):
    out = []
    for o in range(5):
        total = matrix[o][0] * fields[0]
        for i in range(1, 5):
            total = total + matrix[o][i] * fields[i]
        out.append(total)
    return out


def parity(axis):
    return lax.rem(lax.axis_index(axis), 2) == 0


def put_pair(even_ref, odd_ref, index, low_face, high_face, is_even):
    even_ref[index] = jnp.where(is_even, high_face, low_face)
    odd_ref[index] = jnp.where(is_even, low_face, high_face)


def fine_x_faces(u_ref, flag_ref, xo, xe):
    even_x, fx = parity("gx"), flag_ref[0] != 0
    for v in range(5):
        for n in range(4):
            low = pack_low(u_ref[v, 0, n, 0], u_ref[v, 0, n, 1], 0)
            h = [jnp.where(fx, u_ref[v, 3, 3 - n, q], u_ref[v, 3, n, q]) for q in range(2)]
            put_pair(xe, xo, (v, n), low, pack_high(h[0], h[1], 0), even_x)


def fine_y_faces(u_ref, flag_ref, yo, ye):
    even_y, fy = parity("gy"), flag_ref[1] != 0
    for v in range(5):
        for n in range(4):
            low = pack_low(u_ref[v, n, 0, 0], u_ref[v, n, 0, 1], 1)
            h = [jnp.where(fy, u_ref[v, 3 - n, 3, q], u_ref[v, n, 3, q]) for q in range(2)]
            put_pair(ye, yo, (v, n), low, pack_high(h[0], h[1], 1), even_y)


def restrict_c(first, second):
    low = c_low()
    middle = jnp.where(low, second, first)
    return jnp.where(low, first, second) + FAR * middle + NEAR * sroll(middle, 4)


def restrict_four(values):
    return values[0] + NEAR * values[1] + FAR * values[2], values[3] + NEAR * values[2] + FAR * values[1]


def put_coarse_faces(v, lows, highs, flag_ref, pairs):
    for d, axis in ((0, "gx"), (1, "gy")):
        flag = flag_ref[d] != 0
        low, high = lows[d], highs[d]
        turned = [jnp.where(flag, high[1 - m], high[m]) for m in range(2)]
        even_ref, odd_ref = pairs[d]
        put_pair(even_ref, odd_ref, v, pack_low(*low, d), pack_high(*turned, d), parity(axis))


def restricted_faces(u_ref, flag_ref, xo, xe, yo, ye):
    for v in range(5):
        line = {}
        for a in range(4):
            for b in range(4):
                if a in (0, 3) or b in (0, 3):
                    line[a, b] = restrict_c(u_ref[v, a, b, 0], u_ref[v, a, b, 1])
        lows = [restrict_four([line[0, n] for n in range(4)]), restrict_four([line[n, 0] for n in range(4)])]
        highs = [restrict_four([line[3, n] for n in range(4)]), restrict_four([line[n, 3] for n in range(4)])]
        put_coarse_faces(v, lows, highs, flag_ref, ((xe, xo), (ye, yo)))


def smoothed(smooth_ref, fields, a, b):
    out = []
    for o in range(5):
        total = [None, None]
        for i in range(5):
            block = smooth_ref[5 * o + i, a, b].astype(F32)
            for q in range(2):
                term = block[8 * q : 8 * q + 8] * fields[i][q]
                total[q] = term if i == 0 else total[q] + term
        out.append([OMEGA * total[q] for q in range(2)])
    return out


def first_line(src_ref, smooth_ref, u_ref, a, b):
    value = smoothed(smooth_ref, [[src_ref[v, a, b, q] for q in range(2)] for v in range(5)], a, b)
    for v in range(5):
        for q in range(2):
            u_ref[v, a, b, q] = value[v][q]


def line_copy(smooth_hbm, smooth_ref, sem, a, b):
    return pltpu.make_async_copy(smooth_hbm.at[:, a, b], smooth_ref.at[:, a, b], sem)


def first_kernel(
    src_hbm, smooth_hbm, orient_hbm, src_ref, smooth_ref, u_ref, flag_ref, xo, xe, sems, orient_ref, orient_sem
):
    every, inner = slice(0, 4), slice(1, 3)
    src_copy = pltpu.make_async_copy(src_hbm, src_ref, sems.at[4])
    src_copy.start()
    copies = [
        line_copy(smooth_hbm, smooth_ref, sems.at[slot], a, b)
        for slot, (a, b) in enumerate(((0, every), (3, every), (inner, 0), (inner, 3)))
    ]
    for one in copies:
        one.start()
    orient_copy = pltpu.make_async_copy(orient_hbm, orient_ref, orient_sem)
    orient_copy.start()
    orient_copy.wait()
    for d in range(3):
        flag_ref[d] = twice(orient_ref[d])
    src_copy.wait()
    for one, a in zip(copies, (0, 3)):
        one.wait()
        for b in range(4):
            first_line(src_ref, smooth_ref, u_ref, a, b)
    fine_x_faces(u_ref, flag_ref, xo, xe)
    for one in copies[2:]:
        one.wait()


def first_y_kernel(src_ref, smooth_ref, x_lines_ref, flag_ref, u_ref, yo, ye):
    for a in (1, 2):
        for b in (0, 3):
            first_line(src_ref, smooth_ref, u_ref, a, b)
    fine_y_faces(u_ref, flag_ref, yo, ye)


def prepare_tables(jac_ref, damp_ref, jac8_ref, damp8_ref, face_ref):
    damp = twice(damp_ref[...])
    damp8_ref[...] = damp
    for d in range(3):
        for k in range(25):
            value = twice(jac_ref[25 * d + k])
            jac8_ref[25 * d + k] = value
            if d < 2:
                low, step = axis_low(d)
                diagonal = k % 6 == 0
                upper = H4 * (value - damp if diagonal else value)
                lower = H4 * (value + damp if diagonal else value)
                face_ref[2 * d, k] = jnp.where(low, sroll(upper, -step), upper)
                face_ref[2 * d + 1, k] = jnp.where(low, lower, sroll(lower, step))


def volume(src_ref, u_ref, flag_ref, jac_ref, damp_ref, acc_ref, finish_lines):
    damp = H4 * damp_ref[...]

    def jacobian(d):
        return [[jac_ref[25 * d + 5 * o + i] for i in range(5)] for o in range(5)]

    def along(direction, others):
        low, step = axis_low(direction)
        flag = flag_ref[direction] != 0
        flag_before = sroll(flag_ref[direction], step) != 0

        def at(v, n, other, q):
            return (v, n, other, q) if direction == 0 else (v, other, n, q)

        def step_fn(j, carry):
            other, q = others(j // 2), j % 2
            u = [[u_ref[at(v, n, other, q)] for n in range(4)] for v in range(5)]
            waves = []
            jumps = []
            for v in range(5):
                back_low, back_high = u_ref[at(v, 0, 3 - other, q)], u_ref[at(v, 3, 3 - other, q)]
                right = sroll(jnp.where(flag_before, back_low, u[v][0]), -step)
                left = sroll(jnp.where(flag, back_high, u[v][3]), step)
                jump_right = jnp.where(low, right, 0.0) - u[v][3]
                jump_left = jnp.where(low, 0.0, left) - u[v][0]
                w = list(slopes_along(*u[v]))
                w[3] = w[3] + H4 * jump_right
                w[0] = w[0] - H4 * jump_left
                waves.append(w)
                jumps.append((damp * jump_left, None, None, damp * jump_right))
            matrix = jacobian(direction)
            for n in range(4):
                flux = mix(matrix, [waves[v][n] for v in range(5)])
                for v in range(5):
                    if direction == 1:
                        total = src_ref[at(v, n, other, q)] - 2.0 * u[v][n]
                    else:
                        total = acc_ref[at(v, n, other, q)]
                    total = total - flux[v]
                    if jumps[v][n] is not None:
                        total = total + jumps[v][n]
                    acc_ref[at(v, n, other, q)] = total
            return carry

        return step_fn

    low = c_low()
    flag = jnp.where(low, lroll(flag_ref[2], 1), flag_ref[2]) != 0
    damp_z = damp
    coef = [
        [jnp.where(low, float(D4[2 * p, c]), float(D4[2 * p + 1, c ^ 1])).astype(F32) for c in range(4)]
        for p in range(2)
    ]

    def step_z(j, carry):
        a0, b = j // 4, j % 4
        here = (a0, 3 - a0)
        u = [[[u_ref[v, a, b, q] for q in range(2)] for v in range(5)] for a in here]
        turned = [[[sroll(u[s][v][q], 4) for q in range(2)] for v in range(5)] for s in range(2)]
        beside = []
        for s in range(2):
            line = []
            for v in range(5):
                face = jnp.where(low, turned[s][v][1], turned[s][v][0])
                line.append(jnp.where(low, lroll(face, 1), lroll(face, -1)))
            beside.append(line)
        matrix = jacobian(2)
        for s in range(2):
            waves = [[], []]
            jumps = []
            for v in range(5):
                own = jnp.where(low, u[s][v][0], u[s][v][1])
                jump = jnp.where(flag, beside[1 - s][v], beside[s][v]) - own
                jumps.append(damp_z * jump)
                lifted = H4 * jump
                for p in range(2):
                    w = coef[p][0] * u[s][v][0] + coef[p][1] * turned[s][v][0]
                    w = w + (coef[p][2] * u[s][v][1] + coef[p][3] * turned[s][v][1])
                    w = w - jnp.where(low, lifted, 0.0) if p == 0 else w + jnp.where(low, 0.0, lifted)
                    waves[p].append(w)
            for p in range(2):
                flux = mix(matrix, waves[p])
                for v in range(5):
                    part = jnp.where(low, jumps[v], 0.0) if p == 0 else jnp.where(low, 0.0, jumps[v])
                    acc_ref[v, here[s], b, p] = acc_ref[v, here[s], b, p] - flux[v] + part
        return carry

    lax.fori_loop(0, 4, along(1, lambda k: 3 * k), 0)
    lax.fori_loop(0, 4, step_z, 0)
    finish_lines()
    lax.fori_loop(0, 4, along(1, lambda k: 1 + k), 0)
    lax.fori_loop(4, 8, step_z, 0)
    lax.fori_loop(0, 8, along(0, lambda k: k), 0)


def first_volume_kernel(
    smooth_hbm, src_ref, smooth_in, u_in, flag_ref, jac_ref, damp_ref,
    smooth_ref, u_ref, acc_ref, jac8_ref, damp8_ref, face_ref, second_ref, sem,
):
    inner = slice(1, 3)
    copy = line_copy(smooth_hbm, smooth_ref, sem, inner, inner)
    copy.start()
    prepare_tables(jac_ref, damp_ref, jac8_ref, damp8_ref, face_ref)
    lines = [(a, b) for a in (1, 2) for b in (1, 2)]

    def finish_lines():
        copy.wait()
        for a, b in lines:
            first_line(src_ref, smooth_ref, u_ref, a, b)

    volume(src_ref, u_ref, flag_ref, jac8_ref, damp8_ref, acc_ref, finish_lines)
    for a, b in lines:
        change = smoothed(smooth_ref, [[acc_ref[v, a, b, q] for q in range(2)] for v in range(5)], a, b)
        for v in range(5):
            for q in range(2):
                second_ref[v, a, b, q] = u_ref[v, a, b, q] + change[v][q]


def remote_parts(even_refs, odd_refs, flag_ref, face_ref, part_ref):
    for d, axis in ((0, "gx"), (1, "gy")):
        is_even = parity(axis)
        low, step = axis_low(d)
        flag = flag_ref[d]
        flag = jnp.where(low, sroll(flag, -step), flag) != 0
        even, odd = even_refs[d], odd_refs[d]
        matrix = [[face_ref[2 * d, 5 * o + i] for i in range(5)] for o in range(5)]
        for n in range(4):
            take = lambda v, m: jnp.where(is_even, even[v, m], odd[v, m])
            right = [jnp.where(flag, take(v, 3 - n), take(v, n)) for v in range(5)]
            for v, value in enumerate(mix(matrix, right)):
                part_ref[2 * d, v, n, 0] = jnp.where(low, 0.0, -sroll(value, step))
                part_ref[2 * d, v, n, 1] = jnp.where(low, 0.0, -value)
        matrix = [[face_ref[2 * d + 1, 5 * o + i] for i in range(5)] for o in range(5)]
        for n in range(4):
            left = [jnp.where(is_even, odd[v, n], even[v, n]) for v in range(5)]
            for v, value in enumerate(mix(matrix, left)):
                part_ref[2 * d + 1, v, n, 0] = jnp.where(low, value, 0.0)
                part_ref[2 * d + 1, v, n, 1] = jnp.where(low, sroll(value, -step), 0.0)


def whole(acc_ref, part_ref, v, a, b, q):
    total = acc_ref[v, a, b, q]
    if a == 3:
        total = total + part_ref[0, v, b, q]
    if a == 0:
        total = total + part_ref[1, v, b, q]
    if b == 3:
        total = total + part_ref[2, v, a, q]
    if b == 0:
        total = total + part_ref[3, v, a, q]
    return total


def second_kernel(
    acc_ref, u_ref, smooth_ref, flag_ref, face_ref, rxo, rxe, ryo, rye, inner_ref, out_ref, xo, xe, yo, ye, part_ref
):
    remote_parts((rxe, rye), (rxo, ryo), flag_ref, face_ref, part_ref)
    for a in range(4):
        for b in range(4):
            if a in (1, 2) and b in (1, 2):
                continue
            left = [[whole(acc_ref, part_ref, v, a, b, q) for q in range(2)] for v in range(5)]
            change = smoothed(smooth_ref, left, a, b)
            for v in range(5):
                for q in range(2):
                    out_ref[v, a, b, q] = u_ref[v, a, b, q] + change[v][q]
    restricted_faces(out_ref, flag_ref, xo, xe, yo, ye)


def coarse_smooth(smooth_ref, fields):
    out = [[[None, None], [None, None]] for _ in range(5)]
    for i in range(2):
        for o in range(5):
            total = [None, None]
            for k in range(5):
                block = smooth_ref[5 * o + k, i].astype(F32)
                for j in range(2):
                    term = block[8 * j : 8 * j + 8] * fields[k][i][j]
                    total[j] = term if k == 0 else total[j] + term
            for j in range(2):
                out[o][i][j] = OMEGA * total[j]
    return out


def coarse_faces(field, flag_ref, xo, xe, yo, ye):
    for v in range(5):
        c = field[v]
        lows = [[c[0][0], c[0][1]], [c[0][0], c[1][0]]]
        highs = [[c[1][0], c[1][1]], [c[0][1], c[1][1]]]
        put_coarse_faces(v, lows, highs, flag_ref, ((xe, xo), (ye, yo)))


def restricted_volume_kernel(src_ref, u_ref, flag_ref, jac_ref, damp_ref, acc_ref):
    damp = H4 * damp_ref[...]
    low_c = c_low()
    slope = [
        jnp.where(low_c, float(PD[0, c]), float(PD[1, c ^ 1])).astype(F32) for c in range(4)
    ]
    flags = [flag_ref[0] != 0, flag_ref[1] != 0, jnp.where(low_c, lroll(flag_ref[2], 1), flag_ref[2]) != 0]
    sign = jnp.where(low_c, -H4, H4).astype(F32)
    waves = [[[[None] * 5 for _ in range(2)] for _ in range(2)] for _ in range(3)]

    def slopes_four(values):
        return [sum_of([(float(PD[i, n]), values[n]) for n in range(4)]) for i in range(2)]

    for v in range(5):
        line, slope_c, ends = {}, {}, {}
        for a in range(4):
            for b in range(4):
                first, second = u_ref[v, a, b, 0], u_ref[v, a, b, 1]
                line[a, b] = restrict_c(first, second)
                slope_c[a, b] = (slope[0] * first + slope[1] * sroll(first, 4)) + (
                    slope[2] * second + slope[3] * sroll(second, 4)
                )
                ends[a, b] = jnp.where(low_c, first, second)

        def along_b(table):
            return [restrict_four([table[a, b] for b in range(4)]) for a in range(4)]

        def both(table):
            by_b = along_b(table)
            return [restrict_four([by_b[a][j] for a in range(4)]) for j in range(2)]

        by_b = along_b(line)
        by_a = [restrict_four([line[a, b] for a in range(4)]) for b in range(4)]
        flux_z = both(slope_c)
        trace_z = both(ends)
        sources = both({(a, b): restrict_c(src_ref[v, a, b, 0], src_ref[v, a, b, 1]) for a in range(4) for b in range(4)})
        acc = [[None, None], [None, None]]
        for j in range(2):
            value = restrict_four([by_b[a][j] for a in range(4)])
            flux = slopes_four([by_b[a][j] for a in range(4)])
            for i in range(2):
                acc[i][j] = sources[j][i] - 2.0 * value[i]
                waves[0][i][j][v] = flux[i]
        for i in range(2):
            flux = slopes_four([by_a[b][i] for b in range(4)])
            for j in range(2):
                waves[1][i][j][v] = flux[j]
        for d, lo, hi in ((0, by_b[0], by_b[3]), (1, by_a[0], by_a[3])):
            low, step = axis_low(d)
            flag = flags[d]
            flag_before = sroll(flag_ref[d], step) != 0
            for m in range(2):
                right = sroll(jnp.where(flag_before, lo[1 - m], lo[m]), -step)
                left = sroll(jnp.where(flag, hi[1 - m], hi[m]), step)
                jump_right = jnp.where(low, right, 0.0) - hi[m]
                jump_left = jnp.where(low, 0.0, left) - lo[m]
                i, j = (1, m) if d == 0 else (m, 1)
                waves[d][i][j][v] = waves[d][i][j][v] + H4 * jump_right
                acc[i][j] = acc[i][j] + damp * jump_right
                i, j = (0, m) if d == 0 else (m, 0)
                waves[d][i][j][v] = waves[d][i][j][v] - H4 * jump_left
                acc[i][j] = acc[i][j] + damp * jump_left
        beside = []
        for j in range(2):
            turned = [sroll(trace_z[j][i], 4) for i in range(2)]
            beside.append([jnp.where(low_c, lroll(t, 1), lroll(t, -1)) for t in turned])
        for i in range(2):
            for j in range(2):
                jump = jnp.where(flags[2], beside[j][1 - i], beside[j][i]) - trace_z[j][i]
                waves[2][i][j][v] = flux_z[j][i] + sign * jump
                acc_ref[v, i, j] = acc[i][j] + damp * jump
    for d in range(3):
        matrix = [[jac_ref[25 * d + 5 * o + i] for i in range(5)] for o in range(5)]
        for i in range(2):
            for j in range(2):
                for v, value in enumerate(mix(matrix, waves[d][i][j])):
                    acc_ref[v, i, j] = acc_ref[v, i, j] - value


def add_remote(field, scale, flag_ref, face_ref, rxo, rxe, ryo, rye):
    for d, axis in ((0, "gx"), (1, "gy")):
        is_even = parity(axis)
        low, step = axis_low(d)
        flag = flag_ref[d]
        flag = jnp.where(low, sroll(flag, -step), flag) != 0
        even, odd = ((rxe, rxo), (rye, ryo))[d]
        at = (lambda n, m: (n, m)) if d == 0 else (lambda n, m: (m, n))
        right, left = [], []
        for v in range(5):
            value = scale * jnp.where(is_even, even[v], odd[v])
            swapped = jnp.where(low, sroll(value, -step), sroll(value, step))
            right.append(jnp.where(flag, swapped, value))
            left.append(scale * jnp.where(is_even, odd[v], even[v]))
        upper = [[face_ref[2 * d, 5 * o + i] for i in range(5)] for o in range(5)]
        lower = [[face_ref[2 * d + 1, 5 * o + i] for i in range(5)] for o in range(5)]
        for v, value in enumerate(mix(upper, right)):
            for m, part in enumerate((sroll(value, step), value)):
                i, j = at(1, m)
                field[v][i][j] = field[v][i][j] - jnp.where(low, 0.0, part)
        for v, value in enumerate(mix(lower, left)):
            for m, part in enumerate((value, sroll(value, -step))):
                i, j = at(0, m)
                field[v][i][j] = field[v][i][j] + jnp.where(low, part, 0.0)


def restrict_kernel(
    acc_ref, flag_ref, face_ref, smooth_ref, rxo, rxe, ryo, rye, rhs_ref, c_ref, xo, xe, yo, ye
):
    rhs = [[[acc_ref[v, i, j] for j in range(2)] for i in range(2)] for v in range(5)]
    add_remote(rhs, 1.0, flag_ref, face_ref, rxo, rxe, ryo, rye)
    c = coarse_smooth(smooth_ref, rhs)
    for v in range(5):
        for i in range(2):
            for j in range(2):
                rhs_ref[v, i, j] = rhs[v][i][j]
                c_ref[v, i, j] = c[v][i][j]
    coarse_faces(c, flag_ref, xo, xe, yo, ye)


def coarse_local_kernel(c_ref, rhs_ref, smooth_ref, flag_ref, jac_ref, damp_ref, out_ref):
    damp = 0.5 * damp_ref[...]
    c = [[[c_ref[v, i, j] for j in range(2)] for i in range(2)] for v in range(5)]
    acc = [[[rhs_ref[v, i, j] - 2.0 * c[v][i][j] for j in range(2)] for i in range(2)] for v in range(5)]
    for d in range(2):
        low, step = axis_low(d)
        flag = flag_ref[d] != 0
        flag_before = sroll(flag_ref[d], step) != 0
        matrix = [[jac_ref[25 * d + 5 * o + i] for i in range(5)] for o in range(5)]
        at = (lambda n, m: (n, m)) if d == 0 else (lambda n, m: (m, n))
        waves = [[[None] * 5, [None] * 5] for _ in range(2)]
        for v in range(5):
            lo = [c[v][at(0, m)[0]][at(0, m)[1]] for m in range(2)]
            hi = [c[v][at(1, m)[0]][at(1, m)[1]] for m in range(2)]
            for m in range(2):
                right = jnp.where(low, sroll(jnp.where(flag_before, lo[1 - m], lo[m]), -step), 0.0)
                left = jnp.where(low, 0.0, sroll(jnp.where(flag, hi[1 - m], hi[m]), step))
                waves[1][m][v] = 0.5 * (right - lo[m])
                waves[0][m][v] = 0.5 * (hi[m] - left)
                i, j = at(1, m)
                acc[v][i][j] = acc[v][i][j] + damp * (right - hi[m])
                i, j = at(0, m)
                acc[v][i][j] = acc[v][i][j] + damp * (left - lo[m])
        for n in range(2):
            for m in range(2):
                i, j = at(n, m)
                for v, value in enumerate(mix(matrix, waves[n][m])):
                    acc[v][i][j] = acc[v][i][j] - value
    low = c_low()
    flag = jnp.where(low, lroll(flag_ref[2], 1), flag_ref[2]) != 0
    half = jnp.where(low, 0.5, -0.5).astype(F32)
    matrix = [[jac_ref[50 + 5 * o + i] for i in range(5)] for o in range(5)]
    turned = [[[sroll(c[v][i][j], 4) for j in range(2)] for i in range(2)] for v in range(5)]
    beside = [
        [[jnp.where(low, lroll(t, 1), lroll(t, -1)) for t in turned[v][i]] for i in range(2)] for v in range(5)
    ]
    for i in range(2):
        for j in range(2):
            wave = []
            for v in range(5):
                next_to = jnp.where(flag, beside[v][1 - i][j], beside[v][i][j])
                wave.append(half * (turned[v][i][j] - next_to))
                acc[v][i][j] = acc[v][i][j] + damp * (next_to - c[v][i][j])
            for v, value in enumerate(mix(matrix, wave)):
                acc[v][i][j] = acc[v][i][j] - value
    change = coarse_smooth(smooth_ref, acc)
    for v in range(5):
        for i in range(2):
            for j in range(2):
                out_ref[v, i, j] = c[v][i][j] + change[v][i][j]


def coarse_step(c_ref, smooth_ref, flag_ref, face_ref, rxo, rxe, ryo, rye):
    rest = [[[0.0, 0.0], [0.0, 0.0]] for _ in range(5)]
    add_remote(rest, 1.0 / 6.0, flag_ref, face_ref, rxo, rxe, ryo, rye)
    change = coarse_smooth(smooth_ref, rest)
    return [[[c_ref[v, i, j] + change[v][i][j] for j in range(2)] for i in range(2)] for v in range(5)]


def coarse_kernel(c_ref, smooth_ref, flag_ref, face_ref, rxo, rxe, ryo, rye, out_ref, xo, xe, yo, ye):
    c = coarse_step(c_ref, smooth_ref, flag_ref, face_ref, rxo, rxe, ryo, rye)
    for v in range(5):
        for i in range(2):
            for j in range(2):
                out_ref[v, i, j] = c[v][i][j]
    coarse_faces(c, flag_ref, xo, xe, yo, ye)


def spread(first, second):
    return first, NEAR * first + FAR * second, FAR * first + NEAR * second, second


def last_kernel(
    c_ref, smooth_ref, flag_ref, face_ref, rxo, rxe, ryo, rye, second_ref, out_hbm, out_ref, sems
):
    c = coarse_step(c_ref, smooth_ref, flag_ref, face_ref, rxo, rxe, ryo, rye)
    low = c_low()
    copies = []
    for v in range(5):
        by_c = [[None, None], [None, None]]
        for i in range(2):
            for j in range(2):
                value = c[v][i][j]
                inner = FAR * value + NEAR * sroll(value, 4)
                by_c[i][j] = (jnp.where(low, value, inner), jnp.where(low, inner, value))
        for q in range(2):
            lines = [spread(by_c[i][0][q], by_c[i][1][q]) for i in range(2)]
            for b in range(4):
                for a, value in enumerate(spread(lines[0][b], lines[1][b])):
                    out_ref[v, a, b, q] = second_ref[v, a, b, q] + value
        copy = pltpu.make_async_copy(out_ref.at[v], out_hbm.at[v], sems.at[v])
        copy.start()
        copies.append(copy)
    for copy in copies:
        copy.wait()


FINE = (5, 4, 4, 2, 8, 128)
FINE_MESSAGE = (5, 4, 8, 128)
COARSE = (5, 2, 2, 8, 128)
COARSE_MESSAGE = (5, 8, 128)


def vmem(shape, dtype=F32):
    return pltpu.VMEM(shape, dtype)


def here(array):
    return pltpu.with_memory_space_constraint(array, pltpu.VMEM)


def call(kernel, args, outs, in_hbm=(), out_hbm=(), scratch=(), aliases=None, flops=0):
    in_specs = [
        pl.BlockSpec(memory_space=pltpu.HBM if k in in_hbm else pltpu.VMEM) for k in range(len(args))
    ]
    out_specs = [
        pl.BlockSpec(memory_space=pltpu.HBM if k in out_hbm else pltpu.VMEM) for k in range(len(outs))
    ]
    args = [pltpu.with_memory_space_constraint(a, pltpu.HBM) if k in in_hbm else here(a) for k, a in enumerate(args)]
    return pl.pallas_call(
        kernel,
        out_shape=outs,
        in_specs=in_specs,
        out_specs=out_specs,
        scratch_shapes=scratch,
        input_output_aliases=aliases or {},
        compiler_params=pltpu.CompilerParams(vmem_limit_bytes=8 * 2**20),
        cost_estimate=pl.CostEstimate(flops=flops, bytes_accessed=4 * 2**20, transcendentals=0),
    )(*args)


def partners(axis):
    size = lax.axis_size(axis)
    even = [(i, i ^ 1) for i in range(size)]
    odd = [(i, (i - 1) % size if i % 2 == 0 else (i + 1) % size) for i in range(size)]
    return even, odd


def exchange_x(xo, xe):
    even, odd = partners("gx")
    return lax.ppermute(xo, "gx", odd), lax.ppermute(xe, "gx", even)


def exchange_y(yo, ye):
    even, odd = partners("gy")
    return lax.ppermute(yo, "gy", odd), lax.ppermute(ye, "gy", even)


def exchange(xo, xe, yo, ye):
    return *exchange_x(xo, xe), *exchange_y(yo, ye)


def local_sweep(coarse, *rest):
    (out,) = call(coarse_local_kernel, (coarse, *rest), [vmem(COARSE)], flops=4 * 2**20)
    return out


def body(source, jacobian, damping, orient, smoother, coarse_smoother):
    source = source.reshape(FINE)
    smoother = smoother.reshape(25, 4, 4, 16, 128)
    coarse_smoother = coarse_smoother.reshape(25, 2, 16, 128)
    jacobian = jacobian.reshape(75, 4, 128)
    damping = damping.reshape(4, 128)
    orient = orient.reshape(3, 4, 128)
    fine_messages = [vmem(FINE_MESSAGE)] * 4
    coarse_messages = [vmem(COARSE_MESSAGE)] * 4

    held = vmem(smoother.shape, smoother.dtype)
    smoother_in = smoother
    source, smoother, first, flag, xo, xe = call(
        first_kernel,
        (source, smoother_in, orient),
        [vmem(FINE), held, vmem(FINE), vmem((3, 8, 128), jnp.int32)] + fine_messages[:2],
        in_hbm=(0, 1, 2),
        scratch=[pltpu.SemaphoreType.DMA((5,)), pltpu.VMEM((3, 4, 128), jnp.int32), pltpu.SemaphoreType.DMA],
        flops=2 * 25 * 64 * 512,
    )
    got_x = exchange_x(xo, xe)
    first, yo, ye = call(
        first_y_kernel,
        (source, smoother, first, flag),
        [vmem(FINE)] + fine_messages[:2],
        aliases={2: 0},
        flops=25 * 64 * 512,
    )
    got = (*got_x, *exchange_y(yo, ye))
    smoother, first, acc, jac8, damp8, face, second = call(
        first_volume_kernel,
        (smoother_in, source, smoother, first, flag, jacobian, damping),
        [held, vmem(FINE), vmem(FINE), vmem((75, 8, 128)), vmem((8, 128)), vmem((4, 25, 8, 128)), vmem(FINE)],
        in_hbm=(0,),
        aliases={2: 0, 3: 1},
        scratch=[pltpu.SemaphoreType.DMA],
        flops=9 * 2**20,
    )
    second, *sent = call(
        second_kernel,
        (acc, first, smoother, flag, face, *got, second),
        [vmem(FINE)] + coarse_messages,
        aliases={9: 0},
        scratch=[pltpu.VMEM((4, 5, 4, 2, 8, 128), F32)],
        flops=3 * 2**20,
    )
    got = exchange(*sent)
    (acc,) = call(restricted_volume_kernel, (source, second, flag, jac8, damp8), [vmem(COARSE)], flops=4 * 2**20)
    rhs, coarse, *sent = call(
        restrict_kernel,
        (acc, flag, face, coarse_smoother, *got),
        [vmem(COARSE), vmem(COARSE)] + coarse_messages,
        flops=2**20,
    )
    got = exchange(*sent)
    coarse = local_sweep(coarse, rhs, coarse_smoother, flag, jac8, damp8)
    coarse, *sent = call(
        coarse_kernel,
        (coarse, coarse_smoother, flag, face, *got),
        [vmem(COARSE)] + coarse_messages,
        flops=2**20,
    )
    got = exchange(*sent)
    coarse = local_sweep(coarse, rhs, coarse_smoother, flag, jac8, damp8)
    (out,) = call(
        last_kernel,
        (coarse, coarse_smoother, flag, face, *got, second),
        [jax.ShapeDtypeStruct(FINE, F32)],
        out_hbm=(0,),
        scratch=[pltpu.VMEM(FINE, F32), pltpu.SemaphoreType.DMA((5,))],
        flops=2**20,
    )
    return out.reshape(5, 4, 4, 4, 2, 2, 128)


def solution(mesh):
    in_specs = (
        P(None, None, None, None, "gx", "gy", None),
        P(None, None, None, "gx", "gy", None),
        P("gx", "gy", None),
        P(None, "gx", "gy", None),
        P(None, None, None, None, None, "gx", "gy", None),
        P(None, None, None, None, None, "gx", "gy", None),
    )
    out_specs = P(None, None, None, None, "gx", "gy", None)
    return jax.shard_map(body, mesh=mesh, in_specs=in_specs, out_specs=out_specs, check_vma=False)
```

```python
import functools
import math

import jax
import jax.numpy as jnp
import numpy as np
from jax import lax
from jax.experimental import pallas as pl
from jax.experimental.pallas import tpu as pltpu
from jax.sharding import PartitionSpec as P


F32 = jnp.float32
OMEGA = 0.8
FACE_LINES = [(a, b) for a in range(4) for b in range(4) if a in (0, 3) or b in (0, 3)]
H4 = 3.0
ROOT = 1.0 / math.sqrt(5.0)
NEAR = (1.0 + ROOT) / 2.0
FAR = (1.0 - ROOT) / 2.0


def lobatto_slopes():
    points = np.array([-1.0, -ROOT, ROOT, 1.0])
    weights = np.ones(4)
    for i in range(4):
        for j in range(4):
            if i != j:
                weights[i] = weights[i] / (points[i] - points[j])
    slopes = np.zeros((4, 4))
    for i in range(4):
        for j in range(4):
            if i != j:
                slopes[i, j] = weights[j] / weights[i] / (points[i] - points[j])
        slopes[i, i] = -np.sum(slopes[i])
    return slopes


D4 = lobatto_slopes()
PD = np.array([[1.0, NEAR, FAR, 0.0], [0.0, FAR, NEAR, 1.0]]) @ D4


def sum_of(terms):
    total = None
    for weight, value in terms:
        total = weight * value if total is None else total + weight * value
    return total


def rows():
    return lax.broadcasted_iota(jnp.int32, (8, 128), 0)


def x_low():
    return (rows() & 2) == 0


def y_low():
    return (rows() & 1) == 0


def c_low():
    return (rows() & 4) == 0


def sroll(value, shift):
    return pltpu.roll(value, shift % 8, 0)


def lroll(value, shift):
    return pltpu.roll(value, shift % 128, 1)


def twice(value):
    return jnp.concatenate([value, value], axis=0)


def axis_low(direction):
    return (x_low(), 2) if direction == 0 else (y_low(), 1)


def pack_low(first, second, direction):
    low, step = axis_low(direction)
    return jnp.where(low, first, sroll(second, step))


def pack_high(first, second, direction):
    low, step = axis_low(direction)
    return jnp.where(low, sroll(first, -step), second)


def slopes_along(u0, u1, u2, u3):
    e0, o0, e1, o1 = u0 + u3, u0 - u3, u1 + u2, u1 - u2
    diff = e1 - e0
    even_a = float((D4[0, 1] + D4[0, 2]) / 2.0) * diff
    even_b = float((D4[1, 2] - 0.0) / 2.0) * diff
    odd_a = float((D4[0, 0] - D4[0, 3]) / 2.0) * o0 + float((D4[0, 1] - D4[0, 2]) / 2.0) * o1
    odd_b = float((D4[1, 0] - D4[1, 3]) / 2.0) * o0 - float(D4[1, 2] / 2.0) * o1
    return even_a + odd_a, even_b + odd_b, odd_b - even_b, odd_a - even_a


def mix(matrix, fields):
    out = []
    for o in range(5):
        total = matrix[o][0] * fields[0]
        for i in range(1, 5):
            total = total + matrix[o][i] * fields[i]
        out.append(total)
    return out


def parity(axis):
    return lax.rem(lax.axis_index(axis), 2) == 0


def put_pair(even_ref, odd_ref, index, low_face, high_face, is_even):
    even_ref[index] = jnp.where(is_even, high_face, low_face)
    odd_ref[index] = jnp.where(is_even, low_face, high_face)


def fine_faces(u_ref, flag_ref, xo, xe, yo, ye):
    even_x, even_y = parity("gx"), parity("gy")
    fx, fy = flag_ref[0] != 0, flag_ref[1] != 0
    for v in range(5):
        for n in range(4):
            low = pack_low(u_ref[v, 0, n, 0], u_ref[v, 0, n, 1], 0)
            h = [jnp.where(fx, u_ref[v, 3, 3 - n, q], u_ref[v, 3, n, q]) for q in range(2)]
            put_pair(xe, xo, (v, n), low, pack_high(h[0], h[1], 0), even_x)
            low = pack_low(u_ref[v, n, 0, 0], u_ref[v, n, 0, 1], 1)
            h = [jnp.where(fy, u_ref[v, 3 - n, 3, q], u_ref[v, n, 3, q]) for q in range(2)]
            put_pair(ye, yo, (v, n), low, pack_high(h[0], h[1], 1), even_y)


def restrict_c(first, second):
    low = c_low()
    middle = jnp.where(low, second, first)
    return jnp.where(low, first, second) + FAR * middle + NEAR * sroll(middle, 4)


def restrict_four(values):
    return values[0] + NEAR * values[1] + FAR * values[2], values[3] + NEAR * values[2] + FAR * values[1]


def put_coarse_faces(v, lows, highs, flag_ref, pairs):
    for d, axis in ((0, "gx"), (1, "gy")):
        flag = flag_ref[d] != 0
        low, high = lows[d], highs[d]
        turned = [jnp.where(flag, high[1 - m], high[m]) for m in range(2)]
        even_ref, odd_ref = pairs[d]
        put_pair(even_ref, odd_ref, v, pack_low(*low, d), pack_high(*turned, d), parity(axis))


def restricted_faces(u_ref, flag_ref, xo, xe, yo, ye):
    for v in range(5):
        line = {}
        for a in range(4):
            for b in range(4):
                if a in (0, 3) or b in (0, 3):
                    line[a, b] = restrict_c(u_ref[v, a, b, 0], u_ref[v, a, b, 1])
        lows = [restrict_four([line[0, n] for n in range(4)]), restrict_four([line[n, 0] for n in range(4)])]
        highs = [restrict_four([line[3, n] for n in range(4)]), restrict_four([line[n, 3] for n in range(4)])]
        put_coarse_faces(v, lows, highs, flag_ref, ((xe, xo), (ye, yo)))


def smoothed(smooth_ref, fields, a, b):
    out = []
    for o in range(5):
        total = [None, None]
        for i in range(5):
            block = smooth_ref[5 * o + i, a, b].astype(F32)
            for q in range(2):
                term = block[8 * q : 8 * q + 8] * fields[i][q]
                total[q] = term if i == 0 else total[q] + term
        out.append([OMEGA * total[q] for q in range(2)])
    return out


def first_line(src_ref, smooth_ref, u_ref, a, b):
    value = smoothed(smooth_ref, [[src_ref[v, a, b, q] for q in range(2)] for v in range(5)], a, b)
    for v in range(5):
        for q in range(2):
            u_ref[v, a, b, q] = value[v][q]


def line_copy(smooth_hbm, smooth_ref, sem, a, b):
    return pltpu.make_async_copy(smooth_hbm.at[:, a, b], smooth_ref.at[:, a, b], sem)


def first_kernel(
    src_hbm, smooth_hbm, orient_hbm, src_ref, smooth_ref, u_ref, flag_ref, xo, xe, yo, ye, sems, orient_ref, orient_sem
):
    every, inner = slice(0, 4), slice(1, 3)
    src_copy = pltpu.make_async_copy(src_hbm, src_ref, sems.at[4])
    src_copy.start()
    copies = [
        line_copy(smooth_hbm, smooth_ref, sems.at[slot], a, b)
        for slot, (a, b) in enumerate(((0, every), (3, every), (inner, 0), (inner, 3)))
    ]
    for one in copies:
        one.start()
    orient_copy = pltpu.make_async_copy(orient_hbm, orient_ref, orient_sem)
    orient_copy.start()
    orient_copy.wait()
    for d in range(3):
        flag_ref[d] = twice(orient_ref[d])
    lines = [[(0, b) for b in range(4)], [(3, b) for b in range(4)], [(1, 0), (2, 0)], [(1, 3), (2, 3)]]
    src_copy.wait()
    for one, group in zip(copies, lines):
        one.wait()
        for a, b in group:
            first_line(src_ref, smooth_ref, u_ref, a, b)
    fine_faces(u_ref, flag_ref, xo, xe, yo, ye)


def prepare_tables(jac_ref, damp_ref, jac8_ref, damp8_ref, face_ref):
    damp = twice(damp_ref[...])
    damp8_ref[...] = damp
    for d in range(3):
        for k in range(25):
            value = twice(jac_ref[25 * d + k])
            jac8_ref[25 * d + k] = value
            if d < 2:
                low, step = axis_low(d)
                diagonal = k % 6 == 0
                upper = H4 * (value - damp if diagonal else value)
                lower = H4 * (value + damp if diagonal else value)
                face_ref[2 * d, k] = jnp.where(low, sroll(upper, -step), upper)
                face_ref[2 * d + 1, k] = jnp.where(low, lower, sroll(lower, step))


def volume(src_ref, u_ref, flag_ref, jac_ref, damp_ref, acc_ref, finish_lines):
    damp = H4 * damp_ref[...]

    def jacobian(d):
        return [[jac_ref[25 * d + 5 * o + i] for i in range(5)] for o in range(5)]

    def along(direction, others):
        low, step = axis_low(direction)
        flag = flag_ref[direction] != 0
        flag_before = sroll(flag_ref[direction], step) != 0

        def at(v, n, other, q):
            return (v, n, other, q) if direction == 0 else (v, other, n, q)

        def step_fn(j, carry):
            other, q = others(j // 2), j % 2
            u = [[u_ref[at(v, n, other, q)] for n in range(4)] for v in range(5)]
            waves = []
            jumps = []
            for v in range(5):
                back_low, back_high = u_ref[at(v, 0, 3 - other, q)], u_ref[at(v, 3, 3 - other, q)]
                right = sroll(jnp.where(flag_before, back_low, u[v][0]), -step)
                left = sroll(jnp.where(flag, back_high, u[v][3]), step)
                jump_right = jnp.where(low, right, 0.0) - u[v][3]
                jump_left = jnp.where(low, 0.0, left) - u[v][0]
                w = list(slopes_along(*u[v]))
                w[3] = w[3] + H4 * jump_right
                w[0] = w[0] - H4 * jump_left
                waves.append(w)
                jumps.append((damp * jump_left, None, None, damp * jump_right))
            matrix = jacobian(direction)
            for n in range(4):
                flux = mix(matrix, [waves[v][n] for v in range(5)])
                for v in range(5):
                    if direction == 1:
                        total = src_ref[at(v, n, other, q)] - 2.0 * u[v][n]
                    else:
                        total = acc_ref[at(v, n, other, q)]
                    total = total - flux[v]
                    if jumps[v][n] is not None:
                        total = total + jumps[v][n]
                    acc_ref[at(v, n, other, q)] = total
            return carry

        return step_fn

    low = c_low()
    flag = jnp.where(low, lroll(flag_ref[2], 1), flag_ref[2]) != 0
    damp_z = damp
    coef = [
        [jnp.where(low, float(D4[2 * p, c]), float(D4[2 * p + 1, c ^ 1])).astype(F32) for c in range(4)]
        for p in range(2)
    ]

    def step_z(j, carry):
        a0, b = j // 4, j % 4
        here = (a0, 3 - a0)
        u = [[[u_ref[v, a, b, q] for q in range(2)] for v in range(5)] for a in here]
        turned = [[[sroll(u[s][v][q], 4) for q in range(2)] for v in range(5)] for s in range(2)]
        beside = []
        for s in range(2):
            line = []
            for v in range(5):
                face = jnp.where(low, turned[s][v][1], turned[s][v][0])
                line.append(jnp.where(low, lroll(face, 1), lroll(face, -1)))
            beside.append(line)
        matrix = jacobian(2)
        for s in range(2):
            waves = [[], []]
            jumps = []
            for v in range(5):
                own = jnp.where(low, u[s][v][0], u[s][v][1])
                jump = jnp.where(flag, beside[1 - s][v], beside[s][v]) - own
                jumps.append(damp_z * jump)
                lifted = H4 * jump
                for p in range(2):
                    w = coef[p][0] * u[s][v][0] + coef[p][1] * turned[s][v][0]
                    w = w + (coef[p][2] * u[s][v][1] + coef[p][3] * turned[s][v][1])
                    w = w - jnp.where(low, lifted, 0.0) if p == 0 else w + jnp.where(low, 0.0, lifted)
                    waves[p].append(w)
            for p in range(2):
                flux = mix(matrix, waves[p])
                for v in range(5):
                    part = jnp.where(low, jumps[v], 0.0) if p == 0 else jnp.where(low, 0.0, jumps[v])
                    acc_ref[v, here[s], b, p] = acc_ref[v, here[s], b, p] - flux[v] + part
        return carry

    lax.fori_loop(0, 4, along(1, lambda k: 3 * k), 0)
    lax.fori_loop(0, 4, step_z, 0)
    finish_lines()
    lax.fori_loop(0, 4, along(1, lambda k: 1 + k), 0)
    lax.fori_loop(4, 8, step_z, 0)
    lax.fori_loop(0, 8, along(0, lambda k: k), 0)


def first_volume_kernel(
    smooth_hbm, src_ref, smooth_in, u_in, flag_ref, jac_ref, damp_ref,
    smooth_ref, u_ref, acc_ref, jac8_ref, damp8_ref, face_ref, second_ref, scaled_ref, sem,
):
    inner = slice(1, 3)
    copy = line_copy(smooth_hbm, smooth_ref, sem, inner, inner)
    copy.start()
    prepare_tables(jac_ref, damp_ref, jac8_ref, damp8_ref, face_ref)
    lines = [(a, b) for a in (1, 2) for b in (1, 2)]

    def finish_lines():
        copy.wait()
        for a, b in lines:
            first_line(src_ref, smooth_ref, u_ref, a, b)

    volume(src_ref, u_ref, flag_ref, jac8_ref, damp8_ref, acc_ref, finish_lines)
    for a, b in lines:
        change = smoothed(smooth_ref, [[acc_ref[v, a, b, q] for q in range(2)] for v in range(5)], a, b)
        for v in range(5):
            for q in range(2):
                second_ref[v, a, b, q] = u_ref[v, a, b, q] + change[v][q]
    for line, (a, b) in enumerate(FACE_LINES):
        for k in range(25):
            block = OMEGA * smooth_ref[k, a, b].astype(F32)
            for q in range(2):
                scaled_ref[line, k, q] = block[8 * q : 8 * q + 8]


def remote_parts(even_refs, odd_refs, flag_ref, face_ref, part_ref):
    for d, axis in ((0, "gx"), (1, "gy")):
        is_even = parity(axis)
        low, step = axis_low(d)
        flag = flag_ref[d]
        flag = jnp.where(low, sroll(flag, -step), flag) != 0
        even, odd = even_refs[d], odd_refs[d]
        matrix = [[face_ref[2 * d, 5 * o + i] for i in range(5)] for o in range(5)]
        for n in range(4):
            take = lambda v, m: jnp.where(is_even, even[v, m], odd[v, m])
            right = [jnp.where(flag, take(v, 3 - n), take(v, n)) for v in range(5)]
            for v, value in enumerate(mix(matrix, right)):
                part_ref[2 * d, v, n, 0] = jnp.where(low, 0.0, -sroll(value, step))
                part_ref[2 * d, v, n, 1] = jnp.where(low, 0.0, -value)
        matrix = [[face_ref[2 * d + 1, 5 * o + i] for i in range(5)] for o in range(5)]
        for n in range(4):
            left = [jnp.where(is_even, odd[v, n], even[v, n]) for v in range(5)]
            for v, value in enumerate(mix(matrix, left)):
                part_ref[2 * d + 1, v, n, 0] = jnp.where(low, value, 0.0)
                part_ref[2 * d + 1, v, n, 1] = jnp.where(low, sroll(value, -step), 0.0)


def whole(acc_ref, part_ref, v, a, b, q):
    total = acc_ref[v, a, b, q]
    if a == 3:
        total = total + part_ref[0, v, b, q]
    if a == 0:
        total = total + part_ref[1, v, b, q]
    if b == 3:
        total = total + part_ref[2, v, a, q]
    if b == 0:
        total = total + part_ref[3, v, a, q]
    return total


def second_kernel(
    acc_ref, u_ref, scaled_ref, flag_ref, face_ref, rxo, rxe, ryo, rye, inner_ref, out_ref, xo, xe, yo, ye, part_ref
):
    remote_parts((rxe, rye), (rxo, ryo), flag_ref, face_ref, part_ref)
    for line, (a, b) in enumerate(FACE_LINES):
        for q in range(2):
            left = [whole(acc_ref, part_ref, v, a, b, q) for v in range(5)]
            matrix = [[scaled_ref[line, 5 * o + i, q] for i in range(5)] for o in range(5)]
            for v, value in enumerate(mix(matrix, left)):
                out_ref[v, a, b, q] = u_ref[v, a, b, q] + value
    restricted_faces(out_ref, flag_ref, xo, xe, yo, ye)


def coarse_smooth(smooth_ref, fields):
    out = [[[None, None], [None, None]] for _ in range(5)]
    for i in range(2):
        for o in range(5):
            total = [None, None]
            for k in range(5):
                block = smooth_ref[5 * o + k, i].astype(F32)
                for j in range(2):
                    term = block[8 * j : 8 * j + 8] * fields[k][i][j]
                    total[j] = term if k == 0 else total[j] + term
            for j in range(2):
                out[o][i][j] = OMEGA * total[j]
    return out


def coarse_faces(field, flag_ref, xo, xe, yo, ye):
    for v in range(5):
        c = field[v]
        lows = [[c[0][0], c[0][1]], [c[0][0], c[1][0]]]
        highs = [[c[1][0], c[1][1]], [c[0][1], c[1][1]]]
        put_coarse_faces(v, lows, highs, flag_ref, ((xe, xo), (ye, yo)))


def response_kernel(smooth_ref, face_ref, response_ref):
    packed = []
    for k in range(25):
        by_i = [smooth_ref[k, i].astype(F32) for i in range(2)]
        node = [[by_i[i][8 * j : 8 * j + 8] for j in range(2)] for i in range(2)]
        packed.append(
            (
                pack_high(node[1][0], node[1][1], 0),
                pack_low(node[0][0], node[0][1], 0),
                pack_high(node[0][1], node[1][1], 1),
                pack_low(node[0][0], node[1][0], 1),
            )
        )
    for f in range(4):
        for o in range(5):
            for i in range(5):
                total = packed[5 * o][f] * face_ref[f, i]
                for k in range(1, 5):
                    total = total + packed[5 * o + k][f] * face_ref[f, 5 * k + i]
                response_ref[f, 5 * o + i] = (OMEGA / 6.0) * total


def restricted_volume_kernel(src_ref, u_ref, flag_ref, jac_ref, damp_ref, smooth_ref, acc_ref, c_ref):
    damp = H4 * damp_ref[...]
    low_c = c_low()
    slope = [
        jnp.where(low_c, float(PD[0, c]), float(PD[1, c ^ 1])).astype(F32) for c in range(4)
    ]
    flags = [flag_ref[0] != 0, flag_ref[1] != 0, jnp.where(low_c, lroll(flag_ref[2], 1), flag_ref[2]) != 0]
    sign = jnp.where(low_c, -H4, H4).astype(F32)
    waves = [[[[None] * 5 for _ in range(2)] for _ in range(2)] for _ in range(3)]

    def slopes_four(values):
        return [sum_of([(float(PD[i, n]), values[n]) for n in range(4)]) for i in range(2)]

    for v in range(5):
        line, slope_c, ends = {}, {}, {}
        for a in range(4):
            for b in range(4):
                first, second = u_ref[v, a, b, 0], u_ref[v, a, b, 1]
                line[a, b] = restrict_c(first, second)
                slope_c[a, b] = (slope[0] * first + slope[1] * sroll(first, 4)) + (
                    slope[2] * second + slope[3] * sroll(second, 4)
                )
                ends[a, b] = jnp.where(low_c, first, second)

        def along_b(table):
            return [restrict_four([table[a, b] for b in range(4)]) for a in range(4)]

        def both(table):
            by_b = along_b(table)
            return [restrict_four([by_b[a][j] for a in range(4)]) for j in range(2)]

        by_b = along_b(line)
        by_a = [restrict_four([line[a, b] for a in range(4)]) for b in range(4)]
        flux_z = both(slope_c)
        trace_z = both(ends)
        sources = both({(a, b): restrict_c(src_ref[v, a, b, 0], src_ref[v, a, b, 1]) for a in range(4) for b in range(4)})
        acc = [[None, None], [None, None]]
        for j in range(2):
            value = restrict_four([by_b[a][j] for a in range(4)])
            flux = slopes_four([by_b[a][j] for a in range(4)])
            for i in range(2):
                acc[i][j] = sources[j][i] - 2.0 * value[i]
                waves[0][i][j][v] = flux[i]
        for i in range(2):
            flux = slopes_four([by_a[b][i] for b in range(4)])
            for j in range(2):
                waves[1][i][j][v] = flux[j]
        for d, lo, hi in ((0, by_b[0], by_b[3]), (1, by_a[0], by_a[3])):
            low, step = axis_low(d)
            flag = flags[d]
            flag_before = sroll(flag_ref[d], step) != 0
            for m in range(2):
                right = sroll(jnp.where(flag_before, lo[1 - m], lo[m]), -step)
                left = sroll(jnp.where(flag, hi[1 - m], hi[m]), step)
                jump_right = jnp.where(low, right, 0.0) - hi[m]
                jump_left = jnp.where(low, 0.0, left) - lo[m]
                i, j = (1, m) if d == 0 else (m, 1)
                waves[d][i][j][v] = waves[d][i][j][v] + H4 * jump_right
                acc[i][j] = acc[i][j] + damp * jump_right
                i, j = (0, m) if d == 0 else (m, 0)
                waves[d][i][j][v] = waves[d][i][j][v] - H4 * jump_left
                acc[i][j] = acc[i][j] + damp * jump_left
        beside = []
        for j in range(2):
            turned = [sroll(trace_z[j][i], 4) for i in range(2)]
            beside.append([jnp.where(low_c, lroll(t, 1), lroll(t, -1)) for t in turned])
        for i in range(2):
            for j in range(2):
                jump = jnp.where(flags[2], beside[j][1 - i], beside[j][i]) - trace_z[j][i]
                waves[2][i][j][v] = flux_z[j][i] + sign * jump
                acc_ref[v, i, j] = acc[i][j] + damp * jump
    for d in range(3):
        matrix = [[jac_ref[25 * d + 5 * o + i] for i in range(5)] for o in range(5)]
        for i in range(2):
            for j in range(2):
                for v, value in enumerate(mix(matrix, waves[d][i][j])):
                    acc_ref[v, i, j] = acc_ref[v, i, j] - value
    c = coarse_smooth(smooth_ref, [[[acc_ref[v, i, j] for j in range(2)] for i in range(2)] for v in range(5)])
    put_field(c_ref, c)


def put_field(out_ref, c):
    for v in range(5):
        for i in range(2):
            for j in range(2):
                out_ref[v, i, j] = c[v][i][j]


def get_field(ref):
    return [[[ref[v, i, j] for j in range(2)] for i in range(2)] for v in range(5)]


def add_remote(field, scale, flag_ref, face_ref, rxo, rxe, ryo, rye):
    for d, axis in ((0, "gx"), (1, "gy")):
        is_even = parity(axis)
        low, step = axis_low(d)
        flag = flag_ref[d]
        flag = jnp.where(low, sroll(flag, -step), flag) != 0
        even, odd = ((rxe, rxo), (rye, ryo))[d]
        at = (lambda n, m: (n, m)) if d == 0 else (lambda n, m: (m, n))
        right, left = [], []
        for v in range(5):
            value = scale * jnp.where(is_even, even[v], odd[v])
            swapped = jnp.where(low, sroll(value, -step), sroll(value, step))
            right.append(jnp.where(flag, swapped, value))
            left.append(scale * jnp.where(is_even, odd[v], even[v]))
        upper = [[face_ref[2 * d, 5 * o + i] for i in range(5)] for o in range(5)]
        lower = [[face_ref[2 * d + 1, 5 * o + i] for i in range(5)] for o in range(5)]
        for v, value in enumerate(mix(upper, right)):
            for m, part in enumerate((sroll(value, step), value)):
                i, j = at(1, m)
                field[v][i][j] = field[v][i][j] - jnp.where(low, 0.0, part)
        for v, value in enumerate(mix(lower, left)):
            for m, part in enumerate((value, sroll(value, -step))):
                i, j = at(0, m)
                field[v][i][j] = field[v][i][j] + jnp.where(low, part, 0.0)


def restrict_kernel(local_ref, flag_ref, response_ref, rxo, rxe, ryo, rye, c_ref, xo, xe, yo, ye):
    c = get_field(local_ref)
    add_remote(c, 6.0, flag_ref, response_ref, rxo, rxe, ryo, rye)
    put_field(c_ref, c)
    coarse_faces(c, flag_ref, xo, xe, yo, ye)


def first_local_kernel(
    c_ref, acc_ref, smooth_ref, flag_ref, jac_ref, damp_ref, face_ref, rxo, rxe, ryo, rye, out_ref, rhs_ref
):
    rhs = get_field(acc_ref)
    add_remote(rhs, 1.0, flag_ref, face_ref, rxo, rxe, ryo, rye)
    put_field(rhs_ref, rhs)
    coarse_local_kernel(c_ref, rhs_ref, smooth_ref, flag_ref, jac_ref, damp_ref, out_ref)


def coarse_local_kernel(c_ref, rhs_ref, smooth_ref, flag_ref, jac_ref, damp_ref, out_ref):
    damp = 0.5 * damp_ref[...]
    c = [[[c_ref[v, i, j] for j in range(2)] for i in range(2)] for v in range(5)]
    acc = [[[rhs_ref[v, i, j] - 2.0 * c[v][i][j] for j in range(2)] for i in range(2)] for v in range(5)]
    for d in range(2):
        low, step = axis_low(d)
        flag = flag_ref[d] != 0
        flag_before = sroll(flag_ref[d], step) != 0
        matrix = [[jac_ref[25 * d + 5 * o + i] for i in range(5)] for o in range(5)]
        at = (lambda n, m: (n, m)) if d == 0 else (lambda n, m: (m, n))
        waves = [[[None] * 5, [None] * 5] for _ in range(2)]
        for v in range(5):
            lo = [c[v][at(0, m)[0]][at(0, m)[1]] for m in range(2)]
            hi = [c[v][at(1, m)[0]][at(1, m)[1]] for m in range(2)]
            for m in range(2):
                right = jnp.where(low, sroll(jnp.where(flag_before, lo[1 - m], lo[m]), -step), 0.0)
                left = jnp.where(low, 0.0, sroll(jnp.where(flag, hi[1 - m], hi[m]), step))
                waves[1][m][v] = 0.5 * (right - lo[m])
                waves[0][m][v] = 0.5 * (hi[m] - left)
                i, j = at(1, m)
                acc[v][i][j] = acc[v][i][j] + damp * (right - hi[m])
                i, j = at(0, m)
                acc[v][i][j] = acc[v][i][j] + damp * (left - lo[m])
        for n in range(2):
            for m in range(2):
                i, j = at(n, m)
                for v, value in enumerate(mix(matrix, waves[n][m])):
                    acc[v][i][j] = acc[v][i][j] - value
    low = c_low()
    flag = jnp.where(low, lroll(flag_ref[2], 1), flag_ref[2]) != 0
    half = jnp.where(low, 0.5, -0.5).astype(F32)
    matrix = [[jac_ref[50 + 5 * o + i] for i in range(5)] for o in range(5)]
    turned = [[[sroll(c[v][i][j], 4) for j in range(2)] for i in range(2)] for v in range(5)]
    beside = [
        [[jnp.where(low, lroll(t, 1), lroll(t, -1)) for t in turned[v][i]] for i in range(2)] for v in range(5)
    ]
    for i in range(2):
        for j in range(2):
            wave = []
            for v in range(5):
                next_to = jnp.where(flag, beside[v][1 - i][j], beside[v][i][j])
                wave.append(half * (turned[v][i][j] - next_to))
                acc[v][i][j] = acc[v][i][j] + damp * (next_to - c[v][i][j])
            for v, value in enumerate(mix(matrix, wave)):
                acc[v][i][j] = acc[v][i][j] - value
    change = coarse_smooth(smooth_ref, acc)
    for v in range(5):
        for i in range(2):
            for j in range(2):
                out_ref[v, i, j] = c[v][i][j] + change[v][i][j]


def coarse_kernel(c_ref, flag_ref, response_ref, rxo, rxe, ryo, rye, out_ref, xo, xe, yo, ye):
    c = get_field(c_ref)
    add_remote(c, 1.0, flag_ref, response_ref, rxo, rxe, ryo, rye)
    put_field(out_ref, c)
    coarse_faces(c, flag_ref, xo, xe, yo, ye)


def spread(first, second):
    return first, NEAR * first + FAR * second, FAR * first + NEAR * second, second


def last_kernel(
    c_ref, flag_ref, response_ref, rxo, rxe, ryo, rye, second_ref, out_hbm, out_ref, sems
):
    c = get_field(c_ref)
    add_remote(c, 1.0, flag_ref, response_ref, rxo, rxe, ryo, rye)
    low = c_low()
    copies = []
    for v in range(5):
        by_c = [[None, None], [None, None]]
        for i in range(2):
            for j in range(2):
                value = c[v][i][j]
                inner = FAR * value + NEAR * sroll(value, 4)
                by_c[i][j] = (jnp.where(low, value, inner), jnp.where(low, inner, value))
        for q in range(2):
            lines = [spread(by_c[i][0][q], by_c[i][1][q]) for i in range(2)]
            for b in range(4):
                for a, value in enumerate(spread(lines[0][b], lines[1][b])):
                    out_ref[v, a, b, q] = second_ref[v, a, b, q] + value
        copy = pltpu.make_async_copy(out_ref.at[v], out_hbm.at[v], sems.at[v])
        copy.start()
        copies.append(copy)
    for copy in copies:
        copy.wait()


FINE = (5, 4, 4, 2, 8, 128)
FINE_MESSAGE = (5, 4, 8, 128)
COARSE = (5, 2, 2, 8, 128)
COARSE_MESSAGE = (5, 8, 128)


def vmem(shape, dtype=F32):
    return pltpu.VMEM(shape, dtype)


def here(array):
    return pltpu.with_memory_space_constraint(array, pltpu.VMEM)


def call(kernel, args, outs, in_hbm=(), out_hbm=(), scratch=(), aliases=None, flops=0):
    in_specs = [
        pl.BlockSpec(memory_space=pltpu.HBM if k in in_hbm else pltpu.VMEM) for k in range(len(args))
    ]
    out_specs = [
        pl.BlockSpec(memory_space=pltpu.HBM if k in out_hbm else pltpu.VMEM) for k in range(len(outs))
    ]
    args = [pltpu.with_memory_space_constraint(a, pltpu.HBM) if k in in_hbm else here(a) for k, a in enumerate(args)]
    return pl.pallas_call(
        kernel,
        out_shape=outs,
        in_specs=in_specs,
        out_specs=out_specs,
        scratch_shapes=scratch,
        input_output_aliases=aliases or {},
        compiler_params=pltpu.CompilerParams(vmem_limit_bytes=8 * 2**20),
        cost_estimate=pl.CostEstimate(flops=flops, bytes_accessed=4 * 2**20, transcendentals=0),
    )(*args)


def partners(axis):
    size = lax.axis_size(axis)
    even = [(i, i ^ 1) for i in range(size)]
    odd = [(i, (i - 1) % size if i % 2 == 0 else (i + 1) % size) for i in range(size)]
    return even, odd


def exchange(xo, xe, yo, ye):
    even_x, odd_x = partners("gx")
    even_y, odd_y = partners("gy")
    xo = lax.ppermute(xo, "gx", odd_x)
    xe = lax.ppermute(xe, "gx", even_x)
    yo = lax.ppermute(yo, "gy", odd_y)
    ye = lax.ppermute(ye, "gy", even_y)
    return xo, xe, yo, ye


def body(source, jacobian, damping, orient, smoother, coarse_smoother):
    source = source.reshape(FINE)
    smoother = smoother.reshape(25, 4, 4, 16, 128)
    coarse_smoother = coarse_smoother.reshape(25, 2, 16, 128)
    jacobian = jacobian.reshape(75, 4, 128)
    damping = damping.reshape(4, 128)
    orient = orient.reshape(3, 4, 128)
    fine_messages = [vmem(FINE_MESSAGE)] * 4
    coarse_messages = [vmem(COARSE_MESSAGE)] * 4

    held = vmem(smoother.shape, smoother.dtype)
    smoother_in = smoother
    source, smoother, first, flag, *sent = call(
        first_kernel,
        (source, smoother_in, orient),
        [vmem(FINE), held, vmem(FINE), vmem((3, 8, 128), jnp.int32)] + fine_messages,
        in_hbm=(0, 1, 2),
        scratch=[pltpu.SemaphoreType.DMA((5,)), pltpu.VMEM((3, 4, 128), jnp.int32), pltpu.SemaphoreType.DMA],
        flops=2 * 25 * 64 * 512,
    )
    got = exchange(*sent)
    _, first, acc, jac8, damp8, face, second, scaled = call(
        first_volume_kernel,
        (smoother_in, source, smoother, first, flag, jacobian, damping),
        [held, vmem(FINE), vmem(FINE), vmem((75, 8, 128)), vmem((8, 128)), vmem((4, 25, 8, 128)), vmem(FINE), vmem((12, 25, 2, 8, 128))],
        in_hbm=(0,),
        aliases={2: 0, 3: 1},
        scratch=[pltpu.SemaphoreType.DMA],
        flops=9 * 2**20,
    )
    second, *sent = call(
        second_kernel,
        (acc, first, scaled, flag, face, *got, second),
        [vmem(FINE)] + coarse_messages,
        aliases={9: 0},
        scratch=[pltpu.VMEM((4, 5, 4, 2, 8, 128), F32)],
        flops=3 * 2**20,
    )
    got = exchange(*sent)
    (response,) = call(response_kernel, (coarse_smoother, face), [vmem((4, 25, 8, 128))], flops=2**20)
    acc, coarse = call(
        restricted_volume_kernel,
        (source, second, flag, jac8, damp8, coarse_smoother),
        [vmem(COARSE), vmem(COARSE)],
        flops=4 * 2**20,
    )
    coarse, *sent = call(
        restrict_kernel, (coarse, flag, response, *got), [vmem(COARSE)] + coarse_messages, flops=2**20
    )
    second_got, got = got, exchange(*sent)
    coarse, rhs = call(
        first_local_kernel,
        (coarse, acc, coarse_smoother, flag, jac8, damp8, face, *second_got),
        [vmem(COARSE), vmem(COARSE)],
        flops=4 * 2**20,
    )
    coarse, *sent = call(
        coarse_kernel, (coarse, flag, response, *got), [vmem(COARSE)] + coarse_messages, flops=2**20
    )
    got = exchange(*sent)
    (coarse,) = call(
        coarse_local_kernel, (coarse, rhs, coarse_smoother, flag, jac8, damp8), [vmem(COARSE)], flops=4 * 2**20
    )
    (out,) = call(
        last_kernel,
        (coarse, flag, response, *got, second),
        [jax.ShapeDtypeStruct(FINE, F32)],
        out_hbm=(0,),
        scratch=[pltpu.VMEM(FINE, F32), pltpu.SemaphoreType.DMA((5,))],
        flops=2**20,
    )
    return out.reshape(5, 4, 4, 4, 2, 2, 128)


def solution(mesh):
    in_specs = (
        P(None, None, None, None, "gx", "gy", None),
        P(None, None, None, "gx", "gy", None),
        P("gx", "gy", None),
        P(None, "gx", "gy", None),
        P(None, None, None, None, None, "gx", "gy", None),
        P(None, None, None, None, None, "gx", "gy", None),
    )
    out_specs = P(None, None, None, None, "gx", "gy", None)
    return jax.shard_map(body, mesh=mesh, in_specs=in_specs, out_specs=out_specs, check_vma=False)
```

```python
import functools
import math

import jax
import jax.numpy as jnp
import numpy as np
from jax import lax
from jax.experimental import pallas as pl
from jax.experimental.pallas import tpu as pltpu
from jax.sharding import PartitionSpec as P


F32 = jnp.float32
OMEGA = 0.8
FACE_LINES = [(a, b) for a in range(4) for b in range(4) if a in (0, 3) or b in (0, 3)]
H4 = 3.0
ROOT = 1.0 / math.sqrt(5.0)
NEAR = (1.0 + ROOT) / 2.0
FAR = (1.0 - ROOT) / 2.0


def lobatto_slopes():
    points = np.array([-1.0, -ROOT, ROOT, 1.0])
    weights = np.ones(4)
    for i in range(4):
        for j in range(4):
            if i != j:
                weights[i] = weights[i] / (points[i] - points[j])
    slopes = np.zeros((4, 4))
    for i in range(4):
        for j in range(4):
            if i != j:
                slopes[i, j] = weights[j] / weights[i] / (points[i] - points[j])
        slopes[i, i] = -np.sum(slopes[i])
    return slopes


D4 = lobatto_slopes()
PD = np.array([[1.0, NEAR, FAR, 0.0], [0.0, FAR, NEAR, 1.0]]) @ D4


def sum_of(terms):
    total = None
    for weight, value in terms:
        total = weight * value if total is None else total + weight * value
    return total


def rows():
    return lax.broadcasted_iota(jnp.int32, (8, 128), 0)


def x_low():
    return (rows() & 2) == 0


def y_low():
    return (rows() & 1) == 0


def c_low():
    return (rows() & 4) == 0


def sroll(value, shift):
    return pltpu.roll(value, shift % 8, 0)


def lroll(value, shift):
    return pltpu.roll(value, shift % 128, 1)


def twice(value):
    return jnp.concatenate([value, value], axis=0)


def axis_low(direction):
    return (x_low(), 2) if direction == 0 else (y_low(), 1)


def pack_low(first, second, direction):
    low, step = axis_low(direction)
    return jnp.where(low, first, sroll(second, step))


def pack_high(first, second, direction):
    low, step = axis_low(direction)
    return jnp.where(low, sroll(first, -step), second)


def slopes_along(u0, u1, u2, u3):
    e0, o0, e1, o1 = u0 + u3, u0 - u3, u1 + u2, u1 - u2
    diff = e1 - e0
    even_a = float((D4[0, 1] + D4[0, 2]) / 2.0) * diff
    even_b = float((D4[1, 2] - 0.0) / 2.0) * diff
    odd_a = float((D4[0, 0] - D4[0, 3]) / 2.0) * o0 + float((D4[0, 1] - D4[0, 2]) / 2.0) * o1
    odd_b = float((D4[1, 0] - D4[1, 3]) / 2.0) * o0 - float(D4[1, 2] / 2.0) * o1
    return even_a + odd_a, even_b + odd_b, odd_b - even_b, odd_a - even_a


def mix(matrix, fields):
    out = []
    for o in range(5):
        total = matrix[o][0] * fields[0]
        for i in range(1, 5):
            total = total + matrix[o][i] * fields[i]
        out.append(total)
    return out


def parity(axis):
    return lax.rem(lax.axis_index(axis), 2) == 0


def put_pair(even_ref, odd_ref, index, low_face, high_face, is_even):
    even_ref[index] = jnp.where(is_even, high_face, low_face)
    odd_ref[index] = jnp.where(is_even, low_face, high_face)


def fine_faces(u_ref, flag_ref, xo, xe, yo, ye):
    even_x, even_y = parity("gx"), parity("gy")
    fx, fy = flag_ref[0] != 0, flag_ref[1] != 0
    for v in range(5):
        for n in range(4):
            low = pack_low(u_ref[v, 0, n, 0], u_ref[v, 0, n, 1], 0)
            h = [jnp.where(fx, u_ref[v, 3, 3 - n, q], u_ref[v, 3, n, q]) for q in range(2)]
            put_pair(xe, xo, (v, n), low, pack_high(h[0], h[1], 0), even_x)
            low = pack_low(u_ref[v, n, 0, 0], u_ref[v, n, 0, 1], 1)
            h = [jnp.where(fy, u_ref[v, 3 - n, 3, q], u_ref[v, n, 3, q]) for q in range(2)]
            put_pair(ye, yo, (v, n), low, pack_high(h[0], h[1], 1), even_y)


def restrict_c(first, second):
    low = c_low()
    middle = jnp.where(low, second, first)
    return jnp.where(low, first, second) + FAR * middle + NEAR * sroll(middle, 4)


def restrict_four(values):
    return values[0] + NEAR * values[1] + FAR * values[2], values[3] + NEAR * values[2] + FAR * values[1]


def put_coarse_faces(v, lows, highs, flag_ref, pairs):
    for d, axis in ((0, "gx"), (1, "gy")):
        flag = flag_ref[d] != 0
        low, high = lows[d], highs[d]
        turned = [jnp.where(flag, high[1 - m], high[m]) for m in range(2)]
        even_ref, odd_ref = pairs[d]
        put_pair(even_ref, odd_ref, v, pack_low(*low, d), pack_high(*turned, d), parity(axis))


def restricted_faces(u_ref, flag_ref, xo, xe, yo, ye):
    for v in range(5):
        line = {}
        for a in range(4):
            for b in range(4):
                if a in (0, 3) or b in (0, 3):
                    line[a, b] = restrict_c(u_ref[v, a, b, 0], u_ref[v, a, b, 1])
        lows = [restrict_four([line[0, n] for n in range(4)]), restrict_four([line[n, 0] for n in range(4)])]
        highs = [restrict_four([line[3, n] for n in range(4)]), restrict_four([line[n, 3] for n in range(4)])]
        put_coarse_faces(v, lows, highs, flag_ref, ((xe, xo), (ye, yo)))


def smoothed(smooth_ref, fields, a, b):
    out = []
    for o in range(5):
        total = [None, None]
        for i in range(5):
            block = smooth_ref[5 * o + i, a, b].astype(F32)
            for q in range(2):
                term = block[8 * q : 8 * q + 8] * fields[i][q]
                total[q] = term if i == 0 else total[q] + term
        out.append([OMEGA * total[q] for q in range(2)])
    return out


def first_line(src_ref, smooth_ref, u_ref, a, b):
    value = smoothed(smooth_ref, [[src_ref[v, a, b, q] for q in range(2)] for v in range(5)], a, b)
    for v in range(5):
        for q in range(2):
            u_ref[v, a, b, q] = value[v][q]


def line_copy(smooth_hbm, smooth_ref, sem, a, b):
    return pltpu.make_async_copy(smooth_hbm.at[:, a, b], smooth_ref.at[:, a, b], sem)


def first_kernel(
    src_hbm, smooth_hbm, orient_hbm, src_ref, smooth_ref, u_ref, flag_ref, xo, xe, yo, ye, sems, orient_ref, orient_sem
):
    every, inner = slice(0, 4), slice(1, 3)
    src_copy = pltpu.make_async_copy(src_hbm, src_ref, sems.at[4])
    src_copy.start()
    copies = [
        line_copy(smooth_hbm, smooth_ref, sems.at[slot], a, b)
        for slot, (a, b) in enumerate(((0, every), (3, every), (inner, 0), (inner, 3)))
    ]
    for one in copies:
        one.start()
    orient_copy = pltpu.make_async_copy(orient_hbm, orient_ref, orient_sem)
    orient_copy.start()
    orient_copy.wait()
    for d in range(3):
        flag_ref[d] = twice(orient_ref[d])
    lines = [[(0, b) for b in range(4)], [(3, b) for b in range(4)], [(1, 0), (2, 0)], [(1, 3), (2, 3)]]
    src_copy.wait()
    for one, group in zip(copies, lines):
        one.wait()
        for a, b in group:
            first_line(src_ref, smooth_ref, u_ref, a, b)
    fine_faces(u_ref, flag_ref, xo, xe, yo, ye)


def prepare_tables(jac_ref, damp_ref, jac8_ref, damp8_ref, face_ref):
    damp = twice(damp_ref[...])
    damp8_ref[...] = damp
    for d in range(3):
        for k in range(25):
            value = twice(jac_ref[25 * d + k])
            jac8_ref[25 * d + k] = value
            if d < 2:
                low, step = axis_low(d)
                diagonal = k % 6 == 0
                upper = H4 * (value - damp if diagonal else value)
                lower = H4 * (value + damp if diagonal else value)
                face_ref[2 * d, k] = jnp.where(low, sroll(upper, -step), upper)
                face_ref[2 * d + 1, k] = jnp.where(low, lower, sroll(lower, step))


def volume(src_ref, u_ref, flag_ref, jac_ref, damp_ref, acc_ref, finish_lines):
    damp = H4 * damp_ref[...]

    def jacobian(d):
        return [[jac_ref[25 * d + 5 * o + i] for i in range(5)] for o in range(5)]

    def along(direction, others):
        low, step = axis_low(direction)
        flag = flag_ref[direction] != 0
        flag_before = sroll(flag_ref[direction], step) != 0

        def at(v, n, other, q):
            return (v, n, other, q) if direction == 0 else (v, other, n, q)

        def step_fn(j, carry):
            other, q = others(j // 2), j % 2
            u = [[u_ref[at(v, n, other, q)] for n in range(4)] for v in range(5)]
            waves = []
            jumps = []
            for v in range(5):
                back_low, back_high = u_ref[at(v, 0, 3 - other, q)], u_ref[at(v, 3, 3 - other, q)]
                right = sroll(jnp.where(flag_before, back_low, u[v][0]), -step)
                left = sroll(jnp.where(flag, back_high, u[v][3]), step)
                jump_right = jnp.where(low, right, 0.0) - u[v][3]
                jump_left = jnp.where(low, 0.0, left) - u[v][0]
                w = list(slopes_along(*u[v]))
                w[3] = w[3] + H4 * jump_right
                w[0] = w[0] - H4 * jump_left
                waves.append(w)
                jumps.append((damp * jump_left, None, None, damp * jump_right))
            matrix = jacobian(direction)
            for n in range(4):
                flux = mix(matrix, [waves[v][n] for v in range(5)])
                for v in range(5):
                    if direction == 1:
                        total = src_ref[at(v, n, other, q)] - 2.0 * u[v][n]
                    else:
                        total = acc_ref[at(v, n, other, q)]
                    total = total - flux[v]
                    if jumps[v][n] is not None:
                        total = total + jumps[v][n]
                    acc_ref[at(v, n, other, q)] = total
            return carry

        return step_fn

    low = c_low()
    flag = jnp.where(low, lroll(flag_ref[2], 1), flag_ref[2]) != 0
    damp_z = damp
    coef = [
        [jnp.where(low, float(D4[2 * p, c]), float(D4[2 * p + 1, c ^ 1])).astype(F32) for c in range(4)]
        for p in range(2)
    ]

    def step_z(j, carry):
        a0, b = j // 4, j % 4
        here = (a0, 3 - a0)
        u = [[[u_ref[v, a, b, q] for q in range(2)] for v in range(5)] for a in here]
        turned = [[[sroll(u[s][v][q], 4) for q in range(2)] for v in range(5)] for s in range(2)]
        beside = []
        for s in range(2):
            line = []
            for v in range(5):
                face = jnp.where(low, turned[s][v][1], turned[s][v][0])
                line.append(jnp.where(low, lroll(face, 1), lroll(face, -1)))
            beside.append(line)
        matrix = jacobian(2)
        for s in range(2):
            waves = [[], []]
            jumps = []
            for v in range(5):
                own = jnp.where(low, u[s][v][0], u[s][v][1])
                jump = jnp.where(flag, beside[1 - s][v], beside[s][v]) - own
                jumps.append(damp_z * jump)
                lifted = H4 * jump
                for p in range(2):
                    w = coef[p][0] * u[s][v][0] + coef[p][1] * turned[s][v][0]
                    w = w + (coef[p][2] * u[s][v][1] + coef[p][3] * turned[s][v][1])
                    w = w - jnp.where(low, lifted, 0.0) if p == 0 else w + jnp.where(low, 0.0, lifted)
                    waves[p].append(w)
            for p in range(2):
                flux = mix(matrix, waves[p])
                for v in range(5):
                    part = jnp.where(low, jumps[v], 0.0) if p == 0 else jnp.where(low, 0.0, jumps[v])
                    acc_ref[v, here[s], b, p] = acc_ref[v, here[s], b, p] - flux[v] + part
        return carry

    lax.fori_loop(0, 4, along(1, lambda k: 3 * k), 0)
    lax.fori_loop(0, 4, step_z, 0)
    finish_lines()
    lax.fori_loop(0, 4, along(1, lambda k: 1 + k), 0)
    lax.fori_loop(4, 8, step_z, 0)
    lax.fori_loop(0, 8, along(0, lambda k: k), 0)


def first_volume_kernel(
    smooth_hbm, src_ref, smooth_in, u_in, flag_ref, jac_ref, damp_ref,
    smooth_ref, u_ref, acc_ref, jac8_ref, damp8_ref, face_ref, second_ref, scaled_ref, sem,
):
    inner = slice(1, 3)
    copy = line_copy(smooth_hbm, smooth_ref, sem, inner, inner)
    copy.start()
    prepare_tables(jac_ref, damp_ref, jac8_ref, damp8_ref, face_ref)
    lines = [(a, b) for a in (1, 2) for b in (1, 2)]

    def finish_lines():
        copy.wait()
        for a, b in lines:
            first_line(src_ref, smooth_ref, u_ref, a, b)

    volume(src_ref, u_ref, flag_ref, jac8_ref, damp8_ref, acc_ref, finish_lines)
    for a, b in lines:
        change = smoothed(smooth_ref, [[acc_ref[v, a, b, q] for q in range(2)] for v in range(5)], a, b)
        for v in range(5):
            for q in range(2):
                second_ref[v, a, b, q] = u_ref[v, a, b, q] + change[v][q]
    for line, (a, b) in enumerate(FACE_LINES):
        for k in range(25):
            block = OMEGA * smooth_ref[k, a, b].astype(F32)
            for q in range(2):
                scaled_ref[line, k, q] = block[8 * q : 8 * q + 8]


def remote_parts(d, odd, even, flag_ref, face_ref, part_ref):
    is_even = parity(("gx", "gy")[d])
    low, step = axis_low(d)
    flag = flag_ref[d]
    flag = jnp.where(low, sroll(flag, -step), flag) != 0
    matrix = [[face_ref[2 * d, 5 * o + i] for i in range(5)] for o in range(5)]
    for n in range(4):
        take = lambda v, m: jnp.where(is_even, even[v, m], odd[v, m])
        right = [jnp.where(flag, take(v, 3 - n), take(v, n)) for v in range(5)]
        for v, value in enumerate(mix(matrix, right)):
            part_ref[0, v, n, 0] = jnp.where(low, 0.0, -sroll(value, step))
            part_ref[0, v, n, 1] = jnp.where(low, 0.0, -value)
    matrix = [[face_ref[2 * d + 1, 5 * o + i] for i in range(5)] for o in range(5)]
    for n in range(4):
        left = [jnp.where(is_even, odd[v, n], even[v, n]) for v in range(5)]
        for v, value in enumerate(mix(matrix, left)):
            part_ref[1, v, n, 0] = jnp.where(low, value, 0.0)
            part_ref[1, v, n, 1] = jnp.where(low, sroll(value, -step), 0.0)


def second_lines(lines, acc_ref, x_part_ref, y_part_ref, scaled_ref, u_ref, out_ref):
    for a, b in lines:
        line = FACE_LINES.index((a, b))
        for q in range(2):
            left = [acc_ref[v, a, b, q] for v in range(5)]
            for v in range(5):
                if a in (0, 3):
                    left[v] = left[v] + x_part_ref[0 if a == 3 else 1, v, b, q]
                if b in (0, 3):
                    left[v] = left[v] + y_part_ref[0 if b == 3 else 1, v, a, q]
            matrix = [[scaled_ref[line, 5 * o + i, q] for i in range(5)] for o in range(5)]
            for v, value in enumerate(mix(matrix, left)):
                out_ref[v, a, b, q] = u_ref[v, a, b, q] + value


X_LINES = [(a, b) for a in (0, 3) for b in (1, 2)]


def second_x_kernel(acc_ref, u_ref, scaled_ref, flag_ref, face_ref, rxo, rxe, inner_ref, out_ref, part_ref):
    remote_parts(0, rxo, rxe, flag_ref, face_ref, part_ref)
    second_lines(X_LINES, acc_ref, part_ref, None, scaled_ref, u_ref, out_ref)


def second_kernel(
    acc_ref, u_ref, scaled_ref, flag_ref, face_ref, ryo, rye, x_part_ref, held_ref, out_ref, xo, xe, yo, ye, part_ref
):
    remote_parts(1, ryo, rye, flag_ref, face_ref, part_ref)
    lines = [line for line in FACE_LINES if line not in X_LINES]
    second_lines(lines, acc_ref, x_part_ref, part_ref, scaled_ref, u_ref, out_ref)
    restricted_faces(out_ref, flag_ref, xo, xe, yo, ye)


def coarse_smooth(smooth_ref, fields):
    out = [[[None, None], [None, None]] for _ in range(5)]
    for i in range(2):
        for o in range(5):
            total = [None, None]
            for k in range(5):
                block = smooth_ref[5 * o + k, i].astype(F32)
                for j in range(2):
                    term = block[8 * j : 8 * j + 8] * fields[k][i][j]
                    total[j] = term if k == 0 else total[j] + term
            for j in range(2):
                out[o][i][j] = OMEGA * total[j]
    return out


def coarse_faces(field, flag_ref, xo, xe, yo, ye):
    for v in range(5):
        c = field[v]
        lows = [[c[0][0], c[0][1]], [c[0][0], c[1][0]]]
        highs = [[c[1][0], c[1][1]], [c[0][1], c[1][1]]]
        put_coarse_faces(v, lows, highs, flag_ref, ((xe, xo), (ye, yo)))


def response_kernel(smooth_ref, face_ref, response_ref):
    packed = []
    for k in range(25):
        by_i = [smooth_ref[k, i].astype(F32) for i in range(2)]
        node = [[by_i[i][8 * j : 8 * j + 8] for j in range(2)] for i in range(2)]
        packed.append(
            (
                pack_high(node[1][0], node[1][1], 0),
                pack_low(node[0][0], node[0][1], 0),
                pack_high(node[0][1], node[1][1], 1),
                pack_low(node[0][0], node[1][0], 1),
            )
        )
    for f in range(4):
        for o in range(5):
            for i in range(5):
                total = packed[5 * o][f] * face_ref[f, i]
                for k in range(1, 5):
                    total = total + packed[5 * o + k][f] * face_ref[f, 5 * k + i]
                response_ref[f, 5 * o + i] = (OMEGA / 6.0) * total


def restricted_volume_kernel(src_ref, u_ref, flag_ref, jac_ref, damp_ref, smooth_ref, acc_ref, c_ref):
    damp = H4 * damp_ref[...]
    low_c = c_low()
    slope = [
        jnp.where(low_c, float(PD[0, c]), float(PD[1, c ^ 1])).astype(F32) for c in range(4)
    ]
    flags = [flag_ref[0] != 0, flag_ref[1] != 0, jnp.where(low_c, lroll(flag_ref[2], 1), flag_ref[2]) != 0]
    sign = jnp.where(low_c, -H4, H4).astype(F32)
    waves = [[[[None] * 5 for _ in range(2)] for _ in range(2)] for _ in range(3)]

    def slopes_four(values):
        return [sum_of([(float(PD[i, n]), values[n]) for n in range(4)]) for i in range(2)]

    for v in range(5):
        line, slope_c, ends = {}, {}, {}
        for a in range(4):
            for b in range(4):
                first, second = u_ref[v, a, b, 0], u_ref[v, a, b, 1]
                line[a, b] = restrict_c(first, second)
                slope_c[a, b] = (slope[0] * first + slope[1] * sroll(first, 4)) + (
                    slope[2] * second + slope[3] * sroll(second, 4)
                )
                ends[a, b] = jnp.where(low_c, first, second)

        def along_b(table):
            return [restrict_four([table[a, b] for b in range(4)]) for a in range(4)]

        def both(table):
            by_b = along_b(table)
            return [restrict_four([by_b[a][j] for a in range(4)]) for j in range(2)]

        by_b = along_b(line)
        by_a = [restrict_four([line[a, b] for a in range(4)]) for b in range(4)]
        flux_z = both(slope_c)
        trace_z = both(ends)
        sources = both({(a, b): restrict_c(src_ref[v, a, b, 0], src_ref[v, a, b, 1]) for a in range(4) for b in range(4)})
        acc = [[None, None], [None, None]]
        for j in range(2):
            value = restrict_four([by_b[a][j] for a in range(4)])
            flux = slopes_four([by_b[a][j] for a in range(4)])
            for i in range(2):
                acc[i][j] = sources[j][i] - 2.0 * value[i]
                waves[0][i][j][v] = flux[i]
        for i in range(2):
            flux = slopes_four([by_a[b][i] for b in range(4)])
            for j in range(2):
                waves[1][i][j][v] = flux[j]
        for d, lo, hi in ((0, by_b[0], by_b[3]), (1, by_a[0], by_a[3])):
            low, step = axis_low(d)
            flag = flags[d]
            flag_before = sroll(flag_ref[d], step) != 0
            for m in range(2):
                right = sroll(jnp.where(flag_before, lo[1 - m], lo[m]), -step)
                left = sroll(jnp.where(flag, hi[1 - m], hi[m]), step)
                jump_right = jnp.where(low, right, 0.0) - hi[m]
                jump_left = jnp.where(low, 0.0, left) - lo[m]
                i, j = (1, m) if d == 0 else (m, 1)
                waves[d][i][j][v] = waves[d][i][j][v] + H4 * jump_right
                acc[i][j] = acc[i][j] + damp * jump_right
                i, j = (0, m) if d == 0 else (m, 0)
                waves[d][i][j][v] = waves[d][i][j][v] - H4 * jump_left
                acc[i][j] = acc[i][j] + damp * jump_left
        beside = []
        for j in range(2):
            turned = [sroll(trace_z[j][i], 4) for i in range(2)]
            beside.append([jnp.where(low_c, lroll(t, 1), lroll(t, -1)) for t in turned])
        for i in range(2):
            for j in range(2):
                jump = jnp.where(flags[2], beside[j][1 - i], beside[j][i]) - trace_z[j][i]
                waves[2][i][j][v] = flux_z[j][i] + sign * jump
                acc_ref[v, i, j] = acc[i][j] + damp * jump
    for d in range(3):
        matrix = [[jac_ref[25 * d + 5 * o + i] for i in range(5)] for o in range(5)]
        for i in range(2):
            for j in range(2):
                for v, value in enumerate(mix(matrix, waves[d][i][j])):
                    acc_ref[v, i, j] = acc_ref[v, i, j] - value
    c = coarse_smooth(smooth_ref, [[[acc_ref[v, i, j] for j in range(2)] for i in range(2)] for v in range(5)])
    put_field(c_ref, c)


def put_field(out_ref, c):
    for v in range(5):
        for i in range(2):
            for j in range(2):
                out_ref[v, i, j] = c[v][i][j]


def get_field(ref):
    return [[[ref[v, i, j] for j in range(2)] for i in range(2)] for v in range(5)]


def add_remote(field, scale, flag_ref, face_ref, rxo, rxe, ryo, rye):
    for d, axis in ((0, "gx"), (1, "gy")):
        is_even = parity(axis)
        low, step = axis_low(d)
        flag = flag_ref[d]
        flag = jnp.where(low, sroll(flag, -step), flag) != 0
        even, odd = ((rxe, rxo), (rye, ryo))[d]
        at = (lambda n, m: (n, m)) if d == 0 else (lambda n, m: (m, n))
        right, left = [], []
        for v in range(5):
            value = scale * jnp.where(is_even, even[v], odd[v])
            swapped = jnp.where(low, sroll(value, -step), sroll(value, step))
            right.append(jnp.where(flag, swapped, value))
            left.append(scale * jnp.where(is_even, odd[v], even[v]))
        upper = [[face_ref[2 * d, 5 * o + i] for i in range(5)] for o in range(5)]
        lower = [[face_ref[2 * d + 1, 5 * o + i] for i in range(5)] for o in range(5)]
        for v, value in enumerate(mix(upper, right)):
            for m, part in enumerate((sroll(value, step), value)):
                i, j = at(1, m)
                field[v][i][j] = field[v][i][j] - jnp.where(low, 0.0, part)
        for v, value in enumerate(mix(lower, left)):
            for m, part in enumerate((value, sroll(value, -step))):
                i, j = at(0, m)
                field[v][i][j] = field[v][i][j] + jnp.where(low, part, 0.0)


def restrict_kernel(local_ref, flag_ref, response_ref, rxo, rxe, ryo, rye, c_ref, xo, xe, yo, ye):
    c = get_field(local_ref)
    add_remote(c, 6.0, flag_ref, response_ref, rxo, rxe, ryo, rye)
    put_field(c_ref, c)
    coarse_faces(c, flag_ref, xo, xe, yo, ye)


def first_local_kernel(
    c_ref, acc_ref, smooth_ref, flag_ref, jac_ref, damp_ref, face_ref, rxo, rxe, ryo, rye, out_ref, rhs_ref
):
    rhs = get_field(acc_ref)
    add_remote(rhs, 1.0, flag_ref, face_ref, rxo, rxe, ryo, rye)
    put_field(rhs_ref, rhs)
    coarse_local_kernel(c_ref, rhs_ref, smooth_ref, flag_ref, jac_ref, damp_ref, out_ref)


def coarse_local_kernel(c_ref, rhs_ref, smooth_ref, flag_ref, jac_ref, damp_ref, out_ref):
    damp = 0.5 * damp_ref[...]
    c = [[[c_ref[v, i, j] for j in range(2)] for i in range(2)] for v in range(5)]
    acc = [[[rhs_ref[v, i, j] - 2.0 * c[v][i][j] for j in range(2)] for i in range(2)] for v in range(5)]
    for d in range(2):
        low, step = axis_low(d)
        flag = flag_ref[d] != 0
        flag_before = sroll(flag_ref[d], step) != 0
        matrix = [[jac_ref[25 * d + 5 * o + i] for i in range(5)] for o in range(5)]
        at = (lambda n, m: (n, m)) if d == 0 else (lambda n, m: (m, n))
        waves = [[[None] * 5, [None] * 5] for _ in range(2)]
        for v in range(5):
            lo = [c[v][at(0, m)[0]][at(0, m)[1]] for m in range(2)]
            hi = [c[v][at(1, m)[0]][at(1, m)[1]] for m in range(2)]
            for m in range(2):
                right = jnp.where(low, sroll(jnp.where(flag_before, lo[1 - m], lo[m]), -step), 0.0)
                left = jnp.where(low, 0.0, sroll(jnp.where(flag, hi[1 - m], hi[m]), step))
                waves[1][m][v] = 0.5 * (right - lo[m])
                waves[0][m][v] = 0.5 * (hi[m] - left)
                i, j = at(1, m)
                acc[v][i][j] = acc[v][i][j] + damp * (right - hi[m])
                i, j = at(0, m)
                acc[v][i][j] = acc[v][i][j] + damp * (left - lo[m])
        for n in range(2):
            for m in range(2):
                i, j = at(n, m)
                for v, value in enumerate(mix(matrix, waves[n][m])):
                    acc[v][i][j] = acc[v][i][j] - value
    low = c_low()
    flag = jnp.where(low, lroll(flag_ref[2], 1), flag_ref[2]) != 0
    half = jnp.where(low, 0.5, -0.5).astype(F32)
    matrix = [[jac_ref[50 + 5 * o + i] for i in range(5)] for o in range(5)]
    turned = [[[sroll(c[v][i][j], 4) for j in range(2)] for i in range(2)] for v in range(5)]
    beside = [
        [[jnp.where(low, lroll(t, 1), lroll(t, -1)) for t in turned[v][i]] for i in range(2)] for v in range(5)
    ]
    for i in range(2):
        for j in range(2):
            wave = []
            for v in range(5):
                next_to = jnp.where(flag, beside[v][1 - i][j], beside[v][i][j])
                wave.append(half * (turned[v][i][j] - next_to))
                acc[v][i][j] = acc[v][i][j] + damp * (next_to - c[v][i][j])
            for v, value in enumerate(mix(matrix, wave)):
                acc[v][i][j] = acc[v][i][j] - value
    change = coarse_smooth(smooth_ref, acc)
    for v in range(5):
        for i in range(2):
            for j in range(2):
                out_ref[v, i, j] = c[v][i][j] + change[v][i][j]


def coarse_kernel(c_ref, flag_ref, response_ref, rxo, rxe, ryo, rye, out_ref, xo, xe, yo, ye):
    c = get_field(c_ref)
    add_remote(c, 1.0, flag_ref, response_ref, rxo, rxe, ryo, rye)
    put_field(out_ref, c)
    coarse_faces(c, flag_ref, xo, xe, yo, ye)


def spread(first, second):
    return first, NEAR * first + FAR * second, FAR * first + NEAR * second, second


def last_kernel(
    c_ref, flag_ref, response_ref, rxo, rxe, ryo, rye, second_ref, out_hbm, out_ref, sems
):
    c = get_field(c_ref)
    add_remote(c, 1.0, flag_ref, response_ref, rxo, rxe, ryo, rye)
    low = c_low()
    copies = []
    for v in range(5):
        by_c = [[None, None], [None, None]]
        for i in range(2):
            for j in range(2):
                value = c[v][i][j]
                inner = FAR * value + NEAR * sroll(value, 4)
                by_c[i][j] = (jnp.where(low, value, inner), jnp.where(low, inner, value))
        for q in range(2):
            lines = [spread(by_c[i][0][q], by_c[i][1][q]) for i in range(2)]
            for b in range(4):
                for a, value in enumerate(spread(lines[0][b], lines[1][b])):
                    out_ref[v, a, b, q] = second_ref[v, a, b, q] + value
        copy = pltpu.make_async_copy(out_ref.at[v], out_hbm.at[v], sems.at[v])
        copy.start()
        copies.append(copy)
    for copy in copies:
        copy.wait()


FINE = (5, 4, 4, 2, 8, 128)
FINE_MESSAGE = (5, 4, 8, 128)
COARSE = (5, 2, 2, 8, 128)
COARSE_MESSAGE = (5, 8, 128)


def vmem(shape, dtype=F32):
    return pltpu.VMEM(shape, dtype)


def here(array):
    return pltpu.with_memory_space_constraint(array, pltpu.VMEM)


def call(kernel, args, outs, in_hbm=(), out_hbm=(), scratch=(), aliases=None, flops=0):
    in_specs = [
        pl.BlockSpec(memory_space=pltpu.HBM if k in in_hbm else pltpu.VMEM) for k in range(len(args))
    ]
    out_specs = [
        pl.BlockSpec(memory_space=pltpu.HBM if k in out_hbm else pltpu.VMEM) for k in range(len(outs))
    ]
    args = [pltpu.with_memory_space_constraint(a, pltpu.HBM) if k in in_hbm else here(a) for k, a in enumerate(args)]
    return pl.pallas_call(
        kernel,
        out_shape=outs,
        in_specs=in_specs,
        out_specs=out_specs,
        scratch_shapes=scratch,
        input_output_aliases=aliases or {},
        compiler_params=pltpu.CompilerParams(vmem_limit_bytes=8 * 2**20),
        cost_estimate=pl.CostEstimate(flops=flops, bytes_accessed=4 * 2**20, transcendentals=0),
    )(*args)


def partners(axis):
    size = lax.axis_size(axis)
    even = [(i, i ^ 1) for i in range(size)]
    odd = [(i, (i - 1) % size if i % 2 == 0 else (i + 1) % size) for i in range(size)]
    return even, odd


def exchange(xo, xe, yo, ye):
    even_x, odd_x = partners("gx")
    even_y, odd_y = partners("gy")
    xo = lax.ppermute(xo, "gx", odd_x)
    xe = lax.ppermute(xe, "gx", even_x)
    yo = lax.ppermute(yo, "gy", odd_y)
    ye = lax.ppermute(ye, "gy", even_y)
    return xo, xe, yo, ye


def body(source, jacobian, damping, orient, smoother, coarse_smoother):
    source = source.reshape(FINE)
    smoother = smoother.reshape(25, 4, 4, 16, 128)
    coarse_smoother = coarse_smoother.reshape(25, 2, 16, 128)
    jacobian = jacobian.reshape(75, 4, 128)
    damping = damping.reshape(4, 128)
    orient = orient.reshape(3, 4, 128)
    fine_messages = [vmem(FINE_MESSAGE)] * 4
    coarse_messages = [vmem(COARSE_MESSAGE)] * 4

    held = vmem(smoother.shape, smoother.dtype)
    smoother_in = smoother
    source, smoother, first, flag, *sent = call(
        first_kernel,
        (source, smoother_in, orient),
        [vmem(FINE), held, vmem(FINE), vmem((3, 8, 128), jnp.int32)] + fine_messages,
        in_hbm=(0, 1, 2),
        scratch=[pltpu.SemaphoreType.DMA((5,)), pltpu.VMEM((3, 4, 128), jnp.int32), pltpu.SemaphoreType.DMA],
        flops=2 * 25 * 64 * 512,
    )
    got = exchange(*sent)
    _, first, acc, jac8, damp8, face, second, scaled = call(
        first_volume_kernel,
        (smoother_in, source, smoother, first, flag, jacobian, damping),
        [held, vmem(FINE), vmem(FINE), vmem((75, 8, 128)), vmem((8, 128)), vmem((4, 25, 8, 128)), vmem(FINE), vmem((12, 25, 2, 8, 128))],
        in_hbm=(0,),
        aliases={2: 0, 3: 1},
        scratch=[pltpu.SemaphoreType.DMA],
        flops=9 * 2**20,
    )
    part = vmem((2, 5, 4, 2, 8, 128))
    second, x_part = call(
        second_x_kernel,
        (acc, first, scaled, flag, face, *got[:2], second),
        [vmem(FINE), part],
        aliases={7: 0},
        flops=2**20,
    )
    second, *sent = call(
        second_kernel,
        (acc, first, scaled, flag, face, *got[2:], x_part, second),
        [vmem(FINE)] + coarse_messages,
        aliases={8: 0},
        scratch=[pltpu.VMEM((2, 5, 4, 2, 8, 128), F32)],
        flops=2 * 2**20,
    )
    got = exchange(*sent)
    (response,) = call(response_kernel, (coarse_smoother, face), [vmem((4, 25, 8, 128))], flops=2**20)
    acc, coarse = call(
        restricted_volume_kernel,
        (source, second, flag, jac8, damp8, coarse_smoother),
        [vmem(COARSE), vmem(COARSE)],
        flops=4 * 2**20,
    )
    coarse, *sent = call(
        restrict_kernel, (coarse, flag, response, *got), [vmem(COARSE)] + coarse_messages, flops=2**20
    )
    second_got, got = got, exchange(*sent)
    coarse, rhs = call(
        first_local_kernel,
        (coarse, acc, coarse_smoother, flag, jac8, damp8, face, *second_got),
        [vmem(COARSE), vmem(COARSE)],
        flops=4 * 2**20,
    )
    coarse, *sent = call(
        coarse_kernel, (coarse, flag, response, *got), [vmem(COARSE)] + coarse_messages, flops=2**20
    )
    got = exchange(*sent)
    (coarse,) = call(
        coarse_local_kernel, (coarse, rhs, coarse_smoother, flag, jac8, damp8), [vmem(COARSE)], flops=4 * 2**20
    )
    (out,) = call(
        last_kernel,
        (coarse, flag, response, *got, second),
        [jax.ShapeDtypeStruct(FINE, F32)],
        out_hbm=(0,),
        scratch=[pltpu.VMEM(FINE, F32), pltpu.SemaphoreType.DMA((5,))],
        flops=2**20,
    )
    return out.reshape(5, 4, 4, 4, 2, 2, 128)


def solution(mesh):
    in_specs = (
        P(None, None, None, None, "gx", "gy", None),
        P(None, None, None, "gx", "gy", None),
        P("gx", "gy", None),
        P(None, "gx", "gy", None),
        P(None, None, None, None, None, "gx", "gy", None),
        P(None, None, None, None, None, "gx", "gy", None),
    )
    out_specs = P(None, None, None, None, "gx", "gy", None)
    return jax.shard_map(body, mesh=mesh, in_specs=in_specs, out_specs=out_specs, check_vma=False)
```

```python
import functools
import math

import jax
import jax.numpy as jnp
import numpy as np
from jax import lax
from jax.experimental import pallas as pl
from jax.experimental.pallas import tpu as pltpu
from jax.sharding import PartitionSpec as P


F32 = jnp.float32
OMEGA = 0.8
FACE_LINES = [(a, b) for a in range(4) for b in range(4) if a in (0, 3) or b in (0, 3)]
H4 = 3.0
ROOT = 1.0 / math.sqrt(5.0)
NEAR = (1.0 + ROOT) / 2.0
FAR = (1.0 - ROOT) / 2.0


def lobatto_slopes():
    points = np.array([-1.0, -ROOT, ROOT, 1.0])
    weights = np.ones(4)
    for i in range(4):
        for j in range(4):
            if i != j:
                weights[i] = weights[i] / (points[i] - points[j])
    slopes = np.zeros((4, 4))
    for i in range(4):
        for j in range(4):
            if i != j:
                slopes[i, j] = weights[j] / weights[i] / (points[i] - points[j])
        slopes[i, i] = -np.sum(slopes[i])
    return slopes


D4 = lobatto_slopes()
PD = np.array([[1.0, NEAR, FAR, 0.0], [0.0, FAR, NEAR, 1.0]]) @ D4


def sum_of(terms):
    total = None
    for weight, value in terms:
        total = weight * value if total is None else total + weight * value
    return total


def rows():
    return lax.broadcasted_iota(jnp.int32, (8, 128), 0)


def x_low():
    return (rows() & 2) == 0


def y_low():
    return (rows() & 1) == 0


def c_low():
    return (rows() & 4) == 0


def sroll(value, shift):
    return pltpu.roll(value, shift % 8, 0)


def lroll(value, shift):
    return pltpu.roll(value, shift % 128, 1)


def twice(value):
    return jnp.concatenate([value, value], axis=0)


def axis_low(direction):
    return (x_low(), 2) if direction == 0 else (y_low(), 1)


def pack_low(first, second, direction):
    low, step = axis_low(direction)
    return jnp.where(low, first, sroll(second, step))


def pack_high(first, second, direction):
    low, step = axis_low(direction)
    return jnp.where(low, sroll(first, -step), second)


def slopes_along(u0, u1, u2, u3):
    e0, o0, e1, o1 = u0 + u3, u0 - u3, u1 + u2, u1 - u2
    diff = e1 - e0
    even_a = float((D4[0, 1] + D4[0, 2]) / 2.0) * diff
    even_b = float((D4[1, 2] - 0.0) / 2.0) * diff
    odd_a = float((D4[0, 0] - D4[0, 3]) / 2.0) * o0 + float((D4[0, 1] - D4[0, 2]) / 2.0) * o1
    odd_b = float((D4[1, 0] - D4[1, 3]) / 2.0) * o0 - float(D4[1, 2] / 2.0) * o1
    return even_a + odd_a, even_b + odd_b, odd_b - even_b, odd_a - even_a


def mix(matrix, fields):
    out = []
    for o in range(5):
        total = matrix[o][0] * fields[0]
        for i in range(1, 5):
            total = total + matrix[o][i] * fields[i]
        out.append(total)
    return out


def parity(axis):
    return lax.rem(lax.axis_index(axis), 2) == 0


def put_pair(even_ref, odd_ref, index, low_face, high_face, is_even):
    even_ref[index] = jnp.where(is_even, high_face, low_face)
    odd_ref[index] = jnp.where(is_even, low_face, high_face)


def fine_faces(u_ref, flag_ref, xo, xe, yo, ye):
    even_x, even_y = parity("gx"), parity("gy")
    fx, fy = flag_ref[0] != 0, flag_ref[1] != 0
    for v in range(5):
        for n in range(4):
            low = pack_low(u_ref[v, 0, n, 0], u_ref[v, 0, n, 1], 0)
            h = [jnp.where(fx, u_ref[v, 3, 3 - n, q], u_ref[v, 3, n, q]) for q in range(2)]
            put_pair(xe, xo, (v, n), low, pack_high(h[0], h[1], 0), even_x)
            low = pack_low(u_ref[v, n, 0, 0], u_ref[v, n, 0, 1], 1)
            h = [jnp.where(fy, u_ref[v, 3 - n, 3, q], u_ref[v, n, 3, q]) for q in range(2)]
            put_pair(ye, yo, (v, n), low, pack_high(h[0], h[1], 1), even_y)


def restrict_c(first, second):
    low = c_low()
    middle = jnp.where(low, second, first)
    return jnp.where(low, first, second) + FAR * middle + NEAR * sroll(middle, 4)


def restrict_four(values):
    return values[0] + NEAR * values[1] + FAR * values[2], values[3] + NEAR * values[2] + FAR * values[1]


def put_coarse_faces(v, lows, highs, flag_ref, pairs):
    for d, axis in ((0, "gx"), (1, "gy")):
        flag = flag_ref[d] != 0
        low, high = lows[d], highs[d]
        turned = [jnp.where(flag, high[1 - m], high[m]) for m in range(2)]
        even_ref, odd_ref = pairs[d]
        put_pair(even_ref, odd_ref, v, pack_low(*low, d), pack_high(*turned, d), parity(axis))


def restricted_faces(u_ref, flag_ref, xo, xe, yo, ye):
    for v in range(5):
        line = {}
        for a in range(4):
            for b in range(4):
                if a in (0, 3) or b in (0, 3):
                    line[a, b] = restrict_c(u_ref[v, a, b, 0], u_ref[v, a, b, 1])
        lows = [restrict_four([line[0, n] for n in range(4)]), restrict_four([line[n, 0] for n in range(4)])]
        highs = [restrict_four([line[3, n] for n in range(4)]), restrict_four([line[n, 3] for n in range(4)])]
        put_coarse_faces(v, lows, highs, flag_ref, ((xe, xo), (ye, yo)))


def smoothed(smooth_ref, fields, a, b):
    out = []
    for o in range(5):
        total = [None, None]
        for i in range(5):
            block = smooth_ref[5 * o + i, a, b].astype(F32)
            for q in range(2):
                term = block[8 * q : 8 * q + 8] * fields[i][q]
                total[q] = term if i == 0 else total[q] + term
        out.append([OMEGA * total[q] for q in range(2)])
    return out


def first_line(src_ref, smooth_ref, u_ref, a, b):
    value = smoothed(smooth_ref, [[src_ref[v, a, b, q] for q in range(2)] for v in range(5)], a, b)
    for v in range(5):
        for q in range(2):
            u_ref[v, a, b, q] = value[v][q]


def line_copy(smooth_hbm, smooth_ref, sem, a, b):
    return pltpu.make_async_copy(smooth_hbm.at[:, a, b], smooth_ref.at[:, a, b], sem)


def first_kernel(
    src_hbm, smooth_hbm, orient_hbm, src_ref, smooth_ref, u_ref, flag_ref, xo, xe, yo, ye, sems, orient_ref, orient_sem
):
    every, inner = slice(0, 4), slice(1, 3)
    src_copy = pltpu.make_async_copy(src_hbm, src_ref, sems.at[4])
    src_copy.start()
    orient_copy = pltpu.make_async_copy(orient_hbm, orient_ref, orient_sem)
    orient_copy.start()
    copies = [
        line_copy(smooth_hbm, smooth_ref, sems.at[slot], a, b)
        for slot, (a, b) in enumerate(((0, every), (3, every), (inner, 0), (inner, 3)))
    ]
    for one in copies:
        one.start()
    lines = [[(0, b) for b in range(4)], [(3, b) for b in range(4)], [(1, 0), (2, 0)], [(1, 3), (2, 3)]]
    src_copy.wait()
    for one, group in zip(copies, lines):
        one.wait()
        for a, b in group:
            first_line(src_ref, smooth_ref, u_ref, a, b)
    orient_copy.wait()
    for d in range(3):
        flag_ref[d] = twice(orient_ref[d])
    fine_faces(u_ref, flag_ref, xo, xe, yo, ye)


def prepare_tables(jac_ref, damp_ref, jac8_ref, damp8_ref, face_ref):
    damp = twice(damp_ref[...])
    damp8_ref[...] = damp
    for d in range(3):
        for k in range(25):
            value = twice(jac_ref[25 * d + k])
            jac8_ref[25 * d + k] = value
            if d < 2:
                low, step = axis_low(d)
                diagonal = k % 6 == 0
                upper = H4 * (value - damp if diagonal else value)
                lower = H4 * (value + damp if diagonal else value)
                face_ref[2 * d, k] = jnp.where(low, sroll(upper, -step), upper)
                face_ref[2 * d + 1, k] = jnp.where(low, lower, sroll(lower, step))


def volume(src_ref, u_ref, flag_ref, jac_ref, damp_ref, acc_ref, finish_lines):
    damp = H4 * damp_ref[...]

    def jacobian(d):
        return [[jac_ref[25 * d + 5 * o + i] for i in range(5)] for o in range(5)]

    def along(direction, others):
        low, step = axis_low(direction)
        flag = flag_ref[direction] != 0
        flag_before = sroll(flag_ref[direction], step) != 0

        def at(v, n, other, q):
            return (v, n, other, q) if direction == 0 else (v, other, n, q)

        def step_fn(j, carry):
            other, q = others(j // 2), j % 2
            u = [[u_ref[at(v, n, other, q)] for n in range(4)] for v in range(5)]
            waves = []
            jumps = []
            for v in range(5):
                back_low, back_high = u_ref[at(v, 0, 3 - other, q)], u_ref[at(v, 3, 3 - other, q)]
                right = sroll(jnp.where(flag_before, back_low, u[v][0]), -step)
                left = sroll(jnp.where(flag, back_high, u[v][3]), step)
                jump_right = jnp.where(low, right, 0.0) - u[v][3]
                jump_left = jnp.where(low, 0.0, left) - u[v][0]
                w = list(slopes_along(*u[v]))
                w[3] = w[3] + H4 * jump_right
                w[0] = w[0] - H4 * jump_left
                waves.append(w)
                jumps.append((damp * jump_left, None, None, damp * jump_right))
            matrix = jacobian(direction)
            for n in range(4):
                flux = mix(matrix, [waves[v][n] for v in range(5)])
                for v in range(5):
                    if direction == 1:
                        total = src_ref[at(v, n, other, q)] - 2.0 * u[v][n]
                    else:
                        total = acc_ref[at(v, n, other, q)]
                    total = total - flux[v]
                    if jumps[v][n] is not None:
                        total = total + jumps[v][n]
                    acc_ref[at(v, n, other, q)] = total
            return carry

        return step_fn

    low = c_low()
    flag = jnp.where(low, lroll(flag_ref[2], 1), flag_ref[2]) != 0
    damp_z = damp
    coef = [
        [jnp.where(low, float(D4[2 * p, c]), float(D4[2 * p + 1, c ^ 1])).astype(F32) for c in range(4)]
        for p in range(2)
    ]

    def step_z(j, carry):
        a0, b = j // 4, j % 4
        here = (a0, 3 - a0)
        u = [[[u_ref[v, a, b, q] for q in range(2)] for v in range(5)] for a in here]
        turned = [[[sroll(u[s][v][q], 4) for q in range(2)] for v in range(5)] for s in range(2)]
        beside = []
        for s in range(2):
            line = []
            for v in range(5):
                face = jnp.where(low, turned[s][v][1], turned[s][v][0])
                line.append(jnp.where(low, lroll(face, 1), lroll(face, -1)))
            beside.append(line)
        matrix = jacobian(2)
        for s in range(2):
            waves = [[], []]
            jumps = []
            for v in range(5):
                own = jnp.where(low, u[s][v][0], u[s][v][1])
                jump = jnp.where(flag, beside[1 - s][v], beside[s][v]) - own
                jumps.append(damp_z * jump)
                lifted = H4 * jump
                for p in range(2):
                    w = coef[p][0] * u[s][v][0] + coef[p][1] * turned[s][v][0]
                    w = w + (coef[p][2] * u[s][v][1] + coef[p][3] * turned[s][v][1])
                    w = w - jnp.where(low, lifted, 0.0) if p == 0 else w + jnp.where(low, 0.0, lifted)
                    waves[p].append(w)
            for p in range(2):
                flux = mix(matrix, waves[p])
                for v in range(5):
                    part = jnp.where(low, jumps[v], 0.0) if p == 0 else jnp.where(low, 0.0, jumps[v])
                    acc_ref[v, here[s], b, p] = acc_ref[v, here[s], b, p] - flux[v] + part
        return carry

    lax.fori_loop(0, 4, along(1, lambda k: 3 * k), 0)
    lax.fori_loop(0, 4, step_z, 0)
    finish_lines()
    lax.fori_loop(0, 4, along(1, lambda k: 1 + k), 0)
    lax.fori_loop(4, 8, step_z, 0)
    lax.fori_loop(0, 8, along(0, lambda k: k), 0)


def first_volume_kernel(
    smooth_hbm, src_ref, smooth_in, u_in, flag_ref, jac_ref, damp_ref,
    smooth_ref, u_ref, acc_ref, jac8_ref, damp8_ref, face_ref, second_ref, scaled_ref, sem,
):
    inner = slice(1, 3)
    copy = line_copy(smooth_hbm, smooth_ref, sem, inner, inner)
    copy.start()
    prepare_tables(jac_ref, damp_ref, jac8_ref, damp8_ref, face_ref)
    lines = [(a, b) for a in (1, 2) for b in (1, 2)]

    def finish_lines():
        copy.wait()
        for a, b in lines:
            first_line(src_ref, smooth_ref, u_ref, a, b)

    volume(src_ref, u_ref, flag_ref, jac8_ref, damp8_ref, acc_ref, finish_lines)
    for a, b in lines:
        change = smoothed(smooth_ref, [[acc_ref[v, a, b, q] for q in range(2)] for v in range(5)], a, b)
        for v in range(5):
            for q in range(2):
                second_ref[v, a, b, q] = u_ref[v, a, b, q] + change[v][q]
    for line, (a, b) in enumerate(FACE_LINES):
        for k in range(25):
            block = OMEGA * smooth_ref[k, a, b].astype(F32)
            for q in range(2):
                scaled_ref[line, k, q] = block[8 * q : 8 * q + 8]


def remote_parts(d, odd, even, flag_ref, face_ref, part_ref):
    is_even = parity(("gx", "gy")[d])
    low, step = axis_low(d)
    flag = flag_ref[d]
    flag = jnp.where(low, sroll(flag, -step), flag) != 0
    matrix = [[face_ref[2 * d, 5 * o + i] for i in range(5)] for o in range(5)]
    for n in range(4):
        take = lambda v, m: jnp.where(is_even, even[v, m], odd[v, m])
        right = [jnp.where(flag, take(v, 3 - n), take(v, n)) for v in range(5)]
        for v, value in enumerate(mix(matrix, right)):
            part_ref[0, v, n, 0] = jnp.where(low, 0.0, -sroll(value, step))
            part_ref[0, v, n, 1] = jnp.where(low, 0.0, -value)
    matrix = [[face_ref[2 * d + 1, 5 * o + i] for i in range(5)] for o in range(5)]
    for n in range(4):
        left = [jnp.where(is_even, odd[v, n], even[v, n]) for v in range(5)]
        for v, value in enumerate(mix(matrix, left)):
            part_ref[1, v, n, 0] = jnp.where(low, value, 0.0)
            part_ref[1, v, n, 1] = jnp.where(low, sroll(value, -step), 0.0)


def second_lines(lines, acc_ref, x_part_ref, y_part_ref, scaled_ref, u_ref, out_ref):
    for a, b in lines:
        line = FACE_LINES.index((a, b))
        for q in range(2):
            left = [acc_ref[v, a, b, q] for v in range(5)]
            for v in range(5):
                if a in (0, 3):
                    left[v] = left[v] + x_part_ref[0 if a == 3 else 1, v, b, q]
                if b in (0, 3):
                    left[v] = left[v] + y_part_ref[0 if b == 3 else 1, v, a, q]
            matrix = [[scaled_ref[line, 5 * o + i, q] for i in range(5)] for o in range(5)]
            for v, value in enumerate(mix(matrix, left)):
                out_ref[v, a, b, q] = u_ref[v, a, b, q] + value


X_LINES = [(a, b) for a in (0, 3) for b in (1, 2)]


def second_x_kernel(acc_ref, u_ref, scaled_ref, flag_ref, face_ref, rxo, rxe, inner_ref, out_ref, part_ref):
    remote_parts(0, rxo, rxe, flag_ref, face_ref, part_ref)
    second_lines(X_LINES, acc_ref, part_ref, None, scaled_ref, u_ref, out_ref)


def second_kernel(
    acc_ref, u_ref, scaled_ref, flag_ref, face_ref, ryo, rye, x_part_ref, held_ref, out_ref, xo, xe, yo, ye, part_ref
):
    remote_parts(1, ryo, rye, flag_ref, face_ref, part_ref)
    lines = [line for line in FACE_LINES if line not in X_LINES]
    second_lines(lines, acc_ref, x_part_ref, part_ref, scaled_ref, u_ref, out_ref)
    restricted_faces(out_ref, flag_ref, xo, xe, yo, ye)


def coarse_smooth(smooth_ref, fields):
    out = [[[None, None], [None, None]] for _ in range(5)]
    for i in range(2):
        for o in range(5):
            total = [None, None]
            for k in range(5):
                block = smooth_ref[5 * o + k, i].astype(F32)
                for j in range(2):
                    term = block[8 * j : 8 * j + 8] * fields[k][i][j]
                    total[j] = term if k == 0 else total[j] + term
            for j in range(2):
                out[o][i][j] = OMEGA * total[j]
    return out


def coarse_faces(field, flag_ref, xo, xe, yo, ye):
    for v in range(5):
        c = field[v]
        lows = [[c[0][0], c[0][1]], [c[0][0], c[1][0]]]
        highs = [[c[1][0], c[1][1]], [c[0][1], c[1][1]]]
        put_coarse_faces(v, lows, highs, flag_ref, ((xe, xo), (ye, yo)))


def response_kernel(smooth_ref, face_ref, response_ref):
    packed = []
    for k in range(25):
        by_i = [smooth_ref[k, i].astype(F32) for i in range(2)]
        node = [[by_i[i][8 * j : 8 * j + 8] for j in range(2)] for i in range(2)]
        packed.append(
            (
                pack_high(node[1][0], node[1][1], 0),
                pack_low(node[0][0], node[0][1], 0),
                pack_high(node[0][1], node[1][1], 1),
                pack_low(node[0][0], node[1][0], 1),
            )
        )
    for f in range(4):
        for o in range(5):
            for i in range(5):
                total = packed[5 * o][f] * face_ref[f, i]
                for k in range(1, 5):
                    total = total + packed[5 * o + k][f] * face_ref[f, 5 * k + i]
                response_ref[f, 5 * o + i] = (OMEGA / 6.0) * total


def restricted_volume_kernel(src_ref, u_ref, flag_ref, jac_ref, damp_ref, smooth_ref, acc_ref, c_ref):
    damp = H4 * damp_ref[...]
    low_c = c_low()
    slope = [
        jnp.where(low_c, float(PD[0, c]), float(PD[1, c ^ 1])).astype(F32) for c in range(4)
    ]
    flags = [flag_ref[0] != 0, flag_ref[1] != 0, jnp.where(low_c, lroll(flag_ref[2], 1), flag_ref[2]) != 0]
    sign = jnp.where(low_c, -H4, H4).astype(F32)
    waves = [[[[None] * 5 for _ in range(2)] for _ in range(2)] for _ in range(3)]

    def slopes_four(values):
        return [sum_of([(float(PD[i, n]), values[n]) for n in range(4)]) for i in range(2)]

    for v in range(5):
        line, slope_c, ends = {}, {}, {}
        for a in range(4):
            for b in range(4):
                first, second = u_ref[v, a, b, 0], u_ref[v, a, b, 1]
                line[a, b] = restrict_c(first, second)
                slope_c[a, b] = (slope[0] * first + slope[1] * sroll(first, 4)) + (
                    slope[2] * second + slope[3] * sroll(second, 4)
                )
                ends[a, b] = jnp.where(low_c, first, second)

        def along_b(table):
            return [restrict_four([table[a, b] for b in range(4)]) for a in range(4)]

        def both(table):
            by_b = along_b(table)
            return [restrict_four([by_b[a][j] for a in range(4)]) for j in range(2)]

        by_b = along_b(line)
        by_a = [restrict_four([line[a, b] for a in range(4)]) for b in range(4)]
        flux_z = both(slope_c)
        trace_z = both(ends)
        sources = both({(a, b): restrict_c(src_ref[v, a, b, 0], src_ref[v, a, b, 1]) for a in range(4) for b in range(4)})
        acc = [[None, None], [None, None]]
        for j in range(2):
            value = restrict_four([by_b[a][j] for a in range(4)])
            flux = slopes_four([by_b[a][j] for a in range(4)])
            for i in range(2):
                acc[i][j] = sources[j][i] - 2.0 * value[i]
                waves[0][i][j][v] = flux[i]
        for i in range(2):
            flux = slopes_four([by_a[b][i] for b in range(4)])
            for j in range(2):
                waves[1][i][j][v] = flux[j]
        for d, lo, hi in ((0, by_b[0], by_b[3]), (1, by_a[0], by_a[3])):
            low, step = axis_low(d)
            flag = flags[d]
            flag_before = sroll(flag_ref[d], step) != 0
            for m in range(2):
                right = sroll(jnp.where(flag_before, lo[1 - m], lo[m]), -step)
                left = sroll(jnp.where(flag, hi[1 - m], hi[m]), step)
                jump_right = jnp.where(low, right, 0.0) - hi[m]
                jump_left = jnp.where(low, 0.0, left) - lo[m]
                i, j = (1, m) if d == 0 else (m, 1)
                waves[d][i][j][v] = waves[d][i][j][v] + H4 * jump_right
                acc[i][j] = acc[i][j] + damp * jump_right
                i, j = (0, m) if d == 0 else (m, 0)
                waves[d][i][j][v] = waves[d][i][j][v] - H4 * jump_left
                acc[i][j] = acc[i][j] + damp * jump_left
        beside = []
        for j in range(2):
            turned = [sroll(trace_z[j][i], 4) for i in range(2)]
            beside.append([jnp.where(low_c, lroll(t, 1), lroll(t, -1)) for t in turned])
        for i in range(2):
            for j in range(2):
                jump = jnp.where(flags[2], beside[j][1 - i], beside[j][i]) - trace_z[j][i]
                waves[2][i][j][v] = flux_z[j][i] + sign * jump
                acc_ref[v, i, j] = acc[i][j] + damp * jump
    for d in range(3):
        matrix = [[jac_ref[25 * d + 5 * o + i] for i in range(5)] for o in range(5)]
        for i in range(2):
            for j in range(2):
                for v, value in enumerate(mix(matrix, waves[d][i][j])):
                    acc_ref[v, i, j] = acc_ref[v, i, j] - value
    c = coarse_smooth(smooth_ref, [[[acc_ref[v, i, j] for j in range(2)] for i in range(2)] for v in range(5)])
    put_field(c_ref, c)


def put_field(out_ref, c):
    for v in range(5):
        for i in range(2):
            for j in range(2):
                out_ref[v, i, j] = c[v][i][j]


def get_field(ref):
    return [[[ref[v, i, j] for j in range(2)] for i in range(2)] for v in range(5)]


def add_remote(field, scale, flag_ref, face_ref, rxo, rxe, ryo, rye):
    for d, axis in ((0, "gx"), (1, "gy")):
        is_even = parity(axis)
        low, step = axis_low(d)
        flag = flag_ref[d]
        flag = jnp.where(low, sroll(flag, -step), flag) != 0
        even, odd = ((rxe, rxo), (rye, ryo))[d]
        at = (lambda n, m: (n, m)) if d == 0 else (lambda n, m: (m, n))
        right, left = [], []
        for v in range(5):
            value = scale * jnp.where(is_even, even[v], odd[v])
            swapped = jnp.where(low, sroll(value, -step), sroll(value, step))
            right.append(jnp.where(flag, swapped, value))
            left.append(scale * jnp.where(is_even, odd[v], even[v]))
        upper = [[face_ref[2 * d, 5 * o + i] for i in range(5)] for o in range(5)]
        lower = [[face_ref[2 * d + 1, 5 * o + i] for i in range(5)] for o in range(5)]
        for v, value in enumerate(mix(upper, right)):
            for m, part in enumerate((sroll(value, step), value)):
                i, j = at(1, m)
                field[v][i][j] = field[v][i][j] - jnp.where(low, 0.0, part)
        for v, value in enumerate(mix(lower, left)):
            for m, part in enumerate((value, sroll(value, -step))):
                i, j = at(0, m)
                field[v][i][j] = field[v][i][j] + jnp.where(low, part, 0.0)


def restrict_kernel(local_ref, flag_ref, response_ref, rxo, rxe, ryo, rye, c_ref, xo, xe, yo, ye):
    c = get_field(local_ref)
    add_remote(c, 6.0, flag_ref, response_ref, rxo, rxe, ryo, rye)
    put_field(c_ref, c)
    coarse_faces(c, flag_ref, xo, xe, yo, ye)


def first_local_kernel(
    c_ref, acc_ref, smooth_ref, flag_ref, jac_ref, damp_ref, face_ref, rxo, rxe, ryo, rye, out_ref, rhs_ref
):
    rhs = get_field(acc_ref)
    add_remote(rhs, 1.0, flag_ref, face_ref, rxo, rxe, ryo, rye)
    put_field(rhs_ref, rhs)
    coarse_local_kernel(c_ref, rhs_ref, smooth_ref, flag_ref, jac_ref, damp_ref, out_ref)


def coarse_local_kernel(c_ref, rhs_ref, smooth_ref, flag_ref, jac_ref, damp_ref, out_ref):
    damp = 0.5 * damp_ref[...]
    c = [[[c_ref[v, i, j] for j in range(2)] for i in range(2)] for v in range(5)]
    acc = [[[rhs_ref[v, i, j] - 2.0 * c[v][i][j] for j in range(2)] for i in range(2)] for v in range(5)]
    for d in range(2):
        low, step = axis_low(d)
        flag = flag_ref[d] != 0
        flag_before = sroll(flag_ref[d], step) != 0
        matrix = [[jac_ref[25 * d + 5 * o + i] for i in range(5)] for o in range(5)]
        at = (lambda n, m: (n, m)) if d == 0 else (lambda n, m: (m, n))
        waves = [[[None] * 5, [None] * 5] for _ in range(2)]
        for v in range(5):
            lo = [c[v][at(0, m)[0]][at(0, m)[1]] for m in range(2)]
            hi = [c[v][at(1, m)[0]][at(1, m)[1]] for m in range(2)]
            for m in range(2):
                right = jnp.where(low, sroll(jnp.where(flag_before, lo[1 - m], lo[m]), -step), 0.0)
                left = jnp.where(low, 0.0, sroll(jnp.where(flag, hi[1 - m], hi[m]), step))
                waves[1][m][v] = 0.5 * (right - lo[m])
                waves[0][m][v] = 0.5 * (hi[m] - left)
                i, j = at(1, m)
                acc[v][i][j] = acc[v][i][j] + damp * (right - hi[m])
                i, j = at(0, m)
                acc[v][i][j] = acc[v][i][j] + damp * (left - lo[m])
        for n in range(2):
            for m in range(2):
                i, j = at(n, m)
                for v, value in enumerate(mix(matrix, waves[n][m])):
                    acc[v][i][j] = acc[v][i][j] - value
    low = c_low()
    flag = jnp.where(low, lroll(flag_ref[2], 1), flag_ref[2]) != 0
    half = jnp.where(low, 0.5, -0.5).astype(F32)
    matrix = [[jac_ref[50 + 5 * o + i] for i in range(5)] for o in range(5)]
    turned = [[[sroll(c[v][i][j], 4) for j in range(2)] for i in range(2)] for v in range(5)]
    beside = [
        [[jnp.where(low, lroll(t, 1), lroll(t, -1)) for t in turned[v][i]] for i in range(2)] for v in range(5)
    ]
    for i in range(2):
        for j in range(2):
            wave = []
            for v in range(5):
                next_to = jnp.where(flag, beside[v][1 - i][j], beside[v][i][j])
                wave.append(half * (turned[v][i][j] - next_to))
                acc[v][i][j] = acc[v][i][j] + damp * (next_to - c[v][i][j])
            for v, value in enumerate(mix(matrix, wave)):
                acc[v][i][j] = acc[v][i][j] - value
    change = coarse_smooth(smooth_ref, acc)
    for v in range(5):
        for i in range(2):
            for j in range(2):
                out_ref[v, i, j] = c[v][i][j] + change[v][i][j]


def coarse_kernel(c_ref, flag_ref, response_ref, rxo, rxe, ryo, rye, out_ref, xo, xe, yo, ye):
    c = get_field(c_ref)
    add_remote(c, 1.0, flag_ref, response_ref, rxo, rxe, ryo, rye)
    put_field(out_ref, c)
    coarse_faces(c, flag_ref, xo, xe, yo, ye)


def spread(first, second):
    return first, NEAR * first + FAR * second, FAR * first + NEAR * second, second


def last_kernel(
    c_ref, flag_ref, response_ref, rxo, rxe, ryo, rye, second_ref, out_hbm, out_ref, sems
):
    c = get_field(c_ref)
    add_remote(c, 1.0, flag_ref, response_ref, rxo, rxe, ryo, rye)
    low = c_low()
    copies = []
    for v in range(5):
        by_c = [[None, None], [None, None]]
        for i in range(2):
            for j in range(2):
                value = c[v][i][j]
                inner = FAR * value + NEAR * sroll(value, 4)
                by_c[i][j] = (jnp.where(low, value, inner), jnp.where(low, inner, value))
        for q in range(2):
            lines = [spread(by_c[i][0][q], by_c[i][1][q]) for i in range(2)]
            for b in range(4):
                for a, value in enumerate(spread(lines[0][b], lines[1][b])):
                    out_ref[v, a, b, q] = second_ref[v, a, b, q] + value
        copy = pltpu.make_async_copy(out_ref.at[v], out_hbm.at[v], sems.at[v])
        copy.start()
        copies.append(copy)
    for copy in copies:
        copy.wait()


FINE = (5, 4, 4, 2, 8, 128)
FINE_MESSAGE = (5, 4, 8, 128)
COARSE = (5, 2, 2, 8, 128)
COARSE_MESSAGE = (5, 8, 128)


def vmem(shape, dtype=F32):
    return pltpu.VMEM(shape, dtype)


def here(array):
    return pltpu.with_memory_space_constraint(array, pltpu.VMEM)


def call(kernel, args, outs, in_hbm=(), out_hbm=(), scratch=(), aliases=None, flops=0):
    in_specs = [
        pl.BlockSpec(memory_space=pltpu.HBM if k in in_hbm else pltpu.VMEM) for k in range(len(args))
    ]
    out_specs = [
        pl.BlockSpec(memory_space=pltpu.HBM if k in out_hbm else pltpu.VMEM) for k in range(len(outs))
    ]
    args = [pltpu.with_memory_space_constraint(a, pltpu.HBM) if k in in_hbm else here(a) for k, a in enumerate(args)]
    return pl.pallas_call(
        kernel,
        out_shape=outs,
        in_specs=in_specs,
        out_specs=out_specs,
        scratch_shapes=scratch,
        input_output_aliases=aliases or {},
        compiler_params=pltpu.CompilerParams(vmem_limit_bytes=8 * 2**20),
        cost_estimate=pl.CostEstimate(flops=flops, bytes_accessed=4 * 2**20, transcendentals=0),
    )(*args)


def partners(axis):
    size = lax.axis_size(axis)
    even = [(i, i ^ 1) for i in range(size)]
    odd = [(i, (i - 1) % size if i % 2 == 0 else (i + 1) % size) for i in range(size)]
    return even, odd


def exchange(xo, xe, yo, ye):
    even_x, odd_x = partners("gx")
    even_y, odd_y = partners("gy")
    xo = lax.ppermute(xo, "gx", odd_x)
    xe = lax.ppermute(xe, "gx", even_x)
    yo = lax.ppermute(yo, "gy", odd_y)
    ye = lax.ppermute(ye, "gy", even_y)
    return xo, xe, yo, ye


def body(source, jacobian, damping, orient, smoother, coarse_smoother):
    source = source.reshape(FINE)
    smoother = smoother.reshape(25, 4, 4, 16, 128)
    coarse_smoother = coarse_smoother.reshape(25, 2, 16, 128)
    jacobian = jacobian.reshape(75, 4, 128)
    damping = damping.reshape(4, 128)
    orient = orient.reshape(3, 4, 128)
    fine_messages = [vmem(FINE_MESSAGE)] * 4
    coarse_messages = [vmem(COARSE_MESSAGE)] * 4

    held = vmem(smoother.shape, smoother.dtype)
    smoother_in = smoother
    source, smoother, first, flag, *sent = call(
        first_kernel,
        (source, smoother_in, orient),
        [vmem(FINE), held, vmem(FINE), vmem((3, 8, 128), jnp.int32)] + fine_messages,
        in_hbm=(0, 1, 2),
        scratch=[pltpu.SemaphoreType.DMA((5,)), pltpu.VMEM((3, 4, 128), jnp.int32), pltpu.SemaphoreType.DMA],
        flops=2 * 25 * 64 * 512,
    )
    got = exchange(*sent)
    _, first, acc, jac8, damp8, face, second, scaled = call(
        first_volume_kernel,
        (smoother_in, source, smoother, first, flag, jacobian, damping),
        [held, vmem(FINE), vmem(FINE), vmem((75, 8, 128)), vmem((8, 128)), vmem((4, 25, 8, 128)), vmem(FINE), vmem((12, 25, 2, 8, 128))],
        in_hbm=(0,),
        aliases={2: 0, 3: 1},
        scratch=[pltpu.SemaphoreType.DMA],
        flops=9 * 2**20,
    )
    part = vmem((2, 5, 4, 2, 8, 128))
    second, x_part = call(
        second_x_kernel,
        (acc, first, scaled, flag, face, *got[:2], second),
        [vmem(FINE), part],
        aliases={7: 0},
        flops=2**20,
    )
    second, *sent = call(
        second_kernel,
        (acc, first, scaled, flag, face, *got[2:], x_part, second),
        [vmem(FINE)] + coarse_messages,
        aliases={8: 0},
        scratch=[pltpu.VMEM((2, 5, 4, 2, 8, 128), F32)],
        flops=2 * 2**20,
    )
    got = exchange(*sent)
    (response,) = call(response_kernel, (coarse_smoother, face), [vmem((4, 25, 8, 128))], flops=2**20)
    acc, coarse = call(
        restricted_volume_kernel,
        (source, second, flag, jac8, damp8, coarse_smoother),
        [vmem(COARSE), vmem(COARSE)],
        flops=4 * 2**20,
    )
    coarse, *sent = call(
        restrict_kernel, (coarse, flag, response, *got), [vmem(COARSE)] + coarse_messages, flops=2**20
    )
    second_got, got = got, exchange(*sent)
    coarse, rhs = call(
        first_local_kernel,
        (coarse, acc, coarse_smoother, flag, jac8, damp8, face, *second_got),
        [vmem(COARSE), vmem(COARSE)],
        flops=4 * 2**20,
    )
    coarse, *sent = call(
        coarse_kernel, (coarse, flag, response, *got), [vmem(COARSE)] + coarse_messages, flops=2**20
    )
    got = exchange(*sent)
    (coarse,) = call(
        coarse_local_kernel, (coarse, rhs, coarse_smoother, flag, jac8, damp8), [vmem(COARSE)], flops=4 * 2**20
    )
    (out,) = call(
        last_kernel,
        (coarse, flag, response, *got, second),
        [jax.ShapeDtypeStruct(FINE, F32)],
        out_hbm=(0,),
        scratch=[pltpu.VMEM(FINE, F32), pltpu.SemaphoreType.DMA((5,))],
        flops=2**20,
    )
    return out.reshape(5, 4, 4, 4, 2, 2, 128)


def solution(mesh):
    in_specs = (
        P(None, None, None, None, "gx", "gy", None),
        P(None, None, None, "gx", "gy", None),
        P("gx", "gy", None),
        P(None, "gx", "gy", None),
        P(None, None, None, None, None, "gx", "gy", None),
        P(None, None, None, None, None, "gx", "gy", None),
    )
    out_specs = P(None, None, None, None, "gx", "gy", None)
    return jax.shard_map(body, mesh=mesh, in_specs=in_specs, out_specs=out_specs, check_vma=False)
```

```python
import functools
import math

import jax
import jax.numpy as jnp
import numpy as np
from jax import lax
from jax.experimental import pallas as pl
from jax.experimental.pallas import tpu as pltpu
from jax.sharding import PartitionSpec as P


F32 = jnp.float32
OMEGA = 0.8
FACE_LINES = [(a, b) for a in range(4) for b in range(4) if a in (0, 3) or b in (0, 3)]
H4 = 3.0
ROOT = 1.0 / math.sqrt(5.0)
NEAR = (1.0 + ROOT) / 2.0
FAR = (1.0 - ROOT) / 2.0


def lobatto_slopes():
    points = np.array([-1.0, -ROOT, ROOT, 1.0])
    weights = np.ones(4)
    for i in range(4):
        for j in range(4):
            if i != j:
                weights[i] = weights[i] / (points[i] - points[j])
    slopes = np.zeros((4, 4))
    for i in range(4):
        for j in range(4):
            if i != j:
                slopes[i, j] = weights[j] / weights[i] / (points[i] - points[j])
        slopes[i, i] = -np.sum(slopes[i])
    return slopes


D4 = lobatto_slopes()
PD = np.array([[1.0, NEAR, FAR, 0.0], [0.0, FAR, NEAR, 1.0]]) @ D4


def sum_of(terms):
    total = None
    for weight, value in terms:
        total = weight * value if total is None else total + weight * value
    return total


def rows():
    return lax.broadcasted_iota(jnp.int32, (8, 128), 0)


def x_low():
    return (rows() & 2) == 0


def y_low():
    return (rows() & 1) == 0


def c_low():
    return (rows() & 4) == 0


def sroll(value, shift):
    return pltpu.roll(value, shift % 8, 0)


def lroll(value, shift):
    return pltpu.roll(value, shift % 128, 1)


def twice(value):
    return jnp.concatenate([value, value], axis=0)


def axis_low(direction):
    return (x_low(), 2) if direction == 0 else (y_low(), 1)


def pack_low(first, second, direction):
    low, step = axis_low(direction)
    return jnp.where(low, first, sroll(second, step))


def pack_high(first, second, direction):
    low, step = axis_low(direction)
    return jnp.where(low, sroll(first, -step), second)


def slopes_along(u0, u1, u2, u3):
    e0, o0, e1, o1 = u0 + u3, u0 - u3, u1 + u2, u1 - u2
    diff = e1 - e0
    even_a = float((D4[0, 1] + D4[0, 2]) / 2.0) * diff
    even_b = float((D4[1, 2] - 0.0) / 2.0) * diff
    odd_a = float((D4[0, 0] - D4[0, 3]) / 2.0) * o0 + float((D4[0, 1] - D4[0, 2]) / 2.0) * o1
    odd_b = float((D4[1, 0] - D4[1, 3]) / 2.0) * o0 - float(D4[1, 2] / 2.0) * o1
    return even_a + odd_a, even_b + odd_b, odd_b - even_b, odd_a - even_a


def mix(matrix, fields):
    out = []
    for o in range(5):
        total = matrix[o][0] * fields[0]
        for i in range(1, 5):
            total = total + matrix[o][i] * fields[i]
        out.append(total)
    return out


def parity(axis):
    return lax.rem(lax.axis_index(axis), 2) == 0


def put_pair(even_ref, odd_ref, index, low_face, high_face, is_even):
    even_ref[index] = jnp.where(is_even, high_face, low_face)
    odd_ref[index] = jnp.where(is_even, low_face, high_face)


def fine_x_faces(u_ref, flag_ref, xo, xe):
    even_x, fx = parity("gx"), flag_ref[0] != 0
    for v in range(5):
        for n in range(4):
            low = pack_low(u_ref[v, 0, n, 0], u_ref[v, 0, n, 1], 0)
            h = [jnp.where(fx, u_ref[v, 3, 3 - n, q], u_ref[v, 3, n, q]) for q in range(2)]
            put_pair(xe, xo, (v, n), low, pack_high(h[0], h[1], 0), even_x)


def fine_y_faces(u_ref, flag_ref, yo, ye):
    even_y, fy = parity("gy"), flag_ref[1] != 0
    for v in range(5):
        for n in range(4):
            low = pack_low(u_ref[v, n, 0, 0], u_ref[v, n, 0, 1], 1)
            h = [jnp.where(fy, u_ref[v, 3 - n, 3, q], u_ref[v, n, 3, q]) for q in range(2)]
            put_pair(ye, yo, (v, n), low, pack_high(h[0], h[1], 1), even_y)


def restrict_c(first, second):
    low = c_low()
    middle = jnp.where(low, second, first)
    return jnp.where(low, first, second) + FAR * middle + NEAR * sroll(middle, 4)


def restrict_four(values):
    return values[0] + NEAR * values[1] + FAR * values[2], values[3] + NEAR * values[2] + FAR * values[1]


def put_coarse_faces(v, lows, highs, flag_ref, pairs):
    for d, axis in ((0, "gx"), (1, "gy")):
        flag = flag_ref[d] != 0
        low, high = lows[d], highs[d]
        turned = [jnp.where(flag, high[1 - m], high[m]) for m in range(2)]
        even_ref, odd_ref = pairs[d]
        put_pair(even_ref, odd_ref, v, pack_low(*low, d), pack_high(*turned, d), parity(axis))


def restricted_faces(u_ref, flag_ref, xo, xe, yo, ye):
    for v in range(5):
        line = {}
        for a in range(4):
            for b in range(4):
                if a in (0, 3) or b in (0, 3):
                    line[a, b] = restrict_c(u_ref[v, a, b, 0], u_ref[v, a, b, 1])
        lows = [restrict_four([line[0, n] for n in range(4)]), restrict_four([line[n, 0] for n in range(4)])]
        highs = [restrict_four([line[3, n] for n in range(4)]), restrict_four([line[n, 3] for n in range(4)])]
        put_coarse_faces(v, lows, highs, flag_ref, ((xe, xo), (ye, yo)))


def smoothed(smooth_ref, fields, a, b):
    out = []
    for o in range(5):
        total = [None, None]
        for i in range(5):
            block = smooth_ref[5 * o + i, a, b].astype(F32)
            for q in range(2):
                term = block[8 * q : 8 * q + 8] * fields[i][q]
                total[q] = term if i == 0 else total[q] + term
        out.append([OMEGA * total[q] for q in range(2)])
    return out


def first_line(src_ref, smooth_ref, u_ref, a, b):
    value = smoothed(smooth_ref, [[src_ref[v, a, b, q] for q in range(2)] for v in range(5)], a, b)
    for v in range(5):
        for q in range(2):
            u_ref[v, a, b, q] = value[v][q]


def line_copy(smooth_hbm, smooth_ref, sem, a, b):
    return pltpu.make_async_copy(smooth_hbm.at[:, a, b], smooth_ref.at[:, a, b], sem)


def first_kernel(
    src_hbm, smooth_hbm, orient_hbm, src_ref, smooth_ref, u_ref, flag_ref, xo, xe, yo, ye, sems, orient_ref, orient_sem
):
    every, inner = slice(0, 4), slice(1, 3)
    src_copy = pltpu.make_async_copy(src_hbm, src_ref, sems.at[4])
    src_copy.start()
    orient_copy = pltpu.make_async_copy(orient_hbm, orient_ref, orient_sem)
    orient_copy.start()
    copies = [
        line_copy(smooth_hbm, smooth_ref, sems.at[slot], a, b)
        for slot, (a, b) in enumerate(((0, every), (3, every), (inner, 0), (inner, 3)))
    ]
    for one in copies:
        one.start()
    lines = [[(0, b) for b in range(4)], [(3, b) for b in range(4)], [(1, 0), (2, 0)], [(1, 3), (2, 3)]]
    src_copy.wait()
    for slot, (one, group) in enumerate(zip(copies, lines)):
        one.wait()
        for a, b in group:
            first_line(src_ref, smooth_ref, u_ref, a, b)
        if slot == 1:
            orient_copy.wait()
            for d in range(3):
                flag_ref[d] = twice(orient_ref[d])
            fine_x_faces(u_ref, flag_ref, xo, xe)
    fine_y_faces(u_ref, flag_ref, yo, ye)


def prepare_tables(jac_ref, damp_ref, jac8_ref, damp8_ref, face_ref):
    damp = twice(damp_ref[...])
    damp8_ref[...] = damp
    for d in range(3):
        for k in range(25):
            value = twice(jac_ref[25 * d + k])
            jac8_ref[25 * d + k] = value
            if d < 2:
                low, step = axis_low(d)
                diagonal = k % 6 == 0
                upper = H4 * (value - damp if diagonal else value)
                lower = H4 * (value + damp if diagonal else value)
                face_ref[2 * d, k] = jnp.where(low, sroll(upper, -step), upper)
                face_ref[2 * d + 1, k] = jnp.where(low, lower, sroll(lower, step))


def volume(src_ref, u_ref, flag_ref, jac_ref, damp_ref, acc_ref, finish_lines):
    damp = H4 * damp_ref[...]

    def jacobian(d):
        return [[jac_ref[25 * d + 5 * o + i] for i in range(5)] for o in range(5)]

    def along(direction, others):
        low, step = axis_low(direction)
        flag = flag_ref[direction] != 0
        flag_before = sroll(flag_ref[direction], step) != 0

        def at(v, n, other, q):
            return (v, n, other, q) if direction == 0 else (v, other, n, q)

        def step_fn(j, carry):
            other, q = others(j // 2), j % 2
            u = [[u_ref[at(v, n, other, q)] for n in range(4)] for v in range(5)]
            waves = []
            jumps = []
            for v in range(5):
                back_low, back_high = u_ref[at(v, 0, 3 - other, q)], u_ref[at(v, 3, 3 - other, q)]
                right = sroll(jnp.where(flag_before, back_low, u[v][0]), -step)
                left = sroll(jnp.where(flag, back_high, u[v][3]), step)
                jump_right = jnp.where(low, right, 0.0) - u[v][3]
                jump_left = jnp.where(low, 0.0, left) - u[v][0]
                w = list(slopes_along(*u[v]))
                w[3] = w[3] + H4 * jump_right
                w[0] = w[0] - H4 * jump_left
                waves.append(w)
                jumps.append((damp * jump_left, None, None, damp * jump_right))
            matrix = jacobian(direction)
            for n in range(4):
                flux = mix(matrix, [waves[v][n] for v in range(5)])
                for v in range(5):
                    if direction == 1:
                        total = src_ref[at(v, n, other, q)] - 2.0 * u[v][n]
                    else:
                        total = acc_ref[at(v, n, other, q)]
                    total = total - flux[v]
                    if jumps[v][n] is not None:
                        total = total + jumps[v][n]
                    acc_ref[at(v, n, other, q)] = total
            return carry

        return step_fn

    low = c_low()
    flag = jnp.where(low, lroll(flag_ref[2], 1), flag_ref[2]) != 0
    damp_z = damp
    coef = [
        [jnp.where(low, float(D4[2 * p, c]), float(D4[2 * p + 1, c ^ 1])).astype(F32) for c in range(4)]
        for p in range(2)
    ]

    def step_z(j, carry):
        a0, b = j // 4, j % 4
        here = (a0, 3 - a0)
        u = [[[u_ref[v, a, b, q] for q in range(2)] for v in range(5)] for a in here]
        turned = [[[sroll(u[s][v][q], 4) for q in range(2)] for v in range(5)] for s in range(2)]
        beside = []
        for s in range(2):
            line = []
            for v in range(5):
                face = jnp.where(low, turned[s][v][1], turned[s][v][0])
                line.append(jnp.where(low, lroll(face, 1), lroll(face, -1)))
            beside.append(line)
        matrix = jacobian(2)
        for s in range(2):
            waves = [[], []]
            jumps = []
            for v in range(5):
                own = jnp.where(low, u[s][v][0], u[s][v][1])
                jump = jnp.where(flag, beside[1 - s][v], beside[s][v]) - own
                jumps.append(damp_z * jump)
                lifted = H4 * jump
                for p in range(2):
                    w = coef[p][0] * u[s][v][0] + coef[p][1] * turned[s][v][0]
                    w = w + (coef[p][2] * u[s][v][1] + coef[p][3] * turned[s][v][1])
                    w = w - jnp.where(low, lifted, 0.0) if p == 0 else w + jnp.where(low, 0.0, lifted)
                    waves[p].append(w)
            for p in range(2):
                flux = mix(matrix, waves[p])
                for v in range(5):
                    part = jnp.where(low, jumps[v], 0.0) if p == 0 else jnp.where(low, 0.0, jumps[v])
                    acc_ref[v, here[s], b, p] = acc_ref[v, here[s], b, p] - flux[v] + part
        return carry

    lax.fori_loop(0, 4, along(1, lambda k: 3 * k), 0)
    lax.fori_loop(0, 4, step_z, 0)
    finish_lines()
    lax.fori_loop(0, 4, along(1, lambda k: 1 + k), 0)
    lax.fori_loop(4, 8, step_z, 0)
    lax.fori_loop(0, 8, along(0, lambda k: k), 0)


def first_volume_kernel(
    smooth_hbm, src_ref, smooth_in, u_in, flag_ref, jac_ref, damp_ref,
    smooth_ref, u_ref, acc_ref, jac8_ref, damp8_ref, face_ref, second_ref, scaled_ref, sem,
):
    inner = slice(1, 3)
    copy = line_copy(smooth_hbm, smooth_ref, sem, inner, inner)
    copy.start()
    prepare_tables(jac_ref, damp_ref, jac8_ref, damp8_ref, face_ref)
    lines = [(a, b) for a in (1, 2) for b in (1, 2)]

    def finish_lines():
        copy.wait()
        for a, b in lines:
            first_line(src_ref, smooth_ref, u_ref, a, b)

    volume(src_ref, u_ref, flag_ref, jac8_ref, damp8_ref, acc_ref, finish_lines)
    for a, b in lines:
        change = smoothed(smooth_ref, [[acc_ref[v, a, b, q] for q in range(2)] for v in range(5)], a, b)
        for v in range(5):
            for q in range(2):
                second_ref[v, a, b, q] = u_ref[v, a, b, q] + change[v][q]
    for line, (a, b) in enumerate(FACE_LINES):
        for k in range(25):
            block = OMEGA * smooth_ref[k, a, b].astype(F32)
            for q in range(2):
                scaled_ref[line, k, q] = block[8 * q : 8 * q + 8]


def remote_parts(d, odd, even, flag_ref, face_ref, part_ref):
    is_even = parity(("gx", "gy")[d])
    low, step = axis_low(d)
    flag = flag_ref[d]
    flag = jnp.where(low, sroll(flag, -step), flag) != 0
    matrix = [[face_ref[2 * d, 5 * o + i] for i in range(5)] for o in range(5)]
    for n in range(4):
        take = lambda v, m: jnp.where(is_even, even[v, m], odd[v, m])
        right = [jnp.where(flag, take(v, 3 - n), take(v, n)) for v in range(5)]
        for v, value in enumerate(mix(matrix, right)):
            part_ref[0, v, n, 0] = jnp.where(low, 0.0, -sroll(value, step))
            part_ref[0, v, n, 1] = jnp.where(low, 0.0, -value)
    matrix = [[face_ref[2 * d + 1, 5 * o + i] for i in range(5)] for o in range(5)]
    for n in range(4):
        left = [jnp.where(is_even, odd[v, n], even[v, n]) for v in range(5)]
        for v, value in enumerate(mix(matrix, left)):
            part_ref[1, v, n, 0] = jnp.where(low, value, 0.0)
            part_ref[1, v, n, 1] = jnp.where(low, sroll(value, -step), 0.0)


def second_lines(lines, acc_ref, x_part_ref, y_part_ref, scaled_ref, u_ref, out_ref):
    for a, b in lines:
        line = FACE_LINES.index((a, b))
        for q in range(2):
            left = [acc_ref[v, a, b, q] for v in range(5)]
            for v in range(5):
                if a in (0, 3):
                    left[v] = left[v] + x_part_ref[0 if a == 3 else 1, v, b, q]
                if b in (0, 3):
                    left[v] = left[v] + y_part_ref[0 if b == 3 else 1, v, a, q]
            matrix = [[scaled_ref[line, 5 * o + i, q] for i in range(5)] for o in range(5)]
            for v, value in enumerate(mix(matrix, left)):
                out_ref[v, a, b, q] = u_ref[v, a, b, q] + value


X_LINES = [(a, b) for a in (0, 3) for b in (1, 2)]


def second_x_kernel(acc_ref, u_ref, scaled_ref, flag_ref, face_ref, rxo, rxe, inner_ref, out_ref, part_ref):
    remote_parts(0, rxo, rxe, flag_ref, face_ref, part_ref)
    second_lines(X_LINES, acc_ref, part_ref, None, scaled_ref, u_ref, out_ref)


def second_kernel(
    acc_ref, u_ref, scaled_ref, flag_ref, face_ref, ryo, rye, x_part_ref, held_ref, out_ref, xo, xe, yo, ye, part_ref
):
    remote_parts(1, ryo, rye, flag_ref, face_ref, part_ref)
    lines = [line for line in FACE_LINES if line not in X_LINES]
    second_lines(lines, acc_ref, x_part_ref, part_ref, scaled_ref, u_ref, out_ref)
    restricted_faces(out_ref, flag_ref, xo, xe, yo, ye)


def coarse_smooth(smooth_ref, fields):
    out = [[[None, None], [None, None]] for _ in range(5)]
    for i in range(2):
        for o in range(5):
            total = [None, None]
            for k in range(5):
                block = smooth_ref[5 * o + k, i].astype(F32)
                for j in range(2):
                    term = block[8 * j : 8 * j + 8] * fields[k][i][j]
                    total[j] = term if k == 0 else total[j] + term
            for j in range(2):
                out[o][i][j] = OMEGA * total[j]
    return out


def coarse_faces(field, flag_ref, xo, xe, yo, ye):
    for v in range(5):
        c = field[v]
        lows = [[c[0][0], c[0][1]], [c[0][0], c[1][0]]]
        highs = [[c[1][0], c[1][1]], [c[0][1], c[1][1]]]
        put_coarse_faces(v, lows, highs, flag_ref, ((xe, xo), (ye, yo)))


def response_kernel(smooth_ref, face_ref, response_ref):
    packed = []
    for k in range(25):
        by_i = [smooth_ref[k, i].astype(F32) for i in range(2)]
        node = [[by_i[i][8 * j : 8 * j + 8] for j in range(2)] for i in range(2)]
        packed.append(
            (
                pack_high(node[1][0], node[1][1], 0),
                pack_low(node[0][0], node[0][1], 0),
                pack_high(node[0][1], node[1][1], 1),
                pack_low(node[0][0], node[1][0], 1),
            )
        )
    for f in range(4):
        for o in range(5):
            for i in range(5):
                total = packed[5 * o][f] * face_ref[f, i]
                for k in range(1, 5):
                    total = total + packed[5 * o + k][f] * face_ref[f, 5 * k + i]
                response_ref[f, 5 * o + i] = (OMEGA / 6.0) * total


def restricted_volume_kernel(src_ref, u_ref, flag_ref, jac_ref, damp_ref, smooth_ref, acc_ref, c_ref):
    damp = H4 * damp_ref[...]
    low_c = c_low()
    slope = [
        jnp.where(low_c, float(PD[0, c]), float(PD[1, c ^ 1])).astype(F32) for c in range(4)
    ]
    flags = [flag_ref[0] != 0, flag_ref[1] != 0, jnp.where(low_c, lroll(flag_ref[2], 1), flag_ref[2]) != 0]
    sign = jnp.where(low_c, -H4, H4).astype(F32)
    waves = [[[[None] * 5 for _ in range(2)] for _ in range(2)] for _ in range(3)]

    def slopes_four(values):
        return [sum_of([(float(PD[i, n]), values[n]) for n in range(4)]) for i in range(2)]

    for v in range(5):
        line, slope_c, ends = {}, {}, {}
        for a in range(4):
            for b in range(4):
                first, second = u_ref[v, a, b, 0], u_ref[v, a, b, 1]
                line[a, b] = restrict_c(first, second)
                slope_c[a, b] = (slope[0] * first + slope[1] * sroll(first, 4)) + (
                    slope[2] * second + slope[3] * sroll(second, 4)
                )
                ends[a, b] = jnp.where(low_c, first, second)

        def along_b(table):
            return [restrict_four([table[a, b] for b in range(4)]) for a in range(4)]

        def both(table):
            by_b = along_b(table)
            return [restrict_four([by_b[a][j] for a in range(4)]) for j in range(2)]

        by_b = along_b(line)
        by_a = [restrict_four([line[a, b] for a in range(4)]) for b in range(4)]
        flux_z = both(slope_c)
        trace_z = both(ends)
        sources = both({(a, b): restrict_c(src_ref[v, a, b, 0], src_ref[v, a, b, 1]) for a in range(4) for b in range(4)})
        acc = [[None, None], [None, None]]
        for j in range(2):
            value = restrict_four([by_b[a][j] for a in range(4)])
            flux = slopes_four([by_b[a][j] for a in range(4)])
            for i in range(2):
                acc[i][j] = sources[j][i] - 2.0 * value[i]
                waves[0][i][j][v] = flux[i]
        for i in range(2):
            flux = slopes_four([by_a[b][i] for b in range(4)])
            for j in range(2):
                waves[1][i][j][v] = flux[j]
        for d, lo, hi in ((0, by_b[0], by_b[3]), (1, by_a[0], by_a[3])):
            low, step = axis_low(d)
            flag = flags[d]
            flag_before = sroll(flag_ref[d], step) != 0
            for m in range(2):
                right = sroll(jnp.where(flag_before, lo[1 - m], lo[m]), -step)
                left = sroll(jnp.where(flag, hi[1 - m], hi[m]), step)
                jump_right = jnp.where(low, right, 0.0) - hi[m]
                jump_left = jnp.where(low, 0.0, left) - lo[m]
                i, j = (1, m) if d == 0 else (m, 1)
                waves[d][i][j][v] = waves[d][i][j][v] + H4 * jump_right
                acc[i][j] = acc[i][j] + damp * jump_right
                i, j = (0, m) if d == 0 else (m, 0)
                waves[d][i][j][v] = waves[d][i][j][v] - H4 * jump_left
                acc[i][j] = acc[i][j] + damp * jump_left
        beside = []
        for j in range(2):
            turned = [sroll(trace_z[j][i], 4) for i in range(2)]
            beside.append([jnp.where(low_c, lroll(t, 1), lroll(t, -1)) for t in turned])
        for i in range(2):
            for j in range(2):
                jump = jnp.where(flags[2], beside[j][1 - i], beside[j][i]) - trace_z[j][i]
                waves[2][i][j][v] = flux_z[j][i] + sign * jump
                acc_ref[v, i, j] = acc[i][j] + damp * jump
    for d in range(3):
        matrix = [[jac_ref[25 * d + 5 * o + i] for i in range(5)] for o in range(5)]
        for i in range(2):
            for j in range(2):
                for v, value in enumerate(mix(matrix, waves[d][i][j])):
                    acc_ref[v, i, j] = acc_ref[v, i, j] - value
    c = coarse_smooth(smooth_ref, [[[acc_ref[v, i, j] for j in range(2)] for i in range(2)] for v in range(5)])
    put_field(c_ref, c)


def put_field(out_ref, c):
    for v in range(5):
        for i in range(2):
            for j in range(2):
                out_ref[v, i, j] = c[v][i][j]


def get_field(ref):
    return [[[ref[v, i, j] for j in range(2)] for i in range(2)] for v in range(5)]


def add_remote(field, scale, flag_ref, face_ref, rxo, rxe, ryo, rye):
    for d, axis in ((0, "gx"), (1, "gy")):
        is_even = parity(axis)
        low, step = axis_low(d)
        flag = flag_ref[d]
        flag = jnp.where(low, sroll(flag, -step), flag) != 0
        even, odd = ((rxe, rxo), (rye, ryo))[d]
        at = (lambda n, m: (n, m)) if d == 0 else (lambda n, m: (m, n))
        right, left = [], []
        for v in range(5):
            value = scale * jnp.where(is_even, even[v], odd[v])
            swapped = jnp.where(low, sroll(value, -step), sroll(value, step))
            right.append(jnp.where(flag, swapped, value))
            left.append(scale * jnp.where(is_even, odd[v], even[v]))
        upper = [[face_ref[2 * d, 5 * o + i] for i in range(5)] for o in range(5)]
        lower = [[face_ref[2 * d + 1, 5 * o + i] for i in range(5)] for o in range(5)]
        for v, value in enumerate(mix(upper, right)):
            for m, part in enumerate((sroll(value, step), value)):
                i, j = at(1, m)
                field[v][i][j] = field[v][i][j] - jnp.where(low, 0.0, part)
        for v, value in enumerate(mix(lower, left)):
            for m, part in enumerate((value, sroll(value, -step))):
                i, j = at(0, m)
                field[v][i][j] = field[v][i][j] + jnp.where(low, part, 0.0)


def restrict_kernel(local_ref, flag_ref, response_ref, rxo, rxe, ryo, rye, c_ref, xo, xe, yo, ye):
    c = get_field(local_ref)
    add_remote(c, 6.0, flag_ref, response_ref, rxo, rxe, ryo, rye)
    put_field(c_ref, c)
    coarse_faces(c, flag_ref, xo, xe, yo, ye)


def first_local_kernel(
    c_ref, acc_ref, smooth_ref, flag_ref, jac_ref, damp_ref, face_ref, rxo, rxe, ryo, rye, out_ref, rhs_ref
):
    rhs = get_field(acc_ref)
    add_remote(rhs, 1.0, flag_ref, face_ref, rxo, rxe, ryo, rye)
    put_field(rhs_ref, rhs)
    coarse_local_kernel(c_ref, rhs_ref, smooth_ref, flag_ref, jac_ref, damp_ref, out_ref)


def coarse_local_kernel(c_ref, rhs_ref, smooth_ref, flag_ref, jac_ref, damp_ref, out_ref):
    damp = 0.5 * damp_ref[...]
    c = [[[c_ref[v, i, j] for j in range(2)] for i in range(2)] for v in range(5)]
    acc = [[[rhs_ref[v, i, j] - 2.0 * c[v][i][j] for j in range(2)] for i in range(2)] for v in range(5)]
    for d in range(2):
        low, step = axis_low(d)
        flag = flag_ref[d] != 0
        flag_before = sroll(flag_ref[d], step) != 0
        matrix = [[jac_ref[25 * d + 5 * o + i] for i in range(5)] for o in range(5)]
        at = (lambda n, m: (n, m)) if d == 0 else (lambda n, m: (m, n))
        waves = [[[None] * 5, [None] * 5] for _ in range(2)]
        for v in range(5):
            lo = [c[v][at(0, m)[0]][at(0, m)[1]] for m in range(2)]
            hi = [c[v][at(1, m)[0]][at(1, m)[1]] for m in range(2)]
            for m in range(2):
                right = jnp.where(low, sroll(jnp.where(flag_before, lo[1 - m], lo[m]), -step), 0.0)
                left = jnp.where(low, 0.0, sroll(jnp.where(flag, hi[1 - m], hi[m]), step))
                waves[1][m][v] = 0.5 * (right - lo[m])
                waves[0][m][v] = 0.5 * (hi[m] - left)
                i, j = at(1, m)
                acc[v][i][j] = acc[v][i][j] + damp * (right - hi[m])
                i, j = at(0, m)
                acc[v][i][j] = acc[v][i][j] + damp * (left - lo[m])
        for n in range(2):
            for m in range(2):
                i, j = at(n, m)
                for v, value in enumerate(mix(matrix, waves[n][m])):
                    acc[v][i][j] = acc[v][i][j] - value
    low = c_low()
    flag = jnp.where(low, lroll(flag_ref[2], 1), flag_ref[2]) != 0
    half = jnp.where(low, 0.5, -0.5).astype(F32)
    matrix = [[jac_ref[50 + 5 * o + i] for i in range(5)] for o in range(5)]
    turned = [[[sroll(c[v][i][j], 4) for j in range(2)] for i in range(2)] for v in range(5)]
    beside = [
        [[jnp.where(low, lroll(t, 1), lroll(t, -1)) for t in turned[v][i]] for i in range(2)] for v in range(5)
    ]
    for i in range(2):
        for j in range(2):
            wave = []
            for v in range(5):
                next_to = jnp.where(flag, beside[v][1 - i][j], beside[v][i][j])
                wave.append(half * (turned[v][i][j] - next_to))
                acc[v][i][j] = acc[v][i][j] + damp * (next_to - c[v][i][j])
            for v, value in enumerate(mix(matrix, wave)):
                acc[v][i][j] = acc[v][i][j] - value
    change = coarse_smooth(smooth_ref, acc)
    for v in range(5):
        for i in range(2):
            for j in range(2):
                out_ref[v, i, j] = c[v][i][j] + change[v][i][j]


def coarse_kernel(c_ref, flag_ref, response_ref, rxo, rxe, ryo, rye, out_ref, xo, xe, yo, ye):
    c = get_field(c_ref)
    add_remote(c, 1.0, flag_ref, response_ref, rxo, rxe, ryo, rye)
    put_field(out_ref, c)
    coarse_faces(c, flag_ref, xo, xe, yo, ye)


def spread(first, second):
    return first, NEAR * first + FAR * second, FAR * first + NEAR * second, second


def last_kernel(
    c_ref, flag_ref, response_ref, rxo, rxe, ryo, rye, second_ref, out_hbm, out_ref, sems
):
    c = get_field(c_ref)
    add_remote(c, 1.0, flag_ref, response_ref, rxo, rxe, ryo, rye)
    low = c_low()
    copies = []
    for v in range(5):
        by_c = [[None, None], [None, None]]
        for i in range(2):
            for j in range(2):
                value = c[v][i][j]
                inner = FAR * value + NEAR * sroll(value, 4)
                by_c[i][j] = (jnp.where(low, value, inner), jnp.where(low, inner, value))
        for q in range(2):
            lines = [spread(by_c[i][0][q], by_c[i][1][q]) for i in range(2)]
            for b in range(4):
                for a, value in enumerate(spread(lines[0][b], lines[1][b])):
                    out_ref[v, a, b, q] = second_ref[v, a, b, q] + value
        if v in (2, 4):
            part = slice(0, 3) if v == 2 else slice(3, 5)
            copy = pltpu.make_async_copy(out_ref.at[part], out_hbm.at[part], sems.at[len(copies)])
            copy.start()
            copies.append(copy)
    for copy in copies:
        copy.wait()


FINE = (5, 4, 4, 2, 8, 128)
FINE_MESSAGE = (5, 4, 8, 128)
COARSE = (5, 2, 2, 8, 128)
COARSE_MESSAGE = (5, 8, 128)


def vmem(shape, dtype=F32):
    return pltpu.VMEM(shape, dtype)


def here(array):
    return pltpu.with_memory_space_constraint(array, pltpu.VMEM)


def call(kernel, args, outs, in_hbm=(), out_hbm=(), scratch=(), aliases=None, flops=0):
    in_specs = [
        pl.BlockSpec(memory_space=pltpu.HBM if k in in_hbm else pltpu.VMEM) for k in range(len(args))
    ]
    out_specs = [
        pl.BlockSpec(memory_space=pltpu.HBM if k in out_hbm else pltpu.VMEM) for k in range(len(outs))
    ]
    args = [pltpu.with_memory_space_constraint(a, pltpu.HBM) if k in in_hbm else here(a) for k, a in enumerate(args)]
    return pl.pallas_call(
        kernel,
        out_shape=outs,
        in_specs=in_specs,
        out_specs=out_specs,
        scratch_shapes=scratch,
        input_output_aliases=aliases or {},
        compiler_params=pltpu.CompilerParams(vmem_limit_bytes=8 * 2**20),
        cost_estimate=pl.CostEstimate(flops=flops, bytes_accessed=4 * 2**20, transcendentals=0),
    )(*args)


def partners(axis):
    size = lax.axis_size(axis)
    even = [(i, i ^ 1) for i in range(size)]
    odd = [(i, (i - 1) % size if i % 2 == 0 else (i + 1) % size) for i in range(size)]
    return even, odd


def exchange(xo, xe, yo, ye):
    even_x, odd_x = partners("gx")
    even_y, odd_y = partners("gy")
    xo = lax.ppermute(xo, "gx", odd_x)
    xe = lax.ppermute(xe, "gx", even_x)
    yo = lax.ppermute(yo, "gy", odd_y)
    ye = lax.ppermute(ye, "gy", even_y)
    return xo, xe, yo, ye


def body(source, jacobian, damping, orient, smoother, coarse_smoother):
    source = source.reshape(FINE)
    smoother = smoother.reshape(25, 4, 4, 16, 128)
    coarse_smoother = coarse_smoother.reshape(25, 2, 16, 128)
    jacobian = jacobian.reshape(75, 4, 128)
    damping = damping.reshape(4, 128)
    orient = orient.reshape(3, 4, 128)
    fine_messages = [vmem(FINE_MESSAGE)] * 4
    coarse_messages = [vmem(COARSE_MESSAGE)] * 4

    held = vmem(smoother.shape, smoother.dtype)
    smoother_in = smoother
    source, smoother, first, flag, *sent = call(
        first_kernel,
        (source, smoother_in, orient),
        [vmem(FINE), held, vmem(FINE), vmem((3, 8, 128), jnp.int32)] + fine_messages,
        in_hbm=(0, 1, 2),
        scratch=[pltpu.SemaphoreType.DMA((5,)), pltpu.VMEM((3, 4, 128), jnp.int32), pltpu.SemaphoreType.DMA],
        flops=2 * 25 * 64 * 512,
    )
    got = exchange(*sent)
    _, first, acc, jac8, damp8, face, second, scaled = call(
        first_volume_kernel,
        (smoother_in, source, smoother, first, flag, jacobian, damping),
        [held, vmem(FINE), vmem(FINE), vmem((75, 8, 128)), vmem((8, 128)), vmem((4, 25, 8, 128)), vmem(FINE), vmem((12, 25, 2, 8, 128))],
        in_hbm=(0,),
        aliases={2: 0, 3: 1},
        scratch=[pltpu.SemaphoreType.DMA],
        flops=9 * 2**20,
    )
    part = vmem((2, 5, 4, 2, 8, 128))
    second, x_part = call(
        second_x_kernel,
        (acc, first, scaled, flag, face, *got[:2], second),
        [vmem(FINE), part],
        aliases={7: 0},
        flops=2**20,
    )
    second, *sent = call(
        second_kernel,
        (acc, first, scaled, flag, face, *got[2:], x_part, second),
        [vmem(FINE)] + coarse_messages,
        aliases={8: 0},
        scratch=[pltpu.VMEM((2, 5, 4, 2, 8, 128), F32)],
        flops=2 * 2**20,
    )
    got = exchange(*sent)
    (response,) = call(response_kernel, (coarse_smoother, face), [vmem((4, 25, 8, 128))], flops=2**20)
    acc, coarse = call(
        restricted_volume_kernel,
        (source, second, flag, jac8, damp8, coarse_smoother),
        [vmem(COARSE), vmem(COARSE)],
        flops=4 * 2**20,
    )
    coarse, *sent = call(
        restrict_kernel, (coarse, flag, response, *got), [vmem(COARSE)] + coarse_messages, flops=2**20
    )
    second_got, got = got, exchange(*sent)
    coarse, rhs = call(
        first_local_kernel,
        (coarse, acc, coarse_smoother, flag, jac8, damp8, face, *second_got),
        [vmem(COARSE), vmem(COARSE)],
        flops=4 * 2**20,
    )
    coarse, *sent = call(
        coarse_kernel, (coarse, flag, response, *got), [vmem(COARSE)] + coarse_messages, flops=2**20
    )
    got = exchange(*sent)
    (coarse,) = call(
        coarse_local_kernel, (coarse, rhs, coarse_smoother, flag, jac8, damp8), [vmem(COARSE)], flops=4 * 2**20
    )
    (out,) = call(
        last_kernel,
        (coarse, flag, response, *got, second),
        [jax.ShapeDtypeStruct(FINE, F32)],
        out_hbm=(0,),
        scratch=[pltpu.VMEM(FINE, F32), pltpu.SemaphoreType.DMA((2,))],
        flops=2**20,
    )
    return out.reshape(5, 4, 4, 4, 2, 2, 128)


def solution(mesh):
    in_specs = (
        P(None, None, None, None, "gx", "gy", None),
        P(None, None, None, "gx", "gy", None),
        P("gx", "gy", None),
        P(None, "gx", "gy", None),
        P(None, None, None, None, None, "gx", "gy", None),
        P(None, None, None, None, None, "gx", "gy", None),
    )
    out_specs = P(None, None, None, None, "gx", "gy", None)
    return jax.shard_map(body, mesh=mesh, in_specs=in_specs, out_specs=out_specs, check_vma=False)
```

```python
import functools
import math

import jax
import jax.numpy as jnp
import numpy as np
from jax import lax
from jax.experimental import pallas as pl
from jax.experimental.pallas import tpu as pltpu
from jax.sharding import PartitionSpec as P


F32 = jnp.float32
OMEGA = 0.8
FACE_LINES = [(a, b) for a in range(4) for b in range(4) if a in (0, 3) or b in (0, 3)]
H4 = 3.0
ROOT = 1.0 / math.sqrt(5.0)
NEAR = (1.0 + ROOT) / 2.0
FAR = (1.0 - ROOT) / 2.0


def lobatto_slopes():
    points = np.array([-1.0, -ROOT, ROOT, 1.0])
    weights = np.ones(4)
    for i in range(4):
        for j in range(4):
            if i != j:
                weights[i] = weights[i] / (points[i] - points[j])
    slopes = np.zeros((4, 4))
    for i in range(4):
        for j in range(4):
            if i != j:
                slopes[i, j] = weights[j] / weights[i] / (points[i] - points[j])
        slopes[i, i] = -np.sum(slopes[i])
    return slopes


D4 = lobatto_slopes()
PD = np.array([[1.0, NEAR, FAR, 0.0], [0.0, FAR, NEAR, 1.0]]) @ D4


def sum_of(terms):
    total = None
    for weight, value in terms:
        total = weight * value if total is None else total + weight * value
    return total


def rows():
    return lax.broadcasted_iota(jnp.int32, (8, 128), 0)


def x_low():
    return (rows() & 2) == 0


def y_low():
    return (rows() & 1) == 0


def c_low():
    return (rows() & 4) == 0


def sroll(value, shift):
    return pltpu.roll(value, shift % 8, 0)


def lroll(value, shift):
    return pltpu.roll(value, shift % 128, 1)


def twice(value):
    return jnp.concatenate([value, value], axis=0)


def axis_low(direction):
    return (x_low(), 2) if direction == 0 else (y_low(), 1)


def pack_low(first, second, direction):
    low, step = axis_low(direction)
    return jnp.where(low, first, sroll(second, step))


def pack_high(first, second, direction):
    low, step = axis_low(direction)
    return jnp.where(low, sroll(first, -step), second)


def slopes_along(u0, u1, u2, u3):
    e0, o0, e1, o1 = u0 + u3, u0 - u3, u1 + u2, u1 - u2
    diff = e1 - e0
    even_a = float((D4[0, 1] + D4[0, 2]) / 2.0) * diff
    even_b = float((D4[1, 2] - 0.0) / 2.0) * diff
    odd_a = float((D4[0, 0] - D4[0, 3]) / 2.0) * o0 + float((D4[0, 1] - D4[0, 2]) / 2.0) * o1
    odd_b = float((D4[1, 0] - D4[1, 3]) / 2.0) * o0 - float(D4[1, 2] / 2.0) * o1
    return even_a + odd_a, even_b + odd_b, odd_b - even_b, odd_a - even_a


def mix(matrix, fields):
    out = []
    for o in range(5):
        total = matrix[o][0] * fields[0]
        for i in range(1, 5):
            total = total + matrix[o][i] * fields[i]
        out.append(total)
    return out


def parity(axis):
    return lax.rem(lax.axis_index(axis), 2) == 0


def put_pair(even_ref, odd_ref, index, low_face, high_face, is_even):
    even_ref[index] = jnp.where(is_even, high_face, low_face)
    odd_ref[index] = jnp.where(is_even, low_face, high_face)


def fine_faces(u_ref, flag_ref, xo, xe, yo, ye):
    even_x, even_y = parity("gx"), parity("gy")
    fx, fy = flag_ref[0] != 0, flag_ref[1] != 0
    for v in range(5):
        for n in range(4):
            low = pack_low(u_ref[v, 0, n, 0], u_ref[v, 0, n, 1], 0)
            h = [jnp.where(fx, u_ref[v, 3, 3 - n, q], u_ref[v, 3, n, q]) for q in range(2)]
            put_pair(xe, xo, (v, n), low, pack_high(h[0], h[1], 0), even_x)
            low = pack_low(u_ref[v, n, 0, 0], u_ref[v, n, 0, 1], 1)
            h = [jnp.where(fy, u_ref[v, 3 - n, 3, q], u_ref[v, n, 3, q]) for q in range(2)]
            put_pair(ye, yo, (v, n), low, pack_high(h[0], h[1], 1), even_y)


def restrict_c(first, second):
    low = c_low()
    middle = jnp.where(low, second, first)
    return jnp.where(low, first, second) + FAR * middle + NEAR * sroll(middle, 4)


def restrict_four(values):
    return values[0] + NEAR * values[1] + FAR * values[2], values[3] + NEAR * values[2] + FAR * values[1]


def put_coarse_faces(v, lows, highs, flag_ref, pairs):
    for d, axis in ((0, "gx"), (1, "gy")):
        flag = flag_ref[d] != 0
        low, high = lows[d], highs[d]
        turned = [jnp.where(flag, high[1 - m], high[m]) for m in range(2)]
        even_ref, odd_ref = pairs[d]
        put_pair(even_ref, odd_ref, v, pack_low(*low, d), pack_high(*turned, d), parity(axis))


def restricted_faces(u_ref, flag_ref, xo, xe, yo, ye):
    for v in range(5):
        line = {}
        for a in range(4):
            for b in range(4):
                if a in (0, 3) or b in (0, 3):
                    line[a, b] = restrict_c(u_ref[v, a, b, 0], u_ref[v, a, b, 1])
        lows = [restrict_four([line[0, n] for n in range(4)]), restrict_four([line[n, 0] for n in range(4)])]
        highs = [restrict_four([line[3, n] for n in range(4)]), restrict_four([line[n, 3] for n in range(4)])]
        put_coarse_faces(v, lows, highs, flag_ref, ((xe, xo), (ye, yo)))


def smoothed(smooth_ref, fields, a, b):
    out = []
    for o in range(5):
        total = [None, None]
        for i in range(5):
            block = smooth_ref[5 * o + i, a, b].astype(F32)
            for q in range(2):
                term = block[8 * q : 8 * q + 8] * fields[i][q]
                total[q] = term if i == 0 else total[q] + term
        out.append([OMEGA * total[q] for q in range(2)])
    return out


def first_line(src_ref, smooth_ref, u_ref, a, b):
    value = smoothed(smooth_ref, [[src_ref[v, a, b, q] for q in range(2)] for v in range(5)], a, b)
    for v in range(5):
        for q in range(2):
            u_ref[v, a, b, q] = value[v][q]


def line_copy(smooth_hbm, smooth_ref, sem, a, b):
    return pltpu.make_async_copy(smooth_hbm.at[:, a, b], smooth_ref.at[:, a, b], sem)


def first_kernel(
    src_hbm, smooth_hbm, orient_hbm, src_ref, smooth_ref, u_ref, flag_ref, xo, xe, yo, ye, sems, orient_ref, orient_sem
):
    every, inner = slice(0, 4), slice(1, 3)
    src_copy = pltpu.make_async_copy(src_hbm, src_ref, sems.at[4])
    src_copy.start()
    orient_copy = pltpu.make_async_copy(orient_hbm, orient_ref, orient_sem)
    orient_copy.start()
    copies = [
        line_copy(smooth_hbm, smooth_ref, sems.at[slot], a, b)
        for slot, (a, b) in enumerate(((0, every), (3, every), (inner, 0), (inner, 3)))
    ]
    for one in copies:
        one.start()
    lines = [[(0, b) for b in range(4)], [(3, b) for b in range(4)], [(1, 0), (2, 0)], [(1, 3), (2, 3)]]
    src_copy.wait()
    for one, group in zip(copies, lines):
        one.wait()
        for a, b in group:
            first_line(src_ref, smooth_ref, u_ref, a, b)
    orient_copy.wait()
    for d in range(3):
        flag_ref[d] = twice(orient_ref[d])
    fine_faces(u_ref, flag_ref, xo, xe, yo, ye)


def prepare_tables(jac_ref, damp_ref, jac8_ref, damp8_ref, face_ref):
    damp = twice(damp_ref[...])
    damp8_ref[...] = damp
    for d in range(3):
        for k in range(25):
            value = twice(jac_ref[25 * d + k])
            jac8_ref[25 * d + k] = value
            if d < 2:
                low, step = axis_low(d)
                diagonal = k % 6 == 0
                upper = H4 * (value - damp if diagonal else value)
                lower = H4 * (value + damp if diagonal else value)
                face_ref[2 * d, k] = jnp.where(low, sroll(upper, -step), upper)
                face_ref[2 * d + 1, k] = jnp.where(low, lower, sroll(lower, step))


def volume(src_ref, u_ref, flag_ref, jac_ref, damp_ref, acc_ref, finish_lines):
    damp = H4 * damp_ref[...]

    def jacobian(d):
        return [[jac_ref[25 * d + 5 * o + i] for i in range(5)] for o in range(5)]

    def along(direction, others):
        low, step = axis_low(direction)
        flag = flag_ref[direction] != 0
        flag_before = sroll(flag_ref[direction], step) != 0

        def at(v, n, other, q):
            return (v, n, other, q) if direction == 0 else (v, other, n, q)

        def step_fn(j, carry):
            other, q = others(j // 2), j % 2
            u = [[u_ref[at(v, n, other, q)] for n in range(4)] for v in range(5)]
            waves = []
            jumps = []
            for v in range(5):
                back_low, back_high = u_ref[at(v, 0, 3 - other, q)], u_ref[at(v, 3, 3 - other, q)]
                right = sroll(jnp.where(flag_before, back_low, u[v][0]), -step)
                left = sroll(jnp.where(flag, back_high, u[v][3]), step)
                jump_right = jnp.where(low, right, 0.0) - u[v][3]
                jump_left = jnp.where(low, 0.0, left) - u[v][0]
                w = list(slopes_along(*u[v]))
                w[3] = w[3] + H4 * jump_right
                w[0] = w[0] - H4 * jump_left
                waves.append(w)
                jumps.append((damp * jump_left, None, None, damp * jump_right))
            matrix = jacobian(direction)
            for n in range(4):
                flux = mix(matrix, [waves[v][n] for v in range(5)])
                for v in range(5):
                    if direction == 1:
                        total = src_ref[at(v, n, other, q)] - 2.0 * u[v][n]
                    else:
                        total = acc_ref[at(v, n, other, q)]
                    total = total - flux[v]
                    if jumps[v][n] is not None:
                        total = total + jumps[v][n]
                    acc_ref[at(v, n, other, q)] = total
            return carry

        return step_fn

    low = c_low()
    flag = jnp.where(low, lroll(flag_ref[2], 1), flag_ref[2]) != 0
    damp_z = damp
    coef = [
        [jnp.where(low, float(D4[2 * p, c]), float(D4[2 * p + 1, c ^ 1])).astype(F32) for c in range(4)]
        for p in range(2)
    ]

    def step_z(j, carry):
        a0, b = j // 4, j % 4
        here = (a0, 3 - a0)
        u = [[[u_ref[v, a, b, q] for q in range(2)] for v in range(5)] for a in here]
        turned = [[[sroll(u[s][v][q], 4) for q in range(2)] for v in range(5)] for s in range(2)]
        beside = []
        for s in range(2):
            line = []
            for v in range(5):
                face = jnp.where(low, turned[s][v][1], turned[s][v][0])
                line.append(jnp.where(low, lroll(face, 1), lroll(face, -1)))
            beside.append(line)
        matrix = jacobian(2)
        for s in range(2):
            waves = [[], []]
            jumps = []
            for v in range(5):
                own = jnp.where(low, u[s][v][0], u[s][v][1])
                jump = jnp.where(flag, beside[1 - s][v], beside[s][v]) - own
                jumps.append(damp_z * jump)
                lifted = H4 * jump
                for p in range(2):
                    w = coef[p][0] * u[s][v][0] + coef[p][1] * turned[s][v][0]
                    w = w + (coef[p][2] * u[s][v][1] + coef[p][3] * turned[s][v][1])
                    w = w - jnp.where(low, lifted, 0.0) if p == 0 else w + jnp.where(low, 0.0, lifted)
                    waves[p].append(w)
            for p in range(2):
                flux = mix(matrix, waves[p])
                for v in range(5):
                    part = jnp.where(low, jumps[v], 0.0) if p == 0 else jnp.where(low, 0.0, jumps[v])
                    acc_ref[v, here[s], b, p] = acc_ref[v, here[s], b, p] - flux[v] + part
        return carry

    lax.fori_loop(0, 4, along(1, lambda k: 3 * k), 0)
    lax.fori_loop(0, 4, step_z, 0)
    finish_lines()
    lax.fori_loop(0, 4, along(1, lambda k: 1 + k), 0)
    lax.fori_loop(4, 8, step_z, 0)
    lax.fori_loop(0, 8, along(0, lambda k: k), 0)


def first_volume_kernel(
    smooth_hbm, src_ref, smooth_in, u_in, flag_ref, jac_ref, damp_ref,
    smooth_ref, u_ref, acc_ref, jac8_ref, damp8_ref, face_ref, scaled_ref, sem,
):
    inner = slice(1, 3)
    copy = line_copy(smooth_hbm, smooth_ref, sem, inner, inner)
    copy.start()
    prepare_tables(jac_ref, damp_ref, jac8_ref, damp8_ref, face_ref)
    lines = [(a, b) for a in (1, 2) for b in (1, 2)]

    def finish_lines():
        copy.wait()
        for a, b in lines:
            first_line(src_ref, smooth_ref, u_ref, a, b)

    volume(src_ref, u_ref, flag_ref, jac8_ref, damp8_ref, acc_ref, finish_lines)
    for line, (a, b) in enumerate(FACE_LINES):
        for k in range(25):
            block = OMEGA * smooth_ref[k, a, b].astype(F32)
            for q in range(2):
                scaled_ref[line, k, q] = block[8 * q : 8 * q + 8]


def remote_parts(d, odd, even, flag_ref, face_ref, part_ref):
    is_even = parity(("gx", "gy")[d])
    low, step = axis_low(d)
    flag = flag_ref[d]
    flag = jnp.where(low, sroll(flag, -step), flag) != 0
    matrix = [[face_ref[2 * d, 5 * o + i] for i in range(5)] for o in range(5)]
    for n in range(4):
        take = lambda v, m: jnp.where(is_even, even[v, m], odd[v, m])
        right = [jnp.where(flag, take(v, 3 - n), take(v, n)) for v in range(5)]
        for v, value in enumerate(mix(matrix, right)):
            part_ref[0, v, n, 0] = jnp.where(low, 0.0, -sroll(value, step))
            part_ref[0, v, n, 1] = jnp.where(low, 0.0, -value)
    matrix = [[face_ref[2 * d + 1, 5 * o + i] for i in range(5)] for o in range(5)]
    for n in range(4):
        left = [jnp.where(is_even, odd[v, n], even[v, n]) for v in range(5)]
        for v, value in enumerate(mix(matrix, left)):
            part_ref[1, v, n, 0] = jnp.where(low, value, 0.0)
            part_ref[1, v, n, 1] = jnp.where(low, sroll(value, -step), 0.0)


def second_lines(lines, acc_ref, x_part_ref, y_part_ref, scaled_ref, u_ref, out_ref):
    for a, b in lines:
        line = FACE_LINES.index((a, b))
        for q in range(2):
            left = [acc_ref[v, a, b, q] for v in range(5)]
            for v in range(5):
                if a in (0, 3):
                    left[v] = left[v] + x_part_ref[0 if a == 3 else 1, v, b, q]
                if b in (0, 3):
                    left[v] = left[v] + y_part_ref[0 if b == 3 else 1, v, a, q]
            matrix = [[scaled_ref[line, 5 * o + i, q] for i in range(5)] for o in range(5)]
            for v, value in enumerate(mix(matrix, left)):
                out_ref[v, a, b, q] = u_ref[v, a, b, q] + value


X_LINES = [(a, b) for a in (0, 3) for b in (1, 2)]


def second_x_kernel(acc_ref, u_ref, scaled_ref, flag_ref, face_ref, rxo, rxe, out_ref, part_ref):
    remote_parts(0, rxo, rxe, flag_ref, face_ref, part_ref)
    second_lines(X_LINES, acc_ref, part_ref, None, scaled_ref, u_ref, out_ref)


def second_kernel(
    acc_ref, u_ref, scaled_ref, flag_ref, face_ref, ryo, rye, x_part_ref, held_ref, out_ref, xo, xe, yo, ye, part_ref
):
    remote_parts(1, ryo, rye, flag_ref, face_ref, part_ref)
    lines = [line for line in FACE_LINES if line not in X_LINES]
    second_lines(lines, acc_ref, x_part_ref, part_ref, scaled_ref, u_ref, out_ref)
    restricted_faces(out_ref, flag_ref, xo, xe, yo, ye)


def coarse_smooth(smooth_ref, fields):
    out = [[[None, None], [None, None]] for _ in range(5)]
    for i in range(2):
        for o in range(5):
            total = [None, None]
            for k in range(5):
                block = smooth_ref[5 * o + k, i].astype(F32)
                for j in range(2):
                    term = block[8 * j : 8 * j + 8] * fields[k][i][j]
                    total[j] = term if k == 0 else total[j] + term
            for j in range(2):
                out[o][i][j] = OMEGA * total[j]
    return out


def coarse_faces(field, flag_ref, xo, xe, yo, ye):
    for v in range(5):
        c = field[v]
        lows = [[c[0][0], c[0][1]], [c[0][0], c[1][0]]]
        highs = [[c[1][0], c[1][1]], [c[0][1], c[1][1]]]
        put_coarse_faces(v, lows, highs, flag_ref, ((xe, xo), (ye, yo)))


def response_kernel(smooth_ref, face_ref, response_ref):
    packed = []
    for k in range(25):
        by_i = [smooth_ref[k, i].astype(F32) for i in range(2)]
        node = [[by_i[i][8 * j : 8 * j + 8] for j in range(2)] for i in range(2)]
        packed.append(
            (
                pack_high(node[1][0], node[1][1], 0),
                pack_low(node[0][0], node[0][1], 0),
                pack_high(node[0][1], node[1][1], 1),
                pack_low(node[0][0], node[1][0], 1),
            )
        )
    for f in range(4):
        for o in range(5):
            for i in range(5):
                total = packed[5 * o][f] * face_ref[f, i]
                for k in range(1, 5):
                    total = total + packed[5 * o + k][f] * face_ref[f, 5 * k + i]
                response_ref[f, 5 * o + i] = (OMEGA / 6.0) * total


def restricted_volume_kernel(
    src_ref, flag_ref, jac_ref, damp_ref, smooth_ref, fine_acc_ref, first_ref, fine_smooth_ref, faces_ref,
    acc_ref, c_ref, u_ref,
):
    for a in (1, 2):
        for b in (1, 2):
            left = [[fine_acc_ref[v, a, b, q] for q in range(2)] for v in range(5)]
            change = smoothed(fine_smooth_ref, left, a, b)
            for v in range(5):
                for q in range(2):
                    u_ref[v, a, b, q] = first_ref[v, a, b, q] + change[v][q]
    damp = H4 * damp_ref[...]
    low_c = c_low()
    slope = [
        jnp.where(low_c, float(PD[0, c]), float(PD[1, c ^ 1])).astype(F32) for c in range(4)
    ]
    flags = [flag_ref[0] != 0, flag_ref[1] != 0, jnp.where(low_c, lroll(flag_ref[2], 1), flag_ref[2]) != 0]
    sign = jnp.where(low_c, -H4, H4).astype(F32)
    waves = [[[[None] * 5 for _ in range(2)] for _ in range(2)] for _ in range(3)]

    def slopes_four(values):
        return [sum_of([(float(PD[i, n]), values[n]) for n in range(4)]) for i in range(2)]

    for v in range(5):
        line, slope_c, ends = {}, {}, {}
        for a in range(4):
            for b in range(4):
                first, second = u_ref[v, a, b, 0], u_ref[v, a, b, 1]
                line[a, b] = restrict_c(first, second)
                slope_c[a, b] = (slope[0] * first + slope[1] * sroll(first, 4)) + (
                    slope[2] * second + slope[3] * sroll(second, 4)
                )
                ends[a, b] = jnp.where(low_c, first, second)

        def along_b(table):
            return [restrict_four([table[a, b] for b in range(4)]) for a in range(4)]

        def both(table):
            by_b = along_b(table)
            return [restrict_four([by_b[a][j] for a in range(4)]) for j in range(2)]

        by_b = along_b(line)
        by_a = [restrict_four([line[a, b] for a in range(4)]) for b in range(4)]
        flux_z = both(slope_c)
        trace_z = both(ends)
        sources = both({(a, b): restrict_c(src_ref[v, a, b, 0], src_ref[v, a, b, 1]) for a in range(4) for b in range(4)})
        acc = [[None, None], [None, None]]
        for j in range(2):
            value = restrict_four([by_b[a][j] for a in range(4)])
            flux = slopes_four([by_b[a][j] for a in range(4)])
            for i in range(2):
                acc[i][j] = sources[j][i] - 2.0 * value[i]
                waves[0][i][j][v] = flux[i]
        for i in range(2):
            flux = slopes_four([by_a[b][i] for b in range(4)])
            for j in range(2):
                waves[1][i][j][v] = flux[j]
        for d, lo, hi in ((0, by_b[0], by_b[3]), (1, by_a[0], by_a[3])):
            low, step = axis_low(d)
            flag = flags[d]
            flag_before = sroll(flag_ref[d], step) != 0
            for m in range(2):
                right = sroll(jnp.where(flag_before, lo[1 - m], lo[m]), -step)
                left = sroll(jnp.where(flag, hi[1 - m], hi[m]), step)
                jump_right = jnp.where(low, right, 0.0) - hi[m]
                jump_left = jnp.where(low, 0.0, left) - lo[m]
                i, j = (1, m) if d == 0 else (m, 1)
                waves[d][i][j][v] = waves[d][i][j][v] + H4 * jump_right
                acc[i][j] = acc[i][j] + damp * jump_right
                i, j = (0, m) if d == 0 else (m, 0)
                waves[d][i][j][v] = waves[d][i][j][v] - H4 * jump_left
                acc[i][j] = acc[i][j] + damp * jump_left
        beside = []
        for j in range(2):
            turned = [sroll(trace_z[j][i], 4) for i in range(2)]
            beside.append([jnp.where(low_c, lroll(t, 1), lroll(t, -1)) for t in turned])
        for i in range(2):
            for j in range(2):
                jump = jnp.where(flags[2], beside[j][1 - i], beside[j][i]) - trace_z[j][i]
                waves[2][i][j][v] = flux_z[j][i] + sign * jump
                acc_ref[v, i, j] = acc[i][j] + damp * jump
    for d in range(3):
        matrix = [[jac_ref[25 * d + 5 * o + i] for i in range(5)] for o in range(5)]
        for i in range(2):
            for j in range(2):
                for v, value in enumerate(mix(matrix, waves[d][i][j])):
                    acc_ref[v, i, j] = acc_ref[v, i, j] - value
    c = coarse_smooth(smooth_ref, [[[acc_ref[v, i, j] for j in range(2)] for i in range(2)] for v in range(5)])
    put_field(c_ref, c)


def put_field(out_ref, c):
    for v in range(5):
        for i in range(2):
            for j in range(2):
                out_ref[v, i, j] = c[v][i][j]


def get_field(ref):
    return [[[ref[v, i, j] for j in range(2)] for i in range(2)] for v in range(5)]


def add_remote(field, scale, flag_ref, face_ref, rxo, rxe, ryo, rye):
    for d, axis in ((0, "gx"), (1, "gy")):
        is_even = parity(axis)
        low, step = axis_low(d)
        flag = flag_ref[d]
        flag = jnp.where(low, sroll(flag, -step), flag) != 0
        even, odd = ((rxe, rxo), (rye, ryo))[d]
        at = (lambda n, m: (n, m)) if d == 0 else (lambda n, m: (m, n))
        right, left = [], []
        for v in range(5):
            value = scale * jnp.where(is_even, even[v], odd[v])
            swapped = jnp.where(low, sroll(value, -step), sroll(value, step))
            right.append(jnp.where(flag, swapped, value))
            left.append(scale * jnp.where(is_even, odd[v], even[v]))
        upper = [[face_ref[2 * d, 5 * o + i] for i in range(5)] for o in range(5)]
        lower = [[face_ref[2 * d + 1, 5 * o + i] for i in range(5)] for o in range(5)]
        for v, value in enumerate(mix(upper, right)):
            for m, part in enumerate((sroll(value, step), value)):
                i, j = at(1, m)
                field[v][i][j] = field[v][i][j] - jnp.where(low, 0.0, part)
        for v, value in enumerate(mix(lower, left)):
            for m, part in enumerate((value, sroll(value, -step))):
                i, j = at(0, m)
                field[v][i][j] = field[v][i][j] + jnp.where(low, part, 0.0)


def restrict_kernel(local_ref, flag_ref, response_ref, rxo, rxe, ryo, rye, c_ref, xo, xe, yo, ye):
    c = get_field(local_ref)
    add_remote(c, 6.0, flag_ref, response_ref, rxo, rxe, ryo, rye)
    put_field(c_ref, c)
    coarse_faces(c, flag_ref, xo, xe, yo, ye)


def first_local_kernel(
    c_ref, acc_ref, smooth_ref, flag_ref, jac_ref, damp_ref, face_ref, rxo, rxe, ryo, rye, out_ref, rhs_ref
):
    rhs = get_field(acc_ref)
    add_remote(rhs, 1.0, flag_ref, face_ref, rxo, rxe, ryo, rye)
    put_field(rhs_ref, rhs)
    coarse_local_kernel(c_ref, rhs_ref, smooth_ref, flag_ref, jac_ref, damp_ref, out_ref)


def coarse_local_kernel(c_ref, rhs_ref, smooth_ref, flag_ref, jac_ref, damp_ref, out_ref):
    damp = 0.5 * damp_ref[...]
    c = [[[c_ref[v, i, j] for j in range(2)] for i in range(2)] for v in range(5)]
    acc = [[[rhs_ref[v, i, j] - 2.0 * c[v][i][j] for j in range(2)] for i in range(2)] for v in range(5)]
    for d in range(2):
        low, step = axis_low(d)
        flag = flag_ref[d] != 0
        flag_before = sroll(flag_ref[d], step) != 0
        matrix = [[jac_ref[25 * d + 5 * o + i] for i in range(5)] for o in range(5)]
        at = (lambda n, m: (n, m)) if d == 0 else (lambda n, m: (m, n))
        waves = [[[None] * 5, [None] * 5] for _ in range(2)]
        for v in range(5):
            lo = [c[v][at(0, m)[0]][at(0, m)[1]] for m in range(2)]
            hi = [c[v][at(1, m)[0]][at(1, m)[1]] for m in range(2)]
            for m in range(2):
                right = jnp.where(low, sroll(jnp.where(flag_before, lo[1 - m], lo[m]), -step), 0.0)
                left = jnp.where(low, 0.0, sroll(jnp.where(flag, hi[1 - m], hi[m]), step))
                waves[1][m][v] = 0.5 * (right - lo[m])
                waves[0][m][v] = 0.5 * (hi[m] - left)
                i, j = at(1, m)
                acc[v][i][j] = acc[v][i][j] + damp * (right - hi[m])
                i, j = at(0, m)
                acc[v][i][j] = acc[v][i][j] + damp * (left - lo[m])
        for n in range(2):
            for m in range(2):
                i, j = at(n, m)
                for v, value in enumerate(mix(matrix, waves[n][m])):
                    acc[v][i][j] = acc[v][i][j] - value
    low = c_low()
    flag = jnp.where(low, lroll(flag_ref[2], 1), flag_ref[2]) != 0
    half = jnp.where(low, 0.5, -0.5).astype(F32)
    matrix = [[jac_ref[50 + 5 * o + i] for i in range(5)] for o in range(5)]
    turned = [[[sroll(c[v][i][j], 4) for j in range(2)] for i in range(2)] for v in range(5)]
    beside = [
        [[jnp.where(low, lroll(t, 1), lroll(t, -1)) for t in turned[v][i]] for i in range(2)] for v in range(5)
    ]
    for i in range(2):
        for j in range(2):
            wave = []
            for v in range(5):
                next_to = jnp.where(flag, beside[v][1 - i][j], beside[v][i][j])
                wave.append(half * (turned[v][i][j] - next_to))
                acc[v][i][j] = acc[v][i][j] + damp * (next_to - c[v][i][j])
            for v, value in enumerate(mix(matrix, wave)):
                acc[v][i][j] = acc[v][i][j] - value
    change = coarse_smooth(smooth_ref, acc)
    for v in range(5):
        for i in range(2):
            for j in range(2):
                out_ref[v, i, j] = c[v][i][j] + change[v][i][j]


def coarse_kernel(c_ref, flag_ref, response_ref, rxo, rxe, ryo, rye, out_ref, xo, xe, yo, ye):
    c = get_field(c_ref)
    add_remote(c, 1.0, flag_ref, response_ref, rxo, rxe, ryo, rye)
    put_field(out_ref, c)
    coarse_faces(c, flag_ref, xo, xe, yo, ye)


def spread(first, second):
    return first, NEAR * first + FAR * second, FAR * first + NEAR * second, second


def last_kernel(
    c_ref, flag_ref, response_ref, rxo, rxe, ryo, rye, second_ref, out_hbm, out_ref, sems
):
    c = get_field(c_ref)
    add_remote(c, 1.0, flag_ref, response_ref, rxo, rxe, ryo, rye)
    low = c_low()
    copies = []
    for v in range(5):
        by_c = [[None, None], [None, None]]
        for i in range(2):
            for j in range(2):
                value = c[v][i][j]
                inner = FAR * value + NEAR * sroll(value, 4)
                by_c[i][j] = (jnp.where(low, value, inner), jnp.where(low, inner, value))
        for q in range(2):
            lines = [spread(by_c[i][0][q], by_c[i][1][q]) for i in range(2)]
            for b in range(4):
                for a, value in enumerate(spread(lines[0][b], lines[1][b])):
                    out_ref[v, a, b, q] = second_ref[v, a, b, q] + value
        copy = pltpu.make_async_copy(out_ref.at[v], out_hbm.at[v], sems.at[v])
        copy.start()
        copies.append(copy)
    for copy in copies:
        copy.wait()


FINE = (5, 4, 4, 2, 8, 128)
FINE_MESSAGE = (5, 4, 8, 128)
COARSE = (5, 2, 2, 8, 128)
COARSE_MESSAGE = (5, 8, 128)


def vmem(shape, dtype=F32):
    return pltpu.VMEM(shape, dtype)


def here(array):
    return pltpu.with_memory_space_constraint(array, pltpu.VMEM)


def call(kernel, args, outs, in_hbm=(), out_hbm=(), scratch=(), aliases=None, flops=0):
    in_specs = [
        pl.BlockSpec(memory_space=pltpu.HBM if k in in_hbm else pltpu.VMEM) for k in range(len(args))
    ]
    out_specs = [
        pl.BlockSpec(memory_space=pltpu.HBM if k in out_hbm else pltpu.VMEM) for k in range(len(outs))
    ]
    args = [pltpu.with_memory_space_constraint(a, pltpu.HBM) if k in in_hbm else here(a) for k, a in enumerate(args)]
    return pl.pallas_call(
        kernel,
        out_shape=outs,
        in_specs=in_specs,
        out_specs=out_specs,
        scratch_shapes=scratch,
        input_output_aliases=aliases or {},
        compiler_params=pltpu.CompilerParams(vmem_limit_bytes=8 * 2**20),
        cost_estimate=pl.CostEstimate(flops=flops, bytes_accessed=4 * 2**20, transcendentals=0),
    )(*args)


def partners(axis):
    size = lax.axis_size(axis)
    even = [(i, i ^ 1) for i in range(size)]
    odd = [(i, (i - 1) % size if i % 2 == 0 else (i + 1) % size) for i in range(size)]
    return even, odd


def exchange(xo, xe, yo, ye):
    even_x, odd_x = partners("gx")
    even_y, odd_y = partners("gy")
    xo = lax.ppermute(xo, "gx", odd_x)
    xe = lax.ppermute(xe, "gx", even_x)
    yo = lax.ppermute(yo, "gy", odd_y)
    ye = lax.ppermute(ye, "gy", even_y)
    return xo, xe, yo, ye


def body(source, jacobian, damping, orient, smoother, coarse_smoother):
    source = source.reshape(FINE)
    smoother = smoother.reshape(25, 4, 4, 16, 128)
    coarse_smoother = coarse_smoother.reshape(25, 2, 16, 128)
    jacobian = jacobian.reshape(75, 4, 128)
    damping = damping.reshape(4, 128)
    orient = orient.reshape(3, 4, 128)
    fine_messages = [vmem(FINE_MESSAGE)] * 4
    coarse_messages = [vmem(COARSE_MESSAGE)] * 4

    held = vmem(smoother.shape, smoother.dtype)
    smoother_in = smoother
    source, smoother, first, flag, *sent = call(
        first_kernel,
        (source, smoother_in, orient),
        [vmem(FINE), held, vmem(FINE), vmem((3, 8, 128), jnp.int32)] + fine_messages,
        in_hbm=(0, 1, 2),
        scratch=[pltpu.SemaphoreType.DMA((5,)), pltpu.VMEM((3, 4, 128), jnp.int32), pltpu.SemaphoreType.DMA],
        flops=2 * 25 * 64 * 512,
    )
    got = exchange(*sent)
    smoother, first, acc, jac8, damp8, face, scaled = call(
        first_volume_kernel,
        (smoother_in, source, smoother, first, flag, jacobian, damping),
        [held, vmem(FINE), vmem(FINE), vmem((75, 8, 128)), vmem((8, 128)), vmem((4, 25, 8, 128)), vmem((12, 25, 2, 8, 128))],
        in_hbm=(0,),
        aliases={2: 0, 3: 1},
        scratch=[pltpu.SemaphoreType.DMA],
        flops=9 * 2**20,
    )
    part = vmem((2, 5, 4, 2, 8, 128))
    second, x_part = call(
        second_x_kernel,
        (acc, first, scaled, flag, face, *got[:2]),
        [vmem(FINE), part],
        flops=2**20,
    )
    second, *sent = call(
        second_kernel,
        (acc, first, scaled, flag, face, *got[2:], x_part, second),
        [vmem(FINE)] + coarse_messages,
        aliases={8: 0},
        scratch=[pltpu.VMEM((2, 5, 4, 2, 8, 128), F32)],
        flops=2 * 2**20,
    )
    got = exchange(*sent)
    (response,) = call(response_kernel, (coarse_smoother, face), [vmem((4, 25, 8, 128))], flops=2**20)
    acc, coarse, second = call(
        restricted_volume_kernel,
        (source, flag, jac8, damp8, coarse_smoother, acc, first, smoother, second),
        [vmem(COARSE), vmem(COARSE), vmem(FINE)],
        aliases={8: 2},
        flops=4 * 2**20,
    )
    coarse, *sent = call(
        restrict_kernel, (coarse, flag, response, *got), [vmem(COARSE)] + coarse_messages, flops=2**20
    )
    second_got, got = got, exchange(*sent)
    coarse, rhs = call(
        first_local_kernel,
        (coarse, acc, coarse_smoother, flag, jac8, damp8, face, *second_got),
        [vmem(COARSE), vmem(COARSE)],
        flops=4 * 2**20,
    )
    coarse, *sent = call(
        coarse_kernel, (coarse, flag, response, *got), [vmem(COARSE)] + coarse_messages, flops=2**20
    )
    got = exchange(*sent)
    (coarse,) = call(
        coarse_local_kernel, (coarse, rhs, coarse_smoother, flag, jac8, damp8), [vmem(COARSE)], flops=4 * 2**20
    )
    (out,) = call(
        last_kernel,
        (coarse, flag, response, *got, second),
        [jax.ShapeDtypeStruct(FINE, F32)],
        out_hbm=(0,),
        scratch=[pltpu.VMEM(FINE, F32), pltpu.SemaphoreType.DMA((5,))],
        flops=2**20,
    )
    return out.reshape(5, 4, 4, 4, 2, 2, 128)


def solution(mesh):
    in_specs = (
        P(None, None, None, None, "gx", "gy", None),
        P(None, None, None, "gx", "gy", None),
        P("gx", "gy", None),
        P(None, "gx", "gy", None),
        P(None, None, None, None, None, "gx", "gy", None),
        P(None, None, None, None, None, "gx", "gy", None),
    )
    out_specs = P(None, None, None, None, "gx", "gy", None)
    return jax.shard_map(body, mesh=mesh, in_specs=in_specs, out_specs=out_specs, check_vma=False)
```

```python
import functools
import math

import jax
import jax.numpy as jnp
import numpy as np
from jax import lax
from jax.experimental import pallas as pl
from jax.experimental.pallas import tpu as pltpu
from jax.sharding import PartitionSpec as P


F32 = jnp.float32
OMEGA = 0.8
FACE_LINES = [(a, b) for a in range(4) for b in range(4) if a in (0, 3) or b in (0, 3)]
H4 = 3.0
ROOT = 1.0 / math.sqrt(5.0)
NEAR = (1.0 + ROOT) / 2.0
FAR = (1.0 - ROOT) / 2.0


def lobatto_slopes():
    points = np.array([-1.0, -ROOT, ROOT, 1.0])
    weights = np.ones(4)
    for i in range(4):
        for j in range(4):
            if i != j:
                weights[i] = weights[i] / (points[i] - points[j])
    slopes = np.zeros((4, 4))
    for i in range(4):
        for j in range(4):
            if i != j:
                slopes[i, j] = weights[j] / weights[i] / (points[i] - points[j])
        slopes[i, i] = -np.sum(slopes[i])
    return slopes


D4 = lobatto_slopes()
PD = np.array([[1.0, NEAR, FAR, 0.0], [0.0, FAR, NEAR, 1.0]]) @ D4


def sum_of(terms):
    total = None
    for weight, value in terms:
        total = weight * value if total is None else total + weight * value
    return total


def rows():
    return lax.broadcasted_iota(jnp.int32, (8, 128), 0)


def x_low():
    return (rows() & 2) == 0


def y_low():
    return (rows() & 1) == 0


def c_low():
    return (rows() & 4) == 0


def sroll(value, shift):
    return pltpu.roll(value, shift % 8, 0)


def lroll(value, shift):
    return pltpu.roll(value, shift % 128, 1)


def twice(value):
    return jnp.concatenate([value, value], axis=0)


def axis_low(direction):
    return (x_low(), 2) if direction == 0 else (y_low(), 1)


def pack_low(first, second, direction):
    low, step = axis_low(direction)
    return jnp.where(low, first, sroll(second, step))


def pack_high(first, second, direction):
    low, step = axis_low(direction)
    return jnp.where(low, sroll(first, -step), second)


def slopes_along(u0, u1, u2, u3):
    e0, o0, e1, o1 = u0 + u3, u0 - u3, u1 + u2, u1 - u2
    diff = e1 - e0
    even_a = float((D4[0, 1] + D4[0, 2]) / 2.0) * diff
    even_b = float((D4[1, 2] - 0.0) / 2.0) * diff
    odd_a = float((D4[0, 0] - D4[0, 3]) / 2.0) * o0 + float((D4[0, 1] - D4[0, 2]) / 2.0) * o1
    odd_b = float((D4[1, 0] - D4[1, 3]) / 2.0) * o0 - float(D4[1, 2] / 2.0) * o1
    return even_a + odd_a, even_b + odd_b, odd_b - even_b, odd_a - even_a


def mix(matrix, fields):
    out = []
    for o in range(5):
        total = matrix[o][0] * fields[0]
        for i in range(1, 5):
            total = total + matrix[o][i] * fields[i]
        out.append(total)
    return out


def parity(axis):
    return lax.rem(lax.axis_index(axis), 2) == 0


def put_pair(even_ref, odd_ref, index, low_face, high_face, is_even):
    even_ref[index] = jnp.where(is_even, high_face, low_face)
    odd_ref[index] = jnp.where(is_even, low_face, high_face)


def fine_faces(u_ref, flag_ref, xo, xe, yo, ye):
    even_x, even_y = parity("gx"), parity("gy")
    fx, fy = flag_ref[0] != 0, flag_ref[1] != 0
    for v in range(5):
        for n in range(4):
            low = pack_low(u_ref[v, 0, n, 0], u_ref[v, 0, n, 1], 0)
            h = [jnp.where(fx, u_ref[v, 3, 3 - n, q], u_ref[v, 3, n, q]) for q in range(2)]
            put_pair(xe, xo, (v, n), low, pack_high(h[0], h[1], 0), even_x)
            low = pack_low(u_ref[v, n, 0, 0], u_ref[v, n, 0, 1], 1)
            h = [jnp.where(fy, u_ref[v, 3 - n, 3, q], u_ref[v, n, 3, q]) for q in range(2)]
            put_pair(ye, yo, (v, n), low, pack_high(h[0], h[1], 1), even_y)


def restrict_c(first, second):
    low = c_low()
    middle = jnp.where(low, second, first)
    return jnp.where(low, first, second) + FAR * middle + NEAR * sroll(middle, 4)


def restrict_four(values):
    return values[0] + NEAR * values[1] + FAR * values[2], values[3] + NEAR * values[2] + FAR * values[1]


def put_coarse_faces(v, lows, highs, flag_ref, pairs):
    for d, axis in ((0, "gx"), (1, "gy")):
        flag = flag_ref[d] != 0
        low, high = lows[d], highs[d]
        turned = [jnp.where(flag, high[1 - m], high[m]) for m in range(2)]
        even_ref, odd_ref = pairs[d]
        put_pair(even_ref, odd_ref, v, pack_low(*low, d), pack_high(*turned, d), parity(axis))


def restricted_faces(u_ref, flag_ref, xo, xe, yo, ye):
    for v in range(5):
        line = {}
        for a in range(4):
            for b in range(4):
                if a in (0, 3) or b in (0, 3):
                    line[a, b] = restrict_c(u_ref[v, a, b, 0], u_ref[v, a, b, 1])
        lows = [restrict_four([line[0, n] for n in range(4)]), restrict_four([line[n, 0] for n in range(4)])]
        highs = [restrict_four([line[3, n] for n in range(4)]), restrict_four([line[n, 3] for n in range(4)])]
        put_coarse_faces(v, lows, highs, flag_ref, ((xe, xo), (ye, yo)))


def smoothed(smooth_ref, fields, a, b):
    out = []
    for o in range(5):
        total = [None, None]
        for i in range(5):
            block = smooth_ref[5 * o + i, a, b].astype(F32)
            for q in range(2):
                term = block[8 * q : 8 * q + 8] * fields[i][q]
                total[q] = term if i == 0 else total[q] + term
        out.append([OMEGA * total[q] for q in range(2)])
    return out


def first_line(src_ref, smooth_ref, u_ref, a, b):
    value = smoothed(smooth_ref, [[src_ref[v, a, b, q] for q in range(2)] for v in range(5)], a, b)
    for v in range(5):
        for q in range(2):
            u_ref[v, a, b, q] = value[v][q]


def line_copy(smooth_hbm, smooth_ref, sem, a, b):
    return pltpu.make_async_copy(smooth_hbm.at[:, a, b], smooth_ref.at[:, a, b], sem)


def first_kernel(
    src_hbm, smooth_hbm, orient_hbm, src_ref, smooth_ref, u_ref, flag_ref, xo, xe, yo, ye, sems, orient_ref, orient_sem
):
    every, inner = slice(0, 4), slice(1, 3)
    src_copy = pltpu.make_async_copy(src_hbm, src_ref, sems.at[4])
    src_copy.start()
    orient_copy = pltpu.make_async_copy(orient_hbm, orient_ref, orient_sem)
    orient_copy.start()
    copies = [
        line_copy(smooth_hbm, smooth_ref, sems.at[slot], a, b)
        for slot, (a, b) in enumerate(((0, every), (3, every), (inner, 0), (inner, 3)))
    ]
    for one in copies:
        one.start()
    lines = [[(0, b) for b in range(4)], [(3, b) for b in range(4)], [(1, 0), (2, 0)], [(1, 3), (2, 3)]]
    src_copy.wait()
    for one, group in zip(copies, lines):
        one.wait()
        for a, b in group:
            first_line(src_ref, smooth_ref, u_ref, a, b)
    orient_copy.wait()
    for d in range(3):
        flag_ref[d] = twice(orient_ref[d])
    fine_faces(u_ref, flag_ref, xo, xe, yo, ye)


def prepare_tables(jac_ref, damp_ref, jac8_ref, damp8_ref, face_ref):
    damp = twice(damp_ref[...])
    damp8_ref[...] = damp
    for d in range(3):
        for k in range(25):
            value = twice(jac_ref[25 * d + k])
            jac8_ref[25 * d + k] = value
            if d < 2:
                low, step = axis_low(d)
                diagonal = k % 6 == 0
                upper = H4 * (value - damp if diagonal else value)
                lower = H4 * (value + damp if diagonal else value)
                face_ref[2 * d, k] = jnp.where(low, sroll(upper, -step), upper)
                face_ref[2 * d + 1, k] = jnp.where(low, lower, sroll(lower, step))


def volume(src_ref, u_ref, flag_ref, jac_ref, damp_ref, acc_ref, finish_lines):
    damp = H4 * damp_ref[...]

    def jacobian(d):
        return [[jac_ref[25 * d + 5 * o + i] for i in range(5)] for o in range(5)]

    def along(direction, others):
        low, step = axis_low(direction)
        flag = flag_ref[direction] != 0
        flag_before = sroll(flag_ref[direction], step) != 0

        def at(v, n, other, q):
            return (v, n, other, q) if direction == 0 else (v, other, n, q)

        def step_fn(j, carry):
            other, q = others(j // 2), j % 2
            u = [[u_ref[at(v, n, other, q)] for n in range(4)] for v in range(5)]
            waves = []
            jumps = []
            for v in range(5):
                back_low, back_high = u_ref[at(v, 0, 3 - other, q)], u_ref[at(v, 3, 3 - other, q)]
                right = sroll(jnp.where(flag_before, back_low, u[v][0]), -step)
                left = sroll(jnp.where(flag, back_high, u[v][3]), step)
                jump_right = jnp.where(low, right, 0.0) - u[v][3]
                jump_left = jnp.where(low, 0.0, left) - u[v][0]
                w = list(slopes_along(*u[v]))
                w[3] = w[3] + H4 * jump_right
                w[0] = w[0] - H4 * jump_left
                waves.append(w)
                jumps.append((damp * jump_left, None, None, damp * jump_right))
            matrix = jacobian(direction)
            for n in range(4):
                flux = mix(matrix, [waves[v][n] for v in range(5)])
                for v in range(5):
                    if direction == 1:
                        total = src_ref[at(v, n, other, q)] - 2.0 * u[v][n]
                    else:
                        total = acc_ref[at(v, n, other, q)]
                    total = total - flux[v]
                    if jumps[v][n] is not None:
                        total = total + jumps[v][n]
                    acc_ref[at(v, n, other, q)] = total
            return carry

        return step_fn

    low = c_low()
    flag = jnp.where(low, lroll(flag_ref[2], 1), flag_ref[2]) != 0
    damp_z = damp
    coef = [
        [jnp.where(low, float(D4[2 * p, c]), float(D4[2 * p + 1, c ^ 1])).astype(F32) for c in range(4)]
        for p in range(2)
    ]

    def step_z(j, carry):
        a0, b = j // 4, j % 4
        here = (a0, 3 - a0)
        u = [[[u_ref[v, a, b, q] for q in range(2)] for v in range(5)] for a in here]
        turned = [[[sroll(u[s][v][q], 4) for q in range(2)] for v in range(5)] for s in range(2)]
        beside = []
        for s in range(2):
            line = []
            for v in range(5):
                face = jnp.where(low, turned[s][v][1], turned[s][v][0])
                line.append(jnp.where(low, lroll(face, 1), lroll(face, -1)))
            beside.append(line)
        matrix = jacobian(2)
        for s in range(2):
            waves = [[], []]
            jumps = []
            for v in range(5):
                own = jnp.where(low, u[s][v][0], u[s][v][1])
                jump = jnp.where(flag, beside[1 - s][v], beside[s][v]) - own
                jumps.append(damp_z * jump)
                lifted = H4 * jump
                for p in range(2):
                    w = coef[p][0] * u[s][v][0] + coef[p][1] * turned[s][v][0]
                    w = w + (coef[p][2] * u[s][v][1] + coef[p][3] * turned[s][v][1])
                    w = w - jnp.where(low, lifted, 0.0) if p == 0 else w + jnp.where(low, 0.0, lifted)
                    waves[p].append(w)
            for p in range(2):
                flux = mix(matrix, waves[p])
                for v in range(5):
                    part = jnp.where(low, jumps[v], 0.0) if p == 0 else jnp.where(low, 0.0, jumps[v])
                    acc_ref[v, here[s], b, p] = acc_ref[v, here[s], b, p] - flux[v] + part
        return carry

    lax.fori_loop(0, 4, along(1, lambda k: 3 * k), 0)
    lax.fori_loop(0, 4, step_z, 0)
    finish_lines()
    lax.fori_loop(0, 4, along(1, lambda k: 1 + k), 0)
    lax.fori_loop(4, 8, step_z, 0)
    lax.fori_loop(0, 8, along(0, lambda k: k), 0)


def first_volume_kernel(
    smooth_hbm, src_ref, smooth_in, u_in, flag_ref, jac_ref, damp_ref,
    smooth_ref, u_ref, acc_ref, jac8_ref, damp8_ref, face_ref, second_ref, scaled_ref, sem,
):
    inner = slice(1, 3)
    copy = line_copy(smooth_hbm, smooth_ref, sem, inner, inner)
    copy.start()
    prepare_tables(jac_ref, damp_ref, jac8_ref, damp8_ref, face_ref)
    lines = [(a, b) for a in (1, 2) for b in (1, 2)]

    def finish_lines():
        copy.wait()
        for a, b in lines:
            first_line(src_ref, smooth_ref, u_ref, a, b)

    volume(src_ref, u_ref, flag_ref, jac8_ref, damp8_ref, acc_ref, finish_lines)
    for a, b in lines:
        change = smoothed(smooth_ref, [[acc_ref[v, a, b, q] for q in range(2)] for v in range(5)], a, b)
        for v in range(5):
            for q in range(2):
                second_ref[v, a, b, q] = u_ref[v, a, b, q] + change[v][q]
    for line, (a, b) in enumerate(FACE_LINES):
        for k in range(25):
            block = OMEGA * smooth_ref[k, a, b].astype(F32)
            for q in range(2):
                scaled_ref[line, k, q] = block[8 * q : 8 * q + 8]


def remote_parts(d, odd, even, flag_ref, face_ref, part_ref):
    is_even = parity(("gx", "gy")[d])
    low, step = axis_low(d)
    flag = flag_ref[d]
    flag = jnp.where(low, sroll(flag, -step), flag) != 0
    matrix = [[face_ref[2 * d, 5 * o + i] for i in range(5)] for o in range(5)]
    for n in range(4):
        take = lambda v, m: jnp.where(is_even, even[v, m], odd[v, m])
        right = [jnp.where(flag, take(v, 3 - n), take(v, n)) for v in range(5)]
        for v, value in enumerate(mix(matrix, right)):
            part_ref[0, v, n, 0] = jnp.where(low, 0.0, -sroll(value, step))
            part_ref[0, v, n, 1] = jnp.where(low, 0.0, -value)
    matrix = [[face_ref[2 * d + 1, 5 * o + i] for i in range(5)] for o in range(5)]
    for n in range(4):
        left = [jnp.where(is_even, odd[v, n], even[v, n]) for v in range(5)]
        for v, value in enumerate(mix(matrix, left)):
            part_ref[1, v, n, 0] = jnp.where(low, value, 0.0)
            part_ref[1, v, n, 1] = jnp.where(low, sroll(value, -step), 0.0)


def second_lines(lines, acc_ref, x_part_ref, y_part_ref, scaled_ref, u_ref, out_ref):
    for a, b in lines:
        line = FACE_LINES.index((a, b))
        for q in range(2):
            left = [acc_ref[v, a, b, q] for v in range(5)]
            for v in range(5):
                if a in (0, 3):
                    left[v] = left[v] + x_part_ref[0 if a == 3 else 1, v, b, q]
                if b in (0, 3):
                    left[v] = left[v] + y_part_ref[0 if b == 3 else 1, v, a, q]
            matrix = [[scaled_ref[line, 5 * o + i, q] for i in range(5)] for o in range(5)]
            for v, value in enumerate(mix(matrix, left)):
                out_ref[v, a, b, q] = u_ref[v, a, b, q] + value


X_LINES = [(a, b) for a in (0, 3) for b in (1, 2)]


def second_x_kernel(acc_ref, u_ref, scaled_ref, flag_ref, face_ref, rxo, rxe, inner_ref, out_ref, part_ref):
    remote_parts(0, rxo, rxe, flag_ref, face_ref, part_ref)
    second_lines(X_LINES, acc_ref, part_ref, None, scaled_ref, u_ref, out_ref)


def second_kernel(
    acc_ref, u_ref, scaled_ref, flag_ref, face_ref, ryo, rye, x_part_ref, held_ref, out_ref, xo, xe, yo, ye, part_ref
):
    remote_parts(1, ryo, rye, flag_ref, face_ref, part_ref)
    lines = [line for line in FACE_LINES if line not in X_LINES]
    second_lines(lines, acc_ref, x_part_ref, part_ref, scaled_ref, u_ref, out_ref)
    restricted_faces(out_ref, flag_ref, xo, xe, yo, ye)


def coarse_smooth(smooth_ref, fields):
    out = [[[None, None], [None, None]] for _ in range(5)]
    for i in range(2):
        for o in range(5):
            total = [None, None]
            for k in range(5):
                block = smooth_ref[5 * o + k, i].astype(F32)
                for j in range(2):
                    term = block[8 * j : 8 * j + 8] * fields[k][i][j]
                    total[j] = term if k == 0 else total[j] + term
            for j in range(2):
                out[o][i][j] = OMEGA * total[j]
    return out


def coarse_faces(field, flag_ref, xo, xe, yo, ye):
    for v in range(5):
        c = field[v]
        lows = [[c[0][0], c[0][1]], [c[0][0], c[1][0]]]
        highs = [[c[1][0], c[1][1]], [c[0][1], c[1][1]]]
        put_coarse_faces(v, lows, highs, flag_ref, ((xe, xo), (ye, yo)))


def response_kernel(smooth_ref, face_ref, response_ref):
    packed = []
    for k in range(25):
        by_i = [smooth_ref[k, i].astype(F32) for i in range(2)]
        node = [[by_i[i][8 * j : 8 * j + 8] for j in range(2)] for i in range(2)]
        packed.append(
            (
                pack_high(node[1][0], node[1][1], 0),
                pack_low(node[0][0], node[0][1], 0),
                pack_high(node[0][1], node[1][1], 1),
                pack_low(node[0][0], node[1][0], 1),
            )
        )
    for f in range(4):
        for o in range(5):
            for i in range(5):
                total = packed[5 * o][f] * face_ref[f, i]
                for k in range(1, 5):
                    total = total + packed[5 * o + k][f] * face_ref[f, 5 * k + i]
                response_ref[f, 5 * o + i] = (OMEGA / 6.0) * total


def restricted_volume_kernel(src_ref, u_ref, flag_ref, jac_ref, damp_ref, smooth_ref, acc_ref, c_ref):
    damp = H4 * damp_ref[...]
    low_c = c_low()
    slope = [
        jnp.where(low_c, float(PD[0, c]), float(PD[1, c ^ 1])).astype(F32) for c in range(4)
    ]
    flags = [flag_ref[0] != 0, flag_ref[1] != 0, jnp.where(low_c, lroll(flag_ref[2], 1), flag_ref[2]) != 0]
    sign = jnp.where(low_c, -H4, H4).astype(F32)
    waves = [[[[None] * 5 for _ in range(2)] for _ in range(2)] for _ in range(3)]

    def slopes_four(values):
        return [sum_of([(float(PD[i, n]), values[n]) for n in range(4)]) for i in range(2)]

    for v in range(5):
        line, slope_c, ends = {}, {}, {}
        for a in range(4):
            for b in range(4):
                first, second = u_ref[v, a, b, 0], u_ref[v, a, b, 1]
                line[a, b] = restrict_c(first, second)
                slope_c[a, b] = (slope[0] * first + slope[1] * sroll(first, 4)) + (
                    slope[2] * second + slope[3] * sroll(second, 4)
                )
                ends[a, b] = jnp.where(low_c, first, second)

        def along_b(table):
            return [restrict_four([table[a, b] for b in range(4)]) for a in range(4)]

        def both(table):
            by_b = along_b(table)
            return [restrict_four([by_b[a][j] for a in range(4)]) for j in range(2)]

        by_b = along_b(line)
        by_a = [restrict_four([line[a, b] for a in range(4)]) for b in range(4)]
        flux_z = both(slope_c)
        trace_z = both(ends)
        sources = both({(a, b): restrict_c(src_ref[v, a, b, 0], src_ref[v, a, b, 1]) for a in range(4) for b in range(4)})
        acc = [[None, None], [None, None]]
        for j in range(2):
            value = restrict_four([by_b[a][j] for a in range(4)])
            flux = slopes_four([by_b[a][j] for a in range(4)])
            for i in range(2):
                acc[i][j] = sources[j][i] - 2.0 * value[i]
                waves[0][i][j][v] = flux[i]
        for i in range(2):
            flux = slopes_four([by_a[b][i] for b in range(4)])
            for j in range(2):
                waves[1][i][j][v] = flux[j]
        for d, lo, hi in ((0, by_b[0], by_b[3]), (1, by_a[0], by_a[3])):
            low, step = axis_low(d)
            flag = flags[d]
            flag_before = sroll(flag_ref[d], step) != 0
            for m in range(2):
                right = sroll(jnp.where(flag_before, lo[1 - m], lo[m]), -step)
                left = sroll(jnp.where(flag, hi[1 - m], hi[m]), step)
                jump_right = jnp.where(low, right, 0.0) - hi[m]
                jump_left = jnp.where(low, 0.0, left) - lo[m]
                i, j = (1, m) if d == 0 else (m, 1)
                waves[d][i][j][v] = waves[d][i][j][v] + H4 * jump_right
                acc[i][j] = acc[i][j] + damp * jump_right
                i, j = (0, m) if d == 0 else (m, 0)
                waves[d][i][j][v] = waves[d][i][j][v] - H4 * jump_left
                acc[i][j] = acc[i][j] + damp * jump_left
        beside = []
        for j in range(2):
            turned = [sroll(trace_z[j][i], 4) for i in range(2)]
            beside.append([jnp.where(low_c, lroll(t, 1), lroll(t, -1)) for t in turned])
        for i in range(2):
            for j in range(2):
                jump = jnp.where(flags[2], beside[j][1 - i], beside[j][i]) - trace_z[j][i]
                waves[2][i][j][v] = flux_z[j][i] + sign * jump
                acc_ref[v, i, j] = acc[i][j] + damp * jump
    for d in range(3):
        matrix = [[jac_ref[25 * d + 5 * o + i] for i in range(5)] for o in range(5)]
        for i in range(2):
            for j in range(2):
                for v, value in enumerate(mix(matrix, waves[d][i][j])):
                    acc_ref[v, i, j] = acc_ref[v, i, j] - value
    c = coarse_smooth(smooth_ref, [[[acc_ref[v, i, j] for j in range(2)] for i in range(2)] for v in range(5)])
    put_field(c_ref, c)


def put_field(out_ref, c):
    for v in range(5):
        for i in range(2):
            for j in range(2):
                out_ref[v, i, j] = c[v][i][j]


def get_field(ref):
    return [[[ref[v, i, j] for j in range(2)] for i in range(2)] for v in range(5)]


def add_remote(field, scale, flag_ref, face_ref, rxo, rxe, ryo, rye):
    for d, axis in ((0, "gx"), (1, "gy")):
        is_even = parity(axis)
        low, step = axis_low(d)
        flag = flag_ref[d]
        flag = jnp.where(low, sroll(flag, -step), flag) != 0
        even, odd = ((rxe, rxo), (rye, ryo))[d]
        at = (lambda n, m: (n, m)) if d == 0 else (lambda n, m: (m, n))
        right, left = [], []
        for v in range(5):
            value = scale * jnp.where(is_even, even[v], odd[v])
            swapped = jnp.where(low, sroll(value, -step), sroll(value, step))
            right.append(jnp.where(flag, swapped, value))
            left.append(scale * jnp.where(is_even, odd[v], even[v]))
        upper = [[face_ref[2 * d, 5 * o + i] for i in range(5)] for o in range(5)]
        lower = [[face_ref[2 * d + 1, 5 * o + i] for i in range(5)] for o in range(5)]
        for v, value in enumerate(mix(upper, right)):
            for m, part in enumerate((sroll(value, step), value)):
                i, j = at(1, m)
                field[v][i][j] = field[v][i][j] - jnp.where(low, 0.0, part)
        for v, value in enumerate(mix(lower, left)):
            for m, part in enumerate((value, sroll(value, -step))):
                i, j = at(0, m)
                field[v][i][j] = field[v][i][j] + jnp.where(low, part, 0.0)


def restrict_kernel(local_ref, flag_ref, response_ref, rxo, rxe, ryo, rye, c_ref, xo, xe, yo, ye):
    c = get_field(local_ref)
    add_remote(c, 6.0, flag_ref, response_ref, rxo, rxe, ryo, rye)
    put_field(c_ref, c)
    coarse_faces(c, flag_ref, xo, xe, yo, ye)


def first_local_kernel(
    c_ref, acc_ref, smooth_ref, flag_ref, jac_ref, damp_ref, face_ref, rxo, rxe, ryo, rye, out_ref, rhs_ref
):
    rhs = get_field(acc_ref)
    add_remote(rhs, 1.0, flag_ref, face_ref, rxo, rxe, ryo, rye)
    put_field(rhs_ref, rhs)
    coarse_local_kernel(c_ref, rhs_ref, smooth_ref, flag_ref, jac_ref, damp_ref, out_ref)


def coarse_local_kernel(c_ref, rhs_ref, smooth_ref, flag_ref, jac_ref, damp_ref, out_ref):
    damp = 0.5 * damp_ref[...]
    c = [[[c_ref[v, i, j] for j in range(2)] for i in range(2)] for v in range(5)]
    acc = [[[rhs_ref[v, i, j] - 2.0 * c[v][i][j] for j in range(2)] for i in range(2)] for v in range(5)]
    for d in range(2):
        low, step = axis_low(d)
        flag = flag_ref[d] != 0
        flag_before = sroll(flag_ref[d], step) != 0
        matrix = [[jac_ref[25 * d + 5 * o + i] for i in range(5)] for o in range(5)]
        at = (lambda n, m: (n, m)) if d == 0 else (lambda n, m: (m, n))
        waves = [[[None] * 5, [None] * 5] for _ in range(2)]
        for v in range(5):
            lo = [c[v][at(0, m)[0]][at(0, m)[1]] for m in range(2)]
            hi = [c[v][at(1, m)[0]][at(1, m)[1]] for m in range(2)]
            for m in range(2):
                right = jnp.where(low, sroll(jnp.where(flag_before, lo[1 - m], lo[m]), -step), 0.0)
                left = jnp.where(low, 0.0, sroll(jnp.where(flag, hi[1 - m], hi[m]), step))
                waves[1][m][v] = 0.5 * (right - lo[m])
                waves[0][m][v] = 0.5 * (hi[m] - left)
                i, j = at(1, m)
                acc[v][i][j] = acc[v][i][j] + damp * (right - hi[m])
                i, j = at(0, m)
                acc[v][i][j] = acc[v][i][j] + damp * (left - lo[m])
        for n in range(2):
            for m in range(2):
                i, j = at(n, m)
                for v, value in enumerate(mix(matrix, waves[n][m])):
                    acc[v][i][j] = acc[v][i][j] - value
    low = c_low()
    flag = jnp.where(low, lroll(flag_ref[2], 1), flag_ref[2]) != 0
    half = jnp.where(low, 0.5, -0.5).astype(F32)
    matrix = [[jac_ref[50 + 5 * o + i] for i in range(5)] for o in range(5)]
    turned = [[[sroll(c[v][i][j], 4) for j in range(2)] for i in range(2)] for v in range(5)]
    beside = [
        [[jnp.where(low, lroll(t, 1), lroll(t, -1)) for t in turned[v][i]] for i in range(2)] for v in range(5)
    ]
    for i in range(2):
        for j in range(2):
            wave = []
            for v in range(5):
                next_to = jnp.where(flag, beside[v][1 - i][j], beside[v][i][j])
                wave.append(half * (turned[v][i][j] - next_to))
                acc[v][i][j] = acc[v][i][j] + damp * (next_to - c[v][i][j])
            for v, value in enumerate(mix(matrix, wave)):
                acc[v][i][j] = acc[v][i][j] - value
    change = coarse_smooth(smooth_ref, acc)
    for v in range(5):
        for i in range(2):
            for j in range(2):
                out_ref[v, i, j] = c[v][i][j] + change[v][i][j]


def coarse_kernel(c_ref, flag_ref, response_ref, rxo, rxe, ryo, rye, out_ref, xo, xe, yo, ye):
    c = get_field(c_ref)
    add_remote(c, 1.0, flag_ref, response_ref, rxo, rxe, ryo, rye)
    put_field(out_ref, c)
    coarse_faces(c, flag_ref, xo, xe, yo, ye)


def spread(first, second):
    return first, NEAR * first + FAR * second, FAR * first + NEAR * second, second


def last_kernel(
    c_ref, flag_ref, response_ref, rxo, rxe, ryo, rye, second_ref, out_hbm, out_ref, sems
):
    c = get_field(c_ref)
    add_remote(c, 1.0, flag_ref, response_ref, rxo, rxe, ryo, rye)
    low = c_low()
    copies = []
    for v in range(5):
        by_c = [[None, None], [None, None]]
        for i in range(2):
            for j in range(2):
                value = c[v][i][j]
                inner = FAR * value + NEAR * sroll(value, 4)
                by_c[i][j] = (jnp.where(low, value, inner), jnp.where(low, inner, value))
        lines = [[spread(by_c[i][0][q], by_c[i][1][q]) for i in range(2)] for q in range(2)]
        for part in (slice(0, 2), slice(2, 4)) if v == 4 else (slice(0, 4),):
            for b in range(part.start, part.stop):
                for q in range(2):
                    for a, value in enumerate(spread(lines[q][0][b], lines[q][1][b])):
                        out_ref[v, a, b, q] = second_ref[v, a, b, q] + value
            copy = pltpu.make_async_copy(out_ref.at[v, :, part], out_hbm.at[v, :, part], sems.at[len(copies)])
            copy.start()
            copies.append(copy)
    for copy in copies:
        copy.wait()


FINE = (5, 4, 4, 2, 8, 128)
FINE_MESSAGE = (5, 4, 8, 128)
COARSE = (5, 2, 2, 8, 128)
COARSE_MESSAGE = (5, 8, 128)


def vmem(shape, dtype=F32):
    return pltpu.VMEM(shape, dtype)


def here(array):
    return pltpu.with_memory_space_constraint(array, pltpu.VMEM)


def call(kernel, args, outs, in_hbm=(), out_hbm=(), scratch=(), aliases=None, flops=0):
    in_specs = [
        pl.BlockSpec(memory_space=pltpu.HBM if k in in_hbm else pltpu.VMEM) for k in range(len(args))
    ]
    out_specs = [
        pl.BlockSpec(memory_space=pltpu.HBM if k in out_hbm else pltpu.VMEM) for k in range(len(outs))
    ]
    args = [pltpu.with_memory_space_constraint(a, pltpu.HBM) if k in in_hbm else here(a) for k, a in enumerate(args)]
    return pl.pallas_call(
        kernel,
        out_shape=outs,
        in_specs=in_specs,
        out_specs=out_specs,
        scratch_shapes=scratch,
        input_output_aliases=aliases or {},
        compiler_params=pltpu.CompilerParams(vmem_limit_bytes=8 * 2**20),
        cost_estimate=pl.CostEstimate(flops=flops, bytes_accessed=4 * 2**20, transcendentals=0),
    )(*args)


def partners(axis):
    size = lax.axis_size(axis)
    even = [(i, i ^ 1) for i in range(size)]
    odd = [(i, (i - 1) % size if i % 2 == 0 else (i + 1) % size) for i in range(size)]
    return even, odd


def exchange(xo, xe, yo, ye):
    even_x, odd_x = partners("gx")
    even_y, odd_y = partners("gy")
    xo = lax.ppermute(xo, "gx", odd_x)
    xe = lax.ppermute(xe, "gx", even_x)
    yo = lax.ppermute(yo, "gy", odd_y)
    ye = lax.ppermute(ye, "gy", even_y)
    return xo, xe, yo, ye


def body(source, jacobian, damping, orient, smoother, coarse_smoother):
    source = source.reshape(FINE)
    smoother = smoother.reshape(25, 4, 4, 16, 128)
    coarse_smoother = coarse_smoother.reshape(25, 2, 16, 128)
    jacobian = jacobian.reshape(75, 4, 128)
    damping = damping.reshape(4, 128)
    orient = orient.reshape(3, 4, 128)
    fine_messages = [vmem(FINE_MESSAGE)] * 4
    coarse_messages = [vmem(COARSE_MESSAGE)] * 4

    held = vmem(smoother.shape, smoother.dtype)
    smoother_in = smoother
    source, smoother, first, flag, *sent = call(
        first_kernel,
        (source, smoother_in, orient),
        [vmem(FINE), held, vmem(FINE), vmem((3, 8, 128), jnp.int32)] + fine_messages,
        in_hbm=(0, 1, 2),
        scratch=[pltpu.SemaphoreType.DMA((5,)), pltpu.VMEM((3, 4, 128), jnp.int32), pltpu.SemaphoreType.DMA],
        flops=2 * 25 * 64 * 512,
    )
    got = exchange(*sent)
    _, first, acc, jac8, damp8, face, second, scaled = call(
        first_volume_kernel,
        (smoother_in, source, smoother, first, flag, jacobian, damping),
        [held, vmem(FINE), vmem(FINE), vmem((75, 8, 128)), vmem((8, 128)), vmem((4, 25, 8, 128)), vmem(FINE), vmem((12, 25, 2, 8, 128))],
        in_hbm=(0,),
        aliases={2: 0, 3: 1},
        scratch=[pltpu.SemaphoreType.DMA],
        flops=9 * 2**20,
    )
    part = vmem((2, 5, 4, 2, 8, 128))
    second, x_part = call(
        second_x_kernel,
        (acc, first, scaled, flag, face, *got[:2], second),
        [vmem(FINE), part],
        aliases={7: 0},
        flops=2**20,
    )
    second, *sent = call(
        second_kernel,
        (acc, first, scaled, flag, face, *got[2:], x_part, second),
        [vmem(FINE)] + coarse_messages,
        aliases={8: 0},
        scratch=[pltpu.VMEM((2, 5, 4, 2, 8, 128), F32)],
        flops=2 * 2**20,
    )
    got = exchange(*sent)
    (response,) = call(response_kernel, (coarse_smoother, face), [vmem((4, 25, 8, 128))], flops=2**20)
    acc, coarse = call(
        restricted_volume_kernel,
        (source, second, flag, jac8, damp8, coarse_smoother),
        [vmem(COARSE), vmem(COARSE)],
        flops=4 * 2**20,
    )
    coarse, *sent = call(
        restrict_kernel, (coarse, flag, response, *got), [vmem(COARSE)] + coarse_messages, flops=2**20
    )
    second_got, got = got, exchange(*sent)
    coarse, rhs = call(
        first_local_kernel,
        (coarse, acc, coarse_smoother, flag, jac8, damp8, face, *second_got),
        [vmem(COARSE), vmem(COARSE)],
        flops=4 * 2**20,
    )
    coarse, *sent = call(
        coarse_kernel, (coarse, flag, response, *got), [vmem(COARSE)] + coarse_messages, flops=2**20
    )
    got = exchange(*sent)
    (coarse,) = call(
        coarse_local_kernel, (coarse, rhs, coarse_smoother, flag, jac8, damp8), [vmem(COARSE)], flops=4 * 2**20
    )
    (out,) = call(
        last_kernel,
        (coarse, flag, response, *got, second),
        [jax.ShapeDtypeStruct(FINE, F32)],
        out_hbm=(0,),
        scratch=[pltpu.VMEM(FINE, F32), pltpu.SemaphoreType.DMA((6,))],
        flops=2**20,
    )
    return out.reshape(5, 4, 4, 4, 2, 2, 128)


def solution(mesh):
    in_specs = (
        P(None, None, None, None, "gx", "gy", None),
        P(None, None, None, "gx", "gy", None),
        P("gx", "gy", None),
        P(None, "gx", "gy", None),
        P(None, None, None, None, None, "gx", "gy", None),
        P(None, None, None, None, None, "gx", "gy", None),
    )
    out_specs = P(None, None, None, None, "gx", "gy", None)
    return jax.shard_map(body, mesh=mesh, in_specs=in_specs, out_specs=out_specs, check_vma=False)
```
